32 devices in a mesh: groups: 1, rec: 32 (over z, y, x, core).
Axes of the slice: x: 2, y: 2, z: 4, core: 2. Of those that a mesh axis runs over, the one named last changes fastest.
Arguments:
- records: bfloat16 [4, 512, 2, 128], P(None, ('groups', 'rec')), may hold values from -6 to 6
- dest: int32 [512, 4], P('groups'), may hold values from 0 to 31, as said below
- w_in: bfloat16 [64, 36], replicated, may hold values from -1 to 1
- b_in: float32 [64], replicated, may hold values from -3 to 3
- w_mid: bfloat16 [64, 64], replicated, may hold values from -0.75 to 0.75
- b_mid: float32 [64], replicated, may hold values from -3 to 3
- w_out: bfloat16 [64, 36], replicated, may hold values from -0.25 to 0.25
Outputs:
- residual: float32 [4, 512, 2, 128], P(None, ('groups', 'rec'))
- grad_w_in: float32 [64, 36], P('groups')
- grad_b_in: float32 [64], P('groups')
- grad_w_mid: float32 [64, 64], P('groups')
- grad_b_mid: float32 [64], P('groups')
- grad_w_out: float32 [64, 36], P('groups')
The draws below stay inside these ranges and needn't reach their ends.
Inputs may be any that keep to these rules, and one draw needn't show every extreme that they name: `dest`: from the 16 blocks of one record device at most 2 copies go to one owner; in every draw one owner receives exactly 2 copies from every record device.
All inputs are finite; a program needn't handle non-finite values.
Results may differ from the reference program's by a relative error of at most 0.0005.
The reference program's roundings to bfloat16 on the way count: a program that leaves them out, or rounds other values in their place, can miss the bound.
Values may be sent and summed in bfloat16 or wider, within the bound.
No kernel may reach another device: no remote copies, remote signals or barrier semaphores. Data moves between devices by JAX's collectives and lax.ppermute only.
A program may use at most 192 MiB of HBM per device.

```python
import math
import jax
import jax.numpy as jnp
from jax import lax

C = 64
CMP = 4
VES = 4
CAP = 2
TR = 2
S = 128
CH = 16
BLOCKS = 512
N_REC = 32


def draw_dest(key, part):
    total = VES * CH
    slots = CAP * N_REC
    key_busy, key_rows = jax.random.split(jax.random.fold_in(key, 17))
    busy = jax.random.randint(key_busy, (), 0, N_REC)
    tokens = jnp.arange(slots, dtype=jnp.int32)
    owner = tokens // CAP

    def one_device(row_key):
        key_score, key_perm = jax.random.split(row_key)
        score = jax.random.randint(key_score, (slots,), 0, 1048576) * slots + tokens
        score = jnp.where(owner == busy, tokens - slots, score)
        order = jnp.argsort(score, stable=True)
        chosen = owner[order[:total]]
        return chosen[jax.random.permutation(key_perm, total)]
    rows = jax.vmap(one_device)(jax.random.split(key_rows, N_REC))
    return rows.reshape(N_REC * CH, VES).astype(jnp.int32)


def steps_of(own_key, dims, pieces, low, high):
    gain = 1.0
    for axis_at, shards_of in pieces:
        draws = jax.random.uniform(jax.random.fold_in(jax.random.fold_in(own_key, 6), axis_at), (shards_of,), jnp.float32, low / len(pieces), high / len(pieces))
        gain = gain * jnp.repeat(jnp.exp(draws), dims[axis_at] // shards_of).reshape((-1,) + (1,) * (len(dims) - 1 - axis_at))
    return gain


def normal_values(stream_key, shape, scale, reach, cuts=(), kind=jnp.bfloat16):
    loudness = steps_of(stream_key, shape, cuts, -0.22, 0.18) if cuts else 1.0
    drawn = jax.random.normal(stream_key, shape, jnp.float32) * scale * loudness
    return jnp.minimum(jnp.maximum(drawn, -reach), reach).astype(kind)


def setup_inputs(seed: int = 0, part: int = 0) -> dict:
    arg_keys = jax.random.split(jax.random.key(seed), 8)
    part_keys = jax.random.split(jax.random.fold_in(arg_keys[7], part), 8)
    return {
        "records": normal_values(part_keys[0], (CMP, BLOCKS, TR, S), 1.0, 6.0, ((1, 32),)),
        "dest": draw_dest(jax.random.fold_in(jax.random.fold_in(arg_keys[7], part), 71), part),
        "w_in": normal_values(arg_keys[2], (C, CMP * 9), (CMP * 9) ** -0.5, 1.0),
        "b_in": normal_values(arg_keys[3], (C,), 0.5, 3.0, (), jnp.float32),
        "w_mid": normal_values(arg_keys[4], (C, C), C ** -0.5, 0.75),
        "b_mid": normal_values(arg_keys[5], (C,), 0.5, 3.0, (), jnp.float32),
        "w_out": normal_values(arg_keys[6], (C, CMP * 9), (C * 9) ** -0.5, 0.25),
    }


def patches(field, flip):
    count, height, width = field.shape
    padded = jnp.pad(field, ((0, 0), (1, 1), (1, 1)))
    taps = []
    for row in range(3):
        for col in range(3):
            top = 2 - row if flip else row
            left = 2 - col if flip else col
            taps.append(padded[:, top:top + height, left:left + width])
    return jnp.stack(taps, axis=1).reshape(count * 9, height, width)

def collect(terms, parts):
    height, width = (terms.shape[1], terms.shape[2])
    stacked = jnp.pad(terms.reshape(parts, 9, height, width), ((0, 0), (0, 0), (1, 1), (1, 1)))
    total = jnp.zeros((parts, height, width), jnp.float32)
    for row in range(3):
        for col in range(3):
            total = total + stacked[:, 3 * row + col, row:row + height, col:col + width]
    return total

def silu_grad(z):
    sig = jax.nn.sigmoid(z)
    return sig * (1.0 + z * (1.0 - sig))

def forward(image, w_in, b_in, w_mid, b_mid, w_out):
    inputs = patches(image, False)
    z1 = jnp.einsum('cu,uhw->chw', w_in.astype(jnp.float32), inputs.astype(jnp.float32)) + b_in[:, None, None]
    a1 = jax.nn.silu(z1).astype(jnp.bfloat16)
    z2 = jnp.einsum('dc,chw->dhw', w_mid.astype(jnp.float32), a1.astype(jnp.float32)) + b_mid[:, None, None]
    a2 = jax.nn.silu(z2).astype(jnp.bfloat16)
    terms = jnp.einsum('cu,chw->uhw', w_out.astype(jnp.float32), a2.astype(jnp.float32))
    estimate = collect(terms, image.shape[0])
    return (estimate, (inputs, z1, a1, z2, a2))

def backward(grad_image, w_mid, w_out, saved):
    inputs, z1, a1, z2, a2 = saved
    flipped = patches(grad_image, True).astype(jnp.float32)
    dw_out = jnp.einsum('chw,uhw->cu', a2.astype(jnp.float32), flipped)
    da2 = jnp.einsum('cu,uhw->chw', w_out.astype(jnp.float32), flipped)
    dz2 = (da2 * silu_grad(z2)).astype(jnp.bfloat16).astype(jnp.float32)
    dw_mid = jnp.einsum('dhw,chw->dc', dz2, a1.astype(jnp.float32))
    db_mid = lax.optimization_barrier(jnp.sum(dz2, axis=(1, 2)))
    da1 = jnp.einsum('dc,dhw->chw', w_mid.astype(jnp.float32), dz2)
    dz1 = (da1 * silu_grad(z1)).astype(jnp.bfloat16).astype(jnp.float32)
    dw_in = jnp.einsum('chw,uhw->cu', dz1, inputs.astype(jnp.float32))
    db_in = lax.optimization_barrier(jnp.sum(dz1, axis=(1, 2)))
    return (dw_in, db_in, dw_mid, db_mid, dw_out)

def reference(records, dest, w_in, b_in, w_mid, b_mid, w_out):
    count = N_REC
    items = CH * VES
    table = dest.reshape(count, items).astype(jnp.int32)
    owners = jnp.arange(count, dtype=jnp.int32)
    sources = jnp.arange(count, dtype=jnp.int32)[:, None] * CH + jnp.arange(items, dtype=jnp.int32)[None, :] // VES
    ranks_k = jnp.arange(CAP, dtype=jnp.int32)

    def owner_index(owner):
        hits = (table == owner).astype(jnp.int32)
        ranks = jnp.cumsum(hits, axis=1) - 1
        chosen = hits[:, None, :] * (ranks[:, None, :] == ranks_k[None, :, None]).astype(jnp.int32)
        pick = lax.optimization_barrier(jnp.sum(chosen * sources[:, None, :], axis=2)).reshape(count * CAP)
        valid = lax.optimization_barrier(jnp.sum(chosen, axis=2)).reshape(count * CAP)
        return (pick.astype(jnp.int32), valid)

    def assemble(field, owner):
        pick, valid = owner_index(owner)
        taken = jnp.take(field, pick, axis=1) * valid.astype(field.dtype)[None, :, None, None]
        return taken.reshape(CMP, count * CAP * TR, S)

    def make_estimate(owner):
        estimate, saved = forward(assemble(records, owner), w_in, b_in, w_mid, b_mid, w_out)
        return estimate.astype(jnp.bfloat16).reshape(CMP, count * CAP, TR, S)
    estimates = lax.map(make_estimate, owners)
    hits3 = (table[:, :, None] == owners[None, None, :]).astype(jnp.int32)
    rank = lax.optimization_barrier(jnp.sum((jnp.cumsum(hits3, axis=1) - 1) * hits3, axis=2))
    slot = (jnp.arange(count, dtype=jnp.int32)[:, None] * CAP + rank).reshape(-1).astype(jnp.int32)
    values = estimates[table.reshape(-1), :, slot]
    values = values.astype(jnp.float32).reshape(count, CH, VES, CMP, TR, S)
    reblend = lax.optimization_barrier(jnp.sum(values, axis=2)).reshape(count * CH, CMP, TR, S)
    reblend = jnp.transpose(reblend, (1, 0, 2, 3))
    residual = reblend - records.astype(jnp.float32)
    rounded = residual.astype(jnp.bfloat16)

    def owner_grads(owner):
        estimate, saved = forward(assemble(records, owner), w_in, b_in, w_mid, b_mid, w_out)
        return backward(assemble(rounded, owner), w_mid, w_out, saved)
    terms = lax.map(owner_grads, owners)
    scale = 1.0 / math.sqrt(CMP * BLOCKS * TR * S)
    grads = tuple((lax.optimization_barrier(jnp.sum(term, axis=0)) * scale for term in terms))
    return (residual, grads[0], grads[1], grads[2], grads[3], grads[4])
```

```python
import functools
import math

import jax
import jax.numpy as jnp
from jax import lax
from jax.experimental import pallas as pl
from jax.experimental.pallas import tpu as pltpu
from jax.sharding import PartitionSpec as P

CAP = 2
VMEM = pl.BlockSpec(memory_space=pltpu.VMEM)
SMEM = pl.BlockSpec(memory_space=pltpu.SMEM)
RESIDENT = 24 << 20


def run(start, step, end, steps, blocked):
    if blocked:
        n = pl.program_id(0)
        pl.when(n == 0)(start)
        step(n, 0)
        pl.when(n == steps - 1)(end)
        return
    start()
    lax.fori_loop(0, steps, lambda n, carry: step(n, n), None)
    end()


def group_of(owners):
    for size in (4, 2):
        if owners % size == 0:
            return size
    return 1


def fill_table(table, wide, pieces, tiles, flip, fill):
    for n, piece in enumerate(pieces):
        x = piece[...].astype(jnp.float32)
        samples = x.shape[2]
        lane = lax.broadcasted_iota(jnp.int32, x.shape, 2)
        before = jnp.where(lane == 0, 0.0, pltpu.roll(x, 1, 2))
        after = jnp.where(lane == samples - 1, 0.0, pltpu.roll(x, samples - 1, 2))
        at = pl.ds(n * tiles, tiles)
        wide[at, 0:4, :] = after if flip else before
        wide[at, 4:8, :] = x
        wide[at, 8:12, :] = before if flip else after
    last = len(pieces) * tiles
    wide[pl.ds(last, 2), 0:12, :] = jnp.zeros((2, 12, wide.shape[2]), jnp.float32)
    wide[:, 12:16, :] = jnp.full((last + 2, 4, wide.shape[2]), fill, jnp.float32)
    table[...] = wide[...].astype(jnp.bfloat16)


def act(y):
    t = jnp.tanh(y)
    q = 1.0 + t
    a = y * q
    return t, q, a


def own_of(x, group, samples):
    return jnp.concatenate(
        [x[:, (u * 6 + 1) * samples : (u * 6 + 5) * samples] for u in range(group)], axis=1
    )


def forward_kernel(
    group, blocked, pick, meta, left, mine, right, w1, w2, w3,
    res, g, table, a1_ref, a2_ref, d1_ref, d2_ref, wide, est,
):
    tiles, parts, samples = mine.shape
    owners = pick.shape[1]
    items = tiles // 2 * 4
    has_left = meta[items].astype(jnp.float32)
    has_right = meta[items + 1].astype(jnp.float32)
    lane = lax.broadcasted_iota(jnp.int32, (8, samples), 1)
    low = (lane > 0).astype(jnp.float32)
    high = (lane < samples - 1).astype(jnp.float32)

    def start():
        fill_table(table, wide, (left, mine, right), tiles, False, 1.0)

    def step(n, block):
        tile = []
        for u in range(group):
            e = n * group + u
            line = []
            for r in range(4):
                at = pick[r, e]
                line += [table[at], table[at + 1]]
            tile.append(line)
        rhs = jnp.concatenate(
            [
                jnp.concatenate([tile[u][i + h] for u in range(group) for h in range(6)], axis=1)
                for i in range(3)
            ],
            axis=0,
        )
        y1 = jnp.dot(w1[...], rhs, preferred_element_type=jnp.float32)
        t, q, a = act(y1)
        a1 = a.astype(jnp.bfloat16)
        a1_ref[block] = own_of(a1, group, samples)
        d1_ref[block] = own_of(q + a * (1.0 - t), group, samples)
        ones = jnp.ones((16, a1.shape[1]), jnp.bfloat16)
        y2 = jnp.dot(
            w2[...], jnp.concatenate([a1, ones], axis=0), preferred_element_type=jnp.float32
        )
        t, q, a = act(y2)
        d2_ref[block] = own_of(q + a * (1.0 - t), group, samples)
        cut = []
        for u in range(group):
            for h in range(6):
                part = a[:, (u * 6 + h) * samples : (u * 6 + h + 1) * samples]
                if h == 0:
                    part = part * has_left
                if h == 5:
                    part = part * has_right
                cut.append(part.astype(jnp.bfloat16))
        a2_ref[block] = jnp.concatenate(
            [cut[u * 6 + h + 1] for u in range(group) for h in range(4)], axis=1
        )
        rhs = jnp.concatenate(
            [
                jnp.concatenate([cut[u * 6 + h + i] for u in range(group) for h in range(4)], axis=1)
                for i in range(3)
            ],
            axis=0,
        )
        terms = jnp.dot(w3[...], rhs, preferred_element_type=jnp.float32)
        for k in range(group * 4):
            part = terms[:, k * samples : (k + 1) * samples]
            total = (
                part[8:16]
                + pltpu.roll(part[0:8], 1, 1) * low
                + pltpu.roll(part[16:24], samples - 1, 1) * high
            )
            est[n * group * 4 + k] = total.astype(jnp.bfloat16).astype(jnp.float32)

    def end():
        for c in range(tiles // 2):
            at = [meta[c * 4 + v] for v in range(4)]
            for k in range(2):
                total = (est[at[0] + k] + est[at[1] + k]) + (est[at[2] + k] + est[at[3] + k])
                value = total[0:parts] - mine[c * 2 + k].astype(jnp.float32)
                res[c * 2 + k] = value
                g[c * 2 + k] = value.astype(jnp.bfloat16)

    run(start, step, end, owners // group, blocked)


def backward_kernel(
    group, blocked, pick, left, mine, right, wo, wm, table, a1_ref, a2_ref, d1_ref, d2_ref,
    out, gtable, wide, acc_in, acc_mid, acc_out,
):
    tiles, parts, samples = mine.shape
    owners = pick.shape[1]
    channels = wo.shape[0]
    nt = functools.partial(
        lax.dot_general,
        dimension_numbers=(((1,), (1,)), ((), ())),
        preferred_element_type=jnp.float32,
    )

    def start():
        fill_table(gtable, wide, (left, mine, right), tiles, True, 0.0)
        acc_in[...] = jnp.zeros_like(acc_in)
        acc_mid[...] = jnp.zeros_like(acc_mid)
        acc_out[...] = jnp.zeros_like(acc_out)

    def step(n, block):
        tile, gtile = [], []
        for u in range(group):
            e = n * group + u
            at = [pick[r, e] for r in range(4)]
            tile.append(
                [table[at[0] + 1]] + [table[at[r] + k] for r in (1, 2) for k in (0, 1)] + [table[at[3]]]
            )
            gtile.append(
                [gtable[at[0] + 1]] + [gtable[at[r] + k] for r in (1, 2) for k in (0, 1)] + [gtable[at[3]]]
            )
        fields = jnp.concatenate(
            [
                jnp.concatenate([gtile[u][2 - i + h] for u in range(group) for h in range(4)], axis=1)
                for i in range(3)
            ],
            axis=0,
        )
        inputs = jnp.concatenate(
            [
                jnp.concatenate([tile[u][i + h] for u in range(group) for h in range(4)], axis=1)
                for i in range(3)
            ],
            axis=0,
        )
        da2 = jnp.dot(wo[...], fields, preferred_element_type=jnp.float32)
        dz2 = (da2 * d2_ref[block]).astype(jnp.bfloat16)
        acc_out[...] += nt(fields, a2_ref[block])
        da1 = jnp.dot(wm[...], dz2, preferred_element_type=jnp.float32)
        ones = jnp.ones((16, dz2.shape[1]), jnp.bfloat16)
        acc_mid[...] += nt(jnp.concatenate([a1_ref[block], ones], axis=0), dz2)
        dz1 = (da1 * d1_ref[block]).astype(jnp.bfloat16)
        acc_in[...] += nt(inputs, dz1)
    def end():
        out[0:48, 0:channels] = acc_in[...]
        out[0:48, channels : 2 * channels] = acc_out[...]
        out[12:13, 0:channels] = acc_mid[channels : channels + 1, :]
        mid = acc_mid[0:channels, :].T
        out[48 : 48 + channels // 2, 0:channels] = mid[0 : channels // 2]
        out[48 : 48 + channels // 2, channels : 2 * channels] = mid[channels // 2 : channels]

    run(start, step, end, owners // group, blocked)


def finish_kernel(scale, parts, *refs):
    total = None
    terms, (g_in, g_bin, g_mid, g_bmid, g_out, held) = refs[:-6], refs[-6:]
    values = [ref[...] for ref in terms]
    while len(values) > 1:
        values = [values[k] + values[k + 1] for k in range(0, len(values), 2)]
    held[...] = values[0] * scale
    channels = g_mid.shape[0]
    for o in range(parts):
        for i in range(3):
            for j in range(3):
                row = held[i * 16 + j * 4 + o : i * 16 + j * 4 + o + 1, :]
                at = o * 9 + 3 * i + j
                g_in[at : at + 1, :] = row[:, 0:channels]
                g_out[at : at + 1, :] = row[:, channels : 2 * channels]
    g_bin[...] = held[28:29, 0:channels]
    g_bmid[...] = held[12:13, 0:channels]
    half = channels // 2
    g_mid[0:half] = held[48 : 48 + half, 0:channels]
    g_mid[half:channels] = held[48 : 48 + half, channels : 2 * channels]


def split3(b):
    high = lax.reduce_precision(b, 8, 7)
    rest = b - high
    mid = lax.reduce_precision(rest, 8, 7)
    return jnp.stack([high, mid, rest - mid, jnp.zeros_like(b)], axis=1).astype(jnp.bfloat16)


def taps(w, extra):
    channels = w.shape[0]
    parts = w.shape[1] // 9
    by_row = w.reshape(channels, parts, 3, 3).transpose(0, 2, 3, 1).reshape(channels, 3, 3 * parts)
    none = jnp.zeros((channels, 4), w.dtype)
    side = jnp.stack([none, none if extra is None else extra, none], axis=1)
    return jnp.concatenate([by_row, side], axis=2).reshape(channels, 48)


def local(records, dest, w_in, b_in, w_mid, b_mid, w_out):
    count = lax.axis_size("rec")
    me = lax.axis_index("rec")
    parts, blocks, traces, samples = records.shape
    ves = dest.shape[1]
    items = blocks * ves
    tiles = blocks * traces
    channels = w_in.shape[0]
    group = group_of(count)
    steps = count // group
    width = group * 4 * samples
    up = [(s, s + 1) for s in range(count - 1)]
    down = [(s + 1, s) for s in range(count - 1)]

    flat = records.transpose(1, 2, 0, 3).reshape(tiles, parts, samples)
    from_left = lax.ppermute(flat, "rec", up)
    from_right = lax.ppermute(flat, "rec", down)

    near = lax.dynamic_slice_in_dim(
        jnp.pad(dest, ((blocks, blocks), (0, 0)), constant_values=-1), me * blocks, 3 * blocks, 0
    ).reshape(3, items)
    order = jnp.arange(items, dtype=jnp.int32)
    same = (near[:, :, None] == near[:, None, :]) & (order[None, :] < order[:, None])[None]
    rank = jnp.sum(same.astype(jnp.int32), axis=2)
    slot = jnp.where(near < 0, -1, near * CAP + rank)
    of_line = jnp.stack([slot[0], slot[1], slot[1], slot[2]])
    rank_of_line = jnp.array([1, 0, 1, 0], jnp.int32)
    first = jnp.array([0, tiles, tiles, 2 * tiles], jnp.int32)
    empty = 3 * tiles
    want = jnp.arange(count, dtype=jnp.int32)[None, :] * CAP + rank_of_line[:, None]
    place = first[:, None] + (order // ves * 2)[None, :] - empty
    pick = empty + jnp.sum(
        jnp.where(of_line[:, None, :] == want[:, :, None], place[:, None, :], 0), axis=2
    )
    meta = jnp.concatenate(
        [slot[1] * 2, jnp.stack([me > 0, me < count - 1]).astype(jnp.int32)]
    )

    half = jnp.bfloat16(0.5)
    w1 = taps(w_in, split3(b_in)) * half
    w2 = jnp.concatenate(
        [w_mid, split3(b_mid), jnp.zeros((channels, 12), jnp.bfloat16)], axis=1
    ) * half
    w3 = jnp.pad(
        w_out.reshape(channels, parts, 3, 3).transpose(3, 1, 2, 0), ((0, 0), (0, 4), (0, 0), (0, 0))
    ).reshape(24, 3 * channels)
    wo = taps(w_out, None) * half
    wm = w_mid.T * half

    f32, bf16 = jnp.float32, jnp.bfloat16
    shape = (steps, channels, width)
    blocked = 12 * math.prod(shape) > RESIDENT
    saved = [
        jax.ShapeDtypeStruct(shape, kind) if blocked else pltpu.VMEM(shape, kind)
        for kind in (bf16, bf16, f32, f32)
    ]
    held = [VMEM] * 4
    if blocked:
        held = [pl.BlockSpec((1, channels, width), lambda n: (n, 0, 0))] * 4
    grid = (steps,) if blocked else ()
    params = pltpu.CompilerParams(vmem_limit_bytes=28 << 20)
    res, g, table, a1, a2, d1, d2 = pl.pallas_call(
        functools.partial(forward_kernel, group, blocked),
        grid=grid,
        out_shape=[
            jax.ShapeDtypeStruct((tiles, parts, samples), f32),
            jax.ShapeDtypeStruct((tiles, parts, samples), bf16),
            pltpu.VMEM((3 * tiles + 2, 16, samples), bf16),
            *saved,
        ],
        in_specs=[SMEM, SMEM] + [VMEM] * 6,
        out_specs=[VMEM] * 3 + held,
        scratch_shapes=[
            pltpu.VMEM((3 * tiles + 2, 16, samples), f32),
            pltpu.VMEM((count * 4, 8, samples), f32),
        ],
        compiler_params=params,
        name="forward",
    )(pick, meta, from_left, flat, from_right, w1, w2, w3)

    g_left = lax.ppermute(g, "rec", up)
    g_right = lax.ppermute(g, "rec", down)
    sums = pl.pallas_call(
        functools.partial(backward_kernel, group, blocked),
        grid=grid,
        out_shape=jax.ShapeDtypeStruct((48 + channels // 2, 2 * channels), f32),
        in_specs=[SMEM] + [VMEM] * 6 + held,
        out_specs=VMEM,
        scratch_shapes=[
            pltpu.VMEM((3 * tiles + 2, 16, samples), bf16),
            pltpu.VMEM((3 * tiles + 2, 16, samples), f32),
            pltpu.VMEM((48, channels), f32),
            pltpu.VMEM((channels + 16, channels), f32),
            pltpu.VMEM((48, channels), f32),
        ],
        compiler_params=params,
        name="backward",
    )(pick, g_left, g, g_right, wo, wm, table, a1, a2, d1, d2)

    if count & (count - 1):
        terms = [lax.psum(sums, "rec")]
    else:
        terms = [sums]
        at = 1
        while at < count:
            wide = 2 if at == 1 or 2 * at == count else 4
            value = terms[0]
            if len(terms) == 2:
                value = terms[0] + terms[1]
            if len(terms) == 4:
                value = (terms[0] + terms[1]) + (terms[2] + terms[3])
            terms = [value] + [
                lax.ppermute(value, "rec", [(s, s ^ (k * at)) for s in range(count)])
                for k in range(1, wide)
            ]
            at *= wide

    scale = 1.0 / math.sqrt(parts * blocks * count * traces * samples)
    g_in, g_bin, g_mid, g_bmid, g_out = pl.pallas_call(
        functools.partial(finish_kernel, scale, parts),
        out_shape=[
            jax.ShapeDtypeStruct(shape, f32)
            for shape in (
                (parts * 9, channels), (1, channels), (channels, channels), (1, channels),
                (parts * 9, channels),
            )
        ],
        in_specs=[VMEM] * len(terms),
        out_specs=[VMEM] * 5,
        scratch_shapes=[pltpu.VMEM(sums.shape, f32)],
        name="finish",
    )(*terms)
    residual = res.reshape(blocks, traces, parts, samples).transpose(2, 0, 1, 3)
    return (
        residual,
        g_in.T,
        g_bin.reshape(channels),
        g_mid,
        g_bmid.reshape(channels),
        g_out.T,
    )


def solution(mesh):
    return jax.shard_map(
        local,
        mesh=mesh,
        in_specs=(
            P(None, ("groups", "rec"), None, None),
            P("groups", None),
            P(),
            P(),
            P(),
            P(),
            P(),
        ),
        out_specs=(
            P(None, ("groups", "rec"), None, None),
            P("groups", None),
            P("groups"),
            P("groups", None),
            P("groups"),
            P("groups", None),
        ),
        check_vma=False,
    )
```

```python
import functools
import math

import jax
import jax.numpy as jnp
from jax import lax
from jax.experimental import pallas as pl
from jax.experimental.pallas import tpu as pltpu
from jax.sharding import PartitionSpec as P

CAP = 2
VMEM = pl.BlockSpec(memory_space=pltpu.VMEM)
SMEM = pl.BlockSpec(memory_space=pltpu.SMEM)
RESIDENT = 24 << 20


def run(start, step, end, steps, blocked):
    if blocked:
        n = pl.program_id(0)
        pl.when(n == 0)(start)
        step(n, 0)
        pl.when(n == steps - 1)(end)
        return
    start()
    lax.fori_loop(0, steps, lambda n, carry: step(n, n), None)
    end()


def group_of(owners):
    for size in (4, 2):
        if owners % size == 0:
            return size
    return 1


def fill_table(table, wide, pieces, tiles, flip, fill):
    for n, piece in enumerate(pieces):
        x = piece[...].astype(jnp.float32)
        samples = x.shape[2]
        lane = lax.broadcasted_iota(jnp.int32, x.shape, 2)
        before = jnp.where(lane == 0, 0.0, pltpu.roll(x, 1, 2))
        after = jnp.where(lane == samples - 1, 0.0, pltpu.roll(x, samples - 1, 2))
        at = pl.ds(n * tiles, tiles)
        wide[at, 0:4, :] = after if flip else before
        wide[at, 4:8, :] = x
        wide[at, 8:12, :] = before if flip else after
    last = len(pieces) * tiles
    wide[pl.ds(last, 2), 0:12, :] = jnp.zeros((2, 12, wide.shape[2]), jnp.float32)
    wide[:, 12:16, :] = jnp.full((last + 2, 4, wide.shape[2]), fill, jnp.float32)
    table[...] = wide[...].astype(jnp.bfloat16)


def act(y):
    t = jnp.tanh(y)
    q = 1.0 + t
    a = y * q
    return t, q, a


def own_of(x, group, samples):
    return jnp.concatenate(
        [x[:, (u * 6 + 1) * samples : (u * 6 + 5) * samples] for u in range(group)], axis=1
    )


def forward_kernel(
    group, blocked, idx, left, mine, right, w1, w2, w3,
    res, g, table, a1_ref, a2_ref, d1_ref, d2_ref, wide, est,
):
    tiles, parts, samples = mine.shape
    count = lax.axis_size("rec")
    me = lax.axis_index("rec")
    has_left = (me > 0).astype(jnp.float32)
    has_right = (me < count - 1).astype(jnp.float32)
    lane = lax.broadcasted_iota(jnp.int32, (8, samples), 1)
    low = (lane > 0).astype(jnp.float32)
    high = (lane < samples - 1).astype(jnp.float32)

    def start():
        fill_table(table, wide, (left, mine, right), tiles, False, 1.0)

    def step(n, block):
        tile = []
        for u in range(group):
            e = n * group + u
            line = []
            for r in range(4):
                at = idx[r, e]
                line += [table[at], table[at + 1]]
            tile.append(line)
        rhs = jnp.concatenate(
            [
                jnp.concatenate([tile[u][i + h] for u in range(group) for h in range(6)], axis=1)
                for i in range(3)
            ],
            axis=0,
        )
        y1 = jnp.dot(w1[...], rhs, preferred_element_type=jnp.float32)
        t, q, a = act(y1)
        a1 = a.astype(jnp.bfloat16)
        a1_ref[block] = own_of(a1, group, samples)
        d1_ref[block] = own_of(q + a * (1.0 - t), group, samples)
        ones = jnp.ones((16, a1.shape[1]), jnp.bfloat16)
        y2 = jnp.dot(
            w2[...], jnp.concatenate([a1, ones], axis=0), preferred_element_type=jnp.float32
        )
        t, q, a = act(y2)
        d2_ref[block] = own_of(q + a * (1.0 - t), group, samples)
        cut = []
        for u in range(group):
            for h in range(6):
                part = a[:, (u * 6 + h) * samples : (u * 6 + h + 1) * samples]
                if h == 0:
                    part = part * has_left
                if h == 5:
                    part = part * has_right
                cut.append(part.astype(jnp.bfloat16))
        a2_ref[block] = jnp.concatenate(
            [cut[u * 6 + h + 1] for u in range(group) for h in range(4)], axis=1
        )
        rhs = jnp.concatenate(
            [
                jnp.concatenate([cut[u * 6 + h + i] for u in range(group) for h in range(4)], axis=1)
                for i in range(3)
            ],
            axis=0,
        )
        terms = jnp.dot(w3[...], rhs, preferred_element_type=jnp.float32)
        for k in range(group * 4):
            part = terms[:, k * samples : (k + 1) * samples]
            total = (
                part[8:16]
                + pltpu.roll(part[0:8], 1, 1) * low
                + pltpu.roll(part[16:24], samples - 1, 1) * high
            )
            est[n * group * 4 + k] = total.astype(jnp.bfloat16).astype(jnp.float32)

    def end():
        for c in range(tiles // 2):
            at = [idx[4 + v, tiles // 2 + c] for v in range(4)]
            for k in range(2):
                total = (est[at[0] + k] + est[at[1] + k]) + (est[at[2] + k] + est[at[3] + k])
                value = total[0:parts] - mine[c * 2 + k].astype(jnp.float32)
                for o in range(parts):
                    res[o, c, k : k + 1, :] = value[o : o + 1]
                g[c * 2 + k] = value.astype(jnp.bfloat16)

    run(start, step, end, count // group, blocked)


def backward_kernel(
    group, blocked, idx, left, mine, right, wo, wm, table, a1_ref, a2_ref, d1_ref, d2_ref,
    out, gtable, wide, acc_in, acc_mid, acc_out,
):
    tiles, parts, samples = mine.shape
    owners = lax.axis_size("rec")
    channels = wo.shape[0]
    nt = functools.partial(
        lax.dot_general,
        dimension_numbers=(((1,), (1,)), ((), ())),
        preferred_element_type=jnp.float32,
    )

    def start():
        fill_table(gtable, wide, (left, mine, right), tiles, True, 0.0)
        acc_in[...] = jnp.zeros_like(acc_in)
        acc_mid[...] = jnp.zeros_like(acc_mid)
        acc_out[...] = jnp.zeros_like(acc_out)

    def step(n, block):
        tile, gtile = [], []
        for u in range(group):
            e = n * group + u
            at = [idx[r, e] for r in range(4)]
            tile.append(
                [table[at[0] + 1]] + [table[at[r] + k] for r in (1, 2) for k in (0, 1)] + [table[at[3]]]
            )
            gtile.append(
                [gtable[at[0] + 1]] + [gtable[at[r] + k] for r in (1, 2) for k in (0, 1)] + [gtable[at[3]]]
            )
        fields = jnp.concatenate(
            [
                jnp.concatenate([gtile[u][2 - i + h] for u in range(group) for h in range(4)], axis=1)
                for i in range(3)
            ],
            axis=0,
        )
        inputs = jnp.concatenate(
            [
                jnp.concatenate([tile[u][i + h] for u in range(group) for h in range(4)], axis=1)
                for i in range(3)
            ],
            axis=0,
        )
        da2 = jnp.dot(wo[...], fields, preferred_element_type=jnp.float32)
        dz2 = (da2 * d2_ref[block]).astype(jnp.bfloat16)
        acc_out[...] += nt(fields, a2_ref[block])
        da1 = jnp.dot(wm[...], dz2, preferred_element_type=jnp.float32)
        ones = jnp.ones((16, dz2.shape[1]), jnp.bfloat16)
        acc_mid[...] += nt(jnp.concatenate([a1_ref[block], ones], axis=0), dz2)
        dz1 = (da1 * d1_ref[block]).astype(jnp.bfloat16)
        acc_in[...] += nt(inputs, dz1)
    def end():
        out[0:48, 0:channels] = acc_in[...]
        out[0:48, channels : 2 * channels] = acc_out[...]
        out[12:13, 0:channels] = acc_mid[channels : channels + 1, :]
        mid = acc_mid[0:channels, :].T
        out[48 : 48 + channels // 2, 0:channels] = mid[0 : channels // 2]
        out[48 : 48 + channels // 2, channels : 2 * channels] = mid[channels // 2 : channels]

    run(start, step, end, owners // group, blocked)


def finish_kernel(scale, parts, *refs):
    terms, (g_in, g_bin, g_mid, g_bmid, g_out, held) = refs[:-6], refs[-6:]
    values = [ref[...] for ref in terms]
    while len(values) > 1:
        values = [values[k] + values[k + 1] for k in range(0, len(values), 2)]
    held[...] = values[0] * scale
    channels = g_mid.shape[0]
    for o in range(parts):
        for i in range(3):
            for j in range(3):
                row = held[i * 16 + j * 4 + o : i * 16 + j * 4 + o + 1, :]
                at = o * 9 + 3 * i + j
                g_in[at : at + 1, :] = row[:, 0:channels]
                g_out[at : at + 1, :] = row[:, channels : 2 * channels]
    g_bin[...] = held[28:29, 0:channels]
    g_bmid[...] = held[12:13, 0:channels]
    half = channels // 2
    g_mid[0:half] = held[48 : 48 + half, 0:channels]
    g_mid[half:channels] = held[48 : 48 + half, channels : 2 * channels]


def halves(b):
    high = b.astype(jnp.bfloat16).astype(jnp.float32)
    rest = b - high
    mid = rest.astype(jnp.bfloat16).astype(jnp.float32)
    return [high, mid, rest - mid]


def one_hot(a, b):
    return (a == b).astype(jnp.float32).astype(jnp.bfloat16)


def iota(shape, dim):
    return lax.broadcasted_iota(jnp.int32, shape, dim)


def product(a, b, over):
    return lax.dot_general(
        a, b, dimension_numbers=(((over[0],), (over[1],)), ((), ())),
        preferred_element_type=jnp.float32,
    )


def prep_kernel(blocks, dest, w_in, b_in, w_mid, b_mid, w_out, idx, w1, w2, w3, wo, wm, rows):
    count = lax.axis_size("rec")
    me = lax.axis_index("rec")
    ves, total = dest.shape
    channels = w_mid.shape[0]
    empty = 6 * blocks
    at = lax.rem((count + 1 - me) * blocks, total)
    wide = jnp.concatenate([dest[...], jnp.zeros((8 - ves, total), jnp.int32)], axis=0)
    near = pltpu.roll(wide, at, 1)[:, 0:128]
    lane = iota((8, 128), 1)
    low = jnp.where(me > 0, 0, blocks)
    high = jnp.where(me < count - 1, 3 * blocks, 2 * blocks)
    near = jnp.where((lane >= low) & (lane < high), near, -1)
    owner = iota((count, 128), 0)
    hits = [(near[v : v + 1] == owner).astype(jnp.float32) for v in range(ves)]
    before = iota((128, 128), 0)
    after = iota((128, 128), 1)
    segment = (after >= blocks).astype(jnp.int32) + (after >= 2 * blocks).astype(jnp.int32)
    tri = ((before < after) & (before >= segment * blocks)).astype(jnp.float32).astype(jnp.bfloat16)
    rank = product((hits[0] + hits[1] + hits[2] + hits[3]).astype(jnp.bfloat16), tri, (1, 0))
    zeroth = jnp.zeros((count, 128), jnp.float32)
    first = jnp.zeros((count, 128), jnp.float32)
    for v in range(ves):
        zeroth += hits[v] * (rank == 0.0).astype(jnp.float32)
        first += hits[v] * (rank == 1.0).astype(jnp.float32)
        item = jnp.sum(hits[v] * rank, axis=0, keepdims=True)
        idx[4 + v : 5 + v, 0:128] = near[v : v + 1] * 4 + item.astype(jnp.int32) * 2
        rank = rank + hits[v]
    line = iota((8, 128), 0)
    inside = lambda k: (lane >= k * blocks) & (lane < (k + 1) * blocks)
    place = (2 * lane - empty).astype(jnp.float32)
    ones = jnp.where((line == 0) & inside(0) | (line == 2) & inside(1), place, 0.0)
    zeros = jnp.where((line == 1) & inside(1) | (line == 3) & inside(2), place, 0.0)
    pick = product(ones.astype(jnp.bfloat16), first.astype(jnp.bfloat16), (1, 1)) + product(
        zeros.astype(jnp.bfloat16), zeroth.astype(jnp.bfloat16), (1, 1)
    )
    idx[0:4, 0:count] = pick[0:4].astype(jnp.int32) + empty

    taps = w_in.shape[0]
    row, col = iota((48, 40), 0), iota((48, 40), 1)
    tap, extra = row & 15, (row & 15) - 12
    target = (row & 3) * 9 + 3 * (row >> 4) + ((row >> 2) & 3)
    target = jnp.where(tap < 12, target, jnp.where((row >> 4) == 1, taps + extra, -1))
    order = one_hot(col, target)
    rows[...] = jnp.zeros_like(rows)
    rows[0:taps, :] = w_in[...].astype(jnp.float32)
    for n, part in enumerate(halves(b_in[...])):
        rows[taps + n : taps + n + 1, :] = part
    w1[...] = (0.5 * product(rows[...].astype(jnp.bfloat16), order, (0, 1))).astype(jnp.bfloat16)
    rows[...] = jnp.zeros_like(rows)
    for n, part in enumerate(halves(b_mid[...])):
        rows[n : n + 1, :] = part
    row, col = iota((40, channels + 16), 0), iota((40, channels + 16), 1)
    bias = product(rows[...].astype(jnp.bfloat16), one_hot(col, row + channels), (0, 0))
    row, col = iota((channels, channels + 16), 0), iota((channels, channels + 16), 1)
    w2[...] = (0.5 * (product(w_mid[...], one_hot(row, col), (1, 0)) + bias)).astype(jnp.bfloat16)
    rows[...] = jnp.zeros_like(rows)
    rows[0:taps, :] = w_out[...].astype(jnp.float32)
    outs = rows[...].astype(jnp.bfloat16)
    wo[...] = (0.5 * product(outs, order, (0, 1))).astype(jnp.bfloat16)
    row, col = iota((24, 40), 0), iota((24, 40), 1)
    for i in range(3):
        target = jnp.where((row & 7) < 4, (row & 3) * 9 + 3 * i + (row >> 3), -1)
        part = product(one_hot(col, target), outs, (1, 0))
        w3[:, i * channels : (i + 1) * channels] = part.astype(jnp.bfloat16)
    eye = one_hot(iota((channels, channels), 0), iota((channels, channels), 1))
    wm[...] = (0.5 * product(w_mid[...], eye, (0, 0))).astype(jnp.bfloat16)


def local(records, dest, w_in, b_in, w_mid, b_mid, w_out):
    count = lax.axis_size("rec")
    me = lax.axis_index("rec")
    parts, blocks, traces, samples = records.shape
    ves = dest.shape[1]
    tiles = blocks * traces
    channels = w_in.shape[0]
    group = group_of(count)
    steps = count // group
    width = group * 4 * samples
    up = [(s, s + 1) for s in range(count - 1)]
    down = [(s + 1, s) for s in range(count - 1)]

    flat = records.transpose(1, 2, 0, 3).reshape(tiles, parts, samples)
    from_left = lax.ppermute(flat, "rec", up)
    from_right = lax.ppermute(flat, "rec", down)

    f32, bf16 = jnp.float32, jnp.bfloat16
    shape = (steps, channels, width)
    blocked = 12 * math.prod(shape) > RESIDENT
    saved = [
        jax.ShapeDtypeStruct(shape, kind) if blocked else pltpu.VMEM(shape, kind)
        for kind in (bf16, bf16, f32, f32)
    ]
    held = [VMEM] * 4
    if blocked:
        held = [pl.BlockSpec((1, channels, width), lambda n: (n, 0, 0))] * 4
    grid = (steps,) if blocked else ()
    params = pltpu.CompilerParams(vmem_limit_bytes=16 << 20)
    idx, w1, w2, w3, wo, wm = pl.pallas_call(
        functools.partial(prep_kernel, blocks),
        out_shape=[jax.ShapeDtypeStruct((8, max(128, count)), jnp.int32)]
        + [
            jax.ShapeDtypeStruct(size, bf16)
            for size in (
                (channels, 48), (channels, channels + 16), (24, 3 * channels), (channels, 48),
                (channels, channels),
            )
        ],
        in_specs=[VMEM] * 6,
        out_specs=[VMEM] * 6,
        scratch_shapes=[pltpu.VMEM((40, channels), f32)],
        compiler_params=params,
        name="prepare",
    )(
        dest.T, w_in.T, b_in.reshape(1, channels), w_mid, b_mid.reshape(1, channels), w_out.T
    )
    res, g, table, a1, a2, d1, d2 = pl.pallas_call(
        functools.partial(forward_kernel, group, blocked),
        grid=grid,
        out_shape=[
            jax.ShapeDtypeStruct(records.shape, f32),
            jax.ShapeDtypeStruct((tiles, parts, samples), bf16),
            pltpu.VMEM((3 * tiles + 2, 16, samples), bf16),
            *saved,
        ],
        in_specs=[SMEM] + [VMEM] * 6,
        out_specs=[VMEM] * 3 + held,
        scratch_shapes=[
            pltpu.VMEM((3 * tiles + 2, 16, samples), f32),
            pltpu.VMEM((count * 4, 8, samples), f32),
        ],
        compiler_params=params,
        name="forward",
    )(idx, from_left, flat, from_right, w1, w2, w3)

    g_left = lax.ppermute(g, "rec", up)
    g_right = lax.ppermute(g, "rec", down)
    sums = pl.pallas_call(
        functools.partial(backward_kernel, group, blocked),
        grid=grid,
        out_shape=jax.ShapeDtypeStruct((48 + channels // 2, 2 * channels), f32),
        in_specs=[SMEM] + [VMEM] * 6 + held,
        out_specs=VMEM,
        scratch_shapes=[
            pltpu.VMEM((3 * tiles + 2, 16, samples), bf16),
            pltpu.VMEM((3 * tiles + 2, 16, samples), f32),
            pltpu.VMEM((48, channels), f32),
            pltpu.VMEM((channels + 16, channels), f32),
            pltpu.VMEM((48, channels), f32),
        ],
        compiler_params=params,
        name="backward",
    )(idx, g_left, g, g_right, wo, wm, table, a1, a2, d1, d2)

    if count & (count - 1):
        terms = [lax.psum(sums, "rec")]
    else:
        terms = [sums]
        at = 1
        while at < count:
            wide = 2 if at == 1 or 2 * at == count else 4
            value = terms[0]
            if len(terms) == 2:
                value = terms[0] + terms[1]
            if len(terms) == 4:
                value = (terms[0] + terms[1]) + (terms[2] + terms[3])
            terms = [value] + [
                lax.ppermute(value, "rec", [(s, s ^ (k * at)) for s in range(count)])
                for k in range(1, wide)
            ]
            at *= wide

    scale = 1.0 / math.sqrt(parts * blocks * count * traces * samples)
    g_in, g_bin, g_mid, g_bmid, g_out = pl.pallas_call(
        functools.partial(finish_kernel, scale, parts),
        out_shape=[
            jax.ShapeDtypeStruct(shape, f32)
            for shape in (
                (parts * 9, channels), (1, channels), (channels, channels), (1, channels),
                (parts * 9, channels),
            )
        ],
        in_specs=[VMEM] * len(terms),
        out_specs=[VMEM] * 5,
        scratch_shapes=[pltpu.VMEM(sums.shape, f32)],
        compiler_params=params,
        name="finish",
    )(*terms)
    return (
        res,
        g_in.T,
        g_bin.reshape(channels),
        g_mid,
        g_bmid.reshape(channels),
        g_out.T,
    )


def solution(mesh):
    return jax.shard_map(
        local,
        mesh=mesh,
        in_specs=(
            P(None, ("groups", "rec"), None, None),
            P("groups", None),
            P(),
            P(),
            P(),
            P(),
            P(),
        ),
        out_specs=(
            P(None, ("groups", "rec"), None, None),
            P("groups", None),
            P("groups"),
            P("groups", None),
            P("groups"),
            P("groups", None),
        ),
        check_vma=False,
    )
```

```python
import functools
import math

import jax
import jax.numpy as jnp
from jax import lax
from jax.experimental import pallas as pl
from jax.experimental.pallas import tpu as pltpu
from jax.sharding import PartitionSpec as P

CAP = 2
VMEM = pl.BlockSpec(memory_space=pltpu.VMEM)
SMEM = pl.BlockSpec(memory_space=pltpu.SMEM)
RESIDENT = 24 << 20


def run(start, step, end, steps, blocked):
    if blocked:
        n = pl.program_id(0)
        pl.when(n == 0)(start)
        step(n, 0)
        pl.when(n == steps - 1)(end)
        return
    start()
    lax.fori_loop(0, steps, lambda n, carry: step(n, n), None)
    end()


def group_of(owners):
    for size in (4, 2):
        if owners % size == 0:
            return size
    return 1


def fill_table(table, wide, pieces, tiles, flip, fill):
    for n, piece in enumerate(pieces):
        x = piece[...].astype(jnp.float32)
        samples = x.shape[2]
        lane = lax.broadcasted_iota(jnp.int32, x.shape, 2)
        before = jnp.where(lane == 0, 0.0, pltpu.roll(x, 1, 2))
        after = jnp.where(lane == samples - 1, 0.0, pltpu.roll(x, samples - 1, 2))
        at = pl.ds(n * tiles, tiles)
        wide[at, 0:4, :] = after if flip else before
        wide[at, 4:8, :] = x
        wide[at, 8:12, :] = before if flip else after
    last = len(pieces) * tiles
    wide[pl.ds(last, 2), 0:12, :] = jnp.zeros((2, 12, wide.shape[2]), jnp.float32)
    wide[:, 12:16, :] = jnp.full((last + 2, 4, wide.shape[2]), fill, jnp.float32)
    table[...] = wide[...].astype(jnp.bfloat16)


def act(y):
    t = jnp.tanh(y)
    q = 1.0 + t
    a = y * q
    return t, q, a


def own_of(x, group, samples):
    return jnp.concatenate(
        [x[:, (u * 6 + 1) * samples : (u * 6 + 5) * samples] for u in range(group)], axis=1
    )


def forward_kernel(
    group, blocked, idx, left, mine, right, w1, w2, w3,
    res, g, table, a1_ref, a2_ref, d1_ref, d2_ref, wide, est,
):
    tiles, parts, samples = mine.shape
    count = lax.axis_size("rec")
    me = lax.axis_index("rec")
    has_left = (me > 0).astype(jnp.float32)
    has_right = (me < count - 1).astype(jnp.float32)
    lane = lax.broadcasted_iota(jnp.int32, (8, samples), 1)
    low = (lane > 0).astype(jnp.float32)
    high = (lane < samples - 1).astype(jnp.float32)

    def start():
        fill_table(table, wide, (left, mine, right), tiles, False, 1.0)

    def step(n, block):
        tile = []
        for u in range(group):
            e = n * group + u
            line = []
            for r in range(4):
                at = idx[r, e]
                line += [table[at], table[at + 1]]
            tile.append(line)
        rhs = jnp.concatenate(
            [
                jnp.concatenate([tile[u][i + h] for u in range(group) for h in range(6)], axis=1)
                for i in range(3)
            ],
            axis=0,
        )
        y1 = jnp.dot(w1[...], rhs, preferred_element_type=jnp.float32)
        t, q, a = act(y1)
        a1 = a.astype(jnp.bfloat16)
        a1_ref[block] = own_of(a1, group, samples)
        d1_ref[block] = own_of(q + a * (1.0 - t), group, samples)
        ones = jnp.ones((16, a1.shape[1]), jnp.bfloat16)
        y2 = jnp.dot(
            w2[...], jnp.concatenate([a1, ones], axis=0), preferred_element_type=jnp.float32
        )
        t, q, a = act(y2)
        d2_ref[block] = own_of(q + a * (1.0 - t), group, samples)
        cut = []
        for u in range(group):
            for h in range(6):
                part = a[:, (u * 6 + h) * samples : (u * 6 + h + 1) * samples]
                if h == 0:
                    part = part * has_left
                if h == 5:
                    part = part * has_right
                cut.append(part.astype(jnp.bfloat16))
        a2_ref[block] = jnp.concatenate(
            [cut[u * 6 + h + 1] for u in range(group) for h in range(4)], axis=1
        )
        rhs = jnp.concatenate(
            [
                jnp.concatenate([cut[u * 6 + h + i] for u in range(group) for h in range(4)], axis=1)
                for i in range(3)
            ],
            axis=0,
        )
        terms = jnp.dot(w3[...], rhs, preferred_element_type=jnp.float32)
        for k in range(group * 4):
            part = terms[:, k * samples : (k + 1) * samples]
            total = (
                part[8:16]
                + pltpu.roll(part[0:8], 1, 1) * low
                + pltpu.roll(part[16:24], samples - 1, 1) * high
            )
            est[n * group * 4 + k] = total.astype(jnp.bfloat16).astype(jnp.float32)

    def end():
        for c in range(tiles // 2):
            at = [idx[4 + v, tiles // 2 + c] for v in range(4)]
            for k in range(2):
                total = (est[at[0] + k] + est[at[1] + k]) + (est[at[2] + k] + est[at[3] + k])
                value = total[0:parts] - mine[c * 2 + k].astype(jnp.float32)
                for o in range(parts):
                    res[o, c, k : k + 1, :] = value[o : o + 1]
                g[c * 2 + k] = value.astype(jnp.bfloat16)

    run(start, step, end, count // group, blocked)


def backward_kernel(
    group, blocked, idx, left, mine, right, wo, wm, table, a1_ref, a2_ref, d1_ref, d2_ref,
    out, gtable, wide, acc_in, acc_mid, acc_out,
):
    tiles, parts, samples = mine.shape
    owners = lax.axis_size("rec")
    channels = wo.shape[0]
    nt = functools.partial(
        lax.dot_general,
        dimension_numbers=(((1,), (1,)), ((), ())),
        preferred_element_type=jnp.float32,
    )

    def start():
        fill_table(gtable, wide, (left, mine, right), tiles, True, 0.0)
        acc_in[...] = jnp.zeros_like(acc_in)
        acc_mid[...] = jnp.zeros_like(acc_mid)
        acc_out[...] = jnp.zeros_like(acc_out)

    def step(n, block):
        tile, gtile = [], []
        for u in range(group):
            e = n * group + u
            at = [idx[r, e] for r in range(4)]
            tile.append(
                [table[at[0] + 1]] + [table[at[r] + k] for r in (1, 2) for k in (0, 1)] + [table[at[3]]]
            )
            gtile.append(
                [gtable[at[0] + 1]] + [gtable[at[r] + k] for r in (1, 2) for k in (0, 1)] + [gtable[at[3]]]
            )
        fields = jnp.concatenate(
            [
                jnp.concatenate([gtile[u][2 - i + h] for u in range(group) for h in range(4)], axis=1)
                for i in range(3)
            ],
            axis=0,
        )
        inputs = jnp.concatenate(
            [
                jnp.concatenate([tile[u][i + h] for u in range(group) for h in range(4)], axis=1)
                for i in range(3)
            ],
            axis=0,
        )
        da2 = jnp.dot(wo[...], fields, preferred_element_type=jnp.float32)
        dz2 = (da2 * d2_ref[block]).astype(jnp.bfloat16)
        acc_out[...] += nt(fields, a2_ref[block])
        da1 = jnp.dot(wm[...], dz2, preferred_element_type=jnp.float32)
        ones = jnp.ones((16, dz2.shape[1]), jnp.bfloat16)
        acc_mid[...] += nt(jnp.concatenate([a1_ref[block], ones], axis=0), dz2)
        dz1 = (da1 * d1_ref[block]).astype(jnp.bfloat16)
        acc_in[...] += nt(inputs, dz1)
    def end():
        out[0:48, 0:channels] = acc_in[...]
        out[0:48, channels : 2 * channels] = acc_out[...]
        out[12:13, 0:channels] = acc_mid[channels : channels + 1, :]
        mid = acc_mid[0:channels, :].T
        out[48 : 48 + channels // 2, 0:channels] = mid[0 : channels // 2]
        out[48 : 48 + channels // 2, channels : 2 * channels] = mid[channels // 2 : channels]

    run(start, step, end, owners // group, blocked)


def finish_kernel(scale, parts, terms, g_in, g_bin, g_mid, g_bmid, g_out, held):
    total = terms[0]
    for n in range(1, terms.shape[0]):
        total += terms[n]
    held[...] = total * scale
    channels = g_mid.shape[0]
    for o in range(parts):
        for i in range(3):
            for j in range(3):
                row = held[i * 16 + j * 4 + o : i * 16 + j * 4 + o + 1, :]
                at = o * 9 + 3 * i + j
                g_in[at : at + 1, :] = row[:, 0:channels]
                g_out[at : at + 1, :] = row[:, channels : 2 * channels]
    g_bin[...] = held[28:29, 0:channels]
    g_bmid[...] = held[12:13, 0:channels]
    half = channels // 2
    g_mid[0:half] = held[48 : 48 + half, 0:channels]
    g_mid[half:channels] = held[48 : 48 + half, channels : 2 * channels]


def halves(b):
    high = b.astype(jnp.bfloat16).astype(jnp.float32)
    rest = b - high
    mid = rest.astype(jnp.bfloat16).astype(jnp.float32)
    return [high, mid, rest - mid]


def one_hot(a, b):
    return (a == b).astype(jnp.float32).astype(jnp.bfloat16)


def iota(shape, dim):
    return lax.broadcasted_iota(jnp.int32, shape, dim)


def product(a, b, over):
    return lax.dot_general(
        a, b, dimension_numbers=(((over[0],), (over[1],)), ((), ())),
        preferred_element_type=jnp.float32,
    )


def prep_kernel(blocks, *refs):
    args, (idx, w1, w2, w3, wo, wm, rows), held, sems = refs[:6], refs[6:13], refs[13:19], refs[19]
    copies = [
        pltpu.make_async_copy(src, dst, sems.at[n]) for n, (src, dst) in enumerate(zip(args, held))
    ]
    for copy in copies:
        copy.start()
    for copy in copies:
        copy.wait()
    dest, w_in, b_in, w_mid, b_mid, w_out = held
    count = lax.axis_size("rec")
    me = lax.axis_index("rec")
    ves, total = dest.shape
    channels = w_mid.shape[0]
    empty = 6 * blocks
    at = lax.rem((count + 1 - me) * blocks, total)
    wide = jnp.concatenate([dest[...], jnp.zeros((8 - ves, total), jnp.int32)], axis=0)
    near = pltpu.roll(wide, at, 1)[:, 0:128]
    lane = iota((8, 128), 1)
    low = jnp.where(me > 0, 0, blocks)
    high = jnp.where(me < count - 1, 3 * blocks, 2 * blocks)
    near = jnp.where((lane >= low) & (lane < high), near, -1)
    owner = iota((count, 128), 0)
    hits = [(near[v : v + 1] == owner).astype(jnp.float32) for v in range(ves)]
    before = iota((128, 128), 0)
    after = iota((128, 128), 1)
    segment = (after >= blocks).astype(jnp.int32) + (after >= 2 * blocks).astype(jnp.int32)
    tri = ((before < after) & (before >= segment * blocks)).astype(jnp.float32).astype(jnp.bfloat16)
    rank = product((hits[0] + hits[1] + hits[2] + hits[3]).astype(jnp.bfloat16), tri, (1, 0))
    zeroth = jnp.zeros((count, 128), jnp.float32)
    first = jnp.zeros((count, 128), jnp.float32)
    for v in range(ves):
        zeroth += hits[v] * (rank == 0.0).astype(jnp.float32)
        first += hits[v] * (rank == 1.0).astype(jnp.float32)
        item = jnp.sum(hits[v] * rank, axis=0, keepdims=True)
        idx[4 + v : 5 + v, 0:128] = near[v : v + 1] * 4 + item.astype(jnp.int32) * 2
        rank = rank + hits[v]
    line = iota((8, 128), 0)
    inside = lambda k: (lane >= k * blocks) & (lane < (k + 1) * blocks)
    place = (2 * lane - empty).astype(jnp.float32)
    ones = jnp.where((line == 0) & inside(0) | (line == 2) & inside(1), place, 0.0)
    zeros = jnp.where((line == 1) & inside(1) | (line == 3) & inside(2), place, 0.0)
    pick = product(ones.astype(jnp.bfloat16), first.astype(jnp.bfloat16), (1, 1)) + product(
        zeros.astype(jnp.bfloat16), zeroth.astype(jnp.bfloat16), (1, 1)
    )
    idx[0:4, 0:count] = pick[0:4].astype(jnp.int32) + empty

    taps = w_in.shape[0]
    row, col = iota((48, 40), 0), iota((48, 40), 1)
    tap, extra = row & 15, (row & 15) - 12
    target = (row & 3) * 9 + 3 * (row >> 4) + ((row >> 2) & 3)
    target = jnp.where(tap < 12, target, jnp.where((row >> 4) == 1, taps + extra, -1))
    order = one_hot(col, target)
    rows[...] = jnp.zeros_like(rows)
    rows[0:taps, :] = w_in[...].astype(jnp.float32)
    for n, part in enumerate(halves(b_in[...])):
        rows[taps + n : taps + n + 1, :] = part
    w1[...] = (0.5 * product(rows[...].astype(jnp.bfloat16), order, (0, 1))).astype(jnp.bfloat16)
    rows[...] = jnp.zeros_like(rows)
    for n, part in enumerate(halves(b_mid[...])):
        rows[n : n + 1, :] = part
    row, col = iota((40, channels + 16), 0), iota((40, channels + 16), 1)
    bias = product(rows[...].astype(jnp.bfloat16), one_hot(col, row + channels), (0, 0))
    row, col = iota((channels, channels + 16), 0), iota((channels, channels + 16), 1)
    w2[...] = (0.5 * (product(w_mid[...], one_hot(row, col), (1, 0)) + bias)).astype(jnp.bfloat16)
    rows[...] = jnp.zeros_like(rows)
    rows[0:taps, :] = w_out[...].astype(jnp.float32)
    outs = rows[...].astype(jnp.bfloat16)
    wo[...] = (0.5 * product(outs, order, (0, 1))).astype(jnp.bfloat16)
    row, col = iota((24, 40), 0), iota((24, 40), 1)
    for i in range(3):
        target = jnp.where((row & 7) < 4, (row & 3) * 9 + 3 * i + (row >> 3), -1)
        part = product(one_hot(col, target), outs, (1, 0))
        w3[:, i * channels : (i + 1) * channels] = part.astype(jnp.bfloat16)
    eye = one_hot(iota((channels, channels), 0), iota((channels, channels), 1))
    wm[...] = (0.5 * product(w_mid[...], eye, (0, 0))).astype(jnp.bfloat16)


def local(records, dest, w_in, b_in, w_mid, b_mid, w_out):
    count = lax.axis_size("rec")
    me = lax.axis_index("rec")
    parts, blocks, traces, samples = records.shape
    ves = dest.shape[1]
    tiles = blocks * traces
    channels = w_in.shape[0]
    group = group_of(count)
    steps = count // group
    width = group * 4 * samples
    up = [(s, s + 1) for s in range(count - 1)]
    down = [(s + 1, s) for s in range(count - 1)]

    flat = records.transpose(1, 2, 0, 3).reshape(tiles, parts, samples)
    from_left = lax.ppermute(flat, "rec", up)
    from_right = lax.ppermute(flat, "rec", down)

    f32, bf16 = jnp.float32, jnp.bfloat16
    shape = (steps, channels, width)
    blocked = 12 * math.prod(shape) > RESIDENT
    saved = [
        jax.ShapeDtypeStruct(shape, kind) if blocked else pltpu.VMEM(shape, kind)
        for kind in (bf16, bf16, f32, f32)
    ]
    held = [VMEM] * 4
    if blocked:
        held = [pl.BlockSpec((1, channels, width), lambda n: (n, 0, 0))] * 4
    grid = (steps,) if blocked else ()
    params = pltpu.CompilerParams(vmem_limit_bytes=16 << 20)
    args = (
        dest.T, w_in.T, b_in.reshape(1, channels), w_mid, b_mid.reshape(1, channels), w_out.T
    )
    idx, w1, w2, w3, wo, wm = pl.pallas_call(
        functools.partial(prep_kernel, blocks),
        out_shape=[jax.ShapeDtypeStruct((8, max(128, count)), jnp.int32)]
        + [
            jax.ShapeDtypeStruct(size, bf16)
            for size in (
                (channels, 48), (channels, channels + 16), (24, 3 * channels), (channels, 48),
                (channels, channels),
            )
        ],
        in_specs=[pl.BlockSpec(memory_space=pltpu.HBM)] * 6,
        out_specs=[VMEM] * 6,
        scratch_shapes=[pltpu.VMEM((40, channels), f32)]
        + [pltpu.VMEM(arg.shape, arg.dtype) for arg in args]
        + [pltpu.SemaphoreType.DMA((6,))],
        compiler_params=params,
        name="prepare",
    )(*[pltpu.with_memory_space_constraint(arg, pltpu.HBM) for arg in args])
    res, g, table, a1, a2, d1, d2 = pl.pallas_call(
        functools.partial(forward_kernel, group, blocked),
        grid=grid,
        out_shape=[
            jax.ShapeDtypeStruct(records.shape, f32),
            jax.ShapeDtypeStruct((tiles, parts, samples), bf16),
            pltpu.VMEM((3 * tiles + 2, 16, samples), bf16),
            *saved,
        ],
        in_specs=[SMEM] + [VMEM] * 6,
        out_specs=[VMEM] * 3 + held,
        scratch_shapes=[
            pltpu.VMEM((3 * tiles + 2, 16, samples), f32),
            pltpu.VMEM((count * 4, 8, samples), f32),
        ],
        compiler_params=params,
        name="forward",
    )(idx, from_left, flat, from_right, w1, w2, w3)

    g_left = lax.ppermute(g, "rec", up)
    g_right = lax.ppermute(g, "rec", down)
    sums = pl.pallas_call(
        functools.partial(backward_kernel, group, blocked),
        grid=grid,
        out_shape=jax.ShapeDtypeStruct((48 + channels // 2, 2 * channels), f32),
        in_specs=[SMEM] + [VMEM] * 6 + held,
        out_specs=VMEM,
        scratch_shapes=[
            pltpu.VMEM((3 * tiles + 2, 16, samples), bf16),
            pltpu.VMEM((3 * tiles + 2, 16, samples), f32),
            pltpu.VMEM((48, channels), f32),
            pltpu.VMEM((channels + 16, channels), f32),
            pltpu.VMEM((48, channels), f32),
        ],
        compiler_params=params,
        name="backward",
    )(idx, g_left, g, g_right, wo, wm, table, a1, a2, d1, d2)

    terms = lax.all_gather(sums, "rec")

    scale = 1.0 / math.sqrt(parts * blocks * count * traces * samples)
    g_in, g_bin, g_mid, g_bmid, g_out = pl.pallas_call(
        functools.partial(finish_kernel, scale, parts),
        out_shape=[
            jax.ShapeDtypeStruct(shape, f32)
            for shape in (
                (parts * 9, channels), (1, channels), (channels, channels), (1, channels),
                (parts * 9, channels),
            )
        ],
        in_specs=[VMEM],
        out_specs=[VMEM] * 5,
        scratch_shapes=[pltpu.VMEM(sums.shape, f32)],
        compiler_params=params,
        name="finish",
    )(terms)
    return (
        res,
        g_in.T,
        g_bin.reshape(channels),
        g_mid,
        g_bmid.reshape(channels),
        g_out.T,
    )


def solution(mesh):
    return jax.shard_map(
        local,
        mesh=mesh,
        in_specs=(
            P(None, ("groups", "rec"), None, None),
            P("groups", None),
            P(),
            P(),
            P(),
            P(),
            P(),
        ),
        out_specs=(
            P(None, ("groups", "rec"), None, None),
            P("groups", None),
            P("groups"),
            P("groups", None),
            P("groups"),
            P("groups", None),
        ),
        check_vma=False,
    )
```

```python
import functools
import math

import jax
import jax.numpy as jnp
from jax import lax
from jax.experimental import pallas as pl
from jax.experimental.pallas import tpu as pltpu
from jax.sharding import PartitionSpec as P

CAP = 2
VMEM = pl.BlockSpec(memory_space=pltpu.VMEM)
SMEM = pl.BlockSpec(memory_space=pltpu.SMEM)
RESIDENT = 24 << 20


def run(start, step, end, steps, blocked):
    if blocked:
        n = pl.program_id(0)
        pl.when(n == 0)(start)
        step(n, 0)
        pl.when(n == steps - 1)(end)
        return
    start()
    lax.fori_loop(0, steps, lambda n, carry: step(n, n), None)
    end()


def group_of(owners):
    for size in (4, 2):
        if owners % size == 0:
            return size
    return 1


def fill_table(table, wide, pieces, tiles, flip, fill):
    for n, piece in enumerate(pieces):
        x = piece[...].astype(jnp.float32)
        samples = x.shape[2]
        lane = lax.broadcasted_iota(jnp.int32, x.shape, 2)
        before = jnp.where(lane == 0, 0.0, pltpu.roll(x, 1, 2))
        after = jnp.where(lane == samples - 1, 0.0, pltpu.roll(x, samples - 1, 2))
        at = pl.ds(n * tiles, tiles)
        wide[at, 0:4, :] = after if flip else before
        wide[at, 4:8, :] = x
        wide[at, 8:12, :] = before if flip else after
    last = len(pieces) * tiles
    wide[pl.ds(last, 2), 0:12, :] = jnp.zeros((2, 12, wide.shape[2]), jnp.float32)
    wide[:, 12:16, :] = jnp.full((last + 2, 4, wide.shape[2]), fill, jnp.float32)
    table[...] = wide[...].astype(jnp.bfloat16)


def act(y):
    t = jnp.tanh(y)
    q = 1.0 + t
    a = y * q
    return t, q, a


def own_of(x, group, samples):
    return jnp.concatenate(
        [x[:, (u * 6 + 1) * samples : (u * 6 + 5) * samples] for u in range(group)], axis=1
    )


def forward_kernel(
    group, blocked, idx, near, mine, far, w1, w2, w3,
    res, g, table, a1_ref, a2_ref, d1_ref, d2_ref, wide, est,
):
    tiles, parts, samples = mine.shape
    count = lax.axis_size("rec")
    me = lax.axis_index("rec")
    has_left = (me > 0).astype(jnp.float32)
    has_right = (me < count - 1).astype(jnp.float32)
    lane = lax.broadcasted_iota(jnp.int32, (8, samples), 1)
    low = (lane > 0).astype(jnp.float32)
    high = (lane < samples - 1).astype(jnp.float32)

    def start():
        fill_table(table, wide, (near, mine, far), tiles, False, 1.0)

    def step(n, block):
        tile = []
        for u in range(group):
            e = n * group + u
            line = []
            for r in range(4):
                at = idx[r, e]
                line += [table[at], table[at + 1]]
            tile.append(line)
        rhs = jnp.concatenate(
            [
                jnp.concatenate([tile[u][i + h] for u in range(group) for h in range(6)], axis=1)
                for i in range(3)
            ],
            axis=0,
        )
        y1 = jnp.dot(w1[...], rhs, preferred_element_type=jnp.float32)
        t, q, a = act(y1)
        a1 = a.astype(jnp.bfloat16)
        a1_ref[block] = own_of(a1, group, samples)
        d1_ref[block] = own_of(q + a * (1.0 - t), group, samples)
        ones = jnp.ones((16, a1.shape[1]), jnp.bfloat16)
        y2 = jnp.dot(
            w2[...], jnp.concatenate([a1, ones], axis=0), preferred_element_type=jnp.float32
        )
        t, q, a = act(y2)
        d2_ref[block] = own_of(q + a * (1.0 - t), group, samples)
        cut = []
        for u in range(group):
            for h in range(6):
                part = a[:, (u * 6 + h) * samples : (u * 6 + h + 1) * samples]
                if h == 0:
                    part = part * has_left
                if h == 5:
                    part = part * has_right
                cut.append(part.astype(jnp.bfloat16))
        a2_ref[block] = jnp.concatenate(
            [cut[u * 6 + h + 1] for u in range(group) for h in range(4)], axis=1
        )
        rhs = jnp.concatenate(
            [
                jnp.concatenate([cut[u * 6 + h + i] for u in range(group) for h in range(4)], axis=1)
                for i in range(3)
            ],
            axis=0,
        )
        terms = jnp.dot(w3[...], rhs, preferred_element_type=jnp.float32)
        for k in range(group * 4):
            part = terms[:, k * samples : (k + 1) * samples]
            total = (
                part[8:16]
                + pltpu.roll(part[0:8], 1, 1) * low
                + pltpu.roll(part[16:24], samples - 1, 1) * high
            )
            est[n * group * 4 + k] = total.astype(jnp.bfloat16).astype(jnp.float32)

    def end():
        for c in range(tiles // 2):
            at = [idx[4 + v, tiles // 2 + c] for v in range(4)]
            for k in range(2):
                total = (est[at[0] + k] + est[at[1] + k]) + (est[at[2] + k] + est[at[3] + k])
                value = total[0:parts] - mine[c * 2 + k].astype(jnp.float32)
                for o in range(parts):
                    res[o, c, k : k + 1, :] = value[o : o + 1]
                g[c * 2 + k] = value.astype(jnp.bfloat16)

    run(start, step, end, count // group, blocked)


def backward_kernel(
    group, blocked, idx, near, mine, far, wo, wm, table, a1_ref, a2_ref, d1_ref, d2_ref,
    out, gtable, wide, acc_in, acc_mid, acc_out,
):
    tiles, parts, samples = mine.shape
    owners = lax.axis_size("rec")
    channels = wo.shape[0]
    nt = functools.partial(
        lax.dot_general,
        dimension_numbers=(((1,), (1,)), ((), ())),
        preferred_element_type=jnp.float32,
    )

    def start():
        fill_table(gtable, wide, (near, mine, far), tiles, True, 0.0)
        acc_in[...] = jnp.zeros_like(acc_in)
        acc_mid[...] = jnp.zeros_like(acc_mid)
        acc_out[...] = jnp.zeros_like(acc_out)

    def step(n, block):
        tile, gtile = [], []
        for u in range(group):
            e = n * group + u
            at = [idx[r, e] for r in range(4)]
            tile.append(
                [table[at[0] + 1]] + [table[at[r] + k] for r in (1, 2) for k in (0, 1)] + [table[at[3]]]
            )
            gtile.append(
                [gtable[at[0] + 1]] + [gtable[at[r] + k] for r in (1, 2) for k in (0, 1)] + [gtable[at[3]]]
            )
        fields = jnp.concatenate(
            [
                jnp.concatenate([gtile[u][2 - i + h] for u in range(group) for h in range(4)], axis=1)
                for i in range(3)
            ],
            axis=0,
        )
        inputs = jnp.concatenate(
            [
                jnp.concatenate([tile[u][i + h] for u in range(group) for h in range(4)], axis=1)
                for i in range(3)
            ],
            axis=0,
        )
        da2 = jnp.dot(wo[...], fields, preferred_element_type=jnp.float32)
        dz2 = (da2 * d2_ref[block]).astype(jnp.bfloat16)
        acc_out[...] += nt(fields, a2_ref[block])
        da1 = jnp.dot(wm[...], dz2, preferred_element_type=jnp.float32)
        ones = jnp.ones((16, dz2.shape[1]), jnp.bfloat16)
        acc_mid[...] += nt(jnp.concatenate([a1_ref[block], ones], axis=0), dz2)
        dz1 = (da1 * d1_ref[block]).astype(jnp.bfloat16)
        acc_in[...] += nt(inputs, dz1)
    def end():
        out[0:48, 0:channels] = acc_in[...]
        out[0:48, channels : 2 * channels] = acc_out[...]
        out[12:13, 0:channels] = acc_mid[channels : channels + 1, :]
        mid = acc_mid[0:channels, :].T
        out[48 : 48 + channels // 2, 0:channels] = mid[0 : channels // 2]
        out[48 : 48 + channels // 2, channels : 2 * channels] = mid[channels // 2 : channels]

    run(start, step, end, owners // group, blocked)


def finish_kernel(scale, parts, *refs):
    terms, (g_in, g_bin, g_mid, g_bmid, g_out, held) = refs[:-6], refs[-6:]
    values = [ref[...] for ref in terms]
    while len(values) > 1:
        values = [values[k] + values[k + 1] for k in range(0, len(values), 2)]
    held[...] = values[0] * scale
    channels = g_mid.shape[0]
    for o in range(parts):
        for i in range(3):
            for j in range(3):
                row = held[i * 16 + j * 4 + o : i * 16 + j * 4 + o + 1, :]
                at = o * 9 + 3 * i + j
                g_in[at : at + 1, :] = row[:, 0:channels]
                g_out[at : at + 1, :] = row[:, channels : 2 * channels]
    g_bin[...] = held[28:29, 0:channels]
    g_bmid[...] = held[12:13, 0:channels]
    half = channels // 2
    g_mid[0:half] = held[48 : 48 + half, 0:channels]
    g_mid[half:channels] = held[48 : 48 + half, channels : 2 * channels]


def halves(b):
    high = b.astype(jnp.bfloat16).astype(jnp.float32)
    rest = b - high
    mid = rest.astype(jnp.bfloat16).astype(jnp.float32)
    return [high, mid, rest - mid]


def one_hot(a, b):
    return (a == b).astype(jnp.float32).astype(jnp.bfloat16)


def iota(shape, dim):
    return lax.broadcasted_iota(jnp.int32, shape, dim)


def product(a, b, over):
    return lax.dot_general(
        a, b, dimension_numbers=(((over[0],), (over[1],)), ((), ())),
        preferred_element_type=jnp.float32,
    )


def prep_kernel(blocks, *refs):
    args, (idx, w1, w2, w3, wo, wm, rows), held, sems = refs[:6], refs[6:13], refs[13:19], refs[19]
    copies = [
        pltpu.make_async_copy(src, dst, sems.at[n]) for n, (src, dst) in enumerate(zip(args, held))
    ]
    for copy in copies:
        copy.start()
    for copy in copies:
        copy.wait()
    dest, w_in, b_in, w_mid, b_mid, w_out = held
    count = lax.axis_size("rec")
    me = lax.axis_index("rec")
    ves, total = dest.shape
    channels = w_mid.shape[0]
    empty = 6 * blocks
    at = lax.rem((count + 1 - me) * blocks, total)
    wide = jnp.concatenate([dest[...], jnp.zeros((8 - ves, total), jnp.int32)], axis=0)
    near = pltpu.roll(wide, at, 1)[:, 0:128]
    lane = iota((8, 128), 1)
    low = jnp.where(me > 0, 0, blocks)
    high = jnp.where(me < count - 1, 3 * blocks, 2 * blocks)
    near = jnp.where((lane >= low) & (lane < high), near, -1)
    owner = iota((count, 128), 0)
    hits = [(near[v : v + 1] == owner).astype(jnp.float32) for v in range(ves)]
    before = iota((128, 128), 0)
    after = iota((128, 128), 1)
    segment = (after >= blocks).astype(jnp.int32) + (after >= 2 * blocks).astype(jnp.int32)
    tri = ((before < after) & (before >= segment * blocks)).astype(jnp.float32).astype(jnp.bfloat16)
    rank = product((hits[0] + hits[1] + hits[2] + hits[3]).astype(jnp.bfloat16), tri, (1, 0))
    zeroth = jnp.zeros((count, 128), jnp.float32)
    first = jnp.zeros((count, 128), jnp.float32)
    for v in range(ves):
        zeroth += hits[v] * (rank == 0.0).astype(jnp.float32)
        first += hits[v] * (rank == 1.0).astype(jnp.float32)
        item = jnp.sum(hits[v] * rank, axis=0, keepdims=True)
        idx[4 + v : 5 + v, 0:128] = near[v : v + 1] * 4 + item.astype(jnp.int32) * 2
        rank = rank + hits[v]
    line = iota((8, 128), 0)
    inside = lambda k: (lane >= k * blocks) & (lane < (k + 1) * blocks)
    place = (2 * lane - empty).astype(jnp.float32)
    swap = jnp.where(lax.rem(me, 2) == 1, 0, 4 * blocks).astype(jnp.float32)
    ones = jnp.where(line == 0, jnp.where(inside(0), place + swap, 0.0), 0.0)
    ones = jnp.where((line == 2) & inside(1), place, ones)
    zeros = jnp.where(line == 3, jnp.where(inside(2), place - swap, 0.0), 0.0)
    zeros = jnp.where((line == 1) & inside(1), place, zeros)
    pick = product(ones.astype(jnp.bfloat16), first.astype(jnp.bfloat16), (1, 1)) + product(
        zeros.astype(jnp.bfloat16), zeroth.astype(jnp.bfloat16), (1, 1)
    )
    idx[0:4, 0:count] = pick[0:4].astype(jnp.int32) + empty

    taps = w_in.shape[0]
    row, col = iota((48, 40), 0), iota((48, 40), 1)
    tap, extra = row & 15, (row & 15) - 12
    target = (row & 3) * 9 + 3 * (row >> 4) + ((row >> 2) & 3)
    target = jnp.where(tap < 12, target, jnp.where((row >> 4) == 1, taps + extra, -1))
    order = one_hot(col, target)
    rows[...] = jnp.zeros_like(rows)
    rows[0:taps, :] = w_in[...].astype(jnp.float32)
    for n, part in enumerate(halves(b_in[...])):
        rows[taps + n : taps + n + 1, :] = part
    w1[...] = (0.5 * product(rows[...].astype(jnp.bfloat16), order, (0, 1))).astype(jnp.bfloat16)
    rows[...] = jnp.zeros_like(rows)
    for n, part in enumerate(halves(b_mid[...])):
        rows[n : n + 1, :] = part
    row, col = iota((40, channels + 16), 0), iota((40, channels + 16), 1)
    bias = product(rows[...].astype(jnp.bfloat16), one_hot(col, row + channels), (0, 0))
    row, col = iota((channels, channels + 16), 0), iota((channels, channels + 16), 1)
    w2[...] = (0.5 * (product(w_mid[...], one_hot(row, col), (1, 0)) + bias)).astype(jnp.bfloat16)
    rows[...] = jnp.zeros_like(rows)
    rows[0:taps, :] = w_out[...].astype(jnp.float32)
    outs = rows[...].astype(jnp.bfloat16)
    wo[...] = (0.5 * product(outs, order, (0, 1))).astype(jnp.bfloat16)
    row, col = iota((24, 40), 0), iota((24, 40), 1)
    for i in range(3):
        target = jnp.where((row & 7) < 4, (row & 3) * 9 + 3 * i + (row >> 3), -1)
        part = product(one_hot(col, target), outs, (1, 0))
        w3[:, i * channels : (i + 1) * channels] = part.astype(jnp.bfloat16)
    eye = one_hot(iota((channels, channels), 0), iota((channels, channels), 1))
    wm[...] = (0.5 * product(w_mid[...], eye, (0, 0))).astype(jnp.bfloat16)


def local(records, dest, w_in, b_in, w_mid, b_mid, w_out):
    count = lax.axis_size("rec")
    me = lax.axis_index("rec")
    parts, blocks, traces, samples = records.shape
    ves = dest.shape[1]
    tiles = blocks * traces
    channels = w_in.shape[0]
    group = group_of(count)
    steps = count // group
    width = group * 4 * samples
    far = [(s, s + 1) for s in range(1, count - 1, 2)]
    far += [(b, a) for a, b in far]
    near = [(s, s + 1) for s in range(0, count - 1, 2)]
    near += [(b, a) for a, b in near]

    flat = records.transpose(1, 2, 0, 3).reshape(tiles, parts, samples)
    from_far = lax.ppermute(flat, "rec", far)
    from_near = lax.ppermute(flat, "rec", near)

    f32, bf16 = jnp.float32, jnp.bfloat16
    shape = (steps, channels, width)
    blocked = 12 * math.prod(shape) > RESIDENT
    saved = [
        jax.ShapeDtypeStruct(shape, kind) if blocked else pltpu.VMEM(shape, kind)
        for kind in (bf16, bf16, f32, f32)
    ]
    held = [VMEM] * 4
    if blocked:
        held = [pl.BlockSpec((1, channels, width), lambda n: (n, 0, 0))] * 4
    grid = (steps,) if blocked else ()
    params = pltpu.CompilerParams(vmem_limit_bytes=16 << 20)
    args = (
        dest.T, w_in.T, b_in.reshape(1, channels), w_mid, b_mid.reshape(1, channels), w_out.T
    )
    idx, w1, w2, w3, wo, wm = pl.pallas_call(
        functools.partial(prep_kernel, blocks),
        out_shape=[jax.ShapeDtypeStruct((8, max(128, count)), jnp.int32)]
        + [
            jax.ShapeDtypeStruct(size, bf16)
            for size in (
                (channels, 48), (channels, channels + 16), (24, 3 * channels), (channels, 48),
                (channels, channels),
            )
        ],
        in_specs=[pl.BlockSpec(memory_space=pltpu.HBM)] * 6,
        out_specs=[VMEM] * 6,
        scratch_shapes=[pltpu.VMEM((40, channels), f32)]
        + [pltpu.VMEM(arg.shape, arg.dtype) for arg in args]
        + [pltpu.SemaphoreType.DMA((6,))],
        compiler_params=params,
        name="prepare",
    )(*[pltpu.with_memory_space_constraint(arg, pltpu.HBM) for arg in args])
    res, g, table, a1, a2, d1, d2 = pl.pallas_call(
        functools.partial(forward_kernel, group, blocked),
        grid=grid,
        out_shape=[
            jax.ShapeDtypeStruct(records.shape, f32),
            jax.ShapeDtypeStruct((tiles, parts, samples), bf16),
            pltpu.VMEM((3 * tiles + 2, 16, samples), bf16),
            *saved,
        ],
        in_specs=[SMEM] + [VMEM] * 6,
        out_specs=[VMEM] * 3 + held,
        scratch_shapes=[
            pltpu.VMEM((3 * tiles + 2, 16, samples), f32),
            pltpu.VMEM((count * 4, 8, samples), f32),
        ],
        compiler_params=params,
        name="forward",
    )(idx, from_near, flat, from_far, w1, w2, w3)

    g_far = lax.ppermute(g, "rec", far)
    g_near = lax.ppermute(g, "rec", near)
    sums = pl.pallas_call(
        functools.partial(backward_kernel, group, blocked),
        grid=grid,
        out_shape=jax.ShapeDtypeStruct((48 + channels // 2, 2 * channels), f32),
        in_specs=[SMEM] + [VMEM] * 6 + held,
        out_specs=VMEM,
        scratch_shapes=[
            pltpu.VMEM((3 * tiles + 2, 16, samples), bf16),
            pltpu.VMEM((3 * tiles + 2, 16, samples), f32),
            pltpu.VMEM((48, channels), f32),
            pltpu.VMEM((channels + 16, channels), f32),
            pltpu.VMEM((48, channels), f32),
        ],
        compiler_params=params,
        name="backward",
    )(idx, g_near, g, g_far, wo, wm, table, a1, a2, d1, d2)

    if count & (count - 1):
        terms = [lax.psum(sums, "rec")]
    else:
        terms = [sums]
        at = 1
        while at < count:
            wide = 2 if at == 1 or 2 * at == count else 4
            value = terms[0]
            if len(terms) == 2:
                value = terms[0] + terms[1]
            if len(terms) == 4:
                value = (terms[0] + terms[1]) + (terms[2] + terms[3])
            terms = [value] + [
                lax.ppermute(value, "rec", [(s, s ^ (k * at)) for s in range(count)])
                for k in range(1, wide)
            ]
            at *= wide

    scale = 1.0 / math.sqrt(parts * blocks * count * traces * samples)
    g_in, g_bin, g_mid, g_bmid, g_out = pl.pallas_call(
        functools.partial(finish_kernel, scale, parts),
        out_shape=[
            jax.ShapeDtypeStruct(shape, f32)
            for shape in (
                (parts * 9, channels), (1, channels), (channels, channels), (1, channels),
                (parts * 9, channels),
            )
        ],
        in_specs=[VMEM] * len(terms),
        out_specs=[VMEM] * 5,
        scratch_shapes=[pltpu.VMEM(sums.shape, f32)],
        compiler_params=params,
        name="finish",
    )(*terms)
    return (
        res,
        g_in.T,
        g_bin.reshape(channels),
        g_mid,
        g_bmid.reshape(channels),
        g_out.T,
    )


def solution(mesh):
    return jax.shard_map(
        local,
        mesh=mesh,
        in_specs=(
            P(None, ("groups", "rec"), None, None),
            P("groups", None),
            P(),
            P(),
            P(),
            P(),
            P(),
        ),
        out_specs=(
            P(None, ("groups", "rec"), None, None),
            P("groups", None),
            P("groups"),
            P("groups", None),
            P("groups"),
            P("groups", None),
        ),
        check_vma=False,
    )
```

```python
import functools
import math

import jax
import jax.numpy as jnp
from jax import lax
from jax.experimental import pallas as pl
from jax.experimental.pallas import tpu as pltpu
from jax.sharding import PartitionSpec as P

CAP = 2
VMEM = pl.BlockSpec(memory_space=pltpu.VMEM)
SMEM = pl.BlockSpec(memory_space=pltpu.SMEM)
RESIDENT = 24 << 20


def run(start, step, end, steps, blocked):
    if blocked:
        n = pl.program_id(0)
        pl.when(n == 0)(start)
        step(n, 0)
        pl.when(n == steps - 1)(end)
        return
    start()
    lax.fori_loop(0, steps, lambda n, carry: step(n, n), None)
    end()


def group_of(owners):
    for size in (8, 4, 2):
        if owners % size == 0:
            return size
    return 1


def fill_table(table, wide, pieces, tiles, flip, fill):
    for n, piece in enumerate(pieces):
        x = piece[...].astype(jnp.float32)
        samples = x.shape[2]
        lane = lax.broadcasted_iota(jnp.int32, x.shape, 2)
        before = jnp.where(lane == 0, 0.0, pltpu.roll(x, 1, 2))
        after = jnp.where(lane == samples - 1, 0.0, pltpu.roll(x, samples - 1, 2))
        at = pl.ds(n * tiles, tiles)
        wide[at, 0:4, :] = after if flip else before
        wide[at, 4:8, :] = x
        wide[at, 8:12, :] = before if flip else after
    last = len(pieces) * tiles
    wide[pl.ds(last, 2), 0:12, :] = jnp.zeros((2, 12, wide.shape[2]), jnp.float32)
    wide[:, 12:16, :] = jnp.full((last + 2, 4, wide.shape[2]), fill, jnp.float32)
    table[...] = wide[...].astype(jnp.bfloat16)


def act(y):
    t = jnp.tanh(y)
    q = 1.0 + t
    a = y * q
    return t, q, a


def own_of(x, group, samples):
    return jnp.concatenate(
        [x[:, (u * 6 + 1) * samples : (u * 6 + 5) * samples] for u in range(group)], axis=1
    )


def forward_kernel(
    group, blocked, idx, near, mine, far, w1, w2, w3,
    res, g, table, a1_ref, a2_ref, d1_ref, d2_ref, wide, est,
):
    tiles, parts, samples = mine.shape
    count = lax.axis_size("rec")
    me = lax.axis_index("rec")
    has_left = (me > 0).astype(jnp.float32)
    has_right = (me < count - 1).astype(jnp.float32)
    lane = lax.broadcasted_iota(jnp.int32, (8, samples), 1)
    low = (lane > 0).astype(jnp.float32)
    high = (lane < samples - 1).astype(jnp.float32)

    def start():
        fill_table(table, wide, (near, mine, far), tiles, False, 1.0)

    def step(n, block):
        tile = []
        for u in range(group):
            e = n * group + u
            line = []
            for r in range(4):
                at = idx[r, e]
                line += [table[at], table[at + 1]]
            tile.append(line)
        rhs = jnp.concatenate(
            [
                jnp.concatenate([tile[u][i + h] for u in range(group) for h in range(6)], axis=1)
                for i in range(3)
            ],
            axis=0,
        )
        y1 = jnp.dot(w1[...], rhs, preferred_element_type=jnp.float32)
        t, q, a = act(y1)
        a1 = a.astype(jnp.bfloat16)
        a1_ref[block] = own_of(a1, group, samples)
        d1_ref[block] = own_of(q + a * (1.0 - t), group, samples)
        ones = jnp.ones((16, a1.shape[1]), jnp.bfloat16)
        y2 = jnp.dot(
            w2[...], jnp.concatenate([a1, ones], axis=0), preferred_element_type=jnp.float32
        )
        t, q, a = act(y2)
        d2_ref[block] = own_of(q + a * (1.0 - t), group, samples)
        cut = []
        for u in range(group):
            for h in range(6):
                part = a[:, (u * 6 + h) * samples : (u * 6 + h + 1) * samples]
                if h == 0:
                    part = part * has_left
                if h == 5:
                    part = part * has_right
                cut.append(part.astype(jnp.bfloat16))
        a2_ref[block] = jnp.concatenate(
            [cut[u * 6 + h + 1] for u in range(group) for h in range(4)], axis=1
        )
        rhs = jnp.concatenate(
            [
                jnp.concatenate([cut[u * 6 + h + i] for u in range(group) for h in range(4)], axis=1)
                for i in range(3)
            ],
            axis=0,
        )
        terms = jnp.dot(w3[...], rhs, preferred_element_type=jnp.float32)
        for k in range(group * 4):
            part = terms[:, k * samples : (k + 1) * samples]
            total = (
                part[8:16]
                + pltpu.roll(part[0:8], 1, 1) * low
                + pltpu.roll(part[16:24], samples - 1, 1) * high
            )
            est[n * group * 4 + k] = total.astype(jnp.bfloat16).astype(jnp.float32)

    def end():
        for c in range(tiles // 2):
            at = [idx[4 + v, tiles // 2 + c] for v in range(4)]
            for k in range(2):
                total = (est[at[0] + k] + est[at[1] + k]) + (est[at[2] + k] + est[at[3] + k])
                value = total[0:parts] - mine[c * 2 + k].astype(jnp.float32)
                for o in range(parts):
                    res[o, c, k : k + 1, :] = value[o : o + 1]
                g[c * 2 + k] = value.astype(jnp.bfloat16)

    run(start, step, end, count // group, blocked)


def backward_kernel(
    group, blocked, idx, near, mine, far, wo, wm, table, a1_ref, a2_ref, d1_ref, d2_ref,
    out, gtable, wide, acc_in, acc_mid, acc_out,
):
    tiles, parts, samples = mine.shape
    owners = lax.axis_size("rec")
    channels = wo.shape[0]
    nt = functools.partial(
        lax.dot_general,
        dimension_numbers=(((1,), (1,)), ((), ())),
        preferred_element_type=jnp.float32,
    )

    def start():
        fill_table(gtable, wide, (near, mine, far), tiles, True, 0.0)
        acc_in[...] = jnp.zeros_like(acc_in)
        acc_mid[...] = jnp.zeros_like(acc_mid)
        acc_out[...] = jnp.zeros_like(acc_out)

    def step(n, block):
        tile, gtile = [], []
        for u in range(group):
            e = n * group + u
            at = [idx[r, e] for r in range(4)]
            tile.append(
                [table[at[0] + 1]] + [table[at[r] + k] for r in (1, 2) for k in (0, 1)] + [table[at[3]]]
            )
            gtile.append(
                [gtable[at[0] + 1]] + [gtable[at[r] + k] for r in (1, 2) for k in (0, 1)] + [gtable[at[3]]]
            )
        fields = jnp.concatenate(
            [
                jnp.concatenate([gtile[u][2 - i + h] for u in range(group) for h in range(4)], axis=1)
                for i in range(3)
            ],
            axis=0,
        )
        inputs = jnp.concatenate(
            [
                jnp.concatenate([tile[u][i + h] for u in range(group) for h in range(4)], axis=1)
                for i in range(3)
            ],
            axis=0,
        )
        da2 = jnp.dot(wo[...], fields, preferred_element_type=jnp.float32)
        dz2 = (da2 * d2_ref[block]).astype(jnp.bfloat16)
        acc_out[...] += nt(fields, a2_ref[block])
        da1 = jnp.dot(wm[...], dz2, preferred_element_type=jnp.float32)
        ones = jnp.ones((16, dz2.shape[1]), jnp.bfloat16)
        acc_mid[...] += nt(jnp.concatenate([a1_ref[block], ones], axis=0), dz2)
        dz1 = (da1 * d1_ref[block]).astype(jnp.bfloat16)
        acc_in[...] += nt(inputs, dz1)
    def end():
        out[0:48, 0:channels] = acc_in[...]
        out[0:48, channels : 2 * channels] = acc_out[...]
        out[12:13, 0:channels] = acc_mid[channels : channels + 1, :]
        mid = acc_mid[0:channels, :].T
        out[48 : 48 + channels // 2, 0:channels] = mid[0 : channels // 2]
        out[48 : 48 + channels // 2, channels : 2 * channels] = mid[channels // 2 : channels]

    run(start, step, end, owners // group, blocked)


def finish_kernel(scale, parts, *refs):
    terms, (g_in, g_bin, g_mid, g_bmid, g_out, held) = refs[:-6], refs[-6:]
    values = [ref[...] for ref in terms]
    while len(values) > 1:
        values = [values[k] + values[k + 1] for k in range(0, len(values), 2)]
    held[...] = values[0] * scale
    channels = g_mid.shape[0]
    for o in range(parts):
        for i in range(3):
            for j in range(3):
                row = held[i * 16 + j * 4 + o : i * 16 + j * 4 + o + 1, :]
                at = o * 9 + 3 * i + j
                g_in[at : at + 1, :] = row[:, 0:channels]
                g_out[at : at + 1, :] = row[:, channels : 2 * channels]
    g_bin[...] = held[28:29, 0:channels]
    g_bmid[...] = held[12:13, 0:channels]
    half = channels // 2
    g_mid[0:half] = held[48 : 48 + half, 0:channels]
    g_mid[half:channels] = held[48 : 48 + half, channels : 2 * channels]


def halves(b):
    high = b.astype(jnp.bfloat16).astype(jnp.float32)
    rest = b - high
    mid = rest.astype(jnp.bfloat16).astype(jnp.float32)
    return [high, mid, rest - mid]


def one_hot(a, b):
    return (a == b).astype(jnp.float32).astype(jnp.bfloat16)


def iota(shape, dim):
    return lax.broadcasted_iota(jnp.int32, shape, dim)


def product(a, b, over):
    return lax.dot_general(
        a, b, dimension_numbers=(((over[0],), (over[1],)), ((), ())),
        preferred_element_type=jnp.float32,
    )


def prep_kernel(blocks, *refs):
    args, (idx, w1, w2, w3, wo, wm, rows), held, sems = refs[:6], refs[6:13], refs[13:19], refs[19]
    copies = [
        pltpu.make_async_copy(src, dst, sems.at[n]) for n, (src, dst) in enumerate(zip(args, held))
    ]
    for copy in copies:
        copy.start()
    for copy in copies:
        copy.wait()
    dest, w_in, b_in, w_mid, b_mid, w_out = held
    count = lax.axis_size("rec")
    me = lax.axis_index("rec")
    ves, total = dest.shape
    channels = w_mid.shape[0]
    empty = 6 * blocks
    at = lax.rem((count + 1 - me) * blocks, total)
    wide = jnp.concatenate([dest[...], jnp.zeros((8 - ves, total), jnp.int32)], axis=0)
    near = pltpu.roll(wide, at, 1)[:, 0:128]
    lane = iota((8, 128), 1)
    low = jnp.where(me > 0, 0, blocks)
    high = jnp.where(me < count - 1, 3 * blocks, 2 * blocks)
    near = jnp.where((lane >= low) & (lane < high), near, -1)
    owner = iota((count, 128), 0)
    hits = [(near[v : v + 1] == owner).astype(jnp.float32) for v in range(ves)]
    before = iota((128, 128), 0)
    after = iota((128, 128), 1)
    segment = (after >= blocks).astype(jnp.int32) + (after >= 2 * blocks).astype(jnp.int32)
    tri = ((before < after) & (before >= segment * blocks)).astype(jnp.float32).astype(jnp.bfloat16)
    rank = product((hits[0] + hits[1] + hits[2] + hits[3]).astype(jnp.bfloat16), tri, (1, 0))
    zeroth = jnp.zeros((count, 128), jnp.float32)
    first = jnp.zeros((count, 128), jnp.float32)
    for v in range(ves):
        zeroth += hits[v] * (rank == 0.0).astype(jnp.float32)
        first += hits[v] * (rank == 1.0).astype(jnp.float32)
        item = jnp.sum(hits[v] * rank, axis=0, keepdims=True)
        idx[4 + v : 5 + v, 0:128] = near[v : v + 1] * 4 + item.astype(jnp.int32) * 2
        rank = rank + hits[v]
    line = iota((8, 128), 0)
    inside = lambda k: (lane >= k * blocks) & (lane < (k + 1) * blocks)
    place = (2 * lane - empty).astype(jnp.float32)
    swap = jnp.where(lax.rem(me, 2) == 1, 0, 4 * blocks).astype(jnp.float32)
    ones = jnp.where(line == 0, jnp.where(inside(0), place + swap, 0.0), 0.0)
    ones = jnp.where((line == 2) & inside(1), place, ones)
    zeros = jnp.where(line == 3, jnp.where(inside(2), place - swap, 0.0), 0.0)
    zeros = jnp.where((line == 1) & inside(1), place, zeros)
    pick = product(ones.astype(jnp.bfloat16), first.astype(jnp.bfloat16), (1, 1)) + product(
        zeros.astype(jnp.bfloat16), zeroth.astype(jnp.bfloat16), (1, 1)
    )
    idx[0:4, 0:count] = pick[0:4].astype(jnp.int32) + empty

    taps = w_in.shape[0]
    row, col = iota((48, 40), 0), iota((48, 40), 1)
    tap, extra = row & 15, (row & 15) - 12
    target = (row & 3) * 9 + 3 * (row >> 4) + ((row >> 2) & 3)
    target = jnp.where(tap < 12, target, jnp.where((row >> 4) == 1, taps + extra, -1))
    order = one_hot(col, target)
    rows[...] = jnp.zeros_like(rows)
    rows[0:taps, :] = w_in[...].astype(jnp.float32)
    for n, part in enumerate(halves(b_in[...])):
        rows[taps + n : taps + n + 1, :] = part
    w1[...] = (0.5 * product(rows[...].astype(jnp.bfloat16), order, (0, 1))).astype(jnp.bfloat16)
    rows[...] = jnp.zeros_like(rows)
    for n, part in enumerate(halves(b_mid[...])):
        rows[n : n + 1, :] = part
    row, col = iota((40, channels + 16), 0), iota((40, channels + 16), 1)
    bias = product(rows[...].astype(jnp.bfloat16), one_hot(col, row + channels), (0, 0))
    row, col = iota((channels, channels + 16), 0), iota((channels, channels + 16), 1)
    w2[...] = (0.5 * (product(w_mid[...], one_hot(row, col), (1, 0)) + bias)).astype(jnp.bfloat16)
    rows[...] = jnp.zeros_like(rows)
    rows[0:taps, :] = w_out[...].astype(jnp.float32)
    outs = rows[...].astype(jnp.bfloat16)
    wo[...] = (0.5 * product(outs, order, (0, 1))).astype(jnp.bfloat16)
    row, col = iota((24, 40), 0), iota((24, 40), 1)
    for i in range(3):
        target = jnp.where((row & 7) < 4, (row & 3) * 9 + 3 * i + (row >> 3), -1)
        part = product(one_hot(col, target), outs, (1, 0))
        w3[:, i * channels : (i + 1) * channels] = part.astype(jnp.bfloat16)
    eye = one_hot(iota((channels, channels), 0), iota((channels, channels), 1))
    wm[...] = (0.5 * product(w_mid[...], eye, (0, 0))).astype(jnp.bfloat16)


def local(records, dest, w_in, b_in, w_mid, b_mid, w_out):
    count = lax.axis_size("rec")
    me = lax.axis_index("rec")
    parts, blocks, traces, samples = records.shape
    ves = dest.shape[1]
    tiles = blocks * traces
    channels = w_in.shape[0]
    group = group_of(count)
    steps = count // group
    width = group * 4 * samples
    far = [(s, s + 1) for s in range(1, count - 1, 2)]
    far += [(b, a) for a, b in far]
    near = [(s, s + 1) for s in range(0, count - 1, 2)]
    near += [(b, a) for a, b in near]

    flat = records.transpose(1, 2, 0, 3).reshape(tiles, parts, samples)
    from_far = lax.ppermute(flat, "rec", far)
    from_near = lax.ppermute(flat, "rec", near)

    f32, bf16 = jnp.float32, jnp.bfloat16
    shape = (steps, channels, width)
    blocked = 12 * math.prod(shape) > RESIDENT
    saved = [
        jax.ShapeDtypeStruct(shape, kind) if blocked else pltpu.VMEM(shape, kind)
        for kind in (bf16, bf16, f32, f32)
    ]
    held = [VMEM] * 4
    if blocked:
        held = [pl.BlockSpec((1, channels, width), lambda n: (n, 0, 0))] * 4
    grid = (steps,) if blocked else ()
    params = pltpu.CompilerParams(vmem_limit_bytes=16 << 20)
    args = (
        dest.T, w_in.T, b_in.reshape(1, channels), w_mid, b_mid.reshape(1, channels), w_out.T
    )
    idx, w1, w2, w3, wo, wm = pl.pallas_call(
        functools.partial(prep_kernel, blocks),
        out_shape=[jax.ShapeDtypeStruct((8, max(128, count)), jnp.int32)]
        + [
            jax.ShapeDtypeStruct(size, bf16)
            for size in (
                (channels, 48), (channels, channels + 16), (24, 3 * channels), (channels, 48),
                (channels, channels),
            )
        ],
        in_specs=[pl.BlockSpec(memory_space=pltpu.HBM)] * 6,
        out_specs=[VMEM] * 6,
        scratch_shapes=[pltpu.VMEM((40, channels), f32)]
        + [pltpu.VMEM(arg.shape, arg.dtype) for arg in args]
        + [pltpu.SemaphoreType.DMA((6,))],
        compiler_params=params,
        name="prepare",
    )(*[pltpu.with_memory_space_constraint(arg, pltpu.HBM) for arg in args])
    res, g, table, a1, a2, d1, d2 = pl.pallas_call(
        functools.partial(forward_kernel, group, blocked),
        grid=grid,
        out_shape=[
            jax.ShapeDtypeStruct(records.shape, f32),
            jax.ShapeDtypeStruct((tiles, parts, samples), bf16),
            pltpu.VMEM((3 * tiles + 2, 16, samples), bf16),
            *saved,
        ],
        in_specs=[SMEM] + [VMEM] * 6,
        out_specs=[VMEM] * 3 + held,
        scratch_shapes=[
            pltpu.VMEM((3 * tiles + 2, 16, samples), f32),
            pltpu.VMEM((count * 4, 8, samples), f32),
        ],
        compiler_params=params,
        name="forward",
    )(idx, from_near, flat, from_far, w1, w2, w3)

    g_far = lax.ppermute(g, "rec", far)
    g_near = lax.ppermute(g, "rec", near)
    sums = pl.pallas_call(
        functools.partial(backward_kernel, group, blocked),
        grid=grid,
        out_shape=jax.ShapeDtypeStruct((48 + channels // 2, 2 * channels), f32),
        in_specs=[SMEM] + [VMEM] * 6 + held,
        out_specs=VMEM,
        scratch_shapes=[
            pltpu.VMEM((3 * tiles + 2, 16, samples), bf16),
            pltpu.VMEM((3 * tiles + 2, 16, samples), f32),
            pltpu.VMEM((48, channels), f32),
            pltpu.VMEM((channels + 16, channels), f32),
            pltpu.VMEM((48, channels), f32),
        ],
        compiler_params=params,
        name="backward",
    )(idx, g_near, g, g_far, wo, wm, table, a1, a2, d1, d2)

    if count & (count - 1):
        terms = [lax.psum(sums, "rec")]
    else:
        terms = [sums]
        at = 1
        while at < count:
            wide = 2 if at == 1 or 2 * at == count else 4
            value = terms[0]
            if len(terms) == 2:
                value = terms[0] + terms[1]
            if len(terms) == 4:
                value = (terms[0] + terms[1]) + (terms[2] + terms[3])
            terms = [value] + [
                lax.ppermute(value, "rec", [(s, s ^ (k * at)) for s in range(count)])
                for k in range(1, wide)
            ]
            at *= wide

    scale = 1.0 / math.sqrt(parts * blocks * count * traces * samples)
    g_in, g_bin, g_mid, g_bmid, g_out = pl.pallas_call(
        functools.partial(finish_kernel, scale, parts),
        out_shape=[
            jax.ShapeDtypeStruct(shape, f32)
            for shape in (
                (parts * 9, channels), (1, channels), (channels, channels), (1, channels),
                (parts * 9, channels),
            )
        ],
        in_specs=[VMEM] * len(terms),
        out_specs=[VMEM] * 5,
        scratch_shapes=[pltpu.VMEM(sums.shape, f32)],
        compiler_params=params,
        name="finish",
    )(*terms)
    return (
        res,
        g_in.T,
        g_bin.reshape(channels),
        g_mid,
        g_bmid.reshape(channels),
        g_out.T,
    )


def solution(mesh):
    return jax.shard_map(
        local,
        mesh=mesh,
        in_specs=(
            P(None, ("groups", "rec"), None, None),
            P("groups", None),
            P(),
            P(),
            P(),
            P(),
            P(),
        ),
        out_specs=(
            P(None, ("groups", "rec"), None, None),
            P("groups", None),
            P("groups"),
            P("groups", None),
            P("groups"),
            P("groups", None),
        ),
        check_vma=False,
    )
```

```python
import functools
import math

import jax
import jax.numpy as jnp
from jax import lax
from jax.experimental import pallas as pl
from jax.experimental.pallas import tpu as pltpu
from jax.sharding import PartitionSpec as P

CAP = 2
VMEM = pl.BlockSpec(memory_space=pltpu.VMEM)
SMEM = pl.BlockSpec(memory_space=pltpu.SMEM)
RESIDENT = 24 << 20


def run(start, step, end, steps, blocked):
    if blocked:
        n = pl.program_id(0)
        pl.when(n == 0)(start)
        step(n, 0)
        pl.when(n == steps - 1)(end)
        return
    start()
    lax.fori_loop(0, steps, lambda n, carry: step(n, n), None)
    end()


def group_of(owners):
    for size in (16, 8, 4, 2):
        if owners % size == 0:
            return size
    return 1


def fill_table(table, wide, pieces, tiles, flip, fill):
    for n, piece in enumerate(pieces):
        x = piece[...].astype(jnp.float32)
        samples = x.shape[2]
        lane = lax.broadcasted_iota(jnp.int32, x.shape, 2)
        before = jnp.where(lane == 0, 0.0, pltpu.roll(x, 1, 2))
        after = jnp.where(lane == samples - 1, 0.0, pltpu.roll(x, samples - 1, 2))
        at = pl.ds(n * tiles, tiles)
        wide[at, 0:4, :] = after if flip else before
        wide[at, 4:8, :] = x
        wide[at, 8:12, :] = before if flip else after
    last = len(pieces) * tiles
    wide[pl.ds(last, 2), 0:12, :] = jnp.zeros((2, 12, wide.shape[2]), jnp.float32)
    wide[:, 12:16, :] = jnp.full((last + 2, 4, wide.shape[2]), fill, jnp.float32)
    table[...] = wide[...].astype(jnp.bfloat16)


def act(y):
    t = jnp.tanh(y)
    q = 1.0 + t
    a = y * q
    return t, q, a


def own_of(x, group, samples):
    return jnp.concatenate(
        [x[:, (u * 6 + 1) * samples : (u * 6 + 5) * samples] for u in range(group)], axis=1
    )


def forward_kernel(
    group, blocked, idx, near, mine, far, w1, w2, w3,
    res, g, table, a1_ref, a2_ref, d1_ref, d2_ref, wide, est,
):
    tiles, parts, samples = mine.shape
    count = lax.axis_size("rec")
    me = lax.axis_index("rec")
    has_left = (me > 0).astype(jnp.float32)
    has_right = (me < count - 1).astype(jnp.float32)
    lane = lax.broadcasted_iota(jnp.int32, (8, samples), 1)
    low = (lane > 0).astype(jnp.float32)
    high = (lane < samples - 1).astype(jnp.float32)

    def start():
        fill_table(table, wide, (near, mine, far), tiles, False, 1.0)

    def step(n, block):
        tile = []
        for u in range(group):
            e = n * group + u
            line = []
            for r in range(4):
                at = idx[r, e]
                line += [table[at], table[at + 1]]
            tile.append(line)
        rhs = jnp.concatenate(
            [
                jnp.concatenate([tile[u][i + h] for u in range(group) for h in range(6)], axis=1)
                for i in range(3)
            ],
            axis=0,
        )
        y1 = jnp.dot(w1[...], rhs, preferred_element_type=jnp.float32)
        t, q, a = act(y1)
        a1 = a.astype(jnp.bfloat16)
        a1_ref[block] = own_of(a1, group, samples)
        d1_ref[block] = own_of(q + a * (1.0 - t), group, samples)
        ones = jnp.ones((16, a1.shape[1]), jnp.bfloat16)
        y2 = jnp.dot(
            w2[...], jnp.concatenate([a1, ones], axis=0), preferred_element_type=jnp.float32
        )
        t, q, a = act(y2)
        d2_ref[block] = own_of(q + a * (1.0 - t), group, samples)
        cut = []
        for u in range(group):
            for h in range(6):
                part = a[:, (u * 6 + h) * samples : (u * 6 + h + 1) * samples]
                if h == 0:
                    part = part * has_left
                if h == 5:
                    part = part * has_right
                cut.append(part.astype(jnp.bfloat16))
        a2_ref[block] = jnp.concatenate(
            [cut[u * 6 + h + 1] for u in range(group) for h in range(4)], axis=1
        )
        rhs = jnp.concatenate(
            [
                jnp.concatenate([cut[u * 6 + h + i] for u in range(group) for h in range(4)], axis=1)
                for i in range(3)
            ],
            axis=0,
        )
        terms = jnp.dot(w3[...], rhs, preferred_element_type=jnp.float32)
        for k in range(group * 4):
            part = terms[:, k * samples : (k + 1) * samples]
            total = (
                part[8:16]
                + pltpu.roll(part[0:8], 1, 1) * low
                + pltpu.roll(part[16:24], samples - 1, 1) * high
            )
            est[n * group * 4 + k] = total.astype(jnp.bfloat16).astype(jnp.float32)

    def end():
        for c in range(tiles // 2):
            at = [idx[4 + v, tiles // 2 + c] for v in range(4)]
            for k in range(2):
                total = (est[at[0] + k] + est[at[1] + k]) + (est[at[2] + k] + est[at[3] + k])
                value = total[0:parts] - mine[c * 2 + k].astype(jnp.float32)
                for o in range(parts):
                    res[o, c, k : k + 1, :] = value[o : o + 1]
                g[c * 2 + k] = value.astype(jnp.bfloat16)

    run(start, step, end, count // group, blocked)


def backward_kernel(
    group, blocked, idx, near, mine, far, wo, wm, table, a1_ref, a2_ref, d1_ref, d2_ref,
    out, gtable, wide, acc_in, acc_mid, acc_out,
):
    tiles, parts, samples = mine.shape
    owners = lax.axis_size("rec")
    channels = wo.shape[0]
    nt = functools.partial(
        lax.dot_general,
        dimension_numbers=(((1,), (1,)), ((), ())),
        preferred_element_type=jnp.float32,
    )

    def start():
        fill_table(gtable, wide, (near, mine, far), tiles, True, 0.0)
        acc_in[...] = jnp.zeros_like(acc_in)
        acc_mid[...] = jnp.zeros_like(acc_mid)
        acc_out[...] = jnp.zeros_like(acc_out)

    def step(n, block):
        tile, gtile = [], []
        for u in range(group):
            e = n * group + u
            at = [idx[r, e] for r in range(4)]
            tile.append(
                [table[at[0] + 1]] + [table[at[r] + k] for r in (1, 2) for k in (0, 1)] + [table[at[3]]]
            )
            gtile.append(
                [gtable[at[0] + 1]] + [gtable[at[r] + k] for r in (1, 2) for k in (0, 1)] + [gtable[at[3]]]
            )
        fields = jnp.concatenate(
            [
                jnp.concatenate([gtile[u][2 - i + h] for u in range(group) for h in range(4)], axis=1)
                for i in range(3)
            ],
            axis=0,
        )
        inputs = jnp.concatenate(
            [
                jnp.concatenate([tile[u][i + h] for u in range(group) for h in range(4)], axis=1)
                for i in range(3)
            ],
            axis=0,
        )
        da2 = jnp.dot(wo[...], fields, preferred_element_type=jnp.float32)
        dz2 = (da2 * d2_ref[block]).astype(jnp.bfloat16)
        acc_out[...] += nt(fields, a2_ref[block])
        da1 = jnp.dot(wm[...], dz2, preferred_element_type=jnp.float32)
        ones = jnp.ones((16, dz2.shape[1]), jnp.bfloat16)
        acc_mid[...] += nt(jnp.concatenate([a1_ref[block], ones], axis=0), dz2)
        dz1 = (da1 * d1_ref[block]).astype(jnp.bfloat16)
        acc_in[...] += nt(inputs, dz1)
    def end():
        out[0:48, 0:channels] = acc_in[...]
        out[0:48, channels : 2 * channels] = acc_out[...]
        out[12:13, 0:channels] = acc_mid[channels : channels + 1, :]
        mid = acc_mid[0:channels, :].T
        out[48 : 48 + channels // 2, 0:channels] = mid[0 : channels // 2]
        out[48 : 48 + channels // 2, channels : 2 * channels] = mid[channels // 2 : channels]

    run(start, step, end, owners // group, blocked)


def finish_kernel(scale, parts, *refs):
    terms, (g_in, g_bin, g_mid, g_bmid, g_out, held) = refs[:-6], refs[-6:]
    values = [ref[...] for ref in terms]
    while len(values) > 1:
        values = [values[k] + values[k + 1] for k in range(0, len(values), 2)]
    held[...] = values[0] * scale
    channels = g_mid.shape[0]
    for o in range(parts):
        for i in range(3):
            for j in range(3):
                row = held[i * 16 + j * 4 + o : i * 16 + j * 4 + o + 1, :]
                at = o * 9 + 3 * i + j
                g_in[at : at + 1, :] = row[:, 0:channels]
                g_out[at : at + 1, :] = row[:, channels : 2 * channels]
    g_bin[...] = held[28:29, 0:channels]
    g_bmid[...] = held[12:13, 0:channels]
    half = channels // 2
    g_mid[0:half] = held[48 : 48 + half, 0:channels]
    g_mid[half:channels] = held[48 : 48 + half, channels : 2 * channels]


def halves(b):
    high = b.astype(jnp.bfloat16).astype(jnp.float32)
    rest = b - high
    mid = rest.astype(jnp.bfloat16).astype(jnp.float32)
    return [high, mid, rest - mid]


def one_hot(a, b):
    return (a == b).astype(jnp.float32).astype(jnp.bfloat16)


def iota(shape, dim):
    return lax.broadcasted_iota(jnp.int32, shape, dim)


def product(a, b, over):
    return lax.dot_general(
        a, b, dimension_numbers=(((over[0],), (over[1],)), ((), ())),
        preferred_element_type=jnp.float32,
    )


def prep_kernel(blocks, *refs):
    args, (idx, w1, w2, w3, wo, wm, rows), held, sems = refs[:6], refs[6:13], refs[13:19], refs[19]
    copies = [
        pltpu.make_async_copy(src, dst, sems.at[n]) for n, (src, dst) in enumerate(zip(args, held))
    ]
    for copy in copies:
        copy.start()
    for copy in copies:
        copy.wait()
    dest, w_in, b_in, w_mid, b_mid, w_out = held
    count = lax.axis_size("rec")
    me = lax.axis_index("rec")
    ves, total = dest.shape
    channels = w_mid.shape[0]
    empty = 6 * blocks
    at = lax.rem((count + 1 - me) * blocks, total)
    wide = jnp.concatenate([dest[...], jnp.zeros((8 - ves, total), jnp.int32)], axis=0)
    near = pltpu.roll(wide, at, 1)[:, 0:128]
    lane = iota((8, 128), 1)
    low = jnp.where(me > 0, 0, blocks)
    high = jnp.where(me < count - 1, 3 * blocks, 2 * blocks)
    near = jnp.where((lane >= low) & (lane < high), near, -1)
    owner = iota((count, 128), 0)
    hits = [(near[v : v + 1] == owner).astype(jnp.float32) for v in range(ves)]
    before = iota((128, 128), 0)
    after = iota((128, 128), 1)
    segment = (after >= blocks).astype(jnp.int32) + (after >= 2 * blocks).astype(jnp.int32)
    tri = ((before < after) & (before >= segment * blocks)).astype(jnp.float32).astype(jnp.bfloat16)
    rank = product((hits[0] + hits[1] + hits[2] + hits[3]).astype(jnp.bfloat16), tri, (1, 0))
    zeroth = jnp.zeros((count, 128), jnp.float32)
    first = jnp.zeros((count, 128), jnp.float32)
    for v in range(ves):
        zeroth += hits[v] * (rank == 0.0).astype(jnp.float32)
        first += hits[v] * (rank == 1.0).astype(jnp.float32)
        item = jnp.sum(hits[v] * rank, axis=0, keepdims=True)
        idx[4 + v : 5 + v, 0:128] = near[v : v + 1] * 4 + item.astype(jnp.int32) * 2
        rank = rank + hits[v]
    line = iota((8, 128), 0)
    inside = lambda k: (lane >= k * blocks) & (lane < (k + 1) * blocks)
    place = (2 * lane - empty).astype(jnp.float32)
    swap = jnp.where(lax.rem(me, 2) == 1, 0, 4 * blocks).astype(jnp.float32)
    ones = jnp.where(line == 0, jnp.where(inside(0), place + swap, 0.0), 0.0)
    ones = jnp.where((line == 2) & inside(1), place, ones)
    zeros = jnp.where(line == 3, jnp.where(inside(2), place - swap, 0.0), 0.0)
    zeros = jnp.where((line == 1) & inside(1), place, zeros)
    pick = product(ones.astype(jnp.bfloat16), first.astype(jnp.bfloat16), (1, 1)) + product(
        zeros.astype(jnp.bfloat16), zeroth.astype(jnp.bfloat16), (1, 1)
    )
    idx[0:4, 0:count] = pick[0:4].astype(jnp.int32) + empty

    taps = w_in.shape[0]
    row, col = iota((48, 40), 0), iota((48, 40), 1)
    tap, extra = row & 15, (row & 15) - 12
    target = (row & 3) * 9 + 3 * (row >> 4) + ((row >> 2) & 3)
    target = jnp.where(tap < 12, target, jnp.where((row >> 4) == 1, taps + extra, -1))
    order = one_hot(col, target)
    rows[...] = jnp.zeros_like(rows)
    rows[0:taps, :] = w_in[...].astype(jnp.float32)
    for n, part in enumerate(halves(b_in[...])):
        rows[taps + n : taps + n + 1, :] = part
    w1[...] = (0.5 * product(rows[...].astype(jnp.bfloat16), order, (0, 1))).astype(jnp.bfloat16)
    rows[...] = jnp.zeros_like(rows)
    for n, part in enumerate(halves(b_mid[...])):
        rows[n : n + 1, :] = part
    row, col = iota((40, channels + 16), 0), iota((40, channels + 16), 1)
    bias = product(rows[...].astype(jnp.bfloat16), one_hot(col, row + channels), (0, 0))
    row, col = iota((channels, channels + 16), 0), iota((channels, channels + 16), 1)
    w2[...] = (0.5 * (product(w_mid[...], one_hot(row, col), (1, 0)) + bias)).astype(jnp.bfloat16)
    rows[...] = jnp.zeros_like(rows)
    rows[0:taps, :] = w_out[...].astype(jnp.float32)
    outs = rows[...].astype(jnp.bfloat16)
    wo[...] = (0.5 * product(outs, order, (0, 1))).astype(jnp.bfloat16)
    row, col = iota((24, 40), 0), iota((24, 40), 1)
    for i in range(3):
        target = jnp.where((row & 7) < 4, (row & 3) * 9 + 3 * i + (row >> 3), -1)
        part = product(one_hot(col, target), outs, (1, 0))
        w3[:, i * channels : (i + 1) * channels] = part.astype(jnp.bfloat16)
    eye = one_hot(iota((channels, channels), 0), iota((channels, channels), 1))
    wm[...] = (0.5 * product(w_mid[...], eye, (0, 0))).astype(jnp.bfloat16)


def local(records, dest, w_in, b_in, w_mid, b_mid, w_out):
    count = lax.axis_size("rec")
    me = lax.axis_index("rec")
    parts, blocks, traces, samples = records.shape
    ves = dest.shape[1]
    tiles = blocks * traces
    channels = w_in.shape[0]
    group = group_of(count)
    steps = count // group
    width = group * 4 * samples
    far = [(s, s + 1) for s in range(1, count - 1, 2)]
    far += [(b, a) for a, b in far]
    near = [(s, s + 1) for s in range(0, count - 1, 2)]
    near += [(b, a) for a, b in near]

    flat = records.transpose(1, 2, 0, 3).reshape(tiles, parts, samples)
    from_far = lax.ppermute(flat, "rec", far)
    from_near = lax.ppermute(flat, "rec", near)

    f32, bf16 = jnp.float32, jnp.bfloat16
    shape = (steps, channels, width)
    blocked = 12 * math.prod(shape) > RESIDENT
    saved = [
        jax.ShapeDtypeStruct(shape, kind) if blocked else pltpu.VMEM(shape, kind)
        for kind in (bf16, bf16, f32, f32)
    ]
    held = [VMEM] * 4
    if blocked:
        held = [pl.BlockSpec((1, channels, width), lambda n: (n, 0, 0))] * 4
    grid = (steps,) if blocked else ()
    params = pltpu.CompilerParams(vmem_limit_bytes=16 << 20)
    args = (
        dest.T, w_in.T, b_in.reshape(1, channels), w_mid, b_mid.reshape(1, channels), w_out.T
    )
    idx, w1, w2, w3, wo, wm = pl.pallas_call(
        functools.partial(prep_kernel, blocks),
        out_shape=[jax.ShapeDtypeStruct((8, max(128, count)), jnp.int32)]
        + [
            jax.ShapeDtypeStruct(size, bf16)
            for size in (
                (channels, 48), (channels, channels + 16), (24, 3 * channels), (channels, 48),
                (channels, channels),
            )
        ],
        in_specs=[pl.BlockSpec(memory_space=pltpu.HBM)] * 6,
        out_specs=[VMEM] * 6,
        scratch_shapes=[pltpu.VMEM((40, channels), f32)]
        + [pltpu.VMEM(arg.shape, arg.dtype) for arg in args]
        + [pltpu.SemaphoreType.DMA((6,))],
        compiler_params=params,
        name="prepare",
    )(*[pltpu.with_memory_space_constraint(arg, pltpu.HBM) for arg in args])
    res, g, table, a1, a2, d1, d2 = pl.pallas_call(
        functools.partial(forward_kernel, group, blocked),
        grid=grid,
        out_shape=[
            jax.ShapeDtypeStruct(records.shape, f32),
            jax.ShapeDtypeStruct((tiles, parts, samples), bf16),
            pltpu.VMEM((3 * tiles + 2, 16, samples), bf16),
            *saved,
        ],
        in_specs=[SMEM] + [VMEM] * 6,
        out_specs=[VMEM] * 3 + held,
        scratch_shapes=[
            pltpu.VMEM((3 * tiles + 2, 16, samples), f32),
            pltpu.VMEM((count * 4, 8, samples), f32),
        ],
        compiler_params=params,
        name="forward",
    )(idx, from_near, flat, from_far, w1, w2, w3)

    g_far = lax.ppermute(g, "rec", far)
    g_near = lax.ppermute(g, "rec", near)
    sums = pl.pallas_call(
        functools.partial(backward_kernel, group, blocked),
        grid=grid,
        out_shape=jax.ShapeDtypeStruct((48 + channels // 2, 2 * channels), f32),
        in_specs=[SMEM] + [VMEM] * 6 + held,
        out_specs=VMEM,
        scratch_shapes=[
            pltpu.VMEM((3 * tiles + 2, 16, samples), bf16),
            pltpu.VMEM((3 * tiles + 2, 16, samples), f32),
            pltpu.VMEM((48, channels), f32),
            pltpu.VMEM((channels + 16, channels), f32),
            pltpu.VMEM((48, channels), f32),
        ],
        compiler_params=params,
        name="backward",
    )(idx, g_near, g, g_far, wo, wm, table, a1, a2, d1, d2)

    if count & (count - 1):
        terms = [lax.psum(sums, "rec")]
    else:
        terms = [sums]
        at = 1
        while at < count:
            wide = 2 if at == 1 or 2 * at == count else 4
            value = terms[0]
            if len(terms) == 2:
                value = terms[0] + terms[1]
            if len(terms) == 4:
                value = (terms[0] + terms[1]) + (terms[2] + terms[3])
            terms = [value] + [
                lax.ppermute(value, "rec", [(s, s ^ (k * at)) for s in range(count)])
                for k in range(1, wide)
            ]
            at *= wide

    scale = 1.0 / math.sqrt(parts * blocks * count * traces * samples)
    g_in, g_bin, g_mid, g_bmid, g_out = pl.pallas_call(
        functools.partial(finish_kernel, scale, parts),
        out_shape=[
            jax.ShapeDtypeStruct(shape, f32)
            for shape in (
                (parts * 9, channels), (1, channels), (channels, channels), (1, channels),
                (parts * 9, channels),
            )
        ],
        in_specs=[VMEM] * len(terms),
        out_specs=[VMEM] * 5,
        scratch_shapes=[pltpu.VMEM(sums.shape, f32)],
        compiler_params=params,
        name="finish",
    )(*terms)
    return (
        res,
        g_in.T,
        g_bin.reshape(channels),
        g_mid,
        g_bmid.reshape(channels),
        g_out.T,
    )


def solution(mesh):
    return jax.shard_map(
        local,
        mesh=mesh,
        in_specs=(
            P(None, ("groups", "rec"), None, None),
            P("groups", None),
            P(),
            P(),
            P(),
            P(),
            P(),
        ),
        out_specs=(
            P(None, ("groups", "rec"), None, None),
            P("groups", None),
            P("groups"),
            P("groups", None),
            P("groups"),
            P("groups", None),
        ),
        check_vma=False,
    )
```

```python
import functools
import math

import jax
import jax.numpy as jnp
from jax import lax
from jax.experimental import pallas as pl
from jax.experimental.pallas import tpu as pltpu
from jax.sharding import PartitionSpec as P

CAP = 2
VMEM = pl.BlockSpec(memory_space=pltpu.VMEM)
SMEM = pl.BlockSpec(memory_space=pltpu.SMEM)
RESIDENT = 24 << 20


def run(start, step, end, steps, blocked):
    if blocked:
        n = pl.program_id(0)
        pl.when(n == 0)(start)
        step(n, 0)
        pl.when(n == steps - 1)(end)
        return
    start()
    lax.fori_loop(0, steps, lambda n, carry: step(n, n), None)
    end()


def group_of(owners):
    for size in (16, 8, 4, 2):
        if owners % size == 0:
            return size
    return 1


def fill_table(table, wide, pieces, tiles, flip, fill):
    for n, piece in enumerate(pieces):
        x = piece[...].astype(jnp.float32)
        samples = x.shape[2]
        lane = lax.broadcasted_iota(jnp.int32, x.shape, 2)
        before = jnp.where(lane == 0, 0.0, pltpu.roll(x, 1, 2))
        after = jnp.where(lane == samples - 1, 0.0, pltpu.roll(x, samples - 1, 2))
        at = pl.ds(n * tiles, tiles)
        wide[at, 0:4, :] = after if flip else before
        wide[at, 4:8, :] = x
        wide[at, 8:12, :] = before if flip else after
    last = len(pieces) * tiles
    wide[pl.ds(last, 2), 0:12, :] = jnp.zeros((2, 12, wide.shape[2]), jnp.float32)
    wide[:, 12:16, :] = jnp.full((last + 2, 4, wide.shape[2]), fill, jnp.float32)
    table[...] = wide[...].astype(jnp.bfloat16)


def act(y):
    t = jnp.tanh(y)
    q = 1.0 + t
    a = y * q
    return t, q, a


def own_of(x, group, samples):
    return jnp.concatenate(
        [x[:, (u * 6 + 1) * samples : (u * 6 + 5) * samples] for u in range(group)], axis=1
    )


def forward_kernel(
    group, blocked, idx, near, mine, far, w1, w2, w3,
    res, g, table, a1_ref, a2_ref, d1_ref, d2_ref, wide, est,
):
    tiles, parts, samples = mine.shape
    channels = w3.shape[1] // 3
    pairs = group // 2
    count = lax.axis_size("rec")
    me = lax.axis_index("rec")
    has_left = (me > 0).astype(jnp.float32)
    has_right = (me < count - 1).astype(jnp.float32)
    lane = lax.broadcasted_iota(jnp.int32, (8, samples), 1)
    low = (lane > 0).astype(jnp.float32)
    high = (lane < samples - 1).astype(jnp.float32)

    def start():
        fill_table(table, wide, (near, mine, far), tiles, False, 1.0)

    def step(n, block):
        tile = []
        for u in range(group):
            line = []
            for r in range(4):
                at = idx[r, n * group + u]
                line += [table[at], table[at + 1]]
            tile.append(line)
        wide_of = lambda half, i, rows: jnp.concatenate(
            [tile[half * pairs + u][i + h] for u in range(pairs) for h in range(rows)], axis=1
        )
        rhs = jnp.concatenate([wide_of(half, i, 6) for half in range(2) for i in range(3)], axis=0)
        y1 = jnp.dot(w1[...], rhs, preferred_element_type=jnp.float32)
        t, q, a = act(y1)
        a1 = a.astype(jnp.bfloat16)
        a1_ref[block] = own_of(a1, pairs, samples)
        d1_ref[block] = own_of(q + a * (1.0 - t), pairs, samples)
        ones = jnp.ones((16, a1.shape[1]), jnp.bfloat16)
        y2 = jnp.dot(
            w2[...], jnp.concatenate([a1, ones], axis=0), preferred_element_type=jnp.float32
        )
        t, q, a = act(y2)
        d2_ref[block] = own_of(q + a * (1.0 - t), pairs, samples)
        cut = []
        for k in range(pairs * 6):
            part = a[:, k * samples : (k + 1) * samples]
            if k % 6 == 0:
                part = part * has_left
            if k % 6 == 5:
                part = part * has_right
            cut.append(part.astype(jnp.bfloat16))
        a2_ref[block] = jnp.concatenate(
            [cut[u * 6 + h + 1] for u in range(pairs) for h in range(4)], axis=1
        )
        for half in range(2):
            rows = slice(half * channels, (half + 1) * channels)
            rhs = jnp.concatenate(
                [
                    jnp.concatenate(
                        [cut[u * 6 + h + i][rows] for u in range(pairs) for h in range(4)], axis=1
                    )
                    for i in range(3)
                ],
                axis=0,
            )
            terms = jnp.dot(w3[...], rhs, preferred_element_type=jnp.float32)
            for k in range(pairs * 4):
                part = terms[:, k * samples : (k + 1) * samples]
                total = (
                    part[8:16]
                    + pltpu.roll(part[0:8], 1, 1) * low
                    + pltpu.roll(part[16:24], samples - 1, 1) * high
                )
                at = (n * group + half * pairs) * 4 + k
                est[at] = total.astype(jnp.bfloat16).astype(jnp.float32)

    def end():
        for c in range(tiles // 2):
            at = [idx[4 + v, tiles // 2 + c] for v in range(4)]
            for k in range(2):
                total = (est[at[0] + k] + est[at[1] + k]) + (est[at[2] + k] + est[at[3] + k])
                value = total[0:parts] - mine[c * 2 + k].astype(jnp.float32)
                for o in range(parts):
                    res[o, c, k : k + 1, :] = value[o : o + 1]
                g[c * 2 + k] = value.astype(jnp.bfloat16)

    run(start, step, end, count // group, blocked)


def backward_kernel(
    group, blocked, idx, near, mine, far, wo, wm, table, a1_ref, a2_ref, d1_ref, d2_ref,
    out, gtable, wide, acc,
):
    tiles, parts, samples = mine.shape
    owners = lax.axis_size("rec")
    pairs = group // 2
    channels = wm.shape[0] // 2

    def start():
        fill_table(gtable, wide, (near, mine, far), tiles, True, 0.0)
        acc[...] = jnp.zeros_like(acc)

    def step(n, block):
        tile, gtile = [], []
        for u in range(group):
            at = [idx[r, n * group + u] for r in range(4)]
            for held, lines in ((table, tile), (gtable, gtile)):
                line = [held[at[r] + k] for r in (1, 2) for k in (0, 1)]
                lines.append([held[at[0] + 1]] + line + [held[at[3]]])
        wide_of = lambda lines, half, i: jnp.concatenate(
            [lines[half * pairs + u][i + h] for u in range(pairs) for h in range(4)], axis=1
        )
        fields = [
            jnp.concatenate([wide_of(gtile, half, 2 - i) for i in range(3)], axis=0)
            for half in range(2)
        ]
        inputs = [
            jnp.concatenate([wide_of(tile, half, i) for i in range(3)], axis=0) for half in range(2)
        ]
        da2 = jnp.dot(
            wo[...], jnp.concatenate(fields, axis=0), preferred_element_type=jnp.float32
        )
        dz2 = (da2 * d2_ref[block]).astype(jnp.bfloat16)
        da1 = jnp.dot(wm[...], dz2, preferred_element_type=jnp.float32)
        dz1 = (da1 * d1_ref[block]).astype(jnp.bfloat16)
        a1, a2 = a1_ref[block], a2_ref[block]
        for half in range(2):
            rows = slice(half * channels, (half + 1) * channels)
            acc[...] += product(
                jnp.concatenate([fields[half], a1[rows], inputs[half]], axis=0),
                jnp.concatenate([a2[rows], dz2[rows], dz1[rows]], axis=0),
                (1, 1),
            )

    def end():
        low, mid = slice(0, channels), slice(channels, 2 * channels)
        high = slice(2 * channels, 3 * channels)
        first = 48 + channels
        out[0:48, low] = acc[first : first + 48, high]
        out[0:48, mid] = acc[0:48, low]
        out[12:13, low] = acc[first + 28 : first + 29, mid]
        middle = acc[48:first, mid].T
        out[48 : 48 + channels // 2, low] = middle[0 : channels // 2]
        out[48 : 48 + channels // 2, mid] = middle[channels // 2 : channels]

    run(start, step, end, owners // group, blocked)


def finish_kernel(scale, parts, *refs):
    terms, (g_in, g_bin, g_mid, g_bmid, g_out, held) = refs[:-6], refs[-6:]
    values = [ref[...] for ref in terms]
    while len(values) > 1:
        values = [values[k] + values[k + 1] for k in range(0, len(values), 2)]
    held[...] = values[0] * scale
    channels = g_mid.shape[0]
    for o in range(parts):
        for i in range(3):
            for j in range(3):
                row = held[i * 16 + j * 4 + o : i * 16 + j * 4 + o + 1, :]
                at = o * 9 + 3 * i + j
                g_in[at : at + 1, :] = row[:, 0:channels]
                g_out[at : at + 1, :] = row[:, channels : 2 * channels]
    g_bin[...] = held[28:29, 0:channels]
    g_bmid[...] = held[12:13, 0:channels]
    half = channels // 2
    g_mid[0:half] = held[48 : 48 + half, 0:channels]
    g_mid[half:channels] = held[48 : 48 + half, channels : 2 * channels]


def halves(b):
    high = b.astype(jnp.bfloat16).astype(jnp.float32)
    rest = b - high
    mid = rest.astype(jnp.bfloat16).astype(jnp.float32)
    return [high, mid, rest - mid]


def one_hot(a, b):
    return (a == b).astype(jnp.float32).astype(jnp.bfloat16)


def iota(shape, dim):
    return lax.broadcasted_iota(jnp.int32, shape, dim)


def product(a, b, over):
    return lax.dot_general(
        a, b, dimension_numbers=(((over[0],), (over[1],)), ((), ())),
        preferred_element_type=jnp.float32,
    )


def twice(ref, w):
    ref[...] = jnp.zeros_like(ref)
    ref[0 : w.shape[0], 0 : w.shape[1]] = w.astype(jnp.bfloat16)
    ref[w.shape[0] : 2 * w.shape[0], w.shape[1] : 2 * w.shape[1]] = w.astype(jnp.bfloat16)


def prep_kernel(blocks, *refs):
    args, (idx, w1, w2, w3, wo, wm, rows), held, sems = refs[:6], refs[6:13], refs[13:19], refs[19]
    copies = [
        pltpu.make_async_copy(src, dst, sems.at[n]) for n, (src, dst) in enumerate(zip(args, held))
    ]
    for copy in copies:
        copy.start()
    for copy in copies:
        copy.wait()
    dest, w_in, b_in, w_mid, b_mid, w_out = held
    count = lax.axis_size("rec")
    me = lax.axis_index("rec")
    ves, total = dest.shape
    channels = w_mid.shape[0]
    empty = 6 * blocks
    at = lax.rem((count + 1 - me) * blocks, total)
    wide = jnp.concatenate([dest[...], jnp.zeros((8 - ves, total), jnp.int32)], axis=0)
    near = pltpu.roll(wide, at, 1)[:, 0:128]
    lane = iota((8, 128), 1)
    low = jnp.where(me > 0, 0, blocks)
    high = jnp.where(me < count - 1, 3 * blocks, 2 * blocks)
    near = jnp.where((lane >= low) & (lane < high), near, -1)
    owner = iota((count, 128), 0)
    hits = [(near[v : v + 1] == owner).astype(jnp.float32) for v in range(ves)]
    before = iota((128, 128), 0)
    after = iota((128, 128), 1)
    segment = (after >= blocks).astype(jnp.int32) + (after >= 2 * blocks).astype(jnp.int32)
    tri = ((before < after) & (before >= segment * blocks)).astype(jnp.float32).astype(jnp.bfloat16)
    rank = product((hits[0] + hits[1] + hits[2] + hits[3]).astype(jnp.bfloat16), tri, (1, 0))
    zeroth = jnp.zeros((count, 128), jnp.float32)
    first = jnp.zeros((count, 128), jnp.float32)
    for v in range(ves):
        zeroth += hits[v] * (rank == 0.0).astype(jnp.float32)
        first += hits[v] * (rank == 1.0).astype(jnp.float32)
        item = jnp.sum(hits[v] * rank, axis=0, keepdims=True)
        idx[4 + v : 5 + v, 0:128] = near[v : v + 1] * 4 + item.astype(jnp.int32) * 2
        rank = rank + hits[v]
    line = iota((8, 128), 0)
    inside = lambda k: (lane >= k * blocks) & (lane < (k + 1) * blocks)
    place = (2 * lane - empty).astype(jnp.float32)
    swap = jnp.where(lax.rem(me, 2) == 1, 0, 4 * blocks).astype(jnp.float32)
    ones = jnp.where(line == 0, jnp.where(inside(0), place + swap, 0.0), 0.0)
    ones = jnp.where((line == 2) & inside(1), place, ones)
    zeros = jnp.where(line == 3, jnp.where(inside(2), place - swap, 0.0), 0.0)
    zeros = jnp.where((line == 1) & inside(1), place, zeros)
    pick = product(ones.astype(jnp.bfloat16), first.astype(jnp.bfloat16), (1, 1)) + product(
        zeros.astype(jnp.bfloat16), zeroth.astype(jnp.bfloat16), (1, 1)
    )
    idx[0:4, 0:count] = pick[0:4].astype(jnp.int32) + empty

    taps = w_in.shape[0]
    row, col = iota((48, 40), 0), iota((48, 40), 1)
    tap, extra = row & 15, (row & 15) - 12
    target = (row & 3) * 9 + 3 * (row >> 4) + ((row >> 2) & 3)
    target = jnp.where(tap < 12, target, jnp.where((row >> 4) == 1, taps + extra, -1))
    order = one_hot(col, target)
    rows[...] = jnp.zeros_like(rows)
    rows[0:taps, :] = w_in[...].astype(jnp.float32)
    for n, part in enumerate(halves(b_in[...])):
        rows[taps + n : taps + n + 1, :] = part
    twice(w1, 0.5 * product(rows[...].astype(jnp.bfloat16), order, (0, 1)))
    rows[...] = jnp.zeros_like(rows)
    for n, part in enumerate(halves(b_mid[...])):
        rows[n : n + 1, :] = part
    row, col = iota((40, 16), 0), iota((40, 16), 1)
    bias = product(rows[...].astype(jnp.bfloat16), one_hot(col, row), (0, 0))
    twice(w2, 0.5 * w_mid[...].astype(jnp.float32))
    for half in range(2):
        rows_of = slice(half * channels, (half + 1) * channels)
        w2[rows_of, 2 * channels : 2 * channels + 16] = (0.5 * bias).astype(jnp.bfloat16)
    rows[...] = jnp.zeros_like(rows)
    rows[0:taps, :] = w_out[...].astype(jnp.float32)
    outs = rows[...].astype(jnp.bfloat16)
    twice(wo, 0.5 * product(outs, order, (0, 1)))
    row, col = iota((24, 40), 0), iota((24, 40), 1)
    for i in range(3):
        target = jnp.where((row & 7) < 4, (row & 3) * 9 + 3 * i + (row >> 3), -1)
        part = product(one_hot(col, target), outs, (1, 0))
        w3[:, i * channels : (i + 1) * channels] = part.astype(jnp.bfloat16)
    eye = one_hot(iota((channels, channels), 0), iota((channels, channels), 1))
    twice(wm, 0.5 * product(w_mid[...], eye, (0, 0)))


def local(records, dest, w_in, b_in, w_mid, b_mid, w_out):
    count = lax.axis_size("rec")
    me = lax.axis_index("rec")
    parts, blocks, traces, samples = records.shape
    ves = dest.shape[1]
    tiles = blocks * traces
    channels = w_in.shape[0]
    group = group_of(count)
    steps = count // group
    width = group // 2 * 4 * samples
    far = [(s, s + 1) for s in range(1, count - 1, 2)]
    far += [(b, a) for a, b in far]
    near = [(s, s + 1) for s in range(0, count - 1, 2)]
    near += [(b, a) for a, b in near]

    flat = records.transpose(1, 2, 0, 3).reshape(tiles, parts, samples)
    from_far = lax.ppermute(flat, "rec", far)
    from_near = lax.ppermute(flat, "rec", near)

    f32, bf16 = jnp.float32, jnp.bfloat16
    shape = (steps, 2 * channels, width)
    blocked = 12 * math.prod(shape) > RESIDENT
    saved = [
        jax.ShapeDtypeStruct(shape, kind) if blocked else pltpu.VMEM(shape, kind)
        for kind in (bf16, bf16, f32, f32)
    ]
    held = [VMEM] * 4
    if blocked:
        held = [pl.BlockSpec((1, 2 * channels, width), lambda n: (n, 0, 0))] * 4
    grid = (steps,) if blocked else ()
    params = pltpu.CompilerParams(vmem_limit_bytes=16 << 20)
    args = (
        dest.T, w_in.T, b_in.reshape(1, channels), w_mid, b_mid.reshape(1, channels), w_out.T
    )
    idx, w1, w2, w3, wo, wm = pl.pallas_call(
        functools.partial(prep_kernel, blocks),
        out_shape=[jax.ShapeDtypeStruct((8, max(128, count)), jnp.int32)]
        + [
            jax.ShapeDtypeStruct(size, bf16)
            for size in (
                (2 * channels, 96), (2 * channels, 2 * channels + 16), (24, 3 * channels),
                (2 * channels, 96), (2 * channels, 2 * channels),
            )
        ],
        in_specs=[pl.BlockSpec(memory_space=pltpu.HBM)] * 6,
        out_specs=[VMEM] * 6,
        scratch_shapes=[pltpu.VMEM((40, channels), f32)]
        + [pltpu.VMEM(arg.shape, arg.dtype) for arg in args]
        + [pltpu.SemaphoreType.DMA((6,))],
        compiler_params=params,
        name="prepare",
    )(*[pltpu.with_memory_space_constraint(arg, pltpu.HBM) for arg in args])
    res, g, table, a1, a2, d1, d2 = pl.pallas_call(
        functools.partial(forward_kernel, group, blocked),
        grid=grid,
        out_shape=[
            jax.ShapeDtypeStruct(records.shape, f32),
            jax.ShapeDtypeStruct((tiles, parts, samples), bf16),
            pltpu.VMEM((3 * tiles + 2, 16, samples), bf16),
            *saved,
        ],
        in_specs=[SMEM] + [VMEM] * 6,
        out_specs=[VMEM] * 3 + held,
        scratch_shapes=[
            pltpu.VMEM((3 * tiles + 2, 16, samples), f32),
            pltpu.VMEM((count * 4, 8, samples), f32),
        ],
        compiler_params=params,
        name="forward",
    )(idx, from_near, flat, from_far, w1, w2, w3)

    g_far = lax.ppermute(g, "rec", far)
    g_near = lax.ppermute(g, "rec", near)
    sums = pl.pallas_call(
        functools.partial(backward_kernel, group, blocked),
        grid=grid,
        out_shape=jax.ShapeDtypeStruct((48 + channels // 2, 2 * channels), f32),
        in_specs=[SMEM] + [VMEM] * 6 + held,
        out_specs=VMEM,
        scratch_shapes=[
            pltpu.VMEM((3 * tiles + 2, 16, samples), bf16),
            pltpu.VMEM((3 * tiles + 2, 16, samples), f32),
            pltpu.VMEM((96 + channels, 3 * channels), f32),
        ],
        compiler_params=params,
        name="backward",
    )(idx, g_near, g, g_far, wo, wm, table, a1, a2, d1, d2)

    if count & (count - 1):
        terms = [lax.psum(sums, "rec")]
    else:
        terms = [sums]
        at = 1
        while at < count:
            wide = 2 if at == 1 or 2 * at == count else 4
            value = terms[0]
            if len(terms) == 2:
                value = terms[0] + terms[1]
            if len(terms) == 4:
                value = (terms[0] + terms[1]) + (terms[2] + terms[3])
            terms = [value] + [
                lax.ppermute(value, "rec", [(s, s ^ (k * at)) for s in range(count)])
                for k in range(1, wide)
            ]
            at *= wide

    scale = 1.0 / math.sqrt(parts * blocks * count * traces * samples)
    g_in, g_bin, g_mid, g_bmid, g_out = pl.pallas_call(
        functools.partial(finish_kernel, scale, parts),
        out_shape=[
            jax.ShapeDtypeStruct(shape, f32)
            for shape in (
                (parts * 9, channels), (1, channels), (channels, channels), (1, channels),
                (parts * 9, channels),
            )
        ],
        in_specs=[VMEM] * len(terms),
        out_specs=[VMEM] * 5,
        scratch_shapes=[pltpu.VMEM(sums.shape, f32)],
        compiler_params=params,
        name="finish",
    )(*terms)
    return (
        res,
        g_in.T,
        g_bin.reshape(channels),
        g_mid,
        g_bmid.reshape(channels),
        g_out.T,
    )


def solution(mesh):
    return jax.shard_map(
        local,
        mesh=mesh,
        in_specs=(
            P(None, ("groups", "rec"), None, None),
            P("groups", None),
            P(),
            P(),
            P(),
            P(),
            P(),
        ),
        out_specs=(
            P(None, ("groups", "rec"), None, None),
            P("groups", None),
            P("groups"),
            P("groups", None),
            P("groups"),
            P("groups", None),
        ),
        check_vma=False,
    )
```

```python
import functools
import math

import jax
import jax.numpy as jnp
from jax import lax
from jax.experimental import pallas as pl
from jax.experimental.pallas import tpu as pltpu
from jax.sharding import PartitionSpec as P

CAP = 2
VMEM = pl.BlockSpec(memory_space=pltpu.VMEM)
SMEM = pl.BlockSpec(memory_space=pltpu.SMEM)
RESIDENT = 24 << 20


def run(start, step, end, steps, blocked):
    if blocked:
        n = pl.program_id(0)
        pl.when(n == 0)(start)
        step(n, 0)
        pl.when(n == steps - 1)(end)
        return
    start()
    lax.fori_loop(0, steps, lambda n, carry: step(n, n), None)
    end()


def group_of(owners):
    for size in (16, 8, 4, 2):
        if owners % size == 0:
            return size
    return 1


def fill_table(table, wide, pieces, tiles, flip, fill):
    for n, piece in enumerate(pieces):
        x = piece[...].astype(jnp.float32)
        samples = x.shape[2]
        lane = lax.broadcasted_iota(jnp.int32, x.shape, 2)
        before = jnp.where(lane == 0, 0.0, pltpu.roll(x, 1, 2))
        after = jnp.where(lane == samples - 1, 0.0, pltpu.roll(x, samples - 1, 2))
        at = pl.ds(n * tiles, tiles)
        wide[at, 0:4, :] = after if flip else before
        wide[at, 4:8, :] = x
        wide[at, 8:12, :] = before if flip else after
    last = len(pieces) * tiles
    wide[pl.ds(last, 2), 0:12, :] = jnp.zeros((2, 12, wide.shape[2]), jnp.float32)
    wide[:, 12:16, :] = jnp.full((last + 2, 4, wide.shape[2]), fill, jnp.float32)
    table[...] = wide[...].astype(jnp.bfloat16)


def act(y):
    t = jnp.tanh(y)
    q = 1.0 + t
    a = y * q
    return t, q, a


def lines_of(idx, own, halo, owners):
    lines = []
    for e in owners:
        line = []
        for r in range(4):
            held = own if r in (1, 2) else halo
            line += [None, None] if held is None else [held[idx[r, e]], held[idx[r, e] + 1]]
        lines.append(line)
    return lines


def stack(lines, traces, flip):
    return jnp.concatenate(
        [
            jnp.concatenate(
                [line[h + 1 + (2 - i if flip else i)] for line in lines for h in traces], axis=1
            )
            for i in range(3)
        ],
        axis=0,
    )


def layers(inputs, w1, w2):
    y1 = jnp.dot(w1[...], inputs, preferred_element_type=jnp.float32)
    t, q, a = act(y1)
    d1 = q + a * (1.0 - t)
    a1 = a.astype(jnp.bfloat16)
    ones = jnp.ones((16, a1.shape[1]), jnp.bfloat16)
    y2 = jnp.dot(w2[...], jnp.concatenate([a1, ones], axis=0), preferred_element_type=jnp.float32)
    t, q, a = act(y2)
    return a1, d1, a, q + a * (1.0 - t)


def forward_inner(
    group, blocked, idx, mine, w1, w2, own, a1_ref, a2_ref, d1_ref, d2_ref, wide
):
    owners = lax.axis_size("rec")

    def start():
        fill_table(own, wide, (mine,), mine.shape[0], False, 1.0)

    def step(n, block):
        lines = lines_of(idx, own, None, [n * group + u for u in range(group)])
        a1, d1, a2, d2 = layers(stack(lines, (1, 2), False), w1, w2)
        a1_ref[block] = a1
        d1_ref[block] = d1
        a2_ref[block] = a2.astype(jnp.bfloat16)
        d2_ref[block] = d2

    run(start, step, lambda: None, owners // group, blocked)


def forward_outer(
    group, blocked, idx, near, mine, far, own, w1, w2, w3, inner,
    res, g, halo, a1_ref, a2_ref, d1_ref, d2_ref, wide, est,
):
    tiles, parts, samples = mine.shape
    count = lax.axis_size("rec")
    me = lax.axis_index("rec")
    has_left = (me > 0).astype(jnp.float32)
    has_right = (me < count - 1).astype(jnp.float32)
    lane = lax.broadcasted_iota(jnp.int32, (8, samples), 1)
    low = (lane > 0).astype(jnp.float32)
    high = (lane < samples - 1).astype(jnp.float32)

    def start():
        fill_table(halo, wide, (near, far), tiles, False, 1.0)

    def step(n, block):
        lines = lines_of(idx, own, halo, [n * group + u for u in range(group)])
        a1, d1, a2, d2 = layers(stack(lines, (-1, 0, 3, 4), False), w1, w2)
        cut = lambda x, u, k: x[:, (u * 4 + k) * samples : (u * 4 + k + 1) * samples]
        middle = lambda x: jnp.concatenate(
            [cut(x, u, k) for u in range(group) for k in (1, 2)], axis=1
        )
        a1_ref[block] = middle(a1)
        d1_ref[block] = middle(d1)
        d2_ref[block] = middle(d2)
        rows = []
        for u in range(group):
            row = [cut(a2, u, 0) * has_left, cut(a2, u, 1), cut(a2, u, 2), cut(a2, u, 3) * has_right]
            row = [part.astype(jnp.bfloat16) for part in row]
            within = [
                inner[block, :, (u * 2 + k) * samples : (u * 2 + k + 1) * samples] for k in range(2)
            ]
            rows.append(row[0:2] + within + row[2:4])
        a2_ref[block] = jnp.concatenate([row[k] for row in rows for k in (1, 4)], axis=1)
        rhs = jnp.concatenate(
            [
                jnp.concatenate([row[h + i] for row in rows for h in range(4)], axis=1)
                for i in range(3)
            ],
            axis=0,
        )
        terms = jnp.dot(w3[...], rhs, preferred_element_type=jnp.float32)
        for k in range(group * 4):
            part = terms[:, k * samples : (k + 1) * samples]
            total = (
                part[8:16]
                + pltpu.roll(part[0:8], 1, 1) * low
                + pltpu.roll(part[16:24], samples - 1, 1) * high
            )
            est[n * group * 4 + k] = total.astype(jnp.bfloat16).astype(jnp.float32)

    def end():
        for c in range(tiles // 2):
            at = [idx[4 + v, tiles // 2 + c] for v in range(4)]
            for k in range(2):
                total = (est[at[0] + k] + est[at[1] + k]) + (est[at[2] + k] + est[at[3] + k])
                value = total[0:parts] - mine[c * 2 + k].astype(jnp.float32)
                for o in range(parts):
                    res[o, c, k : k + 1, :] = value[o : o + 1]
                g[c * 2 + k] = value.astype(jnp.bfloat16)

    run(start, step, end, count // group, blocked)


def weight_terms(acc, fields, inputs, wo, wm, a1, a2, d1, d2):
    channels = wm.shape[0]
    da2 = jnp.dot(wo[...], fields, preferred_element_type=jnp.float32)
    dz2 = (da2 * d2).astype(jnp.bfloat16)
    acc[0:48, :] += product(fields, a2, (1, 1))
    da1 = jnp.dot(wm[...], dz2, preferred_element_type=jnp.float32)
    ones = jnp.ones((16, dz2.shape[1]), jnp.bfloat16)
    acc[48 : 64 + channels, :] += product(jnp.concatenate([a1, ones], axis=0), dz2, (1, 1))
    dz1 = (da1 * d1).astype(jnp.bfloat16)
    acc[64 + channels : 112 + channels, :] += product(inputs, dz1, (1, 1))


def backward_inner(
    group, blocked, idx, mine, wo, wm, own, a1_ref, a2_ref, d1_ref, d2_ref, gown, acc, wide
):
    owners = lax.axis_size("rec")

    def start():
        fill_table(gown, wide, (mine,), mine.shape[0], True, 0.0)
        acc[...] = jnp.zeros_like(acc)

    def step(n, block):
        es = [n * group + u for u in range(group)]
        fields = stack(lines_of(idx, gown, None, es), (1, 2), True)
        inputs = stack(lines_of(idx, own, None, es), (1, 2), False)
        saved = a1_ref[block], a2_ref[block], d1_ref[block], d2_ref[block]
        weight_terms(acc, fields, inputs, wo, wm, *saved)

    run(start, step, lambda: None, owners // group, blocked)


def backward_outer(
    group, blocked, idx, near, far, wo, wm, own, halo, gown, sums, a1_ref, a2_ref, d1_ref, d2_ref,
    out, ghalo, wide, acc,
):
    owners = lax.axis_size("rec")
    channels = wm.shape[0]

    def start():
        fill_table(ghalo, wide, (near, far), near.shape[0], True, 0.0)
        acc[...] = sums[...]

    def step(n, block):
        es = [n * group + u for u in range(group)]
        fields = stack(lines_of(idx, gown, ghalo, es), (0, 3), True)
        inputs = stack(lines_of(idx, own, halo, es), (0, 3), False)
        saved = a1_ref[block], a2_ref[block], d1_ref[block], d2_ref[block]
        weight_terms(acc, fields, inputs, wo, wm, *saved)

    def end():
        first, half = 64 + channels, channels // 2
        low, high = slice(0, channels), slice(channels, 2 * channels)
        out[0:48, low] = acc[first : first + 48, :]
        out[0:48, high] = acc[0:48, :]
        out[12:13, low] = acc[48 + channels : 49 + channels, :]
        middle = acc[48 : 48 + channels, :].T
        out[48 : 48 + half, low] = middle[0:half]
        out[48 : 48 + half, high] = middle[half:channels]

    run(start, step, end, owners // group, blocked)


def finish_kernel(scale, parts, *refs):
    terms, (g_in, g_bin, g_mid, g_bmid, g_out, held) = refs[:-6], refs[-6:]
    values = [ref[...] for ref in terms]
    while len(values) > 1:
        values = [values[k] + values[k + 1] for k in range(0, len(values), 2)]
    held[...] = values[0] * scale
    channels = g_mid.shape[0]
    for o in range(parts):
        for i in range(3):
            for j in range(3):
                row = held[i * 16 + j * 4 + o : i * 16 + j * 4 + o + 1, :]
                at = o * 9 + 3 * i + j
                g_in[at : at + 1, :] = row[:, 0:channels]
                g_out[at : at + 1, :] = row[:, channels : 2 * channels]
    g_bin[...] = held[28:29, 0:channels]
    g_bmid[...] = held[12:13, 0:channels]
    half = channels // 2
    g_mid[0:half] = held[48 : 48 + half, 0:channels]
    g_mid[half:channels] = held[48 : 48 + half, channels : 2 * channels]


def halves(b):
    high = b.astype(jnp.bfloat16).astype(jnp.float32)
    rest = b - high
    mid = rest.astype(jnp.bfloat16).astype(jnp.float32)
    return [high, mid, rest - mid]


def one_hot(a, b):
    return (a == b).astype(jnp.float32).astype(jnp.bfloat16)


def iota(shape, dim):
    return lax.broadcasted_iota(jnp.int32, shape, dim)


def product(a, b, over):
    return lax.dot_general(
        a, b, dimension_numbers=(((over[0],), (over[1],)), ((), ())),
        preferred_element_type=jnp.float32,
    )


def prep_kernel(blocks, *refs):
    args, (idx, w1, w2, w3, wo, wm, rows), held, sems = refs[:6], refs[6:13], refs[13:19], refs[19]
    copies = [
        pltpu.make_async_copy(src, dst, sems.at[n]) for n, (src, dst) in enumerate(zip(args, held))
    ]
    for copy in copies:
        copy.start()
    for copy in copies:
        copy.wait()
    dest, w_in, b_in, w_mid, b_mid, w_out = held
    count = lax.axis_size("rec")
    me = lax.axis_index("rec")
    ves, total = dest.shape
    channels = w_mid.shape[0]
    at = lax.rem((count + 1 - me) * blocks, total)
    wide = jnp.concatenate([dest[...], jnp.zeros((8 - ves, total), jnp.int32)], axis=0)
    near = pltpu.roll(wide, at, 1)[:, 0:128]
    lane = iota((8, 128), 1)
    low = jnp.where(me > 0, 0, blocks)
    high = jnp.where(me < count - 1, 3 * blocks, 2 * blocks)
    near = jnp.where((lane >= low) & (lane < high), near, -1)
    owner = iota((count, 128), 0)
    hits = [(near[v : v + 1] == owner).astype(jnp.float32) for v in range(ves)]
    before = iota((128, 128), 0)
    after = iota((128, 128), 1)
    segment = (after >= blocks).astype(jnp.int32) + (after >= 2 * blocks).astype(jnp.int32)
    tri = ((before < after) & (before >= segment * blocks)).astype(jnp.float32).astype(jnp.bfloat16)
    rank = product((hits[0] + hits[1] + hits[2] + hits[3]).astype(jnp.bfloat16), tri, (1, 0))
    zeroth = jnp.zeros((count, 128), jnp.float32)
    first = jnp.zeros((count, 128), jnp.float32)
    for v in range(ves):
        zeroth += hits[v] * (rank == 0.0).astype(jnp.float32)
        first += hits[v] * (rank == 1.0).astype(jnp.float32)
        item = jnp.sum(hits[v] * rank, axis=0, keepdims=True)
        idx[4 + v : 5 + v, 0:128] = near[v : v + 1] * 4 + item.astype(jnp.int32) * 2
        rank = rank + hits[v]
    line = iota((8, 128), 0)
    inside = lambda k: (lane >= k * blocks) & (lane < (k + 1) * blocks)
    odd = lax.rem(me, 2)
    left = 2 * lane + 2 * blocks * (1 - odd) - 4 * blocks
    middle = 2 * (lane - blocks) - 2 * blocks
    right = 2 * (lane - 2 * blocks) + 2 * blocks * odd - 4 * blocks
    put = lambda r, k, place: jnp.where((line == r) & inside(k), place, 0)
    pick = product(
        (put(0, 0, left) + put(2, 1, middle)).astype(jnp.float32).astype(jnp.bfloat16),
        first.astype(jnp.bfloat16),
        (1, 1),
    ) + product(
        (put(1, 1, middle) + put(3, 2, right)).astype(jnp.float32).astype(jnp.bfloat16),
        zeroth.astype(jnp.bfloat16),
        (1, 1),
    )
    empty = jnp.where((line == 0) | (line == 3), 4 * blocks, 2 * blocks)[0:4, 0:1]
    idx[0:4, 0:count] = pick[0:4].astype(jnp.int32) + empty

    taps = w_in.shape[0]
    row, col = iota((48, 40), 0), iota((48, 40), 1)
    tap, extra = row & 15, (row & 15) - 12
    target = (row & 3) * 9 + 3 * (row >> 4) + ((row >> 2) & 3)
    target = jnp.where(tap < 12, target, jnp.where((row >> 4) == 1, taps + extra, -1))
    order = one_hot(col, target)
    rows[...] = jnp.zeros_like(rows)
    rows[0:taps, :] = w_in[...].astype(jnp.float32)
    for n, part in enumerate(halves(b_in[...])):
        rows[taps + n : taps + n + 1, :] = part
    w1[...] = (0.5 * product(rows[...].astype(jnp.bfloat16), order, (0, 1))).astype(jnp.bfloat16)
    rows[...] = jnp.zeros_like(rows)
    for n, part in enumerate(halves(b_mid[...])):
        rows[n : n + 1, :] = part
    row, col = iota((40, channels + 16), 0), iota((40, channels + 16), 1)
    bias = product(rows[...].astype(jnp.bfloat16), one_hot(col, row + channels), (0, 0))
    row, col = iota((channels, channels + 16), 0), iota((channels, channels + 16), 1)
    w2[...] = (0.5 * (product(w_mid[...], one_hot(row, col), (1, 0)) + bias)).astype(jnp.bfloat16)
    rows[...] = jnp.zeros_like(rows)
    rows[0:taps, :] = w_out[...].astype(jnp.float32)
    outs = rows[...].astype(jnp.bfloat16)
    wo[...] = (0.5 * product(outs, order, (0, 1))).astype(jnp.bfloat16)
    row, col = iota((24, 40), 0), iota((24, 40), 1)
    for i in range(3):
        target = jnp.where((row & 7) < 4, (row & 3) * 9 + 3 * i + (row >> 3), -1)
        part = product(one_hot(col, target), outs, (1, 0))
        w3[:, i * channels : (i + 1) * channels] = part.astype(jnp.bfloat16)
    eye = one_hot(iota((channels, channels), 0), iota((channels, channels), 1))
    wm[...] = (0.5 * product(w_mid[...], eye, (0, 0))).astype(jnp.bfloat16)


def local(records, dest, w_in, b_in, w_mid, b_mid, w_out):
    count = lax.axis_size("rec")
    me = lax.axis_index("rec")
    parts, blocks, traces, samples = records.shape
    ves = dest.shape[1]
    tiles = blocks * traces
    channels = w_in.shape[0]
    group = group_of(count)
    steps = count // group
    width = group * 2 * samples
    far = [(s, s + 1) for s in range(1, count - 1, 2)]
    far += [(b, a) for a, b in far]
    near = [(s, s + 1) for s in range(0, count - 1, 2)]
    near += [(b, a) for a, b in near]

    flat = records.transpose(1, 2, 0, 3).reshape(tiles, parts, samples)
    from_far = lax.ppermute(flat, "rec", far)
    from_near = lax.ppermute(flat, "rec", near)

    f32, bf16 = jnp.float32, jnp.bfloat16
    shape = (steps, channels, width)
    blocked = 24 * math.prod(shape) > RESIDENT
    saved = [
        jax.ShapeDtypeStruct(shape, kind) if blocked else pltpu.VMEM(shape, kind)
        for kind in (bf16, bf16, f32, f32)
    ]
    held = [VMEM] * 4
    if blocked:
        held = [pl.BlockSpec((1, channels, width), lambda n: (n, 0, 0))] * 4
    grid = (steps,) if blocked else ()
    params = pltpu.CompilerParams(vmem_limit_bytes=16 << 20)
    args = (
        dest.T, w_in.T, b_in.reshape(1, channels), w_mid, b_mid.reshape(1, channels), w_out.T
    )
    idx, w1, w2, w3, wo, wm = pl.pallas_call(
        functools.partial(prep_kernel, blocks),
        out_shape=[jax.ShapeDtypeStruct((8, max(128, count)), jnp.int32)]
        + [
            jax.ShapeDtypeStruct(size, bf16)
            for size in (
                (channels, 48), (channels, channels + 16), (24, 3 * channels), (channels, 48),
                (channels, channels),
            )
        ],
        in_specs=[pl.BlockSpec(memory_space=pltpu.HBM)] * 6,
        out_specs=[VMEM] * 6,
        scratch_shapes=[pltpu.VMEM((40, channels), f32)]
        + [pltpu.VMEM(arg.shape, arg.dtype) for arg in args]
        + [pltpu.SemaphoreType.DMA((6,))],
        compiler_params=params,
        name="prepare",
    )(*[pltpu.with_memory_space_constraint(arg, pltpu.HBM) for arg in args])
    def table(pieces, kind):
        return pltpu.VMEM((pieces * tiles + 2, 16, samples), kind)

    def call(kernel, ins, outs, scratch, args, name, owned):
        return pl.pallas_call(
            functools.partial(kernel, group, blocked),
            grid=grid,
            out_shape=outs[0] + saved * outs[1],
            in_specs=[SMEM] + [VMEM] * ins[0] + held[:1] * ins[1],
            out_specs=[VMEM] * len(outs[0]) + held * outs[1],
            scratch_shapes=scratch,
            compiler_params=params,
            cost_estimate=pl.CostEstimate(
                flops=2 * owned * count * samples * channels * (3 * channels),
                bytes_accessed=owned * count * samples * channels * 12,
                transcendentals=0,
            ),
            name=name,
        )(*args)

    total = (112 + channels, channels)
    own, *inner = call(
        forward_inner, (3, 0), ([table(1, bf16)], 1), [table(1, f32)],
        (idx, flat, w1, w2), "forward_inner", 2,
    )
    res, g, halo, *outer = call(
        forward_outer, (7, 1),
        (
            [
                jax.ShapeDtypeStruct(records.shape, f32),
                jax.ShapeDtypeStruct((tiles, parts, samples), bf16),
                table(2, bf16),
            ],
            1,
        ),
        [table(2, f32), pltpu.VMEM((count * 4, 8, samples), f32)],
        (idx, from_near, flat, from_far, own, w1, w2, w3, inner[1]), "forward_outer", 4,
    )
    g_far = lax.ppermute(g, "rec", far)
    g_near = lax.ppermute(g, "rec", near)
    gown, part = call(
        backward_inner, (4, 4), ([table(1, bf16), pltpu.VMEM(total, f32)], 0), [table(1, f32)],
        (idx, g, wo, wm, own, *inner), "backward_inner", 2,
    )
    (sums,) = call(
        backward_outer, (8, 4), ([jax.ShapeDtypeStruct((48 + channels // 2, 2 * channels), f32)], 0),
        [table(2, bf16), table(2, f32), pltpu.VMEM(total, f32)],
        (idx, g_near, g_far, wo, wm, own, halo, gown, part, *outer), "backward_outer", 2,
    )

    if count & (count - 1):
        terms = [lax.psum(sums, "rec")]
    else:
        terms = [sums]
        at = 1
        while at < count:
            wide = 2 if at == 1 or 2 * at == count else 4
            value = terms[0]
            if len(terms) == 2:
                value = terms[0] + terms[1]
            if len(terms) == 4:
                value = (terms[0] + terms[1]) + (terms[2] + terms[3])
            terms = [value] + [
                lax.ppermute(value, "rec", [(s, s ^ (k * at)) for s in range(count)])
                for k in range(1, wide)
            ]
            at *= wide

    scale = 1.0 / math.sqrt(parts * blocks * count * traces * samples)
    g_in, g_bin, g_mid, g_bmid, g_out = pl.pallas_call(
        functools.partial(finish_kernel, scale, parts),
        out_shape=[
            jax.ShapeDtypeStruct(shape, f32)
            for shape in (
                (parts * 9, channels), (1, channels), (channels, channels), (1, channels),
                (parts * 9, channels),
            )
        ],
        in_specs=[VMEM] * len(terms),
        out_specs=[VMEM] * 5,
        scratch_shapes=[pltpu.VMEM(sums.shape, f32)],
        compiler_params=params,
        name="finish",
    )(*terms)
    return (
        res,
        g_in.T,
        g_bin.reshape(channels),
        g_mid,
        g_bmid.reshape(channels),
        g_out.T,
    )


def solution(mesh):
    return jax.shard_map(
        local,
        mesh=mesh,
        in_specs=(
            P(None, ("groups", "rec"), None, None),
            P("groups", None),
            P(),
            P(),
            P(),
            P(),
            P(),
        ),
        out_specs=(
            P(None, ("groups", "rec"), None, None),
            P("groups", None),
            P("groups"),
            P("groups", None),
            P("groups"),
            P("groups", None),
        ),
        check_vma=False,
    )
```

```python
import functools
import math

import jax
import jax.numpy as jnp
from jax import lax
from jax.experimental import pallas as pl
from jax.experimental.pallas import tpu as pltpu
from jax.sharding import PartitionSpec as P

CAP = 2
VMEM = pl.BlockSpec(memory_space=pltpu.VMEM)
SMEM = pl.BlockSpec(memory_space=pltpu.SMEM)
RESIDENT = 24 << 20


def run(start, step, end, steps, blocked):
    if blocked:
        n = pl.program_id(0)
        pl.when(n == 0)(start)
        step(n, 0)
        pl.when(n == steps - 1)(end)
        return
    start()
    lax.fori_loop(0, steps, lambda n, carry: step(n, n), None)
    end()


def group_of(owners):
    for size in (16, 8, 4, 2):
        if owners % size == 0:
            return size
    return 1


def fill_table(table, wide, pieces, tiles, flip, fill):
    for n, piece in enumerate(pieces):
        x = piece[...].astype(jnp.float32)
        samples = x.shape[2]
        lane = lax.broadcasted_iota(jnp.int32, x.shape, 2)
        before = jnp.where(lane == 0, 0.0, pltpu.roll(x, 1, 2))
        after = jnp.where(lane == samples - 1, 0.0, pltpu.roll(x, samples - 1, 2))
        at = pl.ds(n * tiles, tiles)
        wide[at, 0:4, :] = after if flip else before
        wide[at, 4:8, :] = x
        wide[at, 8:12, :] = before if flip else after
    last = len(pieces) * tiles
    wide[pl.ds(last, 2), 0:12, :] = jnp.zeros((2, 12, wide.shape[2]), jnp.float32)
    wide[:, 12:16, :] = jnp.full((last + 2, 4, wide.shape[2]), fill, jnp.float32)
    table[...] = wide[...].astype(jnp.bfloat16)


def act(y):
    t = jnp.tanh(y)
    q = 1.0 + t
    a = y * q
    return t, q, a


def lines_of(idx, own, halo, owners):
    lines = []
    for e in owners:
        line = []
        for r in range(4):
            held = own if r in (1, 2) else halo
            line += [None, None] if held is None else [held[idx[r, e]], held[idx[r, e] + 1]]
        lines.append(line)
    return lines


def stack(lines, traces, flip):
    return jnp.concatenate(
        [
            jnp.concatenate(
                [line[h + 1 + (2 - i if flip else i)] for line in lines for h in traces], axis=1
            )
            for i in range(3)
        ],
        axis=0,
    )


def layers(inputs, w1, w2):
    y1 = jnp.dot(w1[...], inputs, preferred_element_type=jnp.float32)
    t, q, a = act(y1)
    d1 = q + a * (1.0 - t)
    a1 = a.astype(jnp.bfloat16)
    ones = jnp.ones((16, a1.shape[1]), jnp.bfloat16)
    y2 = jnp.dot(w2[...], jnp.concatenate([a1, ones], axis=0), preferred_element_type=jnp.float32)
    t, q, a = act(y2)
    return a1, d1, a, q + a * (1.0 - t)


def forward_inner(
    group, blocked, idx, mine, w1, w2, own, a1_ref, a2_ref, d1_ref, d2_ref, wide
):
    owners = lax.axis_size("rec")

    def start():
        fill_table(own, wide, (mine,), mine.shape[0], False, 1.0)

    def step(n, block):
        lines = lines_of(idx, own, None, [n * group + u for u in range(group)])
        a1, d1, a2, d2 = layers(stack(lines, (1, 2), False), w1, w2)
        a1_ref[block] = a1
        d1_ref[block] = d1
        a2_ref[block] = a2.astype(jnp.bfloat16)
        d2_ref[block] = d2

    run(start, step, lambda: None, owners // group, blocked)


def forward_outer(
    group, blocked, idx, near, mine, far, own, w1, w2, w3, inner,
    res, g, halo, a1_ref, a2_ref, d1_ref, d2_ref, wide, est,
):
    tiles, parts, samples = mine.shape
    count = lax.axis_size("rec")
    me = lax.axis_index("rec")
    has_left = (me > 0).astype(jnp.float32)
    has_right = (me < count - 1).astype(jnp.float32)
    lane = lax.broadcasted_iota(jnp.int32, (8, samples), 1)
    low = (lane > 0).astype(jnp.float32)
    high = (lane < samples - 1).astype(jnp.float32)

    def start():
        fill_table(halo, wide, (near, far), tiles, False, 1.0)

    def step(n, block):
        lines = lines_of(idx, own, halo, [n * group + u for u in range(group)])
        a1, d1, a2, d2 = layers(stack(lines, (-1, 0, 3, 4), False), w1, w2)
        cut = lambda x, u, k: x[:, (u * 4 + k) * samples : (u * 4 + k + 1) * samples]
        middle = lambda x: jnp.concatenate(
            [cut(x, u, k) for u in range(group) for k in (1, 2)], axis=1
        )
        a1_ref[block] = middle(a1)
        d1_ref[block] = middle(d1)
        d2_ref[block] = middle(d2)
        rows = []
        for u in range(group):
            row = [cut(a2, u, 0) * has_left, cut(a2, u, 1), cut(a2, u, 2), cut(a2, u, 3) * has_right]
            row = [part.astype(jnp.bfloat16) for part in row]
            within = [
                inner[block, :, (u * 2 + k) * samples : (u * 2 + k + 1) * samples] for k in range(2)
            ]
            rows.append(row[0:2] + within + row[2:4])
        a2_ref[block] = jnp.concatenate([row[k] for row in rows for k in (1, 4)], axis=1)
        rhs = jnp.concatenate(
            [
                jnp.concatenate([row[h + i] for row in rows for h in range(4)], axis=1)
                for i in range(3)
            ],
            axis=0,
        )
        terms = jnp.dot(w3[...], rhs, preferred_element_type=jnp.float32)
        for k in range(group * 4):
            part = terms[:, k * samples : (k + 1) * samples]
            total = (
                part[8:16]
                + pltpu.roll(part[0:8], 1, 1) * low
                + pltpu.roll(part[16:24], samples - 1, 1) * high
            )
            est[n * group * 4 + k] = total.astype(jnp.bfloat16).astype(jnp.float32)

    def end():
        for c in range(tiles // 2):
            at = [idx[4 + v, tiles // 2 + c] for v in range(4)]
            for k in range(2):
                total = (est[at[0] + k] + est[at[1] + k]) + (est[at[2] + k] + est[at[3] + k])
                value = total[0:parts] - mine[c * 2 + k].astype(jnp.float32)
                for o in range(parts):
                    res[o, c, k : k + 1, :] = value[o : o + 1]
                g[c * 2 + k] = value.astype(jnp.bfloat16)

    run(start, step, end, count // group, blocked)


def weight_terms(acc, fields, inputs, wo, wm, a1, a2, d1, d2):
    channels = wm.shape[0]
    da2 = jnp.dot(wo[...], fields, preferred_element_type=jnp.float32)
    dz2 = (da2 * d2).astype(jnp.bfloat16)
    acc[0:48, :] += product(fields, a2, (1, 1))
    da1 = jnp.dot(wm[...], dz2, preferred_element_type=jnp.float32)
    ones = jnp.ones((16, dz2.shape[1]), jnp.bfloat16)
    acc[48 : 64 + channels, :] += product(jnp.concatenate([a1, ones], axis=0), dz2, (1, 1))
    dz1 = (da1 * d1).astype(jnp.bfloat16)
    acc[64 + channels : 112 + channels, :] += product(inputs, dz1, (1, 1))


def backward_inner(
    group, blocked, idx, mine, wo, wm, own, a1_ref, a2_ref, d1_ref, d2_ref, gown, acc, wide
):
    owners = lax.axis_size("rec")

    def start():
        fill_table(gown, wide, (mine,), mine.shape[0], True, 0.0)
        acc[...] = jnp.zeros_like(acc)

    def step(n, block):
        es = [n * group + u for u in range(group)]
        fields = stack(lines_of(idx, gown, None, es), (1, 2), True)
        inputs = stack(lines_of(idx, own, None, es), (1, 2), False)
        saved = a1_ref[block], a2_ref[block], d1_ref[block], d2_ref[block]
        weight_terms(acc, fields, inputs, wo, wm, *saved)

    run(start, step, lambda: None, owners // group, blocked)


def backward_outer(
    group, blocked, idx, near, far, wo, wm, own, halo, gown, sums, a1_ref, a2_ref, d1_ref, d2_ref,
    out, ghalo, wide, acc,
):
    owners = lax.axis_size("rec")
    channels = wm.shape[0]

    def start():
        fill_table(ghalo, wide, (near, far), near.shape[0], True, 0.0)
        acc[...] = sums[...]

    def step(n, block):
        es = [n * group + u for u in range(group)]
        fields = stack(lines_of(idx, gown, ghalo, es), (0, 3), True)
        inputs = stack(lines_of(idx, own, halo, es), (0, 3), False)
        saved = a1_ref[block], a2_ref[block], d1_ref[block], d2_ref[block]
        weight_terms(acc, fields, inputs, wo, wm, *saved)

    def end():
        first, half = 64 + channels, channels // 2
        low, high = slice(0, channels), slice(channels, 2 * channels)
        out[0:48, low] = acc[first : first + 48, :]
        out[0:48, high] = acc[0:48, :]
        out[12:13, low] = acc[48 + channels : 49 + channels, :]
        middle = acc[48 : 48 + channels, :].T
        out[48 : 48 + half, low] = middle[0:half]
        out[48 : 48 + half, high] = middle[half:channels]

    run(start, step, end, owners // group, blocked)


def finish_kernel(scale, parts, *refs):
    terms, (g_in, g_bin, g_mid, g_bmid, g_out, held) = refs[:-6], refs[-6:]
    values = [ref[...] for ref in terms]
    while len(values) > 1:
        values = [values[k] + values[k + 1] for k in range(0, len(values), 2)]
    held[...] = values[0] * scale
    channels = g_mid.shape[0]
    for o in range(parts):
        for i in range(3):
            for j in range(3):
                row = held[i * 16 + j * 4 + o : i * 16 + j * 4 + o + 1, :]
                at = o * 9 + 3 * i + j
                g_in[at : at + 1, :] = row[:, 0:channels]
                g_out[at : at + 1, :] = row[:, channels : 2 * channels]
    g_bin[...] = held[28:29, 0:channels]
    g_bmid[...] = held[12:13, 0:channels]
    half = channels // 2
    g_mid[0:half] = held[48 : 48 + half, 0:channels]
    g_mid[half:channels] = held[48 : 48 + half, channels : 2 * channels]


def halves(b):
    high = b.astype(jnp.bfloat16).astype(jnp.float32)
    rest = b - high
    mid = rest.astype(jnp.bfloat16).astype(jnp.float32)
    return [high, mid, rest - mid]


def one_hot(a, b):
    return (a == b).astype(jnp.float32).astype(jnp.bfloat16)


def iota(shape, dim):
    return lax.broadcasted_iota(jnp.int32, shape, dim)


def product(a, b, over):
    return lax.dot_general(
        a, b, dimension_numbers=(((over[0],), (over[1],)), ((), ())),
        preferred_element_type=jnp.float32,
    )


def prep_kernel(blocks, *refs):
    args, (idx, w1, w2, w3, wo, wm, rows), held, sems = refs[:6], refs[6:13], refs[13:19], refs[19]
    copies = [
        pltpu.make_async_copy(src, dst, sems.at[n]) for n, (src, dst) in enumerate(zip(args, held))
    ]
    for copy in copies:
        copy.start()
    for copy in copies:
        copy.wait()
    dest, w_in, b_in, w_mid, b_mid, w_out = held
    count = lax.axis_size("rec")
    me = lax.axis_index("rec")
    ves, total = dest.shape
    channels = w_mid.shape[0]
    at = lax.rem((count + 1 - me) * blocks, total)
    wide = jnp.concatenate([dest[...], jnp.zeros((8 - ves, total), jnp.int32)], axis=0)
    near = pltpu.roll(wide, at, 1)[:, 0:128]
    lane = iota((8, 128), 1)
    low = jnp.where(me > 0, 0, blocks)
    high = jnp.where(me < count - 1, 3 * blocks, 2 * blocks)
    near = jnp.where((lane >= low) & (lane < high), near, -1)
    owner = iota((count, 128), 0)
    hits = [(near[v : v + 1] == owner).astype(jnp.float32) for v in range(ves)]
    before = iota((128, 128), 0)
    after = iota((128, 128), 1)
    segment = (after >= blocks).astype(jnp.int32) + (after >= 2 * blocks).astype(jnp.int32)
    tri = ((before < after) & (before >= segment * blocks)).astype(jnp.float32).astype(jnp.bfloat16)
    rank = product((hits[0] + hits[1] + hits[2] + hits[3]).astype(jnp.bfloat16), tri, (1, 0))
    zeroth = jnp.zeros((count, 128), jnp.float32)
    first = jnp.zeros((count, 128), jnp.float32)
    for v in range(ves):
        zeroth += hits[v] * (rank == 0.0).astype(jnp.float32)
        first += hits[v] * (rank == 1.0).astype(jnp.float32)
        item = jnp.sum(hits[v] * rank, axis=0, keepdims=True)
        idx[4 + v : 5 + v, 0:128] = near[v : v + 1] * 4 + item.astype(jnp.int32) * 2
        rank = rank + hits[v]
    line = iota((8, 128), 0)
    inside = lambda k: (lane >= k * blocks) & (lane < (k + 1) * blocks)
    odd = lax.rem(me, 2)
    left = 2 * lane + 2 * blocks * (1 - odd) - 4 * blocks
    middle = 2 * (lane - blocks) - 2 * blocks
    right = 2 * (lane - 2 * blocks) + 2 * blocks * odd - 4 * blocks
    put = lambda r, k, place: jnp.where((line == r) & inside(k), place, 0)
    pick = product(
        (put(0, 0, left) + put(2, 1, middle)).astype(jnp.float32).astype(jnp.bfloat16),
        first.astype(jnp.bfloat16),
        (1, 1),
    ) + product(
        (put(1, 1, middle) + put(3, 2, right)).astype(jnp.float32).astype(jnp.bfloat16),
        zeroth.astype(jnp.bfloat16),
        (1, 1),
    )
    empty = jnp.where((line == 0) | (line == 3), 4 * blocks, 2 * blocks)[0:4, 0:1]
    idx[0:4, 0:count] = pick[0:4].astype(jnp.int32) + empty

    taps = w_in.shape[0]
    row, col = iota((48, 40), 0), iota((48, 40), 1)
    tap, extra = row & 15, (row & 15) - 12
    target = (row & 3) * 9 + 3 * (row >> 4) + ((row >> 2) & 3)
    target = jnp.where(tap < 12, target, jnp.where((row >> 4) == 1, taps + extra, -1))
    order = one_hot(col, target)
    rows[...] = jnp.zeros_like(rows)
    rows[0:taps, :] = w_in[...].astype(jnp.float32)
    for n, part in enumerate(halves(b_in[...])):
        rows[taps + n : taps + n + 1, :] = part
    w1[...] = (0.5 * product(rows[...].astype(jnp.bfloat16), order, (0, 1))).astype(jnp.bfloat16)
    rows[...] = jnp.zeros_like(rows)
    for n, part in enumerate(halves(b_mid[...])):
        rows[n : n + 1, :] = part
    row, col = iota((40, channels + 16), 0), iota((40, channels + 16), 1)
    bias = product(rows[...].astype(jnp.bfloat16), one_hot(col, row + channels), (0, 0))
    row, col = iota((channels, channels + 16), 0), iota((channels, channels + 16), 1)
    w2[...] = (0.5 * (product(w_mid[...], one_hot(row, col), (1, 0)) + bias)).astype(jnp.bfloat16)
    rows[...] = jnp.zeros_like(rows)
    rows[0:taps, :] = w_out[...].astype(jnp.float32)
    outs = rows[...].astype(jnp.bfloat16)
    wo[...] = (0.5 * product(outs, order, (0, 1))).astype(jnp.bfloat16)
    row, col = iota((24, 40), 0), iota((24, 40), 1)
    for i in range(3):
        target = jnp.where((row & 7) < 4, (row & 3) * 9 + 3 * i + (row >> 3), -1)
        part = product(one_hot(col, target), outs, (1, 0))
        w3[:, i * channels : (i + 1) * channels] = part.astype(jnp.bfloat16)
    eye = one_hot(iota((channels, channels), 0), iota((channels, channels), 1))
    wm[...] = (0.5 * product(w_mid[...], eye, (0, 0))).astype(jnp.bfloat16)


def local(records, dest, w_in, b_in, w_mid, b_mid, w_out):
    count = lax.axis_size("rec")
    me = lax.axis_index("rec")
    parts, blocks, traces, samples = records.shape
    ves = dest.shape[1]
    tiles = blocks * traces
    channels = w_in.shape[0]
    group = group_of(count)
    steps = count // group
    width = group * 2 * samples
    far = [(s, s + 1) for s in range(1, count - 1, 2)]
    far += [(b, a) for a, b in far]
    far += [(s, s) for s in range(count) if s not in {a for a, _ in far}]
    near = [(s, s + 1) for s in range(0, count - 1, 2)]
    near += [(b, a) for a, b in near]

    flat = records.transpose(1, 2, 0, 3).reshape(tiles, parts, samples)
    from_far = lax.ppermute(flat, "rec", far)
    from_near = lax.ppermute(flat, "rec", near)

    f32, bf16 = jnp.float32, jnp.bfloat16
    shape = (steps, channels, width)
    blocked = 24 * math.prod(shape) > RESIDENT
    saved = [
        jax.ShapeDtypeStruct(shape, kind) if blocked else pltpu.VMEM(shape, kind)
        for kind in (bf16, bf16, f32, f32)
    ]
    held = [VMEM] * 4
    if blocked:
        held = [pl.BlockSpec((1, channels, width), lambda n: (n, 0, 0))] * 4
    grid = (steps,) if blocked else ()
    params = pltpu.CompilerParams(vmem_limit_bytes=16 << 20)
    args = (
        dest.T, w_in.T, b_in.reshape(1, channels), w_mid, b_mid.reshape(1, channels), w_out.T
    )
    idx, w1, w2, w3, wo, wm = pl.pallas_call(
        functools.partial(prep_kernel, blocks),
        out_shape=[jax.ShapeDtypeStruct((8, max(128, count)), jnp.int32)]
        + [
            jax.ShapeDtypeStruct(size, bf16)
            for size in (
                (channels, 48), (channels, channels + 16), (24, 3 * channels), (channels, 48),
                (channels, channels),
            )
        ],
        in_specs=[pl.BlockSpec(memory_space=pltpu.HBM)] * 6,
        out_specs=[VMEM] * 6,
        scratch_shapes=[pltpu.VMEM((40, channels), f32)]
        + [pltpu.VMEM(arg.shape, arg.dtype) for arg in args]
        + [pltpu.SemaphoreType.DMA((6,))],
        compiler_params=params,
        name="prepare",
    )(*[pltpu.with_memory_space_constraint(arg, pltpu.HBM) for arg in args])
    def table(pieces, kind):
        return pltpu.VMEM((pieces * tiles + 2, 16, samples), kind)

    def call(kernel, ins, outs, scratch, args, name, owned):
        return pl.pallas_call(
            functools.partial(kernel, group, blocked),
            grid=grid,
            out_shape=outs[0] + saved * outs[1],
            in_specs=[SMEM] + [VMEM] * ins[0] + held[:1] * ins[1],
            out_specs=[VMEM] * len(outs[0]) + held * outs[1],
            scratch_shapes=scratch,
            compiler_params=params,
            cost_estimate=pl.CostEstimate(
                flops=2 * owned * count * samples * channels * (3 * channels),
                bytes_accessed=owned * count * samples * channels * 12,
                transcendentals=0,
            ),
            name=name,
        )(*args)

    total = (112 + channels, channels)
    own, *inner = call(
        forward_inner, (3, 0), ([table(1, bf16)], 1), [table(1, f32)],
        (idx, flat, w1, w2), "forward_inner", 2,
    )
    res, g, halo, *outer = call(
        forward_outer, (7, 1),
        (
            [
                jax.ShapeDtypeStruct(records.shape, f32),
                jax.ShapeDtypeStruct((tiles, parts, samples), bf16),
                table(2, bf16),
            ],
            1,
        ),
        [table(2, f32), pltpu.VMEM((count * 4, 8, samples), f32)],
        (idx, from_near, flat, from_far, own, w1, w2, w3, inner[1]), "forward_outer", 4,
    )
    g_far = lax.ppermute(g, "rec", far)
    g_near = lax.ppermute(g, "rec", near)
    gown, part = call(
        backward_inner, (4, 4), ([table(1, bf16), pltpu.VMEM(total, f32)], 0), [table(1, f32)],
        (idx, g, wo, wm, own, *inner), "backward_inner", 2,
    )
    (sums,) = call(
        backward_outer, (8, 4), ([jax.ShapeDtypeStruct((48 + channels // 2, 2 * channels), f32)], 0),
        [table(2, bf16), table(2, f32), pltpu.VMEM(total, f32)],
        (idx, g_near, g_far, wo, wm, own, halo, gown, part, *outer), "backward_outer", 2,
    )

    if count & (count - 1):
        terms = [lax.psum(sums, "rec")]
    else:
        terms = [sums]
        at = 1
        while at < count:
            wide = 2 if at == 1 or 2 * at == count else 4
            value = terms[0]
            if len(terms) == 2:
                value = terms[0] + terms[1]
            if len(terms) == 4:
                value = (terms[0] + terms[1]) + (terms[2] + terms[3])
            terms = [value] + [
                lax.ppermute(value, "rec", [(s, s ^ (k * at)) for s in range(count)])
                for k in range(1, wide)
            ]
            at *= wide

    scale = 1.0 / math.sqrt(parts * blocks * count * traces * samples)
    g_in, g_bin, g_mid, g_bmid, g_out = pl.pallas_call(
        functools.partial(finish_kernel, scale, parts),
        out_shape=[
            jax.ShapeDtypeStruct(shape, f32)
            for shape in (
                (parts * 9, channels), (1, channels), (channels, channels), (1, channels),
                (parts * 9, channels),
            )
        ],
        in_specs=[VMEM] * len(terms),
        out_specs=[VMEM] * 5,
        scratch_shapes=[pltpu.VMEM(sums.shape, f32)],
        compiler_params=params,
        name="finish",
    )(*terms)
    return (
        res,
        g_in.T,
        g_bin.reshape(channels),
        g_mid,
        g_bmid.reshape(channels),
        g_out.T,
    )


def solution(mesh):
    return jax.shard_map(
        local,
        mesh=mesh,
        in_specs=(
            P(None, ("groups", "rec"), None, None),
            P("groups", None),
            P(),
            P(),
            P(),
            P(),
            P(),
        ),
        out_specs=(
            P(None, ("groups", "rec"), None, None),
            P("groups", None),
            P("groups"),
            P("groups", None),
            P("groups"),
            P("groups", None),
        ),
        check_vma=False,
    )
```

```python
import functools
import math

import jax
import jax.numpy as jnp
from jax import lax
from jax.experimental import pallas as pl
from jax.experimental.pallas import tpu as pltpu
from jax.sharding import PartitionSpec as P

CAP = 2
VMEM = pl.BlockSpec(memory_space=pltpu.VMEM)
SMEM = pl.BlockSpec(memory_space=pltpu.SMEM)
RESIDENT = 24 << 20


def run(start, step, end, steps, blocked):
    if blocked:
        n = pl.program_id(0)
        pl.when(n == 0)(start)
        step(n, 0)
        pl.when(n == steps - 1)(end)
        return
    start()
    lax.fori_loop(0, steps, lambda n, carry: step(n, n), None)
    end()


def group_of(owners):
    for size in (16, 8, 4, 2):
        if owners % size == 0:
            return size
    return 1


def fill_table(table, wide, pieces, tiles, flip, fill):
    for n, piece in enumerate(pieces):
        x = piece[...].astype(jnp.float32)
        samples = x.shape[2]
        lane = lax.broadcasted_iota(jnp.int32, x.shape, 2)
        before = jnp.where(lane == 0, 0.0, pltpu.roll(x, 1, 2))
        after = jnp.where(lane == samples - 1, 0.0, pltpu.roll(x, samples - 1, 2))
        at = pl.ds(n * tiles, tiles)
        wide[at, 0:4, :] = after if flip else before
        wide[at, 4:8, :] = x
        wide[at, 8:12, :] = before if flip else after
    last = len(pieces) * tiles
    wide[pl.ds(last, 2), 0:12, :] = jnp.zeros((2, 12, wide.shape[2]), jnp.float32)
    wide[:, 12:16, :] = jnp.full((last + 2, 4, wide.shape[2]), fill, jnp.float32)
    table[...] = wide[...].astype(jnp.bfloat16)


def act(y):
    t = jnp.tanh(y)
    q = 1.0 + t
    a = y * q
    return t, q, a


def lines_of(idx, own, halo, owners):
    lines = []
    for e in owners:
        line = []
        for r in range(4):
            held = own if r in (1, 2) else halo
            line += [None, None] if held is None else [held[idx[r, e]], held[idx[r, e] + 1]]
        lines.append(line)
    return lines


def stack(lines, traces, flip):
    return jnp.concatenate(
        [
            jnp.concatenate(
                [line[h + 1 + (2 - i if flip else i)] for line in lines for h in traces], axis=1
            )
            for i in range(3)
        ],
        axis=0,
    )


def layers(inputs, w1, w2):
    y1 = jnp.dot(w1[...], inputs, preferred_element_type=jnp.float32)
    t, q, a = act(y1)
    d1 = q + a * (1.0 - t)
    a1 = a.astype(jnp.bfloat16)
    ones = jnp.ones((16, a1.shape[1]), jnp.bfloat16)
    y2 = jnp.dot(w2[...], jnp.concatenate([a1, ones], axis=0), preferred_element_type=jnp.float32)
    t, q, a = act(y2)
    return a1, d1, a, q + a * (1.0 - t)


def forward_inner(
    group, blocked, idx, mine, w1, w2, own, a1_ref, a2_ref, d1_ref, d2_ref, wide
):
    owners = lax.axis_size("rec")

    def start():
        fill_table(own, wide, (mine,), mine.shape[0], False, 1.0)

    def step(n, block):
        lines = lines_of(idx, own, None, [n * group + u for u in range(group)])
        a1, d1, a2, d2 = layers(stack(lines, (1, 2), False), w1, w2)
        a1_ref[block] = a1
        d1_ref[block] = d1
        a2_ref[block] = a2.astype(jnp.bfloat16)
        d2_ref[block] = d2

    run(start, step, lambda: None, owners // group, blocked)


def forward_outer(
    group, blocked, idx, near, mine, far, own, w1, w2, w3, inner,
    res, g, halo, a1_ref, a2_ref, d1_ref, d2_ref, wide, est,
):
    tiles, parts, samples = mine.shape
    count = lax.axis_size("rec")
    me = lax.axis_index("rec")
    has_left = (me > 0).astype(jnp.float32)
    has_right = (me < count - 1).astype(jnp.float32)
    lane = lax.broadcasted_iota(jnp.int32, (8, samples), 1)
    low = (lane > 0).astype(jnp.float32)
    high = (lane < samples - 1).astype(jnp.float32)

    def start():
        fill_table(halo, wide, (near, far), tiles, False, 1.0)

    def step(n, block):
        lines = lines_of(idx, own, halo, [n * group + u for u in range(group)])
        a1, d1, a2, d2 = layers(stack(lines, (-1, 0, 3, 4), False), w1, w2)
        cut = lambda x, u, k: x[:, (u * 4 + k) * samples : (u * 4 + k + 1) * samples]
        middle = lambda x: jnp.concatenate(
            [cut(x, u, k) for u in range(group) for k in (1, 2)], axis=1
        )
        a1_ref[block] = middle(a1)
        d1_ref[block] = middle(d1)
        d2_ref[block] = middle(d2)
        rows = []
        for u in range(group):
            row = [cut(a2, u, 0) * has_left, cut(a2, u, 1), cut(a2, u, 2), cut(a2, u, 3) * has_right]
            row = [part.astype(jnp.bfloat16) for part in row]
            within = [
                inner[block, :, (u * 2 + k) * samples : (u * 2 + k + 1) * samples] for k in range(2)
            ]
            rows.append(row[0:2] + within + row[2:4])
        a2_ref[block] = jnp.concatenate([row[k] for row in rows for k in (1, 4)], axis=1)
        rhs = jnp.concatenate(
            [
                jnp.concatenate([row[h + i] for row in rows for h in range(4)], axis=1)
                for i in range(3)
            ],
            axis=0,
        )
        terms = jnp.dot(w3[...], rhs, preferred_element_type=jnp.float32)
        for k in range(group * 4):
            part = terms[:, k * samples : (k + 1) * samples]
            total = (
                part[8:16]
                + pltpu.roll(part[0:8], 1, 1) * low
                + pltpu.roll(part[16:24], samples - 1, 1) * high
            )
            est[n * group * 4 + k] = total.astype(jnp.bfloat16).astype(jnp.float32)

    def end():
        for c in range(tiles // 2):
            at = [idx[4 + v, tiles // 2 + c] for v in range(4)]
            for k in range(2):
                total = (est[at[0] + k] + est[at[1] + k]) + (est[at[2] + k] + est[at[3] + k])
                value = total[0:parts] - mine[c * 2 + k].astype(jnp.float32)
                for o in range(parts):
                    res[o, c, k : k + 1, :] = value[o : o + 1]
                g[c * 2 + k] = value.astype(jnp.bfloat16)

    run(start, step, end, count // group, blocked)


def weight_terms(acc, fields, inputs, wo, wm, a1, a2, d1, d2):
    channels = wm.shape[0]
    da2 = jnp.dot(wo[...], fields, preferred_element_type=jnp.float32)
    dz2 = (da2 * d2).astype(jnp.bfloat16)
    acc[0:48, :] += product(fields, a2, (1, 1))
    da1 = jnp.dot(wm[...], dz2, preferred_element_type=jnp.float32)
    ones = jnp.ones((16, dz2.shape[1]), jnp.bfloat16)
    acc[48 : 64 + channels, :] += product(jnp.concatenate([a1, ones], axis=0), dz2, (1, 1))
    dz1 = (da1 * d1).astype(jnp.bfloat16)
    acc[64 + channels : 112 + channels, :] += product(inputs, dz1, (1, 1))


def backward_inner(
    group, blocked, idx, mine, wo, wm, own, a1_ref, a2_ref, d1_ref, d2_ref, gown, acc, wide
):
    owners = lax.axis_size("rec")

    def start():
        fill_table(gown, wide, (mine,), mine.shape[0], True, 0.0)
        acc[...] = jnp.zeros_like(acc)

    def step(n, block):
        es = [n * group + u for u in range(group)]
        fields = stack(lines_of(idx, gown, None, es), (1, 2), True)
        inputs = stack(lines_of(idx, own, None, es), (1, 2), False)
        saved = a1_ref[block], a2_ref[block], d1_ref[block], d2_ref[block]
        weight_terms(acc, fields, inputs, wo, wm, *saved)

    run(start, step, lambda: None, owners // group, blocked)


def backward_outer(
    group, blocked, idx, near, far, wo, wm, own, halo, gown, sums, a1_ref, a2_ref, d1_ref, d2_ref,
    out, ghalo, wide, acc,
):
    owners = lax.axis_size("rec")
    channels = wm.shape[0]

    def start():
        fill_table(ghalo, wide, (near, far), near.shape[0], True, 0.0)
        acc[...] = sums[...]

    def step(n, block):
        es = [n * group + u for u in range(group)]
        fields = stack(lines_of(idx, gown, ghalo, es), (0, 3), True)
        inputs = stack(lines_of(idx, own, halo, es), (0, 3), False)
        saved = a1_ref[block], a2_ref[block], d1_ref[block], d2_ref[block]
        weight_terms(acc, fields, inputs, wo, wm, *saved)

    def end():
        first, half = 64 + channels, channels // 2
        low, high = slice(0, channels), slice(channels, 2 * channels)
        out[0:48, low] = acc[first : first + 48, :]
        out[0:48, high] = acc[0:48, :]
        out[12:13, low] = acc[48 + channels : 49 + channels, :]
        middle = acc[48 : 48 + channels, :].T
        out[48 : 48 + half, low] = middle[0:half]
        out[48 : 48 + half, high] = middle[half:channels]

    run(start, step, end, owners // group, blocked)


def finish_kernel(scale, parts, *refs):
    terms, (g_in, g_bin, g_mid, g_bmid, g_out, held) = refs[:-6], refs[-6:]
    values = [ref[...] for ref in terms]
    while len(values) > 1:
        values = [values[k] + values[k + 1] for k in range(0, len(values), 2)]
    held[...] = values[0] * scale
    channels = g_mid.shape[0]
    for o in range(parts):
        for i in range(3):
            for j in range(3):
                row = held[i * 16 + j * 4 + o : i * 16 + j * 4 + o + 1, :]
                at = o * 9 + 3 * i + j
                g_in[at : at + 1, :] = row[:, 0:channels]
                g_out[at : at + 1, :] = row[:, channels : 2 * channels]
    g_bin[...] = held[28:29, 0:channels]
    g_bmid[...] = held[12:13, 0:channels]
    half = channels // 2
    g_mid[0:half] = held[48 : 48 + half, 0:channels]
    g_mid[half:channels] = held[48 : 48 + half, channels : 2 * channels]


def halves(b):
    high = b.astype(jnp.bfloat16).astype(jnp.float32)
    rest = b - high
    mid = rest.astype(jnp.bfloat16).astype(jnp.float32)
    return [high, mid, rest - mid]


def one_hot(a, b):
    return (a == b).astype(jnp.float32).astype(jnp.bfloat16)


def iota(shape, dim):
    return lax.broadcasted_iota(jnp.int32, shape, dim)


def product(a, b, over):
    return lax.dot_general(
        a, b, dimension_numbers=(((over[0],), (over[1],)), ((), ())),
        preferred_element_type=jnp.float32,
    )


def prep_kernel(blocks, *refs):
    args, (idx, w1, w2, w3, wo, wm, rows), held, sems = refs[:6], refs[6:13], refs[13:19], refs[19]
    copies = [
        pltpu.make_async_copy(src, dst, sems.at[n]) for n, (src, dst) in enumerate(zip(args, held))
    ]
    for copy in copies:
        copy.start()
    for copy in copies:
        copy.wait()
    dest, w_in, b_in, w_mid, b_mid, w_out = held
    count = lax.axis_size("rec")
    me = lax.axis_index("rec")
    ves, total = dest.shape
    channels = w_mid.shape[0]
    at = lax.rem((count + 1 - me) * blocks, total)
    wide = jnp.concatenate([dest[...], jnp.zeros((8 - ves, total), jnp.int32)], axis=0)
    near = pltpu.roll(wide, at, 1)[:, 0:128]
    lane = iota((8, 128), 1)
    low = jnp.where(me > 0, 0, blocks)
    high = jnp.where(me < count - 1, 3 * blocks, 2 * blocks)
    near = jnp.where((lane >= low) & (lane < high), near, -1)
    owner = iota((count, 128), 0)
    hits = [(near[v : v + 1] == owner).astype(jnp.float32) for v in range(ves)]
    before = iota((128, 128), 0)
    after = iota((128, 128), 1)
    segment = (after >= blocks).astype(jnp.int32) + (after >= 2 * blocks).astype(jnp.int32)
    tri = ((before < after) & (before >= segment * blocks)).astype(jnp.float32).astype(jnp.bfloat16)
    rank = product((hits[0] + hits[1] + hits[2] + hits[3]).astype(jnp.bfloat16), tri, (1, 0))
    zeroth = jnp.zeros((count, 128), jnp.float32)
    first = jnp.zeros((count, 128), jnp.float32)
    for v in range(ves):
        zeroth += hits[v] * (rank == 0.0).astype(jnp.float32)
        first += hits[v] * (rank == 1.0).astype(jnp.float32)
        item = jnp.sum(hits[v] * rank, axis=0, keepdims=True)
        idx[4 + v : 5 + v, 0:128] = near[v : v + 1] * 4 + item.astype(jnp.int32) * 2
        rank = rank + hits[v]
    line = iota((8, 128), 0)
    inside = lambda k: (lane >= k * blocks) & (lane < (k + 1) * blocks)
    odd = lax.rem(me, 2)
    left = 2 * lane + 2 * blocks * (1 - odd) - 4 * blocks
    middle = 2 * (lane - blocks) - 2 * blocks
    right = 2 * (lane - 2 * blocks) + 2 * blocks * odd - 4 * blocks
    put = lambda r, k, place: jnp.where((line == r) & inside(k), place, 0)
    pick = product(
        (put(0, 0, left) + put(2, 1, middle)).astype(jnp.float32).astype(jnp.bfloat16),
        first.astype(jnp.bfloat16),
        (1, 1),
    ) + product(
        (put(1, 1, middle) + put(3, 2, right)).astype(jnp.float32).astype(jnp.bfloat16),
        zeroth.astype(jnp.bfloat16),
        (1, 1),
    )
    empty = jnp.where((line == 0) | (line == 3), 4 * blocks, 2 * blocks)[0:4, 0:1]
    idx[0:4, 0:count] = pick[0:4].astype(jnp.int32) + empty

    taps = w_in.shape[0]
    row, col = iota((48, 40), 0), iota((48, 40), 1)
    tap, extra = row & 15, (row & 15) - 12
    target = (row & 3) * 9 + 3 * (row >> 4) + ((row >> 2) & 3)
    target = jnp.where(tap < 12, target, jnp.where((row >> 4) == 1, taps + extra, -1))
    order = one_hot(col, target)
    rows[...] = jnp.zeros_like(rows)
    rows[0:taps, :] = w_in[...].astype(jnp.float32)
    for n, part in enumerate(halves(b_in[...])):
        rows[taps + n : taps + n + 1, :] = part
    w1[...] = (0.5 * product(rows[...].astype(jnp.bfloat16), order, (0, 1))).astype(jnp.bfloat16)
    rows[...] = jnp.zeros_like(rows)
    for n, part in enumerate(halves(b_mid[...])):
        rows[n : n + 1, :] = part
    row, col = iota((40, channels + 16), 0), iota((40, channels + 16), 1)
    bias = product(rows[...].astype(jnp.bfloat16), one_hot(col, row + channels), (0, 0))
    row, col = iota((channels, channels + 16), 0), iota((channels, channels + 16), 1)
    w2[...] = (0.5 * (product(w_mid[...], one_hot(row, col), (1, 0)) + bias)).astype(jnp.bfloat16)
    rows[...] = jnp.zeros_like(rows)
    rows[0:taps, :] = w_out[...].astype(jnp.float32)
    outs = rows[...].astype(jnp.bfloat16)
    wo[...] = (0.5 * product(outs, order, (0, 1))).astype(jnp.bfloat16)
    row, col = iota((24, 40), 0), iota((24, 40), 1)
    for i in range(3):
        target = jnp.where((row & 7) < 4, (row & 3) * 9 + 3 * i + (row >> 3), -1)
        part = product(one_hot(col, target), outs, (1, 0))
        w3[:, i * channels : (i + 1) * channels] = part.astype(jnp.bfloat16)
    eye = one_hot(iota((channels, channels), 0), iota((channels, channels), 1))
    wm[...] = (0.5 * product(w_mid[...], eye, (0, 0))).astype(jnp.bfloat16)


def local(records, dest, w_in, b_in, w_mid, b_mid, w_out):
    count = lax.axis_size("rec")
    me = lax.axis_index("rec")
    parts, blocks, traces, samples = records.shape
    ves = dest.shape[1]
    tiles = blocks * traces
    channels = w_in.shape[0]
    group = group_of(count)
    steps = count // group
    width = group * 2 * samples
    far = [(s, s + 2) for s in range(0, count - 2, 2)] + [(s, s - 2) for s in range(3, count, 2)]
    near = [(s, s + 1) for s in range(0, count - 1, 2)]
    near += [(b, a) for a, b in near]

    flat = records.transpose(1, 2, 0, 3).reshape(tiles, parts, samples)
    from_near = lax.ppermute(flat, "rec", near)

    f32, bf16 = jnp.float32, jnp.bfloat16
    shape = (steps, channels, width)
    blocked = 24 * math.prod(shape) > RESIDENT
    saved = [
        jax.ShapeDtypeStruct(shape, kind) if blocked else pltpu.VMEM(shape, kind)
        for kind in (bf16, bf16, f32, f32)
    ]
    held = [VMEM] * 4
    if blocked:
        held = [pl.BlockSpec((1, channels, width), lambda n: (n, 0, 0))] * 4
    grid = (steps,) if blocked else ()
    params = pltpu.CompilerParams(vmem_limit_bytes=16 << 20)
    args = (
        dest.T, w_in.T, b_in.reshape(1, channels), w_mid, b_mid.reshape(1, channels), w_out.T
    )
    idx, w1, w2, w3, wo, wm = pl.pallas_call(
        functools.partial(prep_kernel, blocks),
        out_shape=[jax.ShapeDtypeStruct((8, max(128, count)), jnp.int32)]
        + [
            jax.ShapeDtypeStruct(size, bf16)
            for size in (
                (channels, 48), (channels, channels + 16), (24, 3 * channels), (channels, 48),
                (channels, channels),
            )
        ],
        in_specs=[pl.BlockSpec(memory_space=pltpu.HBM)] * 6,
        out_specs=[VMEM] * 6,
        scratch_shapes=[pltpu.VMEM((40, channels), f32)]
        + [pltpu.VMEM(arg.shape, arg.dtype) for arg in args]
        + [pltpu.SemaphoreType.DMA((6,))],
        compiler_params=params,
        name="prepare",
    )(*[pltpu.with_memory_space_constraint(arg, pltpu.HBM) for arg in args])
    from_near, idx = lax.optimization_barrier((from_near, idx))
    from_far = lax.ppermute(from_near, "rec", far)

    def table(pieces, kind):
        return pltpu.VMEM((pieces * tiles + 2, 16, samples), kind)

    def call(kernel, ins, outs, scratch, args, name, owned):
        return pl.pallas_call(
            functools.partial(kernel, group, blocked),
            grid=grid,
            out_shape=outs[0] + saved * outs[1],
            in_specs=[SMEM] + [VMEM] * ins[0] + held[:1] * ins[1],
            out_specs=[VMEM] * len(outs[0]) + held * outs[1],
            scratch_shapes=scratch,
            compiler_params=params,
            cost_estimate=pl.CostEstimate(
                flops=2 * owned * count * samples * channels * (3 * channels),
                bytes_accessed=owned * count * samples * channels * 12,
                transcendentals=0,
            ),
            name=name,
        )(*args)

    total = (112 + channels, channels)
    own, *inner = call(
        forward_inner, (3, 0), ([table(1, bf16)], 1), [table(1, f32)],
        (idx, flat, w1, w2), "forward_inner", 2,
    )
    res, g, halo, *outer = call(
        forward_outer, (7, 1),
        (
            [
                jax.ShapeDtypeStruct(records.shape, f32),
                jax.ShapeDtypeStruct((tiles, parts, samples), bf16),
                table(2, bf16),
            ],
            1,
        ),
        [table(2, f32), pltpu.VMEM((count * 4, 8, samples), f32)],
        (idx, from_near, flat, from_far, own, w1, w2, w3, inner[1]), "forward_outer", 4,
    )
    g_near = lax.ppermute(g, "rec", near)
    g_far = lax.ppermute(g_near, "rec", far)
    gown, part = call(
        backward_inner, (4, 4), ([table(1, bf16), pltpu.VMEM(total, f32)], 0), [table(1, f32)],
        (idx, g, wo, wm, own, *inner), "backward_inner", 2,
    )
    (sums,) = call(
        backward_outer, (8, 4), ([jax.ShapeDtypeStruct((48 + channels // 2, 2 * channels), f32)], 0),
        [table(2, bf16), table(2, f32), pltpu.VMEM(total, f32)],
        (idx, g_near, g_far, wo, wm, own, halo, gown, part, *outer), "backward_outer", 2,
    )

    if count & (count - 1):
        terms = [lax.psum(sums, "rec")]
    else:
        terms = [sums]
        at = 1
        while at < count:
            wide = 2 if at == 1 or 2 * at == count else 4
            value = terms[0]
            if len(terms) == 2:
                value = terms[0] + terms[1]
            if len(terms) == 4:
                value = (terms[0] + terms[1]) + (terms[2] + terms[3])
            terms = [value] + [
                lax.ppermute(value, "rec", [(s, s ^ (k * at)) for s in range(count)])
                for k in range(1, wide)
            ]
            at *= wide

    scale = 1.0 / math.sqrt(parts * blocks * count * traces * samples)
    g_in, g_bin, g_mid, g_bmid, g_out = pl.pallas_call(
        functools.partial(finish_kernel, scale, parts),
        out_shape=[
            jax.ShapeDtypeStruct(shape, f32)
            for shape in (
                (parts * 9, channels), (1, channels), (channels, channels), (1, channels),
                (parts * 9, channels),
            )
        ],
        in_specs=[VMEM] * len(terms),
        out_specs=[VMEM] * 5,
        scratch_shapes=[pltpu.VMEM(sums.shape, f32)],
        compiler_params=params,
        name="finish",
    )(*terms)
    return (
        res,
        g_in.T,
        g_bin.reshape(channels),
        g_mid,
        g_bmid.reshape(channels),
        g_out.T,
    )


def solution(mesh):
    return jax.shard_map(
        local,
        mesh=mesh,
        in_specs=(
            P(None, ("groups", "rec"), None, None),
            P("groups", None),
            P(),
            P(),
            P(),
            P(),
            P(),
        ),
        out_specs=(
            P(None, ("groups", "rec"), None, None),
            P("groups", None),
            P("groups"),
            P("groups", None),
            P("groups"),
            P("groups", None),
        ),
        check_vma=False,
    )
```

```python
import functools
import math

import jax
import jax.numpy as jnp
from jax import lax
from jax.experimental import pallas as pl
from jax.experimental.pallas import tpu as pltpu
from jax.sharding import PartitionSpec as P

CAP = 2
VMEM = pl.BlockSpec(memory_space=pltpu.VMEM)
SMEM = pl.BlockSpec(memory_space=pltpu.SMEM)
RESIDENT = 24 << 20


def run(start, step, end, steps, blocked):
    if blocked:
        n = pl.program_id(0)
        pl.when(n == 0)(start)
        step(n, 0)
        pl.when(n == steps - 1)(end)
        return
    start()
    lax.fori_loop(0, steps, lambda n, carry: step(n, n), None)
    end()


def group_of(owners):
    for size in (16, 8, 4, 2):
        if owners % size == 0:
            return size
    return 1


def fill_table(table, wide, pieces, tiles, flip, fill):
    for n, piece in enumerate(pieces):
        x = piece[...].astype(jnp.float32)
        samples = x.shape[2]
        lane = lax.broadcasted_iota(jnp.int32, x.shape, 2)
        before = jnp.where(lane == 0, 0.0, pltpu.roll(x, 1, 2))
        after = jnp.where(lane == samples - 1, 0.0, pltpu.roll(x, samples - 1, 2))
        at = pl.ds(n * tiles, tiles)
        wide[at, 0:4, :] = after if flip else before
        wide[at, 4:8, :] = x
        wide[at, 8:12, :] = before if flip else after
    last = len(pieces) * tiles
    wide[pl.ds(last, 2), 0:12, :] = jnp.zeros((2, 12, wide.shape[2]), jnp.float32)
    wide[:, 12:16, :] = jnp.full((last + 2, 4, wide.shape[2]), fill, jnp.float32)
    table[...] = wide[...].astype(jnp.bfloat16)


def act(y):
    t = jnp.tanh(y)
    q = 1.0 + t
    a = y * q
    return t, q, a


def partner(me):
    return lax.rem(me, 2)


def lines_of(idx, own, halo, owners):
    lines = []
    for e in owners:
        line = []
        for r in range(4):
            held = own if r in (1, 2) else halo
            line += [None, None] if held is None else [held[idx[r, e]], held[idx[r, e] + 1]]
        lines.append(line)
    return lines


def stack(lines, traces, flip):
    return jnp.concatenate(
        [
            jnp.concatenate(
                [line[h + 1 + (2 - i if flip else i)] for line in lines for h in traces], axis=1
            )
            for i in range(3)
        ],
        axis=0,
    )


def layers(inputs, w1, w2):
    y1 = jnp.dot(w1[...], inputs, preferred_element_type=jnp.float32)
    t, q, a = act(y1)
    d1 = q + a * (1.0 - t)
    a1 = a.astype(jnp.bfloat16)
    ones = jnp.ones((16, a1.shape[1]), jnp.bfloat16)
    y2 = jnp.dot(w2[...], jnp.concatenate([a1, ones], axis=0), preferred_element_type=jnp.float32)
    t, q, a = act(y2)
    return a1, d1, a, q + a * (1.0 - t)


def forward_inner(
    group, blocked, idx, mine, w1, w2, own, a1_ref, a2_ref, d1_ref, d2_ref, wide
):
    owners = lax.axis_size("rec")

    def start():
        fill_table(own, wide, (mine,), mine.shape[0], False, 1.0)

    def step(n, block):
        lines = lines_of(idx, own, None, [n * group + u for u in range(group)])
        a1, d1, a2, d2 = layers(stack(lines, (1, 2), False), w1, w2)
        a1_ref[block] = a1
        d1_ref[block] = d1
        a2_ref[block] = a2.astype(jnp.bfloat16)
        d2_ref[block] = d2

    run(start, step, lambda: None, owners // group, blocked)


def forward_outer(
    group, blocked, idx, near, mine, far, own, w1, w2, w3, inner,
    res, g, halo, a1_ref, a2_ref, d1_ref, d2_ref, wide, est,
):
    tiles, parts, samples = mine.shape
    count = lax.axis_size("rec")
    me = lax.axis_index("rec")
    has_left = (me > 0).astype(jnp.float32)
    has_right = (me < count - 1).astype(jnp.float32)
    lane = lax.broadcasted_iota(jnp.int32, (8, samples), 1)
    low = (lane > 0).astype(jnp.float32)
    high = (lane < samples - 1).astype(jnp.float32)

    def start():
        fill_table(halo, wide, (near, far.at[partner(me)]), tiles, False, 1.0)

    def step(n, block):
        lines = lines_of(idx, own, halo, [n * group + u for u in range(group)])
        a1, d1, a2, d2 = layers(stack(lines, (-1, 0, 3, 4), False), w1, w2)
        cut = lambda x, u, k: x[:, (u * 4 + k) * samples : (u * 4 + k + 1) * samples]
        middle = lambda x: jnp.concatenate(
            [cut(x, u, k) for u in range(group) for k in (1, 2)], axis=1
        )
        a1_ref[block] = middle(a1)
        d1_ref[block] = middle(d1)
        d2_ref[block] = middle(d2)
        rows = []
        for u in range(group):
            row = [cut(a2, u, 0) * has_left, cut(a2, u, 1), cut(a2, u, 2), cut(a2, u, 3) * has_right]
            row = [part.astype(jnp.bfloat16) for part in row]
            within = [
                inner[block, :, (u * 2 + k) * samples : (u * 2 + k + 1) * samples] for k in range(2)
            ]
            rows.append(row[0:2] + within + row[2:4])
        a2_ref[block] = jnp.concatenate([row[k] for row in rows for k in (1, 4)], axis=1)
        rhs = jnp.concatenate(
            [
                jnp.concatenate([row[h + i] for row in rows for h in range(4)], axis=1)
                for i in range(3)
            ],
            axis=0,
        )
        terms = jnp.dot(w3[...], rhs, preferred_element_type=jnp.float32)
        for k in range(group * 4):
            part = terms[:, k * samples : (k + 1) * samples]
            total = (
                part[8:16]
                + pltpu.roll(part[0:8], 1, 1) * low
                + pltpu.roll(part[16:24], samples - 1, 1) * high
            )
            est[n * group * 4 + k] = total.astype(jnp.bfloat16).astype(jnp.float32)

    def end():
        for c in range(tiles // 2):
            at = [idx[4 + v, tiles // 2 + c] for v in range(4)]
            for k in range(2):
                total = (est[at[0] + k] + est[at[1] + k]) + (est[at[2] + k] + est[at[3] + k])
                value = total[0:parts] - mine[c * 2 + k].astype(jnp.float32)
                for o in range(parts):
                    res[o, c, k : k + 1, :] = value[o : o + 1]
                g[c * 2 + k] = value.astype(jnp.bfloat16)

    run(start, step, end, count // group, blocked)


def weight_terms(acc, fields, inputs, wo, wm, a1, a2, d1, d2):
    channels = wm.shape[0]
    da2 = jnp.dot(wo[...], fields, preferred_element_type=jnp.float32)
    dz2 = (da2 * d2).astype(jnp.bfloat16)
    acc[0:48, :] += product(fields, a2, (1, 1))
    da1 = jnp.dot(wm[...], dz2, preferred_element_type=jnp.float32)
    ones = jnp.ones((16, dz2.shape[1]), jnp.bfloat16)
    acc[48 : 64 + channels, :] += product(jnp.concatenate([a1, ones], axis=0), dz2, (1, 1))
    dz1 = (da1 * d1).astype(jnp.bfloat16)
    acc[64 + channels : 112 + channels, :] += product(inputs, dz1, (1, 1))


def backward_inner(
    group, blocked, idx, mine, wo, wm, own, a1_ref, a2_ref, d1_ref, d2_ref, gown, acc, wide
):
    owners = lax.axis_size("rec")

    def start():
        fill_table(gown, wide, (mine,), mine.shape[0], True, 0.0)
        acc[...] = jnp.zeros_like(acc)

    def step(n, block):
        es = [n * group + u for u in range(group)]
        fields = stack(lines_of(idx, gown, None, es), (1, 2), True)
        inputs = stack(lines_of(idx, own, None, es), (1, 2), False)
        saved = a1_ref[block], a2_ref[block], d1_ref[block], d2_ref[block]
        weight_terms(acc, fields, inputs, wo, wm, *saved)

    run(start, step, lambda: None, owners // group, blocked)


def backward_outer(
    group, blocked, idx, near, far, wo, wm, own, halo, gown, sums, a1_ref, a2_ref, d1_ref, d2_ref,
    out, ghalo, wide, acc,
):
    owners = lax.axis_size("rec")
    channels = wm.shape[0]

    def start():
        fill_table(ghalo, wide, (near, far.at[partner(lax.axis_index("rec"))]), near.shape[0], True, 0.0)
        acc[...] = sums[...]

    def step(n, block):
        es = [n * group + u for u in range(group)]
        fields = stack(lines_of(idx, gown, ghalo, es), (0, 3), True)
        inputs = stack(lines_of(idx, own, halo, es), (0, 3), False)
        saved = a1_ref[block], a2_ref[block], d1_ref[block], d2_ref[block]
        weight_terms(acc, fields, inputs, wo, wm, *saved)

    def end():
        first, half = 64 + channels, channels // 2
        low, high = slice(0, channels), slice(channels, 2 * channels)
        out[0:48, low] = acc[first : first + 48, :]
        out[0:48, high] = acc[0:48, :]
        out[12:13, low] = acc[48 + channels : 49 + channels, :]
        middle = acc[48 : 48 + channels, :].T
        out[48 : 48 + half, low] = middle[0:half]
        out[48 : 48 + half, high] = middle[half:channels]

    run(start, step, end, owners // group, blocked)


def finish_kernel(scale, parts, *refs):
    terms, (g_in, g_bin, g_mid, g_bmid, g_out, held) = refs[:-6], refs[-6:]
    values = [ref[...] for ref in terms]
    while len(values) > 1:
        values = [values[k] + values[k + 1] for k in range(0, len(values), 2)]
    held[...] = values[0] * scale
    channels = g_mid.shape[0]
    for o in range(parts):
        for i in range(3):
            for j in range(3):
                row = held[i * 16 + j * 4 + o : i * 16 + j * 4 + o + 1, :]
                at = o * 9 + 3 * i + j
                g_in[at : at + 1, :] = row[:, 0:channels]
                g_out[at : at + 1, :] = row[:, channels : 2 * channels]
    g_bin[...] = held[28:29, 0:channels]
    g_bmid[...] = held[12:13, 0:channels]
    half = channels // 2
    g_mid[0:half] = held[48 : 48 + half, 0:channels]
    g_mid[half:channels] = held[48 : 48 + half, channels : 2 * channels]


def halves(b):
    high = b.astype(jnp.bfloat16).astype(jnp.float32)
    rest = b - high
    mid = rest.astype(jnp.bfloat16).astype(jnp.float32)
    return [high, mid, rest - mid]


def one_hot(a, b):
    return (a == b).astype(jnp.float32).astype(jnp.bfloat16)


def iota(shape, dim):
    return lax.broadcasted_iota(jnp.int32, shape, dim)


def product(a, b, over):
    return lax.dot_general(
        a, b, dimension_numbers=(((over[0],), (over[1],)), ((), ())),
        preferred_element_type=jnp.float32,
    )


def prep_kernel(blocks, *refs):
    args, (idx, w1, w2, w3, wo, wm, rows), held, sems = refs[:6], refs[6:13], refs[13:19], refs[19]
    copies = [
        pltpu.make_async_copy(src, dst, sems.at[n]) for n, (src, dst) in enumerate(zip(args, held))
    ]
    for copy in copies:
        copy.start()
    for copy in copies:
        copy.wait()
    dest, w_in, b_in, w_mid, b_mid, w_out = held
    count = lax.axis_size("rec")
    me = lax.axis_index("rec")
    ves, total = dest.shape
    channels = w_mid.shape[0]
    at = lax.rem((count + 1 - me) * blocks, total)
    wide = jnp.concatenate([dest[...], jnp.zeros((8 - ves, total), jnp.int32)], axis=0)
    near = pltpu.roll(wide, at, 1)[:, 0:128]
    lane = iota((8, 128), 1)
    low = jnp.where(me > 0, 0, blocks)
    high = jnp.where(me < count - 1, 3 * blocks, 2 * blocks)
    near = jnp.where((lane >= low) & (lane < high), near, -1)
    owner = iota((count, 128), 0)
    hits = [(near[v : v + 1] == owner).astype(jnp.float32) for v in range(ves)]
    before = iota((128, 128), 0)
    after = iota((128, 128), 1)
    segment = (after >= blocks).astype(jnp.int32) + (after >= 2 * blocks).astype(jnp.int32)
    tri = ((before < after) & (before >= segment * blocks)).astype(jnp.float32).astype(jnp.bfloat16)
    rank = product((hits[0] + hits[1] + hits[2] + hits[3]).astype(jnp.bfloat16), tri, (1, 0))
    zeroth = jnp.zeros((count, 128), jnp.float32)
    first = jnp.zeros((count, 128), jnp.float32)
    for v in range(ves):
        zeroth += hits[v] * (rank == 0.0).astype(jnp.float32)
        first += hits[v] * (rank == 1.0).astype(jnp.float32)
        item = jnp.sum(hits[v] * rank, axis=0, keepdims=True)
        idx[4 + v : 5 + v, 0:128] = near[v : v + 1] * 4 + item.astype(jnp.int32) * 2
        rank = rank + hits[v]
    line = iota((8, 128), 0)
    inside = lambda k: (lane >= k * blocks) & (lane < (k + 1) * blocks)
    odd = lax.rem(me, 2)
    left = 2 * lane + 2 * blocks * (1 - odd) - 4 * blocks
    middle = 2 * (lane - blocks) - 2 * blocks
    right = 2 * (lane - 2 * blocks) + 2 * blocks * odd - 4 * blocks
    put = lambda r, k, place: jnp.where((line == r) & inside(k), place, 0)
    pick = product(
        (put(0, 0, left) + put(2, 1, middle)).astype(jnp.float32).astype(jnp.bfloat16),
        first.astype(jnp.bfloat16),
        (1, 1),
    ) + product(
        (put(1, 1, middle) + put(3, 2, right)).astype(jnp.float32).astype(jnp.bfloat16),
        zeroth.astype(jnp.bfloat16),
        (1, 1),
    )
    empty = jnp.where((line == 0) | (line == 3), 4 * blocks, 2 * blocks)[0:4, 0:1]
    idx[0:4, 0:count] = pick[0:4].astype(jnp.int32) + empty

    taps = w_in.shape[0]
    row, col = iota((48, 40), 0), iota((48, 40), 1)
    tap, extra = row & 15, (row & 15) - 12
    target = (row & 3) * 9 + 3 * (row >> 4) + ((row >> 2) & 3)
    target = jnp.where(tap < 12, target, jnp.where((row >> 4) == 1, taps + extra, -1))
    order = one_hot(col, target)
    rows[...] = jnp.zeros_like(rows)
    rows[0:taps, :] = w_in[...].astype(jnp.float32)
    for n, part in enumerate(halves(b_in[...])):
        rows[taps + n : taps + n + 1, :] = part
    w1[...] = (0.5 * product(rows[...].astype(jnp.bfloat16), order, (0, 1))).astype(jnp.bfloat16)
    rows[...] = jnp.zeros_like(rows)
    for n, part in enumerate(halves(b_mid[...])):
        rows[n : n + 1, :] = part
    row, col = iota((40, channels + 16), 0), iota((40, channels + 16), 1)
    bias = product(rows[...].astype(jnp.bfloat16), one_hot(col, row + channels), (0, 0))
    row, col = iota((channels, channels + 16), 0), iota((channels, channels + 16), 1)
    w2[...] = (0.5 * (product(w_mid[...], one_hot(row, col), (1, 0)) + bias)).astype(jnp.bfloat16)
    rows[...] = jnp.zeros_like(rows)
    rows[0:taps, :] = w_out[...].astype(jnp.float32)
    outs = rows[...].astype(jnp.bfloat16)
    wo[...] = (0.5 * product(outs, order, (0, 1))).astype(jnp.bfloat16)
    row, col = iota((24, 40), 0), iota((24, 40), 1)
    for i in range(3):
        target = jnp.where((row & 7) < 4, (row & 3) * 9 + 3 * i + (row >> 3), -1)
        part = product(one_hot(col, target), outs, (1, 0))
        w3[:, i * channels : (i + 1) * channels] = part.astype(jnp.bfloat16)
    eye = one_hot(iota((channels, channels), 0), iota((channels, channels), 1))
    wm[...] = (0.5 * product(w_mid[...], eye, (0, 0))).astype(jnp.bfloat16)


def local(records, dest, w_in, b_in, w_mid, b_mid, w_out):
    count = lax.axis_size("rec")
    me = lax.axis_index("rec")
    parts, blocks, traces, samples = records.shape
    ves = dest.shape[1]
    tiles = blocks * traces
    channels = w_in.shape[0]
    group = group_of(count)
    steps = count // group
    width = group * 2 * samples
    far = [[s, (s + 1) % count] for s in range(1, count, 2)]
    near = [(s, s + 1) for s in range(0, count - 1, 2)]
    near += [(b, a) for a, b in near]

    flat = records.transpose(1, 2, 0, 3).reshape(tiles, parts, samples)
    both = jnp.broadcast_to(flat[None], (2, tiles, parts, samples))
    from_far = lax.all_to_all(both, "rec", 0, 0, axis_index_groups=far, tiled=True)
    from_near = lax.ppermute(flat, "rec", near)

    f32, bf16 = jnp.float32, jnp.bfloat16
    shape = (steps, channels, width)
    blocked = 24 * math.prod(shape) > RESIDENT
    saved = [
        jax.ShapeDtypeStruct(shape, kind) if blocked else pltpu.VMEM(shape, kind)
        for kind in (bf16, bf16, f32, f32)
    ]
    held = [VMEM] * 4
    if blocked:
        held = [pl.BlockSpec((1, channels, width), lambda n: (n, 0, 0))] * 4
    grid = (steps,) if blocked else ()
    params = pltpu.CompilerParams(vmem_limit_bytes=16 << 20)
    args = (
        dest.T, w_in.T, b_in.reshape(1, channels), w_mid, b_mid.reshape(1, channels), w_out.T
    )
    idx, w1, w2, w3, wo, wm = pl.pallas_call(
        functools.partial(prep_kernel, blocks),
        out_shape=[jax.ShapeDtypeStruct((8, max(128, count)), jnp.int32)]
        + [
            jax.ShapeDtypeStruct(size, bf16)
            for size in (
                (channels, 48), (channels, channels + 16), (24, 3 * channels), (channels, 48),
                (channels, channels),
            )
        ],
        in_specs=[pl.BlockSpec(memory_space=pltpu.HBM)] * 6,
        out_specs=[VMEM] * 6,
        scratch_shapes=[pltpu.VMEM((40, channels), f32)]
        + [pltpu.VMEM(arg.shape, arg.dtype) for arg in args]
        + [pltpu.SemaphoreType.DMA((6,))],
        compiler_params=params,
        name="prepare",
    )(*[pltpu.with_memory_space_constraint(arg, pltpu.HBM) for arg in args])
    def table(pieces, kind):
        return pltpu.VMEM((pieces * tiles + 2, 16, samples), kind)

    def call(kernel, ins, outs, scratch, args, name, owned):
        return pl.pallas_call(
            functools.partial(kernel, group, blocked),
            grid=grid,
            out_shape=outs[0] + saved * outs[1],
            in_specs=[SMEM] + [VMEM] * ins[0] + held[:1] * ins[1],
            out_specs=[VMEM] * len(outs[0]) + held * outs[1],
            scratch_shapes=scratch,
            compiler_params=params,
            cost_estimate=pl.CostEstimate(
                flops=2 * owned * count * samples * channels * (3 * channels),
                bytes_accessed=owned * count * samples * channels * 12,
                transcendentals=0,
            ),
            name=name,
        )(*args)

    total = (112 + channels, channels)
    own, *inner = call(
        forward_inner, (3, 0), ([table(1, bf16)], 1), [table(1, f32)],
        (idx, flat, w1, w2), "forward_inner", 2,
    )
    res, g, halo, *outer = call(
        forward_outer, (7, 1),
        (
            [
                jax.ShapeDtypeStruct(records.shape, f32),
                jax.ShapeDtypeStruct((tiles, parts, samples), bf16),
                table(2, bf16),
            ],
            1,
        ),
        [table(2, f32), pltpu.VMEM((count * 4, 8, samples), f32)],
        (idx, from_near, flat, from_far, own, w1, w2, w3, inner[1]), "forward_outer", 4,
    )
    both = jnp.broadcast_to(g[None], (2, tiles, parts, samples))
    g_far = lax.all_to_all(both, "rec", 0, 0, axis_index_groups=far, tiled=True)
    g_near = lax.ppermute(g, "rec", near)
    gown, part = call(
        backward_inner, (4, 4), ([table(1, bf16), pltpu.VMEM(total, f32)], 0), [table(1, f32)],
        (idx, g, wo, wm, own, *inner), "backward_inner", 2,
    )
    (sums,) = call(
        backward_outer, (8, 4), ([jax.ShapeDtypeStruct((48 + channels // 2, 2 * channels), f32)], 0),
        [table(2, bf16), table(2, f32), pltpu.VMEM(total, f32)],
        (idx, g_near, g_far, wo, wm, own, halo, gown, part, *outer), "backward_outer", 2,
    )

    if count & (count - 1):
        terms = [lax.psum(sums, "rec")]
    else:
        terms = [sums]
        at = 1
        while at < count:
            wide = 2 if at == 1 or 2 * at == count else 4
            value = terms[0]
            if len(terms) == 2:
                value = terms[0] + terms[1]
            if len(terms) == 4:
                value = (terms[0] + terms[1]) + (terms[2] + terms[3])
            terms = [value] + [
                lax.ppermute(value, "rec", [(s, s ^ (k * at)) for s in range(count)])
                for k in range(1, wide)
            ]
            at *= wide

    scale = 1.0 / math.sqrt(parts * blocks * count * traces * samples)
    g_in, g_bin, g_mid, g_bmid, g_out = pl.pallas_call(
        functools.partial(finish_kernel, scale, parts),
        out_shape=[
            jax.ShapeDtypeStruct(shape, f32)
            for shape in (
                (parts * 9, channels), (1, channels), (channels, channels), (1, channels),
                (parts * 9, channels),
            )
        ],
        in_specs=[VMEM] * len(terms),
        out_specs=[VMEM] * 5,
        scratch_shapes=[pltpu.VMEM(sums.shape, f32)],
        compiler_params=params,
        name="finish",
    )(*terms)
    return (
        res,
        g_in.T,
        g_bin.reshape(channels),
        g_mid,
        g_bmid.reshape(channels),
        g_out.T,
    )


def solution(mesh):
    return jax.shard_map(
        local,
        mesh=mesh,
        in_specs=(
            P(None, ("groups", "rec"), None, None),
            P("groups", None),
            P(),
            P(),
            P(),
            P(),
            P(),
        ),
        out_specs=(
            P(None, ("groups", "rec"), None, None),
            P("groups", None),
            P("groups"),
            P("groups", None),
            P("groups"),
            P("groups", None),
        ),
        check_vma=False,
    )
```

```python
import functools
import math

import jax
import jax.numpy as jnp
from jax import lax
from jax.experimental import pallas as pl
from jax.experimental.pallas import tpu as pltpu
from jax.sharding import PartitionSpec as P

CAP = 2
VMEM = pl.BlockSpec(memory_space=pltpu.VMEM)
SMEM = pl.BlockSpec(memory_space=pltpu.SMEM)
RESIDENT = 24 << 20


def run(start, step, end, steps, blocked):
    if blocked:
        n = pl.program_id(0)
        pl.when(n == 0)(start)
        step(n, 0)
        pl.when(n == steps - 1)(end)
        return
    start()
    lax.fori_loop(0, steps, lambda n, carry: step(n, n), None)
    end()


def group_of(owners):
    for size in (16, 8, 4, 2):
        if owners % size == 0:
            return size
    return 1


def fill_table(table, wide, pieces, tiles, flip, fill):
    for n, piece in enumerate(pieces):
        x = sum(ref[...].astype(jnp.float32) for ref in piece)
        samples = x.shape[2]
        lane = lax.broadcasted_iota(jnp.int32, x.shape, 2)
        before = jnp.where(lane == 0, 0.0, pltpu.roll(x, 1, 2))
        after = jnp.where(lane == samples - 1, 0.0, pltpu.roll(x, samples - 1, 2))
        at = pl.ds(n * tiles, tiles)
        wide[at, 0:4, :] = after if flip else before
        wide[at, 4:8, :] = x
        wide[at, 8:12, :] = before if flip else after
    last = len(pieces) * tiles
    wide[pl.ds(last, 2), 0:12, :] = jnp.zeros((2, 12, wide.shape[2]), jnp.float32)
    wide[:, 12:16, :] = jnp.full((last + 2, 4, wide.shape[2]), fill, jnp.float32)
    table[...] = wide[...].astype(jnp.bfloat16)


def act(y):
    t = jnp.tanh(y)
    q = 1.0 + t
    a = y * q
    return t, q, a


def lines_of(idx, own, halo, owners):
    lines = []
    for e in owners:
        line = []
        for r in range(4):
            held = own if r in (1, 2) else halo
            line += [None, None] if held is None else [held[idx[r, e]], held[idx[r, e] + 1]]
        lines.append(line)
    return lines


def stack(lines, traces, flip):
    return jnp.concatenate(
        [
            jnp.concatenate(
                [line[h + 1 + (2 - i if flip else i)] for line in lines for h in traces], axis=1
            )
            for i in range(3)
        ],
        axis=0,
    )


def layers(inputs, w1, w2):
    y1 = jnp.dot(w1[...], inputs, preferred_element_type=jnp.float32)
    t, q, a = act(y1)
    d1 = q + a * (1.0 - t)
    a1 = a.astype(jnp.bfloat16)
    ones = jnp.ones((16, a1.shape[1]), jnp.bfloat16)
    y2 = jnp.dot(w2[...], jnp.concatenate([a1, ones], axis=0), preferred_element_type=jnp.float32)
    t, q, a = act(y2)
    return a1, d1, a, q + a * (1.0 - t)


def forward_inner(
    group, blocked, idx, mine, w1, w2, own, a1_ref, a2_ref, d1_ref, d2_ref, wide
):
    owners = lax.axis_size("rec")

    def start():
        fill_table(own, wide, ([mine],), mine.shape[0], False, 1.0)

    def step(n, block):
        lines = lines_of(idx, own, None, [n * group + u for u in range(group)])
        a1, d1, a2, d2 = layers(stack(lines, (1, 2), False), w1, w2)
        a1_ref[block] = a1
        d1_ref[block] = d1
        a2_ref[block] = a2.astype(jnp.bfloat16)
        d2_ref[block] = d2

    run(start, step, lambda: None, owners // group, blocked)


def forward_outer(group, blocked, idx, near, mine, *refs, links):
    far, refs = refs[:links], refs[links:]
    own, w1, w2, w3, inner, res, g, halo, a1_ref, a2_ref, d1_ref, d2_ref, wide, est = refs
    tiles, parts, samples = mine.shape
    count = lax.axis_size("rec")
    me = lax.axis_index("rec")
    has_left = (me > 0).astype(jnp.float32)
    has_right = (me < count - 1).astype(jnp.float32)
    lane = lax.broadcasted_iota(jnp.int32, (8, samples), 1)
    low = (lane > 0).astype(jnp.float32)
    high = (lane < samples - 1).astype(jnp.float32)

    def start():
        fill_table(halo, wide, ([near], far), tiles, False, 1.0)

    def step(n, block):
        lines = lines_of(idx, own, halo, [n * group + u for u in range(group)])
        a1, d1, a2, d2 = layers(stack(lines, (-1, 0, 3, 4), False), w1, w2)
        cut = lambda x, u, k: x[:, (u * 4 + k) * samples : (u * 4 + k + 1) * samples]
        middle = lambda x: jnp.concatenate(
            [cut(x, u, k) for u in range(group) for k in (1, 2)], axis=1
        )
        a1_ref[block] = middle(a1)
        d1_ref[block] = middle(d1)
        d2_ref[block] = middle(d2)
        rows = []
        for u in range(group):
            row = [cut(a2, u, 0) * has_left, cut(a2, u, 1), cut(a2, u, 2), cut(a2, u, 3) * has_right]
            row = [part.astype(jnp.bfloat16) for part in row]
            within = [
                inner[block, :, (u * 2 + k) * samples : (u * 2 + k + 1) * samples] for k in range(2)
            ]
            rows.append(row[0:2] + within + row[2:4])
        a2_ref[block] = jnp.concatenate([row[k] for row in rows for k in (1, 4)], axis=1)
        rhs = jnp.concatenate(
            [
                jnp.concatenate([row[h + i] for row in rows for h in range(4)], axis=1)
                for i in range(3)
            ],
            axis=0,
        )
        terms = jnp.dot(w3[...], rhs, preferred_element_type=jnp.float32)
        for k in range(group * 4):
            part = terms[:, k * samples : (k + 1) * samples]
            total = (
                part[8:16]
                + pltpu.roll(part[0:8], 1, 1) * low
                + pltpu.roll(part[16:24], samples - 1, 1) * high
            )
            est[n * group * 4 + k] = total.astype(jnp.bfloat16).astype(jnp.float32)

    def end():
        for c in range(tiles // 2):
            at = [idx[4 + v, tiles // 2 + c] for v in range(4)]
            for k in range(2):
                total = (est[at[0] + k] + est[at[1] + k]) + (est[at[2] + k] + est[at[3] + k])
                value = total[0:parts] - mine[c * 2 + k].astype(jnp.float32)
                for o in range(parts):
                    res[o, c, k : k + 1, :] = value[o : o + 1]
                g[c * 2 + k] = value.astype(jnp.bfloat16)

    run(start, step, end, count // group, blocked)


def weight_terms(acc, fields, inputs, wo, wm, a1, a2, d1, d2):
    channels = wm.shape[0]
    da2 = jnp.dot(wo[...], fields, preferred_element_type=jnp.float32)
    dz2 = (da2 * d2).astype(jnp.bfloat16)
    acc[0:48, :] += product(fields, a2, (1, 1))
    da1 = jnp.dot(wm[...], dz2, preferred_element_type=jnp.float32)
    ones = jnp.ones((16, dz2.shape[1]), jnp.bfloat16)
    acc[48 : 64 + channels, :] += product(jnp.concatenate([a1, ones], axis=0), dz2, (1, 1))
    dz1 = (da1 * d1).astype(jnp.bfloat16)
    acc[64 + channels : 112 + channels, :] += product(inputs, dz1, (1, 1))


def backward_inner(
    group, blocked, idx, mine, wo, wm, own, a1_ref, a2_ref, d1_ref, d2_ref, gown, acc, wide
):
    owners = lax.axis_size("rec")

    def start():
        fill_table(gown, wide, ([mine],), mine.shape[0], True, 0.0)
        acc[...] = jnp.zeros_like(acc)

    def step(n, block):
        es = [n * group + u for u in range(group)]
        fields = stack(lines_of(idx, gown, None, es), (1, 2), True)
        inputs = stack(lines_of(idx, own, None, es), (1, 2), False)
        saved = a1_ref[block], a2_ref[block], d1_ref[block], d2_ref[block]
        weight_terms(acc, fields, inputs, wo, wm, *saved)

    run(start, step, lambda: None, owners // group, blocked)


def backward_outer(group, blocked, idx, near, *refs, links):
    far, refs = refs[:links], refs[links:]
    wo, wm, own, halo, gown, sums, a1_ref, a2_ref, d1_ref, d2_ref, out, ghalo, wide, acc = refs
    owners = lax.axis_size("rec")
    channels = wm.shape[0]

    def start():
        fill_table(ghalo, wide, ([near], far), near.shape[0], True, 0.0)
        acc[...] = sums[...]

    def step(n, block):
        es = [n * group + u for u in range(group)]
        fields = stack(lines_of(idx, gown, ghalo, es), (0, 3), True)
        inputs = stack(lines_of(idx, own, halo, es), (0, 3), False)
        saved = a1_ref[block], a2_ref[block], d1_ref[block], d2_ref[block]
        weight_terms(acc, fields, inputs, wo, wm, *saved)

    def end():
        first, half = 64 + channels, channels // 2
        low, high = slice(0, channels), slice(channels, 2 * channels)
        out[0:48, low] = acc[first : first + 48, :]
        out[0:48, high] = acc[0:48, :]
        out[12:13, low] = acc[48 + channels : 49 + channels, :]
        middle = acc[48 : 48 + channels, :].T
        out[48 : 48 + half, low] = middle[0:half]
        out[48 : 48 + half, high] = middle[half:channels]

    run(start, step, end, owners // group, blocked)


def finish_kernel(scale, parts, *refs):
    terms, (g_in, g_bin, g_mid, g_bmid, g_out, held) = refs[:-6], refs[-6:]
    values = [ref[...] for ref in terms]
    while len(values) > 1:
        values = [values[k] + values[k + 1] for k in range(0, len(values), 2)]
    held[...] = values[0] * scale
    channels = g_mid.shape[0]
    for o in range(parts):
        for i in range(3):
            for j in range(3):
                row = held[i * 16 + j * 4 + o : i * 16 + j * 4 + o + 1, :]
                at = o * 9 + 3 * i + j
                g_in[at : at + 1, :] = row[:, 0:channels]
                g_out[at : at + 1, :] = row[:, channels : 2 * channels]
    g_bin[...] = held[28:29, 0:channels]
    g_bmid[...] = held[12:13, 0:channels]
    half = channels // 2
    g_mid[0:half] = held[48 : 48 + half, 0:channels]
    g_mid[half:channels] = held[48 : 48 + half, channels : 2 * channels]


def halves(b):
    high = b.astype(jnp.bfloat16).astype(jnp.float32)
    rest = b - high
    mid = rest.astype(jnp.bfloat16).astype(jnp.float32)
    return [high, mid, rest - mid]


def one_hot(a, b):
    return (a == b).astype(jnp.float32).astype(jnp.bfloat16)


def iota(shape, dim):
    return lax.broadcasted_iota(jnp.int32, shape, dim)


def product(a, b, over):
    return lax.dot_general(
        a, b, dimension_numbers=(((over[0],), (over[1],)), ((), ())),
        preferred_element_type=jnp.float32,
    )


def prep_kernel(blocks, *refs):
    args, (idx, w1, w2, w3, wo, wm, rows), held, sems = refs[:6], refs[6:13], refs[13:19], refs[19]
    copies = [
        pltpu.make_async_copy(src, dst, sems.at[n]) for n, (src, dst) in enumerate(zip(args, held))
    ]
    for copy in copies:
        copy.start()
    for copy in copies:
        copy.wait()
    dest, w_in, b_in, w_mid, b_mid, w_out = held
    count = lax.axis_size("rec")
    me = lax.axis_index("rec")
    ves, total = dest.shape
    channels = w_mid.shape[0]
    at = lax.rem((count + 1 - me) * blocks, total)
    wide = jnp.concatenate([dest[...], jnp.zeros((8 - ves, total), jnp.int32)], axis=0)
    near = pltpu.roll(wide, at, 1)[:, 0:128]
    lane = iota((8, 128), 1)
    low = jnp.where(me > 0, 0, blocks)
    high = jnp.where(me < count - 1, 3 * blocks, 2 * blocks)
    near = jnp.where((lane >= low) & (lane < high), near, -1)
    owner = iota((count, 128), 0)
    hits = [(near[v : v + 1] == owner).astype(jnp.float32) for v in range(ves)]
    before = iota((128, 128), 0)
    after = iota((128, 128), 1)
    segment = (after >= blocks).astype(jnp.int32) + (after >= 2 * blocks).astype(jnp.int32)
    tri = ((before < after) & (before >= segment * blocks)).astype(jnp.float32).astype(jnp.bfloat16)
    rank = product((hits[0] + hits[1] + hits[2] + hits[3]).astype(jnp.bfloat16), tri, (1, 0))
    zeroth = jnp.zeros((count, 128), jnp.float32)
    first = jnp.zeros((count, 128), jnp.float32)
    for v in range(ves):
        zeroth += hits[v] * (rank == 0.0).astype(jnp.float32)
        first += hits[v] * (rank == 1.0).astype(jnp.float32)
        item = jnp.sum(hits[v] * rank, axis=0, keepdims=True)
        idx[4 + v : 5 + v, 0:128] = near[v : v + 1] * 4 + item.astype(jnp.int32) * 2
        rank = rank + hits[v]
    line = iota((8, 128), 0)
    inside = lambda k: (lane >= k * blocks) & (lane < (k + 1) * blocks)
    odd = lax.rem(me, 2)
    left = 2 * lane + 2 * blocks * (1 - odd) - 4 * blocks
    middle = 2 * (lane - blocks) - 2 * blocks
    right = 2 * (lane - 2 * blocks) + 2 * blocks * odd - 4 * blocks
    put = lambda r, k, place: jnp.where((line == r) & inside(k), place, 0)
    pick = product(
        (put(0, 0, left) + put(2, 1, middle)).astype(jnp.float32).astype(jnp.bfloat16),
        first.astype(jnp.bfloat16),
        (1, 1),
    ) + product(
        (put(1, 1, middle) + put(3, 2, right)).astype(jnp.float32).astype(jnp.bfloat16),
        zeroth.astype(jnp.bfloat16),
        (1, 1),
    )
    empty = jnp.where((line == 0) | (line == 3), 4 * blocks, 2 * blocks)[0:4, 0:1]
    idx[0:4, 0:count] = pick[0:4].astype(jnp.int32) + empty

    taps = w_in.shape[0]
    row, col = iota((48, 40), 0), iota((48, 40), 1)
    tap, extra = row & 15, (row & 15) - 12
    target = (row & 3) * 9 + 3 * (row >> 4) + ((row >> 2) & 3)
    target = jnp.where(tap < 12, target, jnp.where((row >> 4) == 1, taps + extra, -1))
    order = one_hot(col, target)
    rows[...] = jnp.zeros_like(rows)
    rows[0:taps, :] = w_in[...].astype(jnp.float32)
    for n, part in enumerate(halves(b_in[...])):
        rows[taps + n : taps + n + 1, :] = part
    w1[...] = (0.5 * product(rows[...].astype(jnp.bfloat16), order, (0, 1))).astype(jnp.bfloat16)
    rows[...] = jnp.zeros_like(rows)
    for n, part in enumerate(halves(b_mid[...])):
        rows[n : n + 1, :] = part
    row, col = iota((40, channels + 16), 0), iota((40, channels + 16), 1)
    bias = product(rows[...].astype(jnp.bfloat16), one_hot(col, row + channels), (0, 0))
    row, col = iota((channels, channels + 16), 0), iota((channels, channels + 16), 1)
    w2[...] = (0.5 * (product(w_mid[...], one_hot(row, col), (1, 0)) + bias)).astype(jnp.bfloat16)
    rows[...] = jnp.zeros_like(rows)
    rows[0:taps, :] = w_out[...].astype(jnp.float32)
    outs = rows[...].astype(jnp.bfloat16)
    wo[...] = (0.5 * product(outs, order, (0, 1))).astype(jnp.bfloat16)
    row, col = iota((24, 40), 0), iota((24, 40), 1)
    for i in range(3):
        target = jnp.where((row & 7) < 4, (row & 3) * 9 + 3 * i + (row >> 3), -1)
        part = product(one_hot(col, target), outs, (1, 0))
        w3[:, i * channels : (i + 1) * channels] = part.astype(jnp.bfloat16)
    eye = one_hot(iota((channels, channels), 0), iota((channels, channels), 1))
    wm[...] = (0.5 * product(w_mid[...], eye, (0, 0))).astype(jnp.bfloat16)


def local(records, dest, w_in, b_in, w_mid, b_mid, w_out):
    count = lax.axis_size("rec")
    me = lax.axis_index("rec")
    parts, blocks, traces, samples = records.shape
    ves = dest.shape[1]
    tiles = blocks * traces
    channels = w_in.shape[0]
    group = group_of(count)
    steps = count // group
    width = group * 2 * samples
    far = {}
    for s in range(1, count - 1, 2):
        far.setdefault(s ^ (s + 1), []).extend([(s, s + 1), (s + 1, s)])
    near = [(s, s + 1) for s in range(0, count - 1, 2)]
    near += [(b, a) for a, b in near]

    flat = records.transpose(1, 2, 0, 3).reshape(tiles, parts, samples)
    from_far = [lax.ppermute(flat, "rec", far[k]) for k in sorted(far, reverse=True)]
    from_near = lax.ppermute(flat, "rec", near)

    f32, bf16 = jnp.float32, jnp.bfloat16
    shape = (steps, channels, width)
    blocked = 24 * math.prod(shape) > RESIDENT
    saved = [
        jax.ShapeDtypeStruct(shape, kind) if blocked else pltpu.VMEM(shape, kind)
        for kind in (bf16, bf16, f32, f32)
    ]
    held = [VMEM] * 4
    if blocked:
        held = [pl.BlockSpec((1, channels, width), lambda n: (n, 0, 0))] * 4
    grid = (steps,) if blocked else ()
    params = pltpu.CompilerParams(vmem_limit_bytes=16 << 20)
    args = (
        dest.T, w_in.T, b_in.reshape(1, channels), w_mid, b_mid.reshape(1, channels), w_out.T
    )
    idx, w1, w2, w3, wo, wm = pl.pallas_call(
        functools.partial(prep_kernel, blocks),
        out_shape=[jax.ShapeDtypeStruct((8, max(128, count)), jnp.int32)]
        + [
            jax.ShapeDtypeStruct(size, bf16)
            for size in (
                (channels, 48), (channels, channels + 16), (24, 3 * channels), (channels, 48),
                (channels, channels),
            )
        ],
        in_specs=[pl.BlockSpec(memory_space=pltpu.HBM)] * 6,
        out_specs=[VMEM] * 6,
        scratch_shapes=[pltpu.VMEM((40, channels), f32)]
        + [pltpu.VMEM(arg.shape, arg.dtype) for arg in args]
        + [pltpu.SemaphoreType.DMA((6,))],
        compiler_params=params,
        name="prepare",
    )(*[pltpu.with_memory_space_constraint(arg, pltpu.HBM) for arg in args])
    def table(pieces, kind):
        return pltpu.VMEM((pieces * tiles + 2, 16, samples), kind)

    def call(kernel, ins, outs, scratch, args, name, owned):
        return pl.pallas_call(
            functools.partial(kernel, group, blocked),
            grid=grid,
            out_shape=outs[0] + saved * outs[1],
            in_specs=[SMEM] + [VMEM] * ins[0] + held[:1] * ins[1],
            out_specs=[VMEM] * len(outs[0]) + held * outs[1],
            scratch_shapes=scratch,
            compiler_params=params,
            cost_estimate=pl.CostEstimate(
                flops=2 * owned * count * samples * channels * (3 * channels),
                bytes_accessed=owned * count * samples * channels * 12,
                transcendentals=0,
            ),
            name=name,
        )(*args)

    total = (112 + channels, channels)
    own, *inner = call(
        forward_inner, (3, 0), ([table(1, bf16)], 1), [table(1, f32)],
        (idx, flat, w1, w2), "forward_inner", 2,
    )
    res, g, halo, *outer = call(
        functools.partial(forward_outer, links=len(far)), (6 + len(far), 1),
        (
            [
                jax.ShapeDtypeStruct(records.shape, f32),
                jax.ShapeDtypeStruct((tiles, parts, samples), bf16),
                table(2, bf16),
            ],
            1,
        ),
        [table(2, f32), pltpu.VMEM((count * 4, 8, samples), f32)],
        (idx, from_near, flat, *from_far, own, w1, w2, w3, inner[1]), "forward_outer", 4,
    )
    g_far = [lax.ppermute(g, "rec", far[k]) for k in sorted(far, reverse=True)]
    g_near = lax.ppermute(g, "rec", near)
    gown, part = call(
        backward_inner, (4, 4), ([table(1, bf16), pltpu.VMEM(total, f32)], 0), [table(1, f32)],
        (idx, g, wo, wm, own, *inner), "backward_inner", 2,
    )
    (sums,) = call(
        functools.partial(backward_outer, links=len(far)), (7 + len(far), 4), ([jax.ShapeDtypeStruct((48 + channels // 2, 2 * channels), f32)], 0),
        [table(2, bf16), table(2, f32), pltpu.VMEM(total, f32)],
        (idx, g_near, *g_far, wo, wm, own, halo, gown, part, *outer), "backward_outer", 2,
    )

    if count & (count - 1):
        terms = [lax.psum(sums, "rec")]
    else:
        terms = [sums]
        at = 1
        while at < count:
            wide = 2 if at == 1 or 2 * at == count else 4
            value = terms[0]
            if len(terms) == 2:
                value = terms[0] + terms[1]
            if len(terms) == 4:
                value = (terms[0] + terms[1]) + (terms[2] + terms[3])
            terms = [value] + [
                lax.ppermute(value, "rec", [(s, s ^ (k * at)) for s in range(count)])
                for k in range(1, wide)
            ]
            at *= wide

    scale = 1.0 / math.sqrt(parts * blocks * count * traces * samples)
    g_in, g_bin, g_mid, g_bmid, g_out = pl.pallas_call(
        functools.partial(finish_kernel, scale, parts),
        out_shape=[
            jax.ShapeDtypeStruct(shape, f32)
            for shape in (
                (parts * 9, channels), (1, channels), (channels, channels), (1, channels),
                (parts * 9, channels),
            )
        ],
        in_specs=[VMEM] * len(terms),
        out_specs=[VMEM] * 5,
        scratch_shapes=[pltpu.VMEM(sums.shape, f32)],
        compiler_params=params,
        name="finish",
    )(*terms)
    return (
        res,
        g_in.T,
        g_bin.reshape(channels),
        g_mid,
        g_bmid.reshape(channels),
        g_out.T,
    )


def solution(mesh):
    return jax.shard_map(
        local,
        mesh=mesh,
        in_specs=(
            P(None, ("groups", "rec"), None, None),
            P("groups", None),
            P(),
            P(),
            P(),
            P(),
            P(),
        ),
        out_specs=(
            P(None, ("groups", "rec"), None, None),
            P("groups", None),
            P("groups"),
            P("groups", None),
            P("groups"),
            P("groups", None),
        ),
        check_vma=False,
    )
```

```python
import functools
import math

import jax
import jax.numpy as jnp
from jax import lax
from jax.experimental import pallas as pl
from jax.experimental.pallas import tpu as pltpu
from jax.sharding import PartitionSpec as P

CAP = 2
VMEM = pl.BlockSpec(memory_space=pltpu.VMEM)
SMEM = pl.BlockSpec(memory_space=pltpu.SMEM)
RESIDENT = 24 << 20


def run(start, step, end, steps, blocked):
    if blocked:
        n = pl.program_id(0)
        pl.when(n == 0)(start)
        step(n, 0)
        pl.when(n == steps - 1)(end)
        return
    start()
    lax.fori_loop(0, steps, lambda n, carry: step(n, n), None)
    end()


def group_of(owners):
    for size in (32, 16, 8, 4, 2):
        if owners % size == 0:
            return size
    return 1


def fill_table(table, wide, pieces, tiles, flip, fill):
    for n, piece in enumerate(pieces):
        x = piece[...].astype(jnp.float32)
        samples = x.shape[2]
        lane = lax.broadcasted_iota(jnp.int32, x.shape, 2)
        before = jnp.where(lane == 0, 0.0, pltpu.roll(x, 1, 2))
        after = jnp.where(lane == samples - 1, 0.0, pltpu.roll(x, samples - 1, 2))
        at = pl.ds(n * tiles, tiles)
        wide[at, 0:4, :] = after if flip else before
        wide[at, 4:8, :] = x
        wide[at, 8:12, :] = before if flip else after
    last = len(pieces) * tiles
    wide[pl.ds(last, 2), 0:12, :] = jnp.zeros((2, 12, wide.shape[2]), jnp.float32)
    wide[:, 12:16, :] = jnp.full((last + 2, 4, wide.shape[2]), fill, jnp.float32)
    table[...] = wide[...].astype(jnp.bfloat16)


def act(y):
    t = jnp.tanh(y)
    q = 1.0 + t
    a = y * q
    return t, q, a


def lines_of(idx, own, halo, owners):
    lines = []
    for e in owners:
        line = []
        for r in range(4):
            held = own if r in (1, 2) else halo
            line += [None, None] if held is None else [held[idx[r, e]], held[idx[r, e] + 1]]
        lines.append(line)
    return lines


def stack(lines, traces, flip):
    return jnp.concatenate(
        [
            jnp.concatenate(
                [line[h + 1 + (2 - i if flip else i)] for line in lines for h in traces], axis=1
            )
            for i in range(3)
        ],
        axis=0,
    )


def layers(inputs, w1, w2):
    y1 = jnp.dot(w1[...], inputs, preferred_element_type=jnp.float32)
    t, q, a = act(y1)
    d1 = q + a * (1.0 - t)
    a1 = a.astype(jnp.bfloat16)
    ones = jnp.ones((16, a1.shape[1]), jnp.bfloat16)
    y2 = jnp.dot(w2[...], jnp.concatenate([a1, ones], axis=0), preferred_element_type=jnp.float32)
    t, q, a = act(y2)
    return a1, d1, a, q + a * (1.0 - t)


def forward_inner(
    group, blocked, idx, mine, w1, w2, own, a1_ref, a2_ref, d1_ref, d2_ref, wide
):
    owners = lax.axis_size("rec")

    def start():
        fill_table(own, wide, (mine,), mine.shape[0], False, 1.0)

    def step(n, block):
        lines = lines_of(idx, own, None, [n * group + u for u in range(group)])
        a1, d1, a2, d2 = layers(stack(lines, (1, 2), False), w1, w2)
        a1_ref[block] = a1
        d1_ref[block] = d1
        a2_ref[block] = a2.astype(jnp.bfloat16)
        d2_ref[block] = d2

    run(start, step, lambda: None, owners // group, blocked)


def forward_outer(
    group, blocked, idx, near, mine, far, own, w1, w2, w3, inner,
    res, g, halo, a1_ref, a2_ref, d1_ref, d2_ref, wide, est,
):
    tiles, parts, samples = mine.shape
    count = lax.axis_size("rec")
    me = lax.axis_index("rec")
    has_left = (me > 0).astype(jnp.float32)
    has_right = (me < count - 1).astype(jnp.float32)
    lane = lax.broadcasted_iota(jnp.int32, (8, samples), 1)
    low = (lane > 0).astype(jnp.float32)
    high = (lane < samples - 1).astype(jnp.float32)

    def start():
        fill_table(halo, wide, (near, far), tiles, False, 1.0)

    def step(n, block):
        lines = lines_of(idx, own, halo, [n * group + u for u in range(group)])
        a1, d1, a2, d2 = layers(stack(lines, (-1, 0, 3, 4), False), w1, w2)
        cut = lambda x, u, k: x[:, (u * 4 + k) * samples : (u * 4 + k + 1) * samples]
        middle = lambda x: jnp.concatenate(
            [cut(x, u, k) for u in range(group) for k in (1, 2)], axis=1
        )
        a1_ref[block] = middle(a1)
        d1_ref[block] = middle(d1)
        d2_ref[block] = middle(d2)
        rows = []
        for u in range(group):
            row = [cut(a2, u, 0) * has_left, cut(a2, u, 1), cut(a2, u, 2), cut(a2, u, 3) * has_right]
            row = [part.astype(jnp.bfloat16) for part in row]
            within = [
                inner[block, :, (u * 2 + k) * samples : (u * 2 + k + 1) * samples] for k in range(2)
            ]
            rows.append(row[0:2] + within + row[2:4])
        a2_ref[block] = jnp.concatenate([row[k] for row in rows for k in (1, 4)], axis=1)
        rhs = jnp.concatenate(
            [
                jnp.concatenate([row[h + i] for row in rows for h in range(4)], axis=1)
                for i in range(3)
            ],
            axis=0,
        )
        terms = jnp.dot(w3[...], rhs, preferred_element_type=jnp.float32)
        for k in range(group * 4):
            part = terms[:, k * samples : (k + 1) * samples]
            total = (
                part[8:16]
                + pltpu.roll(part[0:8], 1, 1) * low
                + pltpu.roll(part[16:24], samples - 1, 1) * high
            )
            est[n * group * 4 + k] = total.astype(jnp.bfloat16).astype(jnp.float32)

    def end():
        for c in range(tiles // 2):
            at = [idx[4 + v, tiles // 2 + c] for v in range(4)]
            for k in range(2):
                total = (est[at[0] + k] + est[at[1] + k]) + (est[at[2] + k] + est[at[3] + k])
                value = total[0:parts] - mine[c * 2 + k].astype(jnp.float32)
                for o in range(parts):
                    res[o, c, k : k + 1, :] = value[o : o + 1]
                g[c * 2 + k] = value.astype(jnp.bfloat16)

    run(start, step, end, count // group, blocked)


def weight_terms(acc, fields, inputs, wo, wm, a1, a2, d1, d2):
    channels = wm.shape[0]
    da2 = jnp.dot(wo[...], fields, preferred_element_type=jnp.float32)
    dz2 = (da2 * d2).astype(jnp.bfloat16)
    acc[0:48, :] += product(fields, a2, (1, 1))
    da1 = jnp.dot(wm[...], dz2, preferred_element_type=jnp.float32)
    ones = jnp.ones((16, dz2.shape[1]), jnp.bfloat16)
    acc[48 : 64 + channels, :] += product(jnp.concatenate([a1, ones], axis=0), dz2, (1, 1))
    dz1 = (da1 * d1).astype(jnp.bfloat16)
    acc[64 + channels : 112 + channels, :] += product(inputs, dz1, (1, 1))


def backward_inner(
    group, blocked, idx, mine, wo, wm, own, a1_ref, a2_ref, d1_ref, d2_ref, gown, acc, wide
):
    owners = lax.axis_size("rec")

    def start():
        fill_table(gown, wide, (mine,), mine.shape[0], True, 0.0)
        acc[...] = jnp.zeros_like(acc)

    def step(n, block):
        es = [n * group + u for u in range(group)]
        fields = stack(lines_of(idx, gown, None, es), (1, 2), True)
        inputs = stack(lines_of(idx, own, None, es), (1, 2), False)
        saved = a1_ref[block], a2_ref[block], d1_ref[block], d2_ref[block]
        weight_terms(acc, fields, inputs, wo, wm, *saved)

    run(start, step, lambda: None, owners // group, blocked)


def backward_outer(
    group, blocked, idx, near, far, wo, wm, own, halo, gown, sums, a1_ref, a2_ref, d1_ref, d2_ref,
    out, ghalo, wide, acc,
):
    owners = lax.axis_size("rec")
    channels = wm.shape[0]
    taps = 9 * near.shape[1]

    def start():
        fill_table(ghalo, wide, (near, far), near.shape[0], True, 0.0)
        acc[...] = sums[...]

    def step(n, block):
        es = [n * group + u for u in range(group)]
        fields = stack(lines_of(idx, gown, ghalo, es), (0, 3), True)
        inputs = stack(lines_of(idx, own, halo, es), (0, 3), False)
        saved = a1_ref[block], a2_ref[block], d1_ref[block], d2_ref[block]
        weight_terms(acc, fields, inputs, wo, wm, *saved)

    def end():
        first, half = 64 + channels, channels // 2
        low, high = slice(0, channels), slice(channels, 2 * channels)
        for k in range(taps):
            at = k % 9 // 3 * 16 + k % 3 * 4 + k // 9
            out[half + k : half + k + 1, low] = acc[first + at : first + at + 1, :]
            out[half + k : half + k + 1, high] = acc[at : at + 1, :]
        middle = acc[48 : 48 + channels, :].T
        out[0:half, low] = middle[0:half]
        out[0:half, high] = middle[half:channels]
        out[half + taps : half + taps + 1, low] = acc[first + 28 : first + 29, :]
        out[half + taps : half + taps + 1, high] = acc[48 + channels : 49 + channels, :]
        rest = out.shape[0] - half - taps - 1
        out[half + taps + 1 :, :] = jnp.zeros((rest, 2 * channels), jnp.float32)

    run(start, step, end, owners // group, blocked)


def finish_kernel(scale, *refs):
    terms, (g_in, g_bin, g_mid, g_bmid, g_out, held) = refs[:-6], refs[-6:]
    values = [ref[...] for ref in terms]
    while len(values) > 1:
        values = [values[k] + values[k + 1] for k in range(0, len(values), 2)]
    held[...] = values[0] * scale
    channels = g_mid.shape[0]
    half, taps = channels // 2, g_in.shape[0]
    low, high = slice(0, channels), slice(channels, 2 * channels)
    g_mid[0:half] = held[0:half, low]
    g_mid[half:channels] = held[0:half, high]
    g_in[...] = held[half : half + taps, low]
    g_out[...] = held[half : half + taps, high]
    g_bin[...] = held[half + taps : half + taps + 1, low]
    g_bmid[...] = held[half + taps : half + taps + 1, high]


def halves(b):
    high = b.astype(jnp.bfloat16).astype(jnp.float32)
    rest = b - high
    mid = rest.astype(jnp.bfloat16).astype(jnp.float32)
    return [high, mid, rest - mid]


def one_hot(a, b):
    return (a == b).astype(jnp.float32).astype(jnp.bfloat16)


def iota(shape, dim):
    return lax.broadcasted_iota(jnp.int32, shape, dim)


def product(a, b, over):
    return lax.dot_general(
        a, b, dimension_numbers=(((over[0],), (over[1],)), ((), ())),
        preferred_element_type=jnp.float32,
    )


def prep_kernel(blocks, *refs):
    args, (idx, w1, w2, w3, wo, wm, rows), held, sems = refs[:6], refs[6:13], refs[13:19], refs[19]
    copies = [
        pltpu.make_async_copy(src, dst, sems.at[n]) for n, (src, dst) in enumerate(zip(args, held))
    ]
    for copy in copies:
        copy.start()
    for copy in copies:
        copy.wait()
    dest, w_in, b_in, w_mid, b_mid, w_out = held
    count = lax.axis_size("rec")
    me = lax.axis_index("rec")
    ves, total = dest.shape
    channels = w_mid.shape[0]
    at = lax.rem((count + 1 - me) * blocks, total)
    wide = jnp.concatenate([dest[...], jnp.zeros((8 - ves, total), jnp.int32)], axis=0)
    near = pltpu.roll(wide, at, 1)[:, 0:128]
    lane = iota((8, 128), 1)
    low = jnp.where(me > 0, 0, blocks)
    high = jnp.where(me < count - 1, 3 * blocks, 2 * blocks)
    near = jnp.where((lane >= low) & (lane < high), near, -1)
    owner = iota((count, 128), 0)
    hits = [(near[v : v + 1] == owner).astype(jnp.float32) for v in range(ves)]
    before = iota((128, 128), 0)
    after = iota((128, 128), 1)
    segment = (after >= blocks).astype(jnp.int32) + (after >= 2 * blocks).astype(jnp.int32)
    tri = ((before < after) & (before >= segment * blocks)).astype(jnp.float32).astype(jnp.bfloat16)
    rank = product((hits[0] + hits[1] + hits[2] + hits[3]).astype(jnp.bfloat16), tri, (1, 0))
    zeroth = jnp.zeros((count, 128), jnp.float32)
    first = jnp.zeros((count, 128), jnp.float32)
    for v in range(ves):
        zeroth += hits[v] * (rank == 0.0).astype(jnp.float32)
        first += hits[v] * (rank == 1.0).astype(jnp.float32)
        item = jnp.sum(hits[v] * rank, axis=0, keepdims=True)
        idx[4 + v : 5 + v, 0:128] = near[v : v + 1] * 4 + item.astype(jnp.int32) * 2
        rank = rank + hits[v]
    line = iota((8, 128), 0)
    inside = lambda k: (lane >= k * blocks) & (lane < (k + 1) * blocks)
    odd = lax.rem(me, 2)
    left = 2 * lane + 2 * blocks * (1 - odd) - 4 * blocks
    middle = 2 * (lane - blocks) - 2 * blocks
    right = 2 * (lane - 2 * blocks) + 2 * blocks * odd - 4 * blocks
    put = lambda r, k, place: jnp.where((line == r) & inside(k), place, 0)
    pick = product(
        (put(0, 0, left) + put(2, 1, middle)).astype(jnp.float32).astype(jnp.bfloat16),
        first.astype(jnp.bfloat16),
        (1, 1),
    ) + product(
        (put(1, 1, middle) + put(3, 2, right)).astype(jnp.float32).astype(jnp.bfloat16),
        zeroth.astype(jnp.bfloat16),
        (1, 1),
    )
    empty = jnp.where((line == 0) | (line == 3), 4 * blocks, 2 * blocks)[0:4, 0:1]
    idx[0:4, 0:count] = pick[0:4].astype(jnp.int32) + empty

    taps = w_in.shape[0]
    row, col = iota((48, 40), 0), iota((48, 40), 1)
    tap, extra = row & 15, (row & 15) - 12
    target = (row & 3) * 9 + 3 * (row >> 4) + ((row >> 2) & 3)
    target = jnp.where(tap < 12, target, jnp.where((row >> 4) == 1, taps + extra, -1))
    order = one_hot(col, target)
    rows[...] = jnp.zeros_like(rows)
    rows[0:taps, :] = w_in[...].astype(jnp.float32)
    for n, part in enumerate(halves(b_in[...])):
        rows[taps + n : taps + n + 1, :] = part
    w1[...] = (0.5 * product(rows[...].astype(jnp.bfloat16), order, (0, 1))).astype(jnp.bfloat16)
    rows[...] = jnp.zeros_like(rows)
    for n, part in enumerate(halves(b_mid[...])):
        rows[n : n + 1, :] = part
    row, col = iota((40, channels + 16), 0), iota((40, channels + 16), 1)
    bias = product(rows[...].astype(jnp.bfloat16), one_hot(col, row + channels), (0, 0))
    row, col = iota((channels, channels + 16), 0), iota((channels, channels + 16), 1)
    w2[...] = (0.5 * (product(w_mid[...], one_hot(row, col), (1, 0)) + bias)).astype(jnp.bfloat16)
    rows[...] = jnp.zeros_like(rows)
    rows[0:taps, :] = w_out[...].astype(jnp.float32)
    outs = rows[...].astype(jnp.bfloat16)
    wo[...] = (0.5 * product(outs, order, (0, 1))).astype(jnp.bfloat16)
    row, col = iota((24, 40), 0), iota((24, 40), 1)
    for i in range(3):
        target = jnp.where((row & 7) < 4, (row & 3) * 9 + 3 * i + (row >> 3), -1)
        part = product(one_hot(col, target), outs, (1, 0))
        w3[:, i * channels : (i + 1) * channels] = part.astype(jnp.bfloat16)
    eye = one_hot(iota((channels, channels), 0), iota((channels, channels), 1))
    wm[...] = (0.5 * product(w_mid[...], eye, (0, 0))).astype(jnp.bfloat16)


def local(records, dest, w_in, b_in, w_mid, b_mid, w_out):
    count = lax.axis_size("rec")
    me = lax.axis_index("rec")
    parts, blocks, traces, samples = records.shape
    ves = dest.shape[1]
    tiles = blocks * traces
    channels = w_in.shape[0]
    group = group_of(count)
    steps = count // group
    width = group * 2 * samples
    far = [(s, s + 1) for s in range(1, count - 1, 2)]
    far += [(b, a) for a, b in far]
    near = [(s, s + 1) for s in range(0, count - 1, 2)]
    near += [(b, a) for a, b in near]

    flat = records.transpose(1, 2, 0, 3).reshape(tiles, parts, samples)
    from_far = lax.ppermute(flat, "rec", far)
    from_near = lax.ppermute(flat, "rec", near)

    f32, bf16 = jnp.float32, jnp.bfloat16
    shape = (steps, channels, width)
    blocked = 24 * math.prod(shape) > RESIDENT
    saved = [
        jax.ShapeDtypeStruct(shape, kind) if blocked else pltpu.VMEM(shape, kind)
        for kind in (bf16, bf16, f32, f32)
    ]
    held = [VMEM] * 4
    if blocked:
        held = [pl.BlockSpec((1, channels, width), lambda n: (n, 0, 0))] * 4
    grid = (steps,) if blocked else ()
    params = pltpu.CompilerParams(vmem_limit_bytes=16 << 20)
    args = (
        dest.T, w_in.T, b_in.reshape(1, channels), w_mid, b_mid.reshape(1, channels), w_out.T
    )
    idx, w1, w2, w3, wo, wm = pl.pallas_call(
        functools.partial(prep_kernel, blocks),
        out_shape=[jax.ShapeDtypeStruct((8, max(128, count)), jnp.int32)]
        + [
            jax.ShapeDtypeStruct(size, bf16)
            for size in (
                (channels, 48), (channels, channels + 16), (24, 3 * channels), (channels, 48),
                (channels, channels),
            )
        ],
        in_specs=[pl.BlockSpec(memory_space=pltpu.HBM)] * 6,
        out_specs=[VMEM] * 6,
        scratch_shapes=[pltpu.VMEM((40, channels), f32)]
        + [pltpu.VMEM(arg.shape, arg.dtype) for arg in args]
        + [pltpu.SemaphoreType.DMA((6,))],
        compiler_params=params,
        name="prepare",
    )(*[pltpu.with_memory_space_constraint(arg, pltpu.HBM) for arg in args])
    def table(pieces, kind):
        return pltpu.VMEM((pieces * tiles + 2, 16, samples), kind)

    def call(kernel, ins, outs, scratch, args, name, owned):
        return pl.pallas_call(
            functools.partial(kernel, group, blocked),
            grid=grid,
            out_shape=outs[0] + saved * outs[1],
            in_specs=[SMEM] + [VMEM] * ins[0] + held[:1] * ins[1],
            out_specs=[VMEM] * len(outs[0]) + held * outs[1],
            scratch_shapes=scratch,
            compiler_params=params,
            cost_estimate=pl.CostEstimate(
                flops=2 * owned * count * samples * channels * (3 * channels),
                bytes_accessed=owned * count * samples * channels * 12,
                transcendentals=0,
            ),
            name=name,
        )(*args)

    total = (112 + channels, channels)
    rows = (channels // 2 + 9 * parts + 1 + 7) // 8 * 8
    own, *inner = call(
        forward_inner, (3, 0), ([table(1, bf16)], 1), [table(1, f32)],
        (idx, flat, w1, w2), "forward_inner", 2,
    )
    res, g, halo, *outer = call(
        forward_outer, (7, 1),
        (
            [
                jax.ShapeDtypeStruct(records.shape, f32),
                jax.ShapeDtypeStruct((tiles, parts, samples), bf16),
                table(2, bf16),
            ],
            1,
        ),
        [table(2, f32), pltpu.VMEM((count * 4, 8, samples), f32)],
        (idx, from_near, flat, from_far, own, w1, w2, w3, inner[1]), "forward_outer", 4,
    )
    g_far = lax.ppermute(g, "rec", far)
    g_near = lax.ppermute(g, "rec", near)
    gown, part = call(
        backward_inner, (4, 4), ([table(1, bf16), pltpu.VMEM(total, f32)], 0), [table(1, f32)],
        (idx, g, wo, wm, own, *inner), "backward_inner", 2,
    )
    (sums,) = call(
        backward_outer, (8, 4), ([jax.ShapeDtypeStruct((rows, 2 * channels), f32)], 0),
        [table(2, bf16), table(2, f32), pltpu.VMEM(total, f32)],
        (idx, g_near, g_far, wo, wm, own, halo, gown, part, *outer), "backward_outer", 2,
    )

    if count & (count - 1):
        terms = [lax.psum(sums, "rec")]
    else:
        terms = [sums]
        at = 1
        while at < count:
            wide = 4 if at == 2 and 4 * at <= count else 2
            value = terms[0]
            if len(terms) == 2:
                value = terms[0] + terms[1]
            if len(terms) == 4:
                value = (terms[0] + terms[1]) + (terms[2] + terms[3])
            terms = [value] + [
                lax.ppermute(value, "rec", [(s, s ^ (k * at)) for s in range(count)])
                for k in range(1, wide)
            ]
            at *= wide

    scale = 1.0 / math.sqrt(parts * blocks * count * traces * samples)
    g_in, g_bin, g_mid, g_bmid, g_out = pl.pallas_call(
        functools.partial(finish_kernel, scale),
        out_shape=[
            jax.ShapeDtypeStruct(shape, f32)
            for shape in (
                (parts * 9, channels), (1, channels), (channels, channels), (1, channels),
                (parts * 9, channels),
            )
        ],
        in_specs=[VMEM] * len(terms),
        out_specs=[VMEM] * 5,
        scratch_shapes=[pltpu.VMEM(sums.shape, f32)],
        compiler_params=params,
        name="finish",
    )(*terms)
    return (
        res,
        g_in.T,
        g_bin.reshape(channels),
        g_mid,
        g_bmid.reshape(channels),
        g_out.T,
    )


def solution(mesh):
    return jax.shard_map(
        local,
        mesh=mesh,
        in_specs=(
            P(None, ("groups", "rec"), None, None),
            P("groups", None),
            P(),
            P(),
            P(),
            P(),
            P(),
        ),
        out_specs=(
            P(None, ("groups", "rec"), None, None),
            P("groups", None),
            P("groups"),
            P("groups", None),
            P("groups"),
            P("groups", None),
        ),
        check_vma=False,
    )
```

```python
import functools
import math

import jax
import jax.numpy as jnp
from jax import lax
from jax.experimental import pallas as pl
from jax.experimental.pallas import tpu as pltpu
from jax.sharding import PartitionSpec as P

CAP = 2
VMEM = pl.BlockSpec(memory_space=pltpu.VMEM)
SMEM = pl.BlockSpec(memory_space=pltpu.SMEM)
RESIDENT = 24 << 20


def run(start, step, end, steps, blocked):
    if blocked:
        n = pl.program_id(0)
        pl.when(n == 0)(start)
        step(n, 0)
        pl.when(n == steps - 1)(end)
        return
    start()
    lax.fori_loop(0, steps, lambda n, carry: step(n, n), None)
    end()


def group_of(owners):
    for size in (32, 16, 8, 4, 2):
        if owners % size == 0:
            return size
    return 1


def fill_table(table, wide, pieces, tiles, flip, fill):
    for n, piece in enumerate(pieces):
        x = piece[...].astype(jnp.float32)
        samples = x.shape[2]
        lane = lax.broadcasted_iota(jnp.int32, x.shape, 2)
        before = jnp.where(lane == 0, 0.0, pltpu.roll(x, 1, 2))
        after = jnp.where(lane == samples - 1, 0.0, pltpu.roll(x, samples - 1, 2))
        at = pl.ds(n * tiles, tiles)
        wide[at, 0:4, :] = after if flip else before
        wide[at, 4:8, :] = x
        wide[at, 8:12, :] = before if flip else after
    last, count = len(pieces) * tiles, wide.shape[0]
    wide[pl.ds(last, count - last), 0:12, :] = jnp.zeros((count - last, 12, wide.shape[2]), jnp.float32)
    wide[:, 12:16, :] = jnp.full((count, 4, wide.shape[2]), fill, jnp.float32)
    table[...] = wide[...].astype(jnp.bfloat16)


def act(y):
    t = jnp.tanh(y)
    q = 1.0 + t
    a = y * q
    return t, q, a


def lines_of(idx, own, halo, owners, thin=False):
    lines = []
    for e in owners:
        line = []
        for r in range(4):
            held = own if r in (1, 2) else halo
            if thin and r in (0, 3):
                line += [held[lax.div(idx[r, e], 2)]] * 2
                continue
            line += [None, None] if held is None else [held[idx[r, e]], held[idx[r, e] + 1]]
        lines.append(line)
    return lines


def stack(lines, traces, flip):
    return jnp.concatenate(
        [
            jnp.concatenate(
                [line[h + 1 + (2 - i if flip else i)] for line in lines for h in traces], axis=1
            )
            for i in range(3)
        ],
        axis=0,
    )


def layers(inputs, w1, w2):
    y1 = jnp.dot(w1[...], inputs, preferred_element_type=jnp.float32)
    t, q, a = act(y1)
    d1 = q + a * (1.0 - t)
    a1 = a.astype(jnp.bfloat16)
    ones = jnp.ones((16, a1.shape[1]), jnp.bfloat16)
    y2 = jnp.dot(w2[...], jnp.concatenate([a1, ones], axis=0), preferred_element_type=jnp.float32)
    t, q, a = act(y2)
    return a1, d1, a, q + a * (1.0 - t)


def forward_inner(
    group, blocked, idx, mine, w1, w2, own, a1_ref, a2_ref, d1_ref, d2_ref, wide
):
    owners = lax.axis_size("rec")

    def start():
        fill_table(own, wide, (mine,), mine.shape[0], False, 1.0)

    def step(n, block):
        lines = lines_of(idx, own, None, [n * group + u for u in range(group)])
        a1, d1, a2, d2 = layers(stack(lines, (1, 2), False), w1, w2)
        a1_ref[block] = a1
        d1_ref[block] = d1
        a2_ref[block] = a2.astype(jnp.bfloat16)
        d2_ref[block] = d2

    run(start, step, lambda: None, owners // group, blocked)


def forward_outer(
    group, blocked, idx, near, mine, far, own, w1, w2, w3, inner,
    res, g, g_near, g_far, halo, a1_ref, a2_ref, d1_ref, d2_ref, wide, est,
):
    tiles, parts, samples = mine.shape
    count = lax.axis_size("rec")
    me = lax.axis_index("rec")
    has_left = (me > 0).astype(jnp.float32)
    has_right = (me < count - 1).astype(jnp.float32)
    lane = lax.broadcasted_iota(jnp.int32, (8, samples), 1)
    low = (lane > 0).astype(jnp.float32)
    high = (lane < samples - 1).astype(jnp.float32)

    def start():
        fill_table(halo, wide, (near, far), tiles, False, 1.0)

    def step(n, block):
        lines = lines_of(idx, own, halo, [n * group + u for u in range(group)])
        a1, d1, a2, d2 = layers(stack(lines, (-1, 0, 3, 4), False), w1, w2)
        cut = lambda x, u, k: x[:, (u * 4 + k) * samples : (u * 4 + k + 1) * samples]
        middle = lambda x: jnp.concatenate(
            [cut(x, u, k) for u in range(group) for k in (1, 2)], axis=1
        )
        a1_ref[block] = middle(a1)
        d1_ref[block] = middle(d1)
        d2_ref[block] = middle(d2)
        rows = []
        for u in range(group):
            row = [cut(a2, u, 0) * has_left, cut(a2, u, 1), cut(a2, u, 2), cut(a2, u, 3) * has_right]
            row = [part.astype(jnp.bfloat16) for part in row]
            within = [
                inner[block, :, (u * 2 + k) * samples : (u * 2 + k + 1) * samples] for k in range(2)
            ]
            rows.append(row[0:2] + within + row[2:4])
        a2_ref[block] = jnp.concatenate([row[k] for row in rows for k in (1, 4)], axis=1)
        rhs = jnp.concatenate(
            [
                jnp.concatenate([row[h + i] for row in rows for h in range(4)], axis=1)
                for i in range(3)
            ],
            axis=0,
        )
        terms = jnp.dot(w3[...], rhs, preferred_element_type=jnp.float32)
        for k in range(group * 4):
            part = terms[:, k * samples : (k + 1) * samples]
            total = (
                part[8:16]
                + pltpu.roll(part[0:8], 1, 1) * low
                + pltpu.roll(part[16:24], samples - 1, 1) * high
            )
            est[n * group * 4 + k] = total.astype(jnp.bfloat16).astype(jnp.float32)

    def end():
        for c in range(tiles // 2):
            at = [idx[4 + v, tiles // 2 + c] for v in range(4)]
            for k in range(2):
                total = (est[at[0] + k] + est[at[1] + k]) + (est[at[2] + k] + est[at[3] + k])
                value = total[0:parts] - mine[c * 2 + k].astype(jnp.float32)
                for o in range(parts):
                    res[o, c, k : k + 1, :] = value[o : o + 1]
                g[c * 2 + k] = value.astype(jnp.bfloat16)
        odd = lax.rem(me, 2)
        for c in range(tiles // 2):
            g_near[c] = g[c * 2 + 1 - odd]
            g_far[c] = g[c * 2 + odd]

    run(start, step, end, count // group, blocked)


def weight_terms(acc, fields, inputs, wo, wm, a1, a2, d1, d2):
    channels = wm.shape[0]
    da2 = jnp.dot(wo[...], fields, preferred_element_type=jnp.float32)
    dz2 = (da2 * d2).astype(jnp.bfloat16)
    acc[0:48, :] += product(fields, a2, (1, 1))
    da1 = jnp.dot(wm[...], dz2, preferred_element_type=jnp.float32)
    ones = jnp.ones((16, dz2.shape[1]), jnp.bfloat16)
    acc[48 : 64 + channels, :] += product(jnp.concatenate([a1, ones], axis=0), dz2, (1, 1))
    dz1 = (da1 * d1).astype(jnp.bfloat16)
    acc[64 + channels : 112 + channels, :] += product(inputs, dz1, (1, 1))


def backward_inner(
    group, blocked, idx, mine, wo, wm, own, a1_ref, a2_ref, d1_ref, d2_ref, gown, acc, wide
):
    owners = lax.axis_size("rec")

    def start():
        fill_table(gown, wide, (mine,), mine.shape[0], True, 0.0)
        acc[...] = jnp.zeros_like(acc)

    def step(n, block):
        es = [n * group + u for u in range(group)]
        fields = stack(lines_of(idx, gown, None, es), (1, 2), True)
        inputs = stack(lines_of(idx, own, None, es), (1, 2), False)
        saved = a1_ref[block], a2_ref[block], d1_ref[block], d2_ref[block]
        weight_terms(acc, fields, inputs, wo, wm, *saved)

    run(start, step, lambda: None, owners // group, blocked)


def backward_outer(
    group, blocked, idx, near, far, wo, wm, own, halo, gown, sums, a1_ref, a2_ref, d1_ref, d2_ref,
    keep, send, ghalo, wide, acc, halves_of,
):
    owners = lax.axis_size("rec")
    channels = wm.shape[0]
    taps = 9 * near.shape[1]

    def start():
        fill_table(ghalo, wide, (near, far), near.shape[0], True, 0.0)
        acc[...] = sums[...]

    def step(n, block):
        es = [n * group + u for u in range(group)]
        fields = stack(lines_of(idx, gown, ghalo, es, True), (0, 3), True)
        inputs = stack(lines_of(idx, own, halo, es), (0, 3), False)
        saved = a1_ref[block], a2_ref[block], d1_ref[block], d2_ref[block]
        weight_terms(acc, fields, inputs, wo, wm, *saved)

    def end():
        first, half = 64 + channels, channels // 2
        low, high = slice(0, channels), slice(channels, 2 * channels)
        halves_of[...] = jnp.zeros_like(halves_of)
        middle = acc[48 : 48 + channels, :].T
        halves_of[0, 0:half, low] = middle[0:half]
        halves_of[0, 0:half, high] = middle[half:channels]
        halves_of[0, half : half + 1, low] = acc[first + 28 : first + 29, :]
        halves_of[0, half : half + 1, high] = acc[48 + channels : 49 + channels, :]
        for k in range(taps):
            at = k % 9 // 3 * 16 + k % 3 * 4 + k // 9
            halves_of[1, k : k + 1, low] = acc[first + at : first + at + 1, :]
            halves_of[1, k : k + 1, high] = acc[at : at + 1, :]
        core = lax.rem(lax.axis_index("rec"), 2)
        keep[...] = halves_of[core]
        send[...] = halves_of[1 - core]

    run(start, step, end, owners // group, blocked)


def finish_kernel(scale, mine, other, g_in, g_bin, g_mid, g_bmid, g_out, held):
    core = lax.rem(lax.axis_index("rec"), 2)
    held[core] = mine[...] * scale
    held[1 - core] = other[...] * scale
    channels = g_mid.shape[0]
    half, taps = channels // 2, g_in.shape[0]
    low, high = slice(0, channels), slice(channels, 2 * channels)
    g_mid[0:half] = held[0, 0:half, low]
    g_mid[half:channels] = held[0, 0:half, high]
    g_bin[...] = held[0, half : half + 1, low]
    g_bmid[...] = held[0, half : half + 1, high]
    g_in[...] = held[1, 0:taps, low]
    g_out[...] = held[1, 0:taps, high]


def halves(b):
    high = b.astype(jnp.bfloat16).astype(jnp.float32)
    rest = b - high
    mid = rest.astype(jnp.bfloat16).astype(jnp.float32)
    return [high, mid, rest - mid]


def one_hot(a, b):
    return (a == b).astype(jnp.float32).astype(jnp.bfloat16)


def iota(shape, dim):
    return lax.broadcasted_iota(jnp.int32, shape, dim)


def product(a, b, over):
    return lax.dot_general(
        a, b, dimension_numbers=(((over[0],), (over[1],)), ((), ())),
        preferred_element_type=jnp.float32,
    )


def prep_kernel(blocks, *refs):
    args, (idx, w1, w2, w3, wo, wm, rows), held, sems = refs[:6], refs[6:13], refs[13:19], refs[19]
    copies = [
        pltpu.make_async_copy(src, dst, sems.at[n]) for n, (src, dst) in enumerate(zip(args, held))
    ]
    for copy in copies:
        copy.start()
    for copy in copies:
        copy.wait()
    dest, w_in, b_in, w_mid, b_mid, w_out = held
    count = lax.axis_size("rec")
    me = lax.axis_index("rec")
    ves, total = dest.shape
    channels = w_mid.shape[0]
    at = lax.rem((count + 1 - me) * blocks, total)
    wide = jnp.concatenate([dest[...], jnp.zeros((8 - ves, total), jnp.int32)], axis=0)
    near = pltpu.roll(wide, at, 1)[:, 0:128]
    lane = iota((8, 128), 1)
    low = jnp.where(me > 0, 0, blocks)
    high = jnp.where(me < count - 1, 3 * blocks, 2 * blocks)
    near = jnp.where((lane >= low) & (lane < high), near, -1)
    owner = iota((count, 128), 0)
    hits = [(near[v : v + 1] == owner).astype(jnp.float32) for v in range(ves)]
    before = iota((128, 128), 0)
    after = iota((128, 128), 1)
    segment = (after >= blocks).astype(jnp.int32) + (after >= 2 * blocks).astype(jnp.int32)
    tri = ((before < after) & (before >= segment * blocks)).astype(jnp.float32).astype(jnp.bfloat16)
    rank = product((hits[0] + hits[1] + hits[2] + hits[3]).astype(jnp.bfloat16), tri, (1, 0))
    zeroth = jnp.zeros((count, 128), jnp.float32)
    first = jnp.zeros((count, 128), jnp.float32)
    for v in range(ves):
        zeroth += hits[v] * (rank == 0.0).astype(jnp.float32)
        first += hits[v] * (rank == 1.0).astype(jnp.float32)
        item = jnp.sum(hits[v] * rank, axis=0, keepdims=True)
        idx[4 + v : 5 + v, 0:128] = near[v : v + 1] * 4 + item.astype(jnp.int32) * 2
        rank = rank + hits[v]
    line = iota((8, 128), 0)
    inside = lambda k: (lane >= k * blocks) & (lane < (k + 1) * blocks)
    odd = lax.rem(me, 2)
    left = 2 * lane + 2 * blocks * (1 - odd) - 4 * blocks
    middle = 2 * (lane - blocks) - 2 * blocks
    right = 2 * (lane - 2 * blocks) + 2 * blocks * odd - 4 * blocks
    put = lambda r, k, place: jnp.where((line == r) & inside(k), place, 0)
    pick = product(
        (put(0, 0, left) + put(2, 1, middle)).astype(jnp.float32).astype(jnp.bfloat16),
        first.astype(jnp.bfloat16),
        (1, 1),
    ) + product(
        (put(1, 1, middle) + put(3, 2, right)).astype(jnp.float32).astype(jnp.bfloat16),
        zeroth.astype(jnp.bfloat16),
        (1, 1),
    )
    empty = jnp.where((line == 0) | (line == 3), 4 * blocks, 2 * blocks)[0:4, 0:1]
    idx[0:4, 0:count] = pick[0:4].astype(jnp.int32) + empty

    taps = w_in.shape[0]
    row, col = iota((48, 40), 0), iota((48, 40), 1)
    tap, extra = row & 15, (row & 15) - 12
    target = (row & 3) * 9 + 3 * (row >> 4) + ((row >> 2) & 3)
    target = jnp.where(tap < 12, target, jnp.where((row >> 4) == 1, taps + extra, -1))
    order = one_hot(col, target)
    rows[...] = jnp.zeros_like(rows)
    rows[0:taps, :] = w_in[...].astype(jnp.float32)
    for n, part in enumerate(halves(b_in[...])):
        rows[taps + n : taps + n + 1, :] = part
    w1[...] = (0.5 * product(rows[...].astype(jnp.bfloat16), order, (0, 1))).astype(jnp.bfloat16)
    rows[...] = jnp.zeros_like(rows)
    for n, part in enumerate(halves(b_mid[...])):
        rows[n : n + 1, :] = part
    row, col = iota((40, channels + 16), 0), iota((40, channels + 16), 1)
    bias = product(rows[...].astype(jnp.bfloat16), one_hot(col, row + channels), (0, 0))
    row, col = iota((channels, channels + 16), 0), iota((channels, channels + 16), 1)
    w2[...] = (0.5 * (product(w_mid[...], one_hot(row, col), (1, 0)) + bias)).astype(jnp.bfloat16)
    rows[...] = jnp.zeros_like(rows)
    rows[0:taps, :] = w_out[...].astype(jnp.float32)
    outs = rows[...].astype(jnp.bfloat16)
    wo[...] = (0.5 * product(outs, order, (0, 1))).astype(jnp.bfloat16)
    row, col = iota((24, 40), 0), iota((24, 40), 1)
    for i in range(3):
        target = jnp.where((row & 7) < 4, (row & 3) * 9 + 3 * i + (row >> 3), -1)
        part = product(one_hot(col, target), outs, (1, 0))
        w3[:, i * channels : (i + 1) * channels] = part.astype(jnp.bfloat16)
    eye = one_hot(iota((channels, channels), 0), iota((channels, channels), 1))
    wm[...] = (0.5 * product(w_mid[...], eye, (0, 0))).astype(jnp.bfloat16)


def local(records, dest, w_in, b_in, w_mid, b_mid, w_out):
    count = lax.axis_size("rec")
    me = lax.axis_index("rec")
    parts, blocks, traces, samples = records.shape
    ves = dest.shape[1]
    tiles = blocks * traces
    channels = w_in.shape[0]
    group = group_of(count)
    steps = count // group
    width = group * 2 * samples
    far = [(s, s + 1) for s in range(1, count - 1, 2)]
    far += [(b, a) for a, b in far]
    near = [(s, s + 1) for s in range(0, count - 1, 2)]
    near += [(b, a) for a, b in near]

    flat = records.transpose(1, 2, 0, 3).reshape(tiles, parts, samples)
    from_far = lax.ppermute(flat, "rec", far)
    from_near = lax.ppermute(flat, "rec", near)

    f32, bf16 = jnp.float32, jnp.bfloat16
    shape = (steps, channels, width)
    blocked = 24 * math.prod(shape) > RESIDENT
    saved = [
        jax.ShapeDtypeStruct(shape, kind) if blocked else pltpu.VMEM(shape, kind)
        for kind in (bf16, bf16, f32, f32)
    ]
    held = [VMEM] * 4
    if blocked:
        held = [pl.BlockSpec((1, channels, width), lambda n: (n, 0, 0))] * 4
    grid = (steps,) if blocked else ()
    params = pltpu.CompilerParams(vmem_limit_bytes=16 << 20)
    args = (
        dest.T, w_in.T, b_in.reshape(1, channels), w_mid, b_mid.reshape(1, channels), w_out.T
    )
    idx, w1, w2, w3, wo, wm = pl.pallas_call(
        functools.partial(prep_kernel, blocks),
        out_shape=[jax.ShapeDtypeStruct((8, max(128, count)), jnp.int32)]
        + [
            jax.ShapeDtypeStruct(size, bf16)
            for size in (
                (channels, 48), (channels, channels + 16), (24, 3 * channels), (channels, 48),
                (channels, channels),
            )
        ],
        in_specs=[pl.BlockSpec(memory_space=pltpu.HBM)] * 6,
        out_specs=[VMEM] * 6,
        scratch_shapes=[pltpu.VMEM((40, channels), f32)]
        + [pltpu.VMEM(arg.shape, arg.dtype) for arg in args]
        + [pltpu.SemaphoreType.DMA((6,))],
        compiler_params=params,
        name="prepare",
    )(*[pltpu.with_memory_space_constraint(arg, pltpu.HBM) for arg in args])
    def table(pieces, kind):
        return pltpu.VMEM((pieces * tiles + 2, 16, samples), kind)

    def call(kernel, ins, outs, scratch, args, name, owned):
        return pl.pallas_call(
            functools.partial(kernel, group, blocked),
            grid=grid,
            out_shape=outs[0] + saved * outs[1],
            in_specs=[SMEM] + [VMEM] * ins[0] + held[:1] * ins[1],
            out_specs=[VMEM] * len(outs[0]) + held * outs[1],
            scratch_shapes=scratch,
            compiler_params=params,
            cost_estimate=pl.CostEstimate(
                flops=2 * owned * count * samples * channels * (3 * channels),
                bytes_accessed=owned * count * samples * channels * 12,
                transcendentals=0,
            ),
            name=name,
        )(*args)

    total = (112 + channels, channels)
    own, *inner = call(
        forward_inner, (3, 0), ([table(1, bf16)], 1), [table(1, f32)],
        (idx, flat, w1, w2), "forward_inner", 2,
    )
    res, g, g_near, g_far, halo, *outer = call(
        forward_outer, (7, 1),
        (
            [
                jax.ShapeDtypeStruct(records.shape, f32),
                jax.ShapeDtypeStruct((tiles, parts, samples), bf16),
                jax.ShapeDtypeStruct((blocks, parts, samples), bf16),
                jax.ShapeDtypeStruct((blocks, parts, samples), bf16),
                table(2, bf16),
            ],
            1,
        ),
        [table(2, f32), pltpu.VMEM((count * 4, 8, samples), f32)],
        (idx, from_near, flat, from_far, own, w1, w2, w3, inner[1]), "forward_outer", 4,
    )
    g_far = lax.ppermute(g_far, "rec", far)
    g_near = lax.ppermute(g_near, "rec", near)
    gown, part = call(
        backward_inner, (4, 4), ([table(1, bf16), pltpu.VMEM(total, f32)], 0), [table(1, f32)],
        (idx, g, wo, wm, own, *inner), "backward_inner", 2,
    )
    keep, send = call(
        backward_outer, (8, 4), ([jax.ShapeDtypeStruct((40, 2 * channels), f32)] * 2, 0),
        [table(1, bf16), table(1, f32), pltpu.VMEM(total, f32), pltpu.VMEM((2, 40, 2 * channels), f32)],
        (idx, g_near, g_far, wo, wm, own, halo, gown, part, *outer), "backward_outer", 2,
    )

    def swap(value, k):
        return lax.ppermute(value, "rec", [(s, s ^ k) for s in range(count)])

    if count & (count - 1):
        core = lax.rem(me, 2)
        both = jnp.where(core == 0, jnp.stack([keep, send]), jnp.stack([send, keep]))
        both = lax.psum(both, "rec")
        mine, other = both[core], both[1 - core]
    else:
        mine, k = keep + swap(send, 1), 2
        while k < count:
            mine, k = mine + swap(mine, k), 2 * k
        other = swap(mine, 1)

    scale = 1.0 / math.sqrt(parts * blocks * count * traces * samples)
    g_in, g_bin, g_mid, g_bmid, g_out = pl.pallas_call(
        functools.partial(finish_kernel, scale),
        out_shape=[
            jax.ShapeDtypeStruct(shape, f32)
            for shape in (
                (parts * 9, channels), (1, channels), (channels, channels), (1, channels),
                (parts * 9, channels),
            )
        ],
        in_specs=[VMEM] * 2,
        out_specs=[VMEM] * 5,
        scratch_shapes=[pltpu.VMEM((2, *keep.shape), f32)],
        compiler_params=params,
        name="finish",
    )(mine, other)
    return (
        res,
        g_in.T,
        g_bin.reshape(channels),
        g_mid,
        g_bmid.reshape(channels),
        g_out.T,
    )


def solution(mesh):
    return jax.shard_map(
        local,
        mesh=mesh,
        in_specs=(
            P(None, ("groups", "rec"), None, None),
            P("groups", None),
            P(),
            P(),
            P(),
            P(),
            P(),
        ),
        out_specs=(
            P(None, ("groups", "rec"), None, None),
            P("groups", None),
            P("groups"),
            P("groups", None),
            P("groups"),
            P("groups", None),
        ),
        check_vma=False,
    )
```

```python
import functools
import math

import jax
import jax.numpy as jnp
from jax import lax
from jax.experimental import pallas as pl
from jax.experimental.pallas import tpu as pltpu
from jax.sharding import PartitionSpec as P

CAP = 2
VMEM = pl.BlockSpec(memory_space=pltpu.VMEM)
SMEM = pl.BlockSpec(memory_space=pltpu.SMEM)
RESIDENT = 24 << 20


def run(start, step, end, steps, blocked):
    if blocked:
        n = pl.program_id(0)
        pl.when(n == 0)(start)
        step(n, 0)
        pl.when(n == steps - 1)(end)
        return
    start()
    lax.fori_loop(0, steps, lambda n, carry: step(n, n), None)
    end()


def group_of(owners):
    for size in (32, 16, 8, 4, 2):
        if owners % size == 0:
            return size
    return 1


def fill_table(table, wide, pieces, tiles, flip, fill):
    for n, piece in enumerate(pieces):
        x = piece[...].astype(jnp.float32)
        samples = x.shape[2]
        lane = lax.broadcasted_iota(jnp.int32, x.shape, 2)
        before = jnp.where(lane == 0, 0.0, pltpu.roll(x, 1, 2))
        after = jnp.where(lane == samples - 1, 0.0, pltpu.roll(x, samples - 1, 2))
        at = pl.ds(n * tiles, tiles)
        wide[at, 0:4, :] = after if flip else before
        wide[at, 4:8, :] = x
        wide[at, 8:12, :] = before if flip else after
    last, count = len(pieces) * tiles, wide.shape[0]
    wide[pl.ds(last, count - last), 0:12, :] = jnp.zeros((count - last, 12, wide.shape[2]), jnp.float32)
    wide[:, 12:16, :] = jnp.full((count, 4, wide.shape[2]), fill, jnp.float32)
    table[...] = wide[...].astype(jnp.bfloat16)


def act(y):
    t = jnp.tanh(y)
    q = 1.0 + t
    a = y * q
    return t, q, a


def lines_of(idx, own, halo, owners, thin=False):
    lines = []
    for e in owners:
        line = []
        for r in range(4):
            held = own if r in (1, 2) else halo
            if thin and r in (0, 3):
                line += [held[lax.div(idx[r, e], 2)]] * 2
                continue
            line += [None, None] if held is None else [held[idx[r, e]], held[idx[r, e] + 1]]
        lines.append(line)
    return lines


def stack(lines, traces, flip):
    return jnp.concatenate(
        [
            jnp.concatenate(
                [line[h + 1 + (2 - i if flip else i)] for line in lines for h in traces], axis=1
            )
            for i in range(3)
        ],
        axis=0,
    )


def layers(inputs, w1, w2):
    y1 = jnp.dot(w1[...], inputs, preferred_element_type=jnp.float32)
    t, q, a = act(y1)
    d1 = q + a * (1.0 - t)
    a1 = a.astype(jnp.bfloat16)
    ones = jnp.ones((16, a1.shape[1]), jnp.bfloat16)
    y2 = jnp.dot(w2[...], jnp.concatenate([a1, ones], axis=0), preferred_element_type=jnp.float32)
    t, q, a = act(y2)
    return a1, d1, a, q + a * (1.0 - t)


def forward_inner(
    group, blocked, idx, mine, w1, w2, own, a1_ref, a2_ref, d1_ref, d2_ref, wide
):
    owners = lax.axis_size("rec")

    def start():
        fill_table(own, wide, (mine,), mine.shape[0], False, 1.0)

    def step(n, block):
        lines = lines_of(idx, own, None, [n * group + u for u in range(group)])
        a1, d1, a2, d2 = layers(stack(lines, (1, 2), False), w1, w2)
        a1_ref[block] = a1
        d1_ref[block] = d1
        a2_ref[block] = a2.astype(jnp.bfloat16)
        d2_ref[block] = d2

    run(start, step, lambda: None, owners // group, blocked)


def forward_outer(
    group, blocked, idx, near, mine, far, own, w1, w2, w3, inner,
    res, g, g_near, g_far, halo, a1_ref, a2_ref, d1_ref, d2_ref, wide, est,
):
    tiles, parts, samples = mine.shape
    count = lax.axis_size("rec")
    me = lax.axis_index("rec")
    has_left = (me > 0).astype(jnp.float32)
    has_right = (me < count - 1).astype(jnp.float32)
    lane = lax.broadcasted_iota(jnp.int32, (8, samples), 1)
    low = (lane > 0).astype(jnp.float32)
    high = (lane < samples - 1).astype(jnp.float32)

    def start():
        fill_table(halo, wide, (near, far), tiles, False, 1.0)

    def step(n, block):
        lines = lines_of(idx, own, halo, [n * group + u for u in range(group)])
        a1, d1, a2, d2 = layers(stack(lines, (-1, 0, 3, 4), False), w1, w2)
        cut = lambda x, u, k: x[:, (u * 4 + k) * samples : (u * 4 + k + 1) * samples]
        middle = lambda x: jnp.concatenate(
            [cut(x, u, k) for u in range(group) for k in (1, 2)], axis=1
        )
        a1_ref[block] = middle(a1)
        d1_ref[block] = middle(d1)
        d2_ref[block] = middle(d2)
        rows = []
        for u in range(group):
            row = [cut(a2, u, 0) * has_left, cut(a2, u, 1), cut(a2, u, 2), cut(a2, u, 3) * has_right]
            row = [part.astype(jnp.bfloat16) for part in row]
            within = [
                inner[block, :, (u * 2 + k) * samples : (u * 2 + k + 1) * samples] for k in range(2)
            ]
            rows.append(row[0:2] + within + row[2:4])
        a2_ref[block] = jnp.concatenate([row[k] for row in rows for k in (1, 4)], axis=1)
        rhs = jnp.concatenate(
            [
                jnp.concatenate([row[h + i] for row in rows for h in range(4)], axis=1)
                for i in range(3)
            ],
            axis=0,
        )
        terms = jnp.dot(w3[...], rhs, preferred_element_type=jnp.float32)
        for k in range(group * 4):
            part = terms[:, k * samples : (k + 1) * samples]
            total = (
                part[8:16]
                + pltpu.roll(part[0:8], 1, 1) * low
                + pltpu.roll(part[16:24], samples - 1, 1) * high
            )
            est[n * group * 4 + k] = total.astype(jnp.bfloat16).astype(jnp.float32)

    def end():
        for c in range(tiles // 2):
            at = [idx[4 + v, tiles // 2 + c] for v in range(4)]
            for k in range(2):
                total = (est[at[0] + k] + est[at[1] + k]) + (est[at[2] + k] + est[at[3] + k])
                value = total[0:parts] - mine[c * 2 + k].astype(jnp.float32)
                for o in range(parts):
                    res[o, c, k : k + 1, :] = value[o : o + 1]
                g[c * 2 + k] = value.astype(jnp.bfloat16)
        odd = lax.rem(me, 2)
        for c in range(tiles // 2):
            g_near[c] = g[c * 2 + 1 - odd]
            g_far[c] = g[c * 2 + odd]

    run(start, step, end, count // group, blocked)


def weight_terms(acc, fields, inputs, wo, wm, a1, a2, d1, d2):
    channels = wm.shape[0]
    da2 = jnp.dot(wo[...], fields, preferred_element_type=jnp.float32)
    dz2 = (da2 * d2).astype(jnp.bfloat16)
    acc[0:48, :] += product(fields, a2, (1, 1))
    da1 = jnp.dot(wm[...], dz2, preferred_element_type=jnp.float32)
    ones = jnp.ones((16, dz2.shape[1]), jnp.bfloat16)
    acc[48 : 64 + channels, :] += product(jnp.concatenate([a1, ones], axis=0), dz2, (1, 1))
    dz1 = (da1 * d1).astype(jnp.bfloat16)
    acc[64 + channels : 112 + channels, :] += product(inputs, dz1, (1, 1))


def backward_inner(
    group, blocked, idx, mine, wo, wm, own, a1_ref, a2_ref, d1_ref, d2_ref, gown, acc, wide
):
    owners = lax.axis_size("rec")

    def start():
        fill_table(gown, wide, (mine,), mine.shape[0], True, 0.0)
        acc[...] = jnp.zeros_like(acc)

    def step(n, block):
        es = [n * group + u for u in range(group)]
        fields = stack(lines_of(idx, gown, None, es), (1, 2), True)
        inputs = stack(lines_of(idx, own, None, es), (1, 2), False)
        saved = a1_ref[block], a2_ref[block], d1_ref[block], d2_ref[block]
        weight_terms(acc, fields, inputs, wo, wm, *saved)

    run(start, step, lambda: None, owners // group, blocked)


def backward_outer(
    group, blocked, idx, near, far, wo, wm, own, halo, gown, sums, a1_ref, a2_ref, d1_ref, d2_ref,
    keep, send, ghalo, wide, acc, halves_of,
):
    owners = lax.axis_size("rec")
    channels = wm.shape[0]
    taps = 9 * near.shape[1]

    def start():
        fill_table(ghalo, wide, (near, far), near.shape[0], True, 0.0)
        acc[...] = sums[...]

    def step(n, block):
        es = [n * group + u for u in range(group)]
        fields = stack(lines_of(idx, gown, ghalo, es, True), (0, 3), True)
        inputs = stack(lines_of(idx, own, halo, es), (0, 3), False)
        saved = a1_ref[block], a2_ref[block], d1_ref[block], d2_ref[block]
        weight_terms(acc, fields, inputs, wo, wm, *saved)

    def end():
        first, half = 64 + channels, channels // 2
        low, high = slice(0, channels), slice(channels, 2 * channels)
        halves_of[...] = jnp.zeros_like(halves_of)
        middle = acc[48 : 48 + channels, :].T
        halves_of[0, 0:half, low] = middle[0:half]
        halves_of[0, 0:half, high] = middle[half:channels]
        halves_of[0, half : half + 1, low] = acc[first + 28 : first + 29, :]
        halves_of[0, half : half + 1, high] = acc[48 + channels : 49 + channels, :]
        for k in range(taps):
            at = k % 9 // 3 * 16 + k % 3 * 4 + k // 9
            halves_of[1, k : k + 1, low] = acc[first + at : first + at + 1, :]
            halves_of[1, k : k + 1, high] = acc[at : at + 1, :]
        core = lax.rem(lax.axis_index("rec"), 2)
        keep[...] = halves_of[core]
        send[...] = halves_of[1 - core]

    run(start, step, end, owners // group, blocked)


def finish_kernel(scale, mine, other, g_in, g_bin, g_mid, g_bmid, g_out, held):
    core = lax.rem(lax.axis_index("rec"), 2)
    held[core] = mine[...] * scale
    held[1 - core] = other[...] * scale
    channels = g_mid.shape[0]
    half, taps = channels // 2, g_in.shape[0]
    low, high = slice(0, channels), slice(channels, 2 * channels)
    g_mid[0:half] = held[0, 0:half, low]
    g_mid[half:channels] = held[0, 0:half, high]
    g_bin[...] = held[0, half : half + 1, low]
    g_bmid[...] = held[0, half : half + 1, high]
    g_in[...] = held[1, 0:taps, low]
    g_out[...] = held[1, 0:taps, high]


def halves(b):
    high = b.astype(jnp.bfloat16).astype(jnp.float32)
    rest = b - high
    mid = rest.astype(jnp.bfloat16).astype(jnp.float32)
    return [high, mid, rest - mid]


def one_hot(a, b):
    return (a == b).astype(jnp.float32).astype(jnp.bfloat16)


def iota(shape, dim):
    return lax.broadcasted_iota(jnp.int32, shape, dim)


def product(a, b, over):
    return lax.dot_general(
        a, b, dimension_numbers=(((over[0],), (over[1],)), ((), ())),
        preferred_element_type=jnp.float32,
    )


def prep_kernel(blocks, *refs):
    args, (idx, w1, w2, w3, wo, wm, rows), held, sems = refs[:6], refs[6:13], refs[13:19], refs[19]
    copies = [
        pltpu.make_async_copy(src, dst, sems.at[n]) for n, (src, dst) in enumerate(zip(args, held))
    ]
    for copy in copies:
        copy.start()
    for copy in copies:
        copy.wait()
    dest, w_in, b_in, w_mid, b_mid, w_out = held
    count = lax.axis_size("rec")
    me = lax.axis_index("rec")
    ves, total = dest.shape
    channels = w_mid.shape[0]
    at = lax.rem((count + 1 - me) * blocks, total)
    wide = jnp.concatenate([dest[...], jnp.zeros((8 - ves, total), jnp.int32)], axis=0)
    near = pltpu.roll(wide, at, 1)[:, 0:128]
    lane = iota((8, 128), 1)
    low = jnp.where(me > 0, 0, blocks)
    high = jnp.where(me < count - 1, 3 * blocks, 2 * blocks)
    near = jnp.where((lane >= low) & (lane < high), near, -1)
    owner = iota((count, 128), 0)
    hits = [(near[v : v + 1] == owner).astype(jnp.float32) for v in range(ves)]
    before = iota((128, 128), 0)
    after = iota((128, 128), 1)
    segment = (after >= blocks).astype(jnp.int32) + (after >= 2 * blocks).astype(jnp.int32)
    tri = ((before < after) & (before >= segment * blocks)).astype(jnp.float32).astype(jnp.bfloat16)
    rank = product((hits[0] + hits[1] + hits[2] + hits[3]).astype(jnp.bfloat16), tri, (1, 0))
    zeroth = jnp.zeros((count, 128), jnp.float32)
    first = jnp.zeros((count, 128), jnp.float32)
    for v in range(ves):
        zeroth += hits[v] * (rank == 0.0).astype(jnp.float32)
        first += hits[v] * (rank == 1.0).astype(jnp.float32)
        item = jnp.sum(hits[v] * rank, axis=0, keepdims=True)
        idx[4 + v : 5 + v, 0:128] = near[v : v + 1] * 4 + item.astype(jnp.int32) * 2
        rank = rank + hits[v]
    line = iota((8, 128), 0)
    inside = lambda k: (lane >= k * blocks) & (lane < (k + 1) * blocks)
    odd = lax.rem(me, 2)
    left = 2 * lane + 2 * blocks * (1 - odd) - 4 * blocks
    middle = 2 * (lane - blocks) - 2 * blocks
    right = 2 * (lane - 2 * blocks) + 2 * blocks * odd - 4 * blocks
    put = lambda r, k, place: jnp.where((line == r) & inside(k), place, 0)
    pick = product(
        (put(0, 0, left) + put(2, 1, middle)).astype(jnp.float32).astype(jnp.bfloat16),
        first.astype(jnp.bfloat16),
        (1, 1),
    ) + product(
        (put(1, 1, middle) + put(3, 2, right)).astype(jnp.float32).astype(jnp.bfloat16),
        zeroth.astype(jnp.bfloat16),
        (1, 1),
    )
    empty = jnp.where((line == 0) | (line == 3), 4 * blocks, 2 * blocks)[0:4, 0:1]
    idx[0:4, 0:count] = pick[0:4].astype(jnp.int32) + empty

    taps = w_in.shape[0]
    row, col = iota((48, 40), 0), iota((48, 40), 1)
    tap, extra = row & 15, (row & 15) - 12
    target = (row & 3) * 9 + 3 * (row >> 4) + ((row >> 2) & 3)
    target = jnp.where(tap < 12, target, jnp.where((row >> 4) == 1, taps + extra, -1))
    order = one_hot(col, target)
    rows[...] = jnp.zeros_like(rows)
    rows[0:taps, :] = w_in[...].astype(jnp.float32)
    for n, part in enumerate(halves(b_in[...])):
        rows[taps + n : taps + n + 1, :] = part
    w1[...] = (0.5 * product(rows[...].astype(jnp.bfloat16), order, (0, 1))).astype(jnp.bfloat16)
    rows[...] = jnp.zeros_like(rows)
    for n, part in enumerate(halves(b_mid[...])):
        rows[n : n + 1, :] = part
    row, col = iota((40, channels + 16), 0), iota((40, channels + 16), 1)
    bias = product(rows[...].astype(jnp.bfloat16), one_hot(col, row + channels), (0, 0))
    row, col = iota((channels, channels + 16), 0), iota((channels, channels + 16), 1)
    w2[...] = (0.5 * (product(w_mid[...], one_hot(row, col), (1, 0)) + bias)).astype(jnp.bfloat16)
    rows[...] = jnp.zeros_like(rows)
    rows[0:taps, :] = w_out[...].astype(jnp.float32)
    outs = rows[...].astype(jnp.bfloat16)
    wo[...] = (0.5 * product(outs, order, (0, 1))).astype(jnp.bfloat16)
    row, col = iota((24, 40), 0), iota((24, 40), 1)
    for i in range(3):
        target = jnp.where((row & 7) < 4, (row & 3) * 9 + 3 * i + (row >> 3), -1)
        part = product(one_hot(col, target), outs, (1, 0))
        w3[:, i * channels : (i + 1) * channels] = part.astype(jnp.bfloat16)
    eye = one_hot(iota((channels, channels), 0), iota((channels, channels), 1))
    wm[...] = (0.5 * product(w_mid[...], eye, (0, 0))).astype(jnp.bfloat16)


def local(records, dest, w_in, b_in, w_mid, b_mid, w_out):
    count = lax.axis_size("rec")
    me = lax.axis_index("rec")
    parts, blocks, traces, samples = records.shape
    ves = dest.shape[1]
    tiles = blocks * traces
    channels = w_in.shape[0]
    group = group_of(count)
    steps = count // group
    width = group * 2 * samples
    far = [(s, s + 1) for s in range(1, count - 1, 2)]
    far += [(b, a) for a, b in far]
    near = [(s, s + 1) for s in range(0, count - 1, 2)]
    near += [(b, a) for a, b in near]

    flat = records.transpose(1, 2, 0, 3).reshape(tiles, parts, samples)
    from_far = lax.ppermute(flat, "rec", far)
    from_near = lax.ppermute(flat, "rec", near)

    f32, bf16 = jnp.float32, jnp.bfloat16
    shape = (steps, channels, width)
    blocked = 24 * math.prod(shape) > RESIDENT
    saved = [
        jax.ShapeDtypeStruct(shape, kind) if blocked else pltpu.VMEM(shape, kind)
        for kind in (bf16, bf16, f32, f32)
    ]
    held = [VMEM] * 4
    if blocked:
        held = [pl.BlockSpec((1, channels, width), lambda n: (n, 0, 0))] * 4
    grid = (steps,) if blocked else ()
    params = pltpu.CompilerParams(vmem_limit_bytes=16 << 20)
    args = (
        dest.T, w_in.T, b_in.reshape(1, channels), w_mid, b_mid.reshape(1, channels), w_out.T
    )
    idx, w1, w2, w3, wo, wm = pl.pallas_call(
        functools.partial(prep_kernel, blocks),
        out_shape=[jax.ShapeDtypeStruct((8, max(128, count)), jnp.int32)]
        + [
            jax.ShapeDtypeStruct(size, bf16)
            for size in (
                (channels, 48), (channels, channels + 16), (24, 3 * channels), (channels, 48),
                (channels, channels),
            )
        ],
        in_specs=[pl.BlockSpec(memory_space=pltpu.HBM)] * 6,
        out_specs=[VMEM] * 6,
        scratch_shapes=[pltpu.VMEM((40, channels), f32)]
        + [pltpu.VMEM(arg.shape, arg.dtype) for arg in args]
        + [pltpu.SemaphoreType.DMA((6,))],
        compiler_params=params,
        name="prepare",
    )(*[pltpu.with_memory_space_constraint(arg, pltpu.HBM) for arg in args])
    def table(pieces, kind):
        return pltpu.VMEM((pieces * tiles + 2, 16, samples), kind)

    def call(kernel, ins, outs, scratch, args, name, owned):
        return pl.pallas_call(
            functools.partial(kernel, group, blocked),
            grid=grid,
            out_shape=outs[0] + saved * outs[1],
            in_specs=[SMEM] + [VMEM] * ins[0] + held[:1] * ins[1],
            out_specs=[VMEM] * len(outs[0]) + held * outs[1],
            scratch_shapes=scratch,
            compiler_params=params,
            cost_estimate=pl.CostEstimate(
                flops=2 * owned * count * samples * channels * (3 * channels),
                bytes_accessed=owned * count * samples * channels * 12,
                transcendentals=0,
            ),
            name=name,
        )(*args)

    total = (112 + channels, channels)
    own, *inner = call(
        forward_inner, (3, 0), ([table(1, bf16)], 1), [table(1, f32)],
        (idx, flat, w1, w2), "forward_inner", 2,
    )
    res, g, g_near, g_far, halo, *outer = call(
        forward_outer, (7, 1),
        (
            [
                jax.ShapeDtypeStruct(records.shape, f32),
                jax.ShapeDtypeStruct((tiles, parts, samples), bf16),
                jax.ShapeDtypeStruct((blocks, parts, samples), bf16),
                jax.ShapeDtypeStruct((blocks, parts, samples), bf16),
                table(2, bf16),
            ],
            1,
        ),
        [table(2, f32), pltpu.VMEM((count * 4, 8, samples), f32)],
        (idx, from_near, flat, from_far, own, w1, w2, w3, inner[1]), "forward_outer", 4,
    )
    g_far = lax.ppermute(g_far, "rec", far)
    g_near = lax.ppermute(g_near, "rec", near)
    gown, part = call(
        backward_inner, (4, 4), ([table(1, bf16), pltpu.VMEM(total, f32)], 0), [table(1, f32)],
        (idx, g, wo, wm, own, *inner), "backward_inner", 2,
    )
    keep, send = call(
        backward_outer, (8, 4), ([jax.ShapeDtypeStruct((40, 2 * channels), f32)] * 2, 0),
        [table(1, bf16), table(1, f32), pltpu.VMEM(total, f32), pltpu.VMEM((2, 40, 2 * channels), f32)],
        (idx, g_near, g_far, wo, wm, own, halo, gown, part, *outer), "backward_outer", 2,
    )

    def swap(value, k):
        return lax.ppermute(value, "rec", [(s, s ^ k) for s in range(count)])

    if count & (count - 1):
        core = lax.rem(me, 2)
        both = jnp.where(core == 0, jnp.stack([keep, send]), jnp.stack([send, keep]))
        both = lax.psum(both, "rec")
        mine, other = both[core], both[1 - core]
    else:
        mine, k = keep + swap(send, 1), 2
        while k < count:
            got = [swap(mine, k * n) for n in range(1, 4 if 4 * k <= count else 2)]
            mine = mine + got[0] if len(got) == 1 else (mine + got[0]) + (got[1] + got[2])
            k *= len(got) + 1
        other = swap(mine, 1)

    scale = 1.0 / math.sqrt(parts * blocks * count * traces * samples)
    g_in, g_bin, g_mid, g_bmid, g_out = pl.pallas_call(
        functools.partial(finish_kernel, scale),
        out_shape=[
            jax.ShapeDtypeStruct(shape, f32)
            for shape in (
                (parts * 9, channels), (1, channels), (channels, channels), (1, channels),
                (parts * 9, channels),
            )
        ],
        in_specs=[VMEM] * 2,
        out_specs=[VMEM] * 5,
        scratch_shapes=[pltpu.VMEM((2, *keep.shape), f32)],
        compiler_params=params,
        name="finish",
    )(mine, other)
    return (
        res,
        g_in.T,
        g_bin.reshape(channels),
        g_mid,
        g_bmid.reshape(channels),
        g_out.T,
    )


def solution(mesh):
    return jax.shard_map(
        local,
        mesh=mesh,
        in_specs=(
            P(None, ("groups", "rec"), None, None),
            P("groups", None),
            P(),
            P(),
            P(),
            P(),
            P(),
        ),
        out_specs=(
            P(None, ("groups", "rec"), None, None),
            P("groups", None),
            P("groups"),
            P("groups", None),
            P("groups"),
            P("groups", None),
        ),
        check_vma=False,
    )
```

```python
import functools
import math

import jax
import jax.numpy as jnp
from jax import lax
from jax.experimental import pallas as pl
from jax.experimental.pallas import tpu as pltpu
from jax.sharding import PartitionSpec as P

CAP = 2
VMEM = pl.BlockSpec(memory_space=pltpu.VMEM)
SMEM = pl.BlockSpec(memory_space=pltpu.SMEM)
RESIDENT = 24 << 20


def run(start, step, end, steps, blocked):
    if blocked:
        n = pl.program_id(0)
        pl.when(n == 0)(start)
        step(n, 0)
        pl.when(n == steps - 1)(end)
        return
    start()
    lax.fori_loop(0, steps, lambda n, carry: step(n, n), None)
    end()


def group_of(owners):
    for size in (32, 16, 8, 4, 2):
        if owners % size == 0:
            return size
    return 1


def fill_table(table, wide, pieces, tiles, flip, fill):
    for n, piece in enumerate(pieces):
        x = piece[...].astype(jnp.float32)
        samples = x.shape[2]
        lane = lax.broadcasted_iota(jnp.int32, x.shape, 2)
        before = jnp.where(lane == 0, 0.0, pltpu.roll(x, 1, 2))
        after = jnp.where(lane == samples - 1, 0.0, pltpu.roll(x, samples - 1, 2))
        at = pl.ds(n * tiles, tiles)
        wide[at, 0:4, :] = after if flip else before
        wide[at, 4:8, :] = x
        wide[at, 8:12, :] = before if flip else after
    last = len(pieces) * tiles
    wide[pl.ds(last, 2), 0:12, :] = jnp.zeros((2, 12, wide.shape[2]), jnp.float32)
    wide[:, 12:16, :] = jnp.full((last + 2, 4, wide.shape[2]), fill, jnp.float32)
    table[...] = wide[...].astype(jnp.bfloat16)


def act(y):
    t = jnp.tanh(y)
    q = 1.0 + t
    a = y * q
    return t, q, a


def lines_of(idx, own, halo, owners):
    lines = []
    for e in owners:
        line = []
        for r in range(4):
            held = own if r in (1, 2) else halo
            line += [None, None] if held is None else [held[idx[r, e]], held[idx[r, e] + 1]]
        lines.append(line)
    return lines


def stack(lines, traces, flip):
    return jnp.concatenate(
        [
            jnp.concatenate(
                [line[h + 1 + (2 - i if flip else i)] for line in lines for h in traces], axis=1
            )
            for i in range(3)
        ],
        axis=0,
    )


def layers(inputs, w1, w2):
    y1 = jnp.dot(w1[...], inputs, preferred_element_type=jnp.float32)
    t, q, a = act(y1)
    d1 = q + a * (1.0 - t)
    a1 = a.astype(jnp.bfloat16)
    ones = jnp.ones((16, a1.shape[1]), jnp.bfloat16)
    y2 = jnp.dot(w2[...], jnp.concatenate([a1, ones], axis=0), preferred_element_type=jnp.float32)
    t, q, a = act(y2)
    return a1, d1, a, q + a * (1.0 - t)


def forward_inner(
    group, blocked, idx, mine, w1, w2, own, a1_ref, a2_ref, d1_ref, d2_ref, wide
):
    owners = lax.axis_size("rec")

    def start():
        fill_table(own, wide, (mine,), mine.shape[0], False, 1.0)

    def step(n, block):
        lines = lines_of(idx, own, None, [n * group + u for u in range(group)])
        a1, d1, a2, d2 = layers(stack(lines, (1, 2), False), w1, w2)
        a1_ref[block] = a1
        d1_ref[block] = d1
        a2_ref[block] = a2.astype(jnp.bfloat16)
        d2_ref[block] = d2

    run(start, step, lambda: None, owners // group, blocked)


def forward_outer(
    group, blocked, idx, near, mine, far, own, w1, w2, w3, inner,
    res, g, halo, a1_ref, a2_ref, d1_ref, d2_ref, wide, est,
):
    tiles, parts, samples = mine.shape
    count = lax.axis_size("rec")
    me = lax.axis_index("rec")
    has_left = (me > 0).astype(jnp.float32)
    has_right = (me < count - 1).astype(jnp.float32)
    lane = lax.broadcasted_iota(jnp.int32, (8, samples), 1)
    low = (lane > 0).astype(jnp.float32)
    high = (lane < samples - 1).astype(jnp.float32)

    def start():
        fill_table(halo, wide, (near, far), tiles, False, 1.0)

    def step(n, block):
        lines = lines_of(idx, own, halo, [n * group + u for u in range(group)])
        a1, d1, a2, d2 = layers(stack(lines, (-1, 0, 3, 4), False), w1, w2)
        cut = lambda x, u, k: x[:, (u * 4 + k) * samples : (u * 4 + k + 1) * samples]
        middle = lambda x: jnp.concatenate(
            [cut(x, u, k) for u in range(group) for k in (1, 2)], axis=1
        )
        a1_ref[block] = middle(a1)
        d1_ref[block] = middle(d1)
        d2_ref[block] = middle(d2)
        rows = []
        for u in range(group):
            row = [cut(a2, u, 0) * has_left, cut(a2, u, 1), cut(a2, u, 2), cut(a2, u, 3) * has_right]
            row = [part.astype(jnp.bfloat16) for part in row]
            within = [
                inner[block, :, (u * 2 + k) * samples : (u * 2 + k + 1) * samples] for k in range(2)
            ]
            rows.append(row[0:2] + within + row[2:4])
        a2_ref[block] = jnp.concatenate([row[k] for row in rows for k in (1, 4)], axis=1)
        rhs = jnp.concatenate(
            [
                jnp.concatenate([row[h + i] for row in rows for h in range(4)], axis=1)
                for i in range(3)
            ],
            axis=0,
        )
        terms = jnp.dot(w3[...], rhs, preferred_element_type=jnp.float32)
        for k in range(group * 4):
            part = terms[:, k * samples : (k + 1) * samples]
            total = (
                part[8:16]
                + pltpu.roll(part[0:8], 1, 1) * low
                + pltpu.roll(part[16:24], samples - 1, 1) * high
            )
            est[n * group * 4 + k] = total.astype(jnp.bfloat16).astype(jnp.float32)

    def end():
        for c in range(tiles // 2):
            at = [idx[4 + v, tiles // 2 + c] for v in range(4)]
            for k in range(2):
                total = (est[at[0] + k] + est[at[1] + k]) + (est[at[2] + k] + est[at[3] + k])
                value = total[0:parts] - mine[c * 2 + k].astype(jnp.float32)
                for o in range(parts):
                    res[o, c, k : k + 1, :] = value[o : o + 1]
                g[c * 2 + k] = value.astype(jnp.bfloat16)

    run(start, step, end, count // group, blocked)


def weight_terms(acc, fields, inputs, wo, wm, a1, a2, d1, d2):
    channels = wm.shape[0]
    da2 = jnp.dot(wo[...], fields, preferred_element_type=jnp.float32)
    dz2 = (da2 * d2).astype(jnp.bfloat16)
    acc[0:48, :] += product(fields, a2, (1, 1))
    da1 = jnp.dot(wm[...], dz2, preferred_element_type=jnp.float32)
    ones = jnp.ones((16, dz2.shape[1]), jnp.bfloat16)
    acc[48 : 64 + channels, :] += product(jnp.concatenate([a1, ones], axis=0), dz2, (1, 1))
    dz1 = (da1 * d1).astype(jnp.bfloat16)
    acc[64 + channels : 112 + channels, :] += product(inputs, dz1, (1, 1))


def backward_inner(
    group, blocked, idx, mine, wo, wm, own, a1_ref, a2_ref, d1_ref, d2_ref, gown, acc, wide
):
    owners = lax.axis_size("rec")

    def start():
        fill_table(gown, wide, (mine,), mine.shape[0], True, 0.0)
        acc[...] = jnp.zeros_like(acc)

    def step(n, block):
        es = [n * group + u for u in range(group)]
        fields = stack(lines_of(idx, gown, None, es), (1, 2), True)
        inputs = stack(lines_of(idx, own, None, es), (1, 2), False)
        saved = a1_ref[block], a2_ref[block], d1_ref[block], d2_ref[block]
        weight_terms(acc, fields, inputs, wo, wm, *saved)

    run(start, step, lambda: None, owners // group, blocked)


def backward_outer(
    group, blocked, idx, near, far, wo, wm, own, halo, gown, sums, a1_ref, a2_ref, d1_ref, d2_ref,
    out, ghalo, wide, acc,
):
    owners = lax.axis_size("rec")
    channels = wm.shape[0]
    taps = 9 * near.shape[1]

    def start():
        fill_table(ghalo, wide, (near, far), near.shape[0], True, 0.0)
        acc[...] = sums[...]

    def step(n, block):
        es = [n * group + u for u in range(group)]
        fields = stack(lines_of(idx, gown, ghalo, es), (0, 3), True)
        inputs = stack(lines_of(idx, own, halo, es), (0, 3), False)
        saved = a1_ref[block], a2_ref[block], d1_ref[block], d2_ref[block]
        weight_terms(acc, fields, inputs, wo, wm, *saved)

    def end():
        first, half = 64 + channels, channels // 2
        low, high = slice(0, channels), slice(channels, 2 * channels)
        one = out.at[0]
        for k in range(taps):
            at = k % 9 // 3 * 16 + k % 3 * 4 + k // 9
            one[half + k : half + k + 1, low] = acc[first + at : first + at + 1, :]
            one[half + k : half + k + 1, high] = acc[at : at + 1, :]
        middle = acc[48 : 48 + channels, :].T
        one[0:half, low] = middle[0:half]
        one[0:half, high] = middle[half:channels]
        one[half + taps : half + taps + 1, low] = acc[first + 28 : first + 29, :]
        one[half + taps : half + taps + 1, high] = acc[48 + channels : 49 + channels, :]
        rest = out.shape[1] - half - taps - 1
        one[half + taps + 1 :, :] = jnp.zeros((rest, 2 * channels), jnp.float32)
        for n in range(1, out.shape[0]):
            out[n] = one[...]

    run(start, step, end, owners // group, blocked)


def added(terms):
    values = [terms[n] for n in range(terms.shape[0])]
    while len(values) > 1:
        values = [sum(values[k : k + 2]) for k in range(0, len(values), 2)]
    return values[0]


def add_kernel(terms, out):
    total = added(terms)
    for n in range(out.shape[0]):
        out[n] = total


def finish_kernel(scale, terms, g_in, g_bin, g_mid, g_bmid, g_out, held):
    held[...] = added(terms) * scale
    channels = g_mid.shape[0]
    half, taps = channels // 2, g_in.shape[0]
    low, high = slice(0, channels), slice(channels, 2 * channels)
    g_mid[0:half] = held[0:half, low]
    g_mid[half:channels] = held[0:half, high]
    g_in[...] = held[half : half + taps, low]
    g_out[...] = held[half : half + taps, high]
    g_bin[...] = held[half + taps : half + taps + 1, low]
    g_bmid[...] = held[half + taps : half + taps + 1, high]


def halves(b):
    high = b.astype(jnp.bfloat16).astype(jnp.float32)
    rest = b - high
    mid = rest.astype(jnp.bfloat16).astype(jnp.float32)
    return [high, mid, rest - mid]


def one_hot(a, b):
    return (a == b).astype(jnp.float32).astype(jnp.bfloat16)


def iota(shape, dim):
    return lax.broadcasted_iota(jnp.int32, shape, dim)


def product(a, b, over):
    return lax.dot_general(
        a, b, dimension_numbers=(((over[0],), (over[1],)), ((), ())),
        preferred_element_type=jnp.float32,
    )


def prep_kernel(blocks, *refs):
    args, (idx, w1, w2, w3, wo, wm, rows), held, sems = refs[:6], refs[6:13], refs[13:19], refs[19]
    copies = [
        pltpu.make_async_copy(src, dst, sems.at[n]) for n, (src, dst) in enumerate(zip(args, held))
    ]
    for copy in copies:
        copy.start()
    for copy in copies:
        copy.wait()
    dest, w_in, b_in, w_mid, b_mid, w_out = held
    count = lax.axis_size("rec")
    me = lax.axis_index("rec")
    ves, total = dest.shape
    channels = w_mid.shape[0]
    at = lax.rem((count + 1 - me) * blocks, total)
    wide = jnp.concatenate([dest[...], jnp.zeros((8 - ves, total), jnp.int32)], axis=0)
    near = pltpu.roll(wide, at, 1)[:, 0:128]
    lane = iota((8, 128), 1)
    low = jnp.where(me > 0, 0, blocks)
    high = jnp.where(me < count - 1, 3 * blocks, 2 * blocks)
    near = jnp.where((lane >= low) & (lane < high), near, -1)
    owner = iota((count, 128), 0)
    hits = [(near[v : v + 1] == owner).astype(jnp.float32) for v in range(ves)]
    before = iota((128, 128), 0)
    after = iota((128, 128), 1)
    segment = (after >= blocks).astype(jnp.int32) + (after >= 2 * blocks).astype(jnp.int32)
    tri = ((before < after) & (before >= segment * blocks)).astype(jnp.float32).astype(jnp.bfloat16)
    rank = product((hits[0] + hits[1] + hits[2] + hits[3]).astype(jnp.bfloat16), tri, (1, 0))
    zeroth = jnp.zeros((count, 128), jnp.float32)
    first = jnp.zeros((count, 128), jnp.float32)
    for v in range(ves):
        zeroth += hits[v] * (rank == 0.0).astype(jnp.float32)
        first += hits[v] * (rank == 1.0).astype(jnp.float32)
        item = jnp.sum(hits[v] * rank, axis=0, keepdims=True)
        idx[4 + v : 5 + v, 0:128] = near[v : v + 1] * 4 + item.astype(jnp.int32) * 2
        rank = rank + hits[v]
    line = iota((8, 128), 0)
    inside = lambda k: (lane >= k * blocks) & (lane < (k + 1) * blocks)
    odd = lax.rem(me, 2)
    left = 2 * lane + 2 * blocks * (1 - odd) - 4 * blocks
    middle = 2 * (lane - blocks) - 2 * blocks
    right = 2 * (lane - 2 * blocks) + 2 * blocks * odd - 4 * blocks
    put = lambda r, k, place: jnp.where((line == r) & inside(k), place, 0)
    pick = product(
        (put(0, 0, left) + put(2, 1, middle)).astype(jnp.float32).astype(jnp.bfloat16),
        first.astype(jnp.bfloat16),
        (1, 1),
    ) + product(
        (put(1, 1, middle) + put(3, 2, right)).astype(jnp.float32).astype(jnp.bfloat16),
        zeroth.astype(jnp.bfloat16),
        (1, 1),
    )
    empty = jnp.where((line == 0) | (line == 3), 4 * blocks, 2 * blocks)[0:4, 0:1]
    idx[0:4, 0:count] = pick[0:4].astype(jnp.int32) + empty

    taps = w_in.shape[0]
    row, col = iota((48, 40), 0), iota((48, 40), 1)
    tap, extra = row & 15, (row & 15) - 12
    target = (row & 3) * 9 + 3 * (row >> 4) + ((row >> 2) & 3)
    target = jnp.where(tap < 12, target, jnp.where((row >> 4) == 1, taps + extra, -1))
    order = one_hot(col, target)
    rows[...] = jnp.zeros_like(rows)
    rows[0:taps, :] = w_in[...].astype(jnp.float32)
    for n, part in enumerate(halves(b_in[...])):
        rows[taps + n : taps + n + 1, :] = part
    w1[...] = (0.5 * product(rows[...].astype(jnp.bfloat16), order, (0, 1))).astype(jnp.bfloat16)
    rows[...] = jnp.zeros_like(rows)
    for n, part in enumerate(halves(b_mid[...])):
        rows[n : n + 1, :] = part
    row, col = iota((40, channels + 16), 0), iota((40, channels + 16), 1)
    bias = product(rows[...].astype(jnp.bfloat16), one_hot(col, row + channels), (0, 0))
    row, col = iota((channels, channels + 16), 0), iota((channels, channels + 16), 1)
    w2[...] = (0.5 * (product(w_mid[...], one_hot(row, col), (1, 0)) + bias)).astype(jnp.bfloat16)
    rows[...] = jnp.zeros_like(rows)
    rows[0:taps, :] = w_out[...].astype(jnp.float32)
    outs = rows[...].astype(jnp.bfloat16)
    wo[...] = (0.5 * product(outs, order, (0, 1))).astype(jnp.bfloat16)
    row, col = iota((24, 40), 0), iota((24, 40), 1)
    for i in range(3):
        target = jnp.where((row & 7) < 4, (row & 3) * 9 + 3 * i + (row >> 3), -1)
        part = product(one_hot(col, target), outs, (1, 0))
        w3[:, i * channels : (i + 1) * channels] = part.astype(jnp.bfloat16)
    eye = one_hot(iota((channels, channels), 0), iota((channels, channels), 1))
    wm[...] = (0.5 * product(w_mid[...], eye, (0, 0))).astype(jnp.bfloat16)


def local(records, dest, w_in, b_in, w_mid, b_mid, w_out):
    count = lax.axis_size("rec")
    me = lax.axis_index("rec")
    parts, blocks, traces, samples = records.shape
    ves = dest.shape[1]
    tiles = blocks * traces
    channels = w_in.shape[0]
    group = group_of(count)
    steps = count // group
    width = group * 2 * samples
    far = [(s, s + 1) for s in range(1, count - 1, 2)]
    far += [(b, a) for a, b in far]
    near = [(s, s + 1) for s in range(0, count - 1, 2)]
    near += [(b, a) for a, b in near]

    flat = records.transpose(1, 2, 0, 3).reshape(tiles, parts, samples)
    from_far = lax.ppermute(flat, "rec", far)
    from_near = lax.ppermute(flat, "rec", near)

    f32, bf16 = jnp.float32, jnp.bfloat16
    shape = (steps, channels, width)
    blocked = 24 * math.prod(shape) > RESIDENT
    saved = [
        jax.ShapeDtypeStruct(shape, kind) if blocked else pltpu.VMEM(shape, kind)
        for kind in (bf16, bf16, f32, f32)
    ]
    held = [VMEM] * 4
    if blocked:
        held = [pl.BlockSpec((1, channels, width), lambda n: (n, 0, 0))] * 4
    grid = (steps,) if blocked else ()
    params = pltpu.CompilerParams(vmem_limit_bytes=16 << 20)
    args = (
        dest.T, w_in.T, b_in.reshape(1, channels), w_mid, b_mid.reshape(1, channels), w_out.T
    )
    idx, w1, w2, w3, wo, wm = pl.pallas_call(
        functools.partial(prep_kernel, blocks),
        out_shape=[jax.ShapeDtypeStruct((8, max(128, count)), jnp.int32)]
        + [
            jax.ShapeDtypeStruct(size, bf16)
            for size in (
                (channels, 48), (channels, channels + 16), (24, 3 * channels), (channels, 48),
                (channels, channels),
            )
        ],
        in_specs=[pl.BlockSpec(memory_space=pltpu.HBM)] * 6,
        out_specs=[VMEM] * 6,
        scratch_shapes=[pltpu.VMEM((40, channels), f32)]
        + [pltpu.VMEM(arg.shape, arg.dtype) for arg in args]
        + [pltpu.SemaphoreType.DMA((6,))],
        compiler_params=params,
        name="prepare",
    )(*[pltpu.with_memory_space_constraint(arg, pltpu.HBM) for arg in args])
    def table(pieces, kind):
        return pltpu.VMEM((pieces * tiles + 2, 16, samples), kind)

    def call(kernel, ins, outs, scratch, args, name, owned):
        return pl.pallas_call(
            functools.partial(kernel, group, blocked),
            grid=grid,
            out_shape=outs[0] + saved * outs[1],
            in_specs=[SMEM] + [VMEM] * ins[0] + held[:1] * ins[1],
            out_specs=[VMEM] * len(outs[0]) + held * outs[1],
            scratch_shapes=scratch,
            compiler_params=params,
            cost_estimate=pl.CostEstimate(
                flops=2 * owned * count * samples * channels * (3 * channels),
                bytes_accessed=owned * count * samples * channels * 12,
                transcendentals=0,
            ),
            name=name,
        )(*args)

    total = (112 + channels, channels)
    rows = (channels // 2 + 9 * parts + 1 + 7) // 8 * 8
    near_by = math.gcd(count, 8)
    far_off = count // near_by
    own, *inner = call(
        forward_inner, (3, 0), ([table(1, bf16)], 1), [table(1, f32)],
        (idx, flat, w1, w2), "forward_inner", 2,
    )
    res, g, halo, *outer = call(
        forward_outer, (7, 1),
        (
            [
                jax.ShapeDtypeStruct(records.shape, f32),
                jax.ShapeDtypeStruct((tiles, parts, samples), bf16),
                table(2, bf16),
            ],
            1,
        ),
        [table(2, f32), pltpu.VMEM((count * 4, 8, samples), f32)],
        (idx, from_near, flat, from_far, own, w1, w2, w3, inner[1]), "forward_outer", 4,
    )
    g_far = lax.ppermute(g, "rec", far)
    g_near = lax.ppermute(g, "rec", near)
    gown, part = call(
        backward_inner, (4, 4), ([table(1, bf16), pltpu.VMEM(total, f32)], 0), [table(1, f32)],
        (idx, g, wo, wm, own, *inner), "backward_inner", 2,
    )
    (sums,) = call(
        backward_outer, (8, 4), ([jax.ShapeDtypeStruct((near_by, rows, 2 * channels), f32)], 0),
        [table(2, bf16), table(2, f32), pltpu.VMEM(total, f32)],
        (idx, g_near, g_far, wo, wm, own, halo, gown, part, *outer), "backward_outer", 2,
    )

    def spread(copies, groups):
        return lax.all_to_all(copies, "rec", 0, 0, axis_index_groups=groups, tiled=True)

    terms = spread(sums, [[n * near_by + k for k in range(near_by)] for n in range(far_off)])
    terms = pl.pallas_call(
        add_kernel,
        out_shape=jax.ShapeDtypeStruct((far_off, rows, 2 * channels), f32),
        in_specs=[VMEM],
        out_specs=VMEM,
        compiler_params=params,
        name="add",
    )(terms)
    terms = spread(terms, [[n * near_by + k for n in range(far_off)] for k in range(near_by)])

    scale = 1.0 / math.sqrt(parts * blocks * count * traces * samples)
    g_in, g_bin, g_mid, g_bmid, g_out = pl.pallas_call(
        functools.partial(finish_kernel, scale),
        out_shape=[
            jax.ShapeDtypeStruct(shape, f32)
            for shape in (
                (parts * 9, channels), (1, channels), (channels, channels), (1, channels),
                (parts * 9, channels),
            )
        ],
        in_specs=[VMEM],
        out_specs=[VMEM] * 5,
        scratch_shapes=[pltpu.VMEM((rows, 2 * channels), f32)],
        compiler_params=params,
        name="finish",
    )(terms)
    return (
        res,
        g_in.T,
        g_bin.reshape(channels),
        g_mid,
        g_bmid.reshape(channels),
        g_out.T,
    )


def solution(mesh):
    return jax.shard_map(
        local,
        mesh=mesh,
        in_specs=(
            P(None, ("groups", "rec"), None, None),
            P("groups", None),
            P(),
            P(),
            P(),
            P(),
            P(),
        ),
        out_specs=(
            P(None, ("groups", "rec"), None, None),
            P("groups", None),
            P("groups"),
            P("groups", None),
            P("groups"),
            P("groups", None),
        ),
        check_vma=False,
    )
```

```python
import functools
import math

import jax
import jax.numpy as jnp
from jax import lax
from jax.experimental import pallas as pl
from jax.experimental.pallas import tpu as pltpu
from jax.sharding import PartitionSpec as P

CAP = 2
VMEM = pl.BlockSpec(memory_space=pltpu.VMEM)
SMEM = pl.BlockSpec(memory_space=pltpu.SMEM)
RESIDENT = 24 << 20


def run(start, step, end, steps, blocked):
    if blocked:
        n = pl.program_id(0)
        pl.when(n == 0)(start)
        step(n, 0)
        pl.when(n == steps - 1)(end)
        return
    start()
    lax.fori_loop(0, steps, lambda n, carry: step(n, n), None)
    end()


def group_of(owners):
    for size in (32, 16, 8, 4, 2):
        if owners % size == 0:
            return size
    return 1


def fill_table(table, wide, pieces, tiles, flip, fill):
    for n, piece in enumerate(pieces):
        x = piece[...].astype(jnp.float32)
        samples = x.shape[2]
        lane = lax.broadcasted_iota(jnp.int32, x.shape, 2)
        before = jnp.where(lane == 0, 0.0, pltpu.roll(x, 1, 2))
        after = jnp.where(lane == samples - 1, 0.0, pltpu.roll(x, samples - 1, 2))
        at = pl.ds(n * tiles, tiles)
        wide[at, 0:4, :] = after if flip else before
        wide[at, 4:8, :] = x
        wide[at, 8:12, :] = before if flip else after
    last = len(pieces) * tiles
    wide[pl.ds(last, 2), 0:12, :] = jnp.zeros((2, 12, wide.shape[2]), jnp.float32)
    wide[:, 12:16, :] = jnp.full((last + 2, 4, wide.shape[2]), fill, jnp.float32)
    table[...] = wide[...].astype(jnp.bfloat16)


def act(y):
    t = jnp.tanh(y)
    q = 1.0 + t
    a = y * q
    return t, q, a


def lines_of(idx, own, halo, owners):
    lines = []
    for e in owners:
        line = []
        for r in range(4):
            held = own if r in (1, 2) else halo
            line += [None, None] if held is None else [held[idx[r, e]], held[idx[r, e] + 1]]
        lines.append(line)
    return lines


def stack(lines, traces, flip):
    return jnp.concatenate(
        [
            jnp.concatenate(
                [line[h + 1 + (2 - i if flip else i)] for line in lines for h in traces], axis=1
            )
            for i in range(3)
        ],
        axis=0,
    )


def layers(inputs, w1, w2):
    y1 = jnp.dot(w1[...], inputs, preferred_element_type=jnp.float32)
    t, q, a = act(y1)
    d1 = q + a * (1.0 - t)
    a1 = a.astype(jnp.bfloat16)
    ones = jnp.ones((16, a1.shape[1]), jnp.bfloat16)
    y2 = jnp.dot(w2[...], jnp.concatenate([a1, ones], axis=0), preferred_element_type=jnp.float32)
    t, q, a = act(y2)
    return a1, d1, a, q + a * (1.0 - t)


def forward_inner(
    group, blocked, idx, mine, w1, w2, own, a1_ref, a2_ref, d1_ref, d2_ref, wide
):
    owners = lax.axis_size("rec")

    def start():
        fill_table(own, wide, (mine,), mine.shape[0], False, 1.0)

    def step(n, block):
        lines = lines_of(idx, own, None, [n * group + u for u in range(group)])
        a1, d1, a2, d2 = layers(stack(lines, (1, 2), False), w1, w2)
        a1_ref[block] = a1
        d1_ref[block] = d1
        a2_ref[block] = a2.astype(jnp.bfloat16)
        d2_ref[block] = d2

    run(start, step, lambda: None, owners // group, blocked)


def forward_outer(
    group, blocked, idx, near, mine, far, own, w1, w2, w3, inner,
    res, g, halo, a1_ref, a2_ref, d1_ref, d2_ref, wide, est,
):
    tiles, parts, samples = mine.shape
    count = lax.axis_size("rec")
    me = lax.axis_index("rec")
    has_left = (me > 0).astype(jnp.float32)
    has_right = (me < count - 1).astype(jnp.float32)
    lane = lax.broadcasted_iota(jnp.int32, (8, samples), 1)
    low = (lane > 0).astype(jnp.float32)
    high = (lane < samples - 1).astype(jnp.float32)

    def start():
        fill_table(halo, wide, (near, far), tiles, False, 1.0)

    def step(n, block):
        lines = lines_of(idx, own, halo, [n * group + u for u in range(group)])
        a1, d1, a2, d2 = layers(stack(lines, (-1, 0, 3, 4), False), w1, w2)
        cut = lambda x, u, k: x[:, (u * 4 + k) * samples : (u * 4 + k + 1) * samples]
        middle = lambda x: jnp.concatenate(
            [cut(x, u, k) for u in range(group) for k in (1, 2)], axis=1
        )
        a1_ref[block] = middle(a1)
        d1_ref[block] = middle(d1)
        d2_ref[block] = middle(d2)
        rows = []
        for u in range(group):
            row = [cut(a2, u, 0) * has_left, cut(a2, u, 1), cut(a2, u, 2), cut(a2, u, 3) * has_right]
            row = [part.astype(jnp.bfloat16) for part in row]
            within = [
                inner[block, :, (u * 2 + k) * samples : (u * 2 + k + 1) * samples] for k in range(2)
            ]
            rows.append(row[0:2] + within + row[2:4])
        a2_ref[block] = jnp.concatenate([row[k] for row in rows for k in (1, 4)], axis=1)
        rhs = jnp.concatenate(
            [
                jnp.concatenate([row[h + i] for row in rows for h in range(4)], axis=1)
                for i in range(3)
            ],
            axis=0,
        )
        terms = jnp.dot(w3[...], rhs, preferred_element_type=jnp.float32)
        for k in range(group * 4):
            part = terms[:, k * samples : (k + 1) * samples]
            total = (
                part[8:16]
                + pltpu.roll(part[0:8], 1, 1) * low
                + pltpu.roll(part[16:24], samples - 1, 1) * high
            )
            est[n * group * 4 + k] = total.astype(jnp.bfloat16).astype(jnp.float32)

    def end():
        for c in range(tiles // 2):
            at = [idx[4 + v, tiles // 2 + c] for v in range(4)]
            for k in range(2):
                total = (est[at[0] + k] + est[at[1] + k]) + (est[at[2] + k] + est[at[3] + k])
                value = total[0:parts] - mine[c * 2 + k].astype(jnp.float32)
                for o in range(parts):
                    res[o, c, k : k + 1, :] = value[o : o + 1]
                g[c * 2 + k] = value.astype(jnp.bfloat16)

    run(start, step, end, count // group, blocked)


def weight_terms(acc, fields, inputs, wo, wm, a1, a2, d1, d2):
    channels = wm.shape[0]
    da2 = jnp.dot(wo[...], fields, preferred_element_type=jnp.float32)
    dz2 = (da2 * d2).astype(jnp.bfloat16)
    acc[0:48, :] += product(fields, a2, (1, 1))
    da1 = jnp.dot(wm[...], dz2, preferred_element_type=jnp.float32)
    ones = jnp.ones((16, dz2.shape[1]), jnp.bfloat16)
    acc[48 : 64 + channels, :] += product(jnp.concatenate([a1, ones], axis=0), dz2, (1, 1))
    dz1 = (da1 * d1).astype(jnp.bfloat16)
    acc[64 + channels : 112 + channels, :] += product(inputs, dz1, (1, 1))


def backward_inner(
    group, blocked, idx, mine, wo, wm, own, a1_ref, a2_ref, d1_ref, d2_ref, gown, acc, wide
):
    owners = lax.axis_size("rec")

    def start():
        fill_table(gown, wide, (mine,), mine.shape[0], True, 0.0)
        acc[...] = jnp.zeros_like(acc)

    def step(n, block):
        es = [n * group + u for u in range(group)]
        fields = stack(lines_of(idx, gown, None, es), (1, 2), True)
        inputs = stack(lines_of(idx, own, None, es), (1, 2), False)
        saved = a1_ref[block], a2_ref[block], d1_ref[block], d2_ref[block]
        weight_terms(acc, fields, inputs, wo, wm, *saved)

    run(start, step, lambda: None, owners // group, blocked)


def backward_outer(
    group, blocked, idx, near, far, wo, wm, own, halo, gown, sums, a1_ref, a2_ref, d1_ref, d2_ref,
    out, ghalo, wide, acc, flat,
):
    owners = lax.axis_size("rec")
    channels = wm.shape[0]
    taps = 9 * near.shape[1]

    def start():
        fill_table(ghalo, wide, (near, far), near.shape[0], True, 0.0)
        acc[...] = sums[...]

    def step(n, block):
        es = [n * group + u for u in range(group)]
        fields = stack(lines_of(idx, gown, ghalo, es), (0, 3), True)
        inputs = stack(lines_of(idx, own, halo, es), (0, 3), False)
        saved = a1_ref[block], a2_ref[block], d1_ref[block], d2_ref[block]
        weight_terms(acc, fields, inputs, wo, wm, *saved)

    def end():
        first, half = 64 + channels, channels // 2
        low, high = slice(0, channels), slice(channels, 2 * channels)
        one = flat
        for k in range(taps):
            at = k % 9 // 3 * 16 + k % 3 * 4 + k // 9
            one[half + k : half + k + 1, low] = acc[first + at : first + at + 1, :]
            one[half + k : half + k + 1, high] = acc[at : at + 1, :]
        middle = acc[48 : 48 + channels, :].T
        one[0:half, low] = middle[0:half]
        one[0:half, high] = middle[half:channels]
        one[half + taps : half + taps + 1, low] = acc[first + 28 : first + 29, :]
        one[half + taps : half + taps + 1, high] = acc[48 + channels : 49 + channels, :]
        rest = flat.shape[0] - half - taps - 1
        one[half + taps + 1 :, :] = jnp.zeros((rest, 2 * channels), jnp.float32)
        pieces = out.shape[1]
        for n in range(out.shape[0]):
            for k in range(pieces):
                at = (n * pieces + k) * 4
                out[n, k] = flat[at : at + 4, :]

    run(start, step, end, owners // group, blocked)


def added(terms):
    values = [terms[n] for n in range(terms.shape[0])]
    while len(values) > 1:
        values = [sum(values[k : k + 2]) for k in range(0, len(values), 2)]
    return values[0]


def add_kernel(terms, out):
    total = added(terms)
    for n in range(out.shape[0]):
        out[n] = total


def finish_kernel(scale, terms, g_in, g_bin, g_mid, g_bmid, g_out, held):
    pieces = terms.shape[1]
    for n in range(terms.shape[0]):
        for k in range(pieces):
            at = (n * pieces + k) * 4
            held[at : at + 4, :] = terms[n, k] * scale
    channels = g_mid.shape[0]
    half, taps = channels // 2, g_in.shape[0]
    low, high = slice(0, channels), slice(channels, 2 * channels)
    g_mid[0:half] = held[0:half, low]
    g_mid[half:channels] = held[0:half, high]
    g_in[...] = held[half : half + taps, low]
    g_out[...] = held[half : half + taps, high]
    g_bin[...] = held[half + taps : half + taps + 1, low]
    g_bmid[...] = held[half + taps : half + taps + 1, high]


def halves(b):
    high = b.astype(jnp.bfloat16).astype(jnp.float32)
    rest = b - high
    mid = rest.astype(jnp.bfloat16).astype(jnp.float32)
    return [high, mid, rest - mid]


def one_hot(a, b):
    return (a == b).astype(jnp.float32).astype(jnp.bfloat16)


def iota(shape, dim):
    return lax.broadcasted_iota(jnp.int32, shape, dim)


def product(a, b, over):
    return lax.dot_general(
        a, b, dimension_numbers=(((over[0],), (over[1],)), ((), ())),
        preferred_element_type=jnp.float32,
    )


def prep_kernel(blocks, *refs):
    args, (idx, w1, w2, w3, wo, wm, rows), held, sems = refs[:6], refs[6:13], refs[13:19], refs[19]
    copies = [
        pltpu.make_async_copy(src, dst, sems.at[n]) for n, (src, dst) in enumerate(zip(args, held))
    ]
    for copy in copies:
        copy.start()
    for copy in copies:
        copy.wait()
    dest, w_in, b_in, w_mid, b_mid, w_out = held
    count = lax.axis_size("rec")
    me = lax.axis_index("rec")
    ves, total = dest.shape
    channels = w_mid.shape[0]
    at = lax.rem((count + 1 - me) * blocks, total)
    wide = jnp.concatenate([dest[...], jnp.zeros((8 - ves, total), jnp.int32)], axis=0)
    near = pltpu.roll(wide, at, 1)[:, 0:128]
    lane = iota((8, 128), 1)
    low = jnp.where(me > 0, 0, blocks)
    high = jnp.where(me < count - 1, 3 * blocks, 2 * blocks)
    near = jnp.where((lane >= low) & (lane < high), near, -1)
    owner = iota((count, 128), 0)
    hits = [(near[v : v + 1] == owner).astype(jnp.float32) for v in range(ves)]
    before = iota((128, 128), 0)
    after = iota((128, 128), 1)
    segment = (after >= blocks).astype(jnp.int32) + (after >= 2 * blocks).astype(jnp.int32)
    tri = ((before < after) & (before >= segment * blocks)).astype(jnp.float32).astype(jnp.bfloat16)
    rank = product((hits[0] + hits[1] + hits[2] + hits[3]).astype(jnp.bfloat16), tri, (1, 0))
    zeroth = jnp.zeros((count, 128), jnp.float32)
    first = jnp.zeros((count, 128), jnp.float32)
    for v in range(ves):
        zeroth += hits[v] * (rank == 0.0).astype(jnp.float32)
        first += hits[v] * (rank == 1.0).astype(jnp.float32)
        item = jnp.sum(hits[v] * rank, axis=0, keepdims=True)
        idx[4 + v : 5 + v, 0:128] = near[v : v + 1] * 4 + item.astype(jnp.int32) * 2
        rank = rank + hits[v]
    line = iota((8, 128), 0)
    inside = lambda k: (lane >= k * blocks) & (lane < (k + 1) * blocks)
    odd = lax.rem(me, 2)
    left = 2 * lane + 2 * blocks * (1 - odd) - 4 * blocks
    middle = 2 * (lane - blocks) - 2 * blocks
    right = 2 * (lane - 2 * blocks) + 2 * blocks * odd - 4 * blocks
    put = lambda r, k, place: jnp.where((line == r) & inside(k), place, 0)
    pick = product(
        (put(0, 0, left) + put(2, 1, middle)).astype(jnp.float32).astype(jnp.bfloat16),
        first.astype(jnp.bfloat16),
        (1, 1),
    ) + product(
        (put(1, 1, middle) + put(3, 2, right)).astype(jnp.float32).astype(jnp.bfloat16),
        zeroth.astype(jnp.bfloat16),
        (1, 1),
    )
    empty = jnp.where((line == 0) | (line == 3), 4 * blocks, 2 * blocks)[0:4, 0:1]
    idx[0:4, 0:count] = pick[0:4].astype(jnp.int32) + empty

    taps = w_in.shape[0]
    row, col = iota((48, 40), 0), iota((48, 40), 1)
    tap, extra = row & 15, (row & 15) - 12
    target = (row & 3) * 9 + 3 * (row >> 4) + ((row >> 2) & 3)
    target = jnp.where(tap < 12, target, jnp.where((row >> 4) == 1, taps + extra, -1))
    order = one_hot(col, target)
    rows[...] = jnp.zeros_like(rows)
    rows[0:taps, :] = w_in[...].astype(jnp.float32)
    for n, part in enumerate(halves(b_in[...])):
        rows[taps + n : taps + n + 1, :] = part
    w1[...] = (0.5 * product(rows[...].astype(jnp.bfloat16), order, (0, 1))).astype(jnp.bfloat16)
    rows[...] = jnp.zeros_like(rows)
    for n, part in enumerate(halves(b_mid[...])):
        rows[n : n + 1, :] = part
    row, col = iota((40, channels + 16), 0), iota((40, channels + 16), 1)
    bias = product(rows[...].astype(jnp.bfloat16), one_hot(col, row + channels), (0, 0))
    row, col = iota((channels, channels + 16), 0), iota((channels, channels + 16), 1)
    w2[...] = (0.5 * (product(w_mid[...], one_hot(row, col), (1, 0)) + bias)).astype(jnp.bfloat16)
    rows[...] = jnp.zeros_like(rows)
    rows[0:taps, :] = w_out[...].astype(jnp.float32)
    outs = rows[...].astype(jnp.bfloat16)
    wo[...] = (0.5 * product(outs, order, (0, 1))).astype(jnp.bfloat16)
    row, col = iota((24, 40), 0), iota((24, 40), 1)
    for i in range(3):
        target = jnp.where((row & 7) < 4, (row & 3) * 9 + 3 * i + (row >> 3), -1)
        part = product(one_hot(col, target), outs, (1, 0))
        w3[:, i * channels : (i + 1) * channels] = part.astype(jnp.bfloat16)
    eye = one_hot(iota((channels, channels), 0), iota((channels, channels), 1))
    wm[...] = (0.5 * product(w_mid[...], eye, (0, 0))).astype(jnp.bfloat16)


def local(records, dest, w_in, b_in, w_mid, b_mid, w_out):
    count = lax.axis_size("rec")
    me = lax.axis_index("rec")
    parts, blocks, traces, samples = records.shape
    ves = dest.shape[1]
    tiles = blocks * traces
    channels = w_in.shape[0]
    group = group_of(count)
    steps = count // group
    width = group * 2 * samples
    far = [(s, s + 1) for s in range(1, count - 1, 2)]
    far += [(b, a) for a, b in far]
    near = [(s, s + 1) for s in range(0, count - 1, 2)]
    near += [(b, a) for a, b in near]

    flat = records.transpose(1, 2, 0, 3).reshape(tiles, parts, samples)
    from_far = lax.ppermute(flat, "rec", far)
    from_near = lax.ppermute(flat, "rec", near)

    f32, bf16 = jnp.float32, jnp.bfloat16
    shape = (steps, channels, width)
    blocked = 24 * math.prod(shape) > RESIDENT
    saved = [
        jax.ShapeDtypeStruct(shape, kind) if blocked else pltpu.VMEM(shape, kind)
        for kind in (bf16, bf16, f32, f32)
    ]
    held = [VMEM] * 4
    if blocked:
        held = [pl.BlockSpec((1, channels, width), lambda n: (n, 0, 0))] * 4
    grid = (steps,) if blocked else ()
    params = pltpu.CompilerParams(vmem_limit_bytes=16 << 20)
    args = (
        dest.T, w_in.T, b_in.reshape(1, channels), w_mid, b_mid.reshape(1, channels), w_out.T
    )
    idx, w1, w2, w3, wo, wm = pl.pallas_call(
        functools.partial(prep_kernel, blocks),
        out_shape=[jax.ShapeDtypeStruct((8, max(128, count)), jnp.int32)]
        + [
            jax.ShapeDtypeStruct(size, bf16)
            for size in (
                (channels, 48), (channels, channels + 16), (24, 3 * channels), (channels, 48),
                (channels, channels),
            )
        ],
        in_specs=[pl.BlockSpec(memory_space=pltpu.HBM)] * 6,
        out_specs=[VMEM] * 6,
        scratch_shapes=[pltpu.VMEM((40, channels), f32)]
        + [pltpu.VMEM(arg.shape, arg.dtype) for arg in args]
        + [pltpu.SemaphoreType.DMA((6,))],
        compiler_params=params,
        name="prepare",
    )(*[pltpu.with_memory_space_constraint(arg, pltpu.HBM) for arg in args])
    def table(pieces, kind):
        return pltpu.VMEM((pieces * tiles + 2, 16, samples), kind)

    def call(kernel, ins, outs, scratch, args, name, owned):
        return pl.pallas_call(
            functools.partial(kernel, group, blocked),
            grid=grid,
            out_shape=outs[0] + saved * outs[1],
            in_specs=[SMEM] + [VMEM] * ins[0] + held[:1] * ins[1],
            out_specs=[VMEM] * len(outs[0]) + held * outs[1],
            scratch_shapes=scratch,
            compiler_params=params,
            cost_estimate=pl.CostEstimate(
                flops=2 * owned * count * samples * channels * (3 * channels),
                bytes_accessed=owned * count * samples * channels * 12,
                transcendentals=0,
            ),
            name=name,
        )(*args)

    total = (112 + channels, channels)
    near_by = math.gcd(count, 8)
    pieces = -(-(channels // 2 + 9 * parts + 1) // (4 * near_by))
    rows = 4 * near_by * pieces
    far_off = count // near_by
    own, *inner = call(
        forward_inner, (3, 0), ([table(1, bf16)], 1), [table(1, f32)],
        (idx, flat, w1, w2), "forward_inner", 2,
    )
    res, g, halo, *outer = call(
        forward_outer, (7, 1),
        (
            [
                jax.ShapeDtypeStruct(records.shape, f32),
                jax.ShapeDtypeStruct((tiles, parts, samples), bf16),
                table(2, bf16),
            ],
            1,
        ),
        [table(2, f32), pltpu.VMEM((count * 4, 8, samples), f32)],
        (idx, from_near, flat, from_far, own, w1, w2, w3, inner[1]), "forward_outer", 4,
    )
    g_far = lax.ppermute(g, "rec", far)
    g_near = lax.ppermute(g, "rec", near)
    gown, part = call(
        backward_inner, (4, 4), ([table(1, bf16), pltpu.VMEM(total, f32)], 0), [table(1, f32)],
        (idx, g, wo, wm, own, *inner), "backward_inner", 2,
    )
    (sums,) = call(
        backward_outer, (8, 4), ([jax.ShapeDtypeStruct((near_by, pieces, 4, 2 * channels), f32)], 0),
        [table(2, bf16), table(2, f32), pltpu.VMEM(total, f32), pltpu.VMEM((rows, 2 * channels), f32)],
        (idx, g_near, g_far, wo, wm, own, halo, gown, part, *outer), "backward_outer", 2,
    )

    def spread(copies, groups):
        return lax.all_to_all(copies, "rec", 0, 0, axis_index_groups=groups, tiled=True)

    def add(terms, copies):
        return pl.pallas_call(
            add_kernel,
            out_shape=jax.ShapeDtypeStruct((copies, pieces, 4, 2 * channels), f32),
            in_specs=[VMEM],
            out_specs=VMEM,
            compiler_params=params,
            name="add",
        )(terms)

    inside = [[n * near_by + k for k in range(near_by)] for n in range(far_off)]
    across = [[n * near_by + k for n in range(far_off)] for k in range(near_by)]
    terms = add(spread(sums, inside), far_off)
    terms = spread(add(spread(terms, across), near_by), inside)

    scale = 1.0 / math.sqrt(parts * blocks * count * traces * samples)
    g_in, g_bin, g_mid, g_bmid, g_out = pl.pallas_call(
        functools.partial(finish_kernel, scale),
        out_shape=[
            jax.ShapeDtypeStruct(shape, f32)
            for shape in (
                (parts * 9, channels), (1, channels), (channels, channels), (1, channels),
                (parts * 9, channels),
            )
        ],
        in_specs=[VMEM],
        out_specs=[VMEM] * 5,
        scratch_shapes=[pltpu.VMEM((rows, 2 * channels), f32)],
        compiler_params=params,
        name="finish",
    )(terms)
    return (
        res,
        g_in.T,
        g_bin.reshape(channels),
        g_mid,
        g_bmid.reshape(channels),
        g_out.T,
    )


def solution(mesh):
    return jax.shard_map(
        local,
        mesh=mesh,
        in_specs=(
            P(None, ("groups", "rec"), None, None),
            P("groups", None),
            P(),
            P(),
            P(),
            P(),
            P(),
        ),
        out_specs=(
            P(None, ("groups", "rec"), None, None),
            P("groups", None),
            P("groups"),
            P("groups", None),
            P("groups"),
            P("groups", None),
        ),
        check_vma=False,
    )
```

```python
import functools
import math

import jax
import jax.numpy as jnp
from jax import lax
from jax.experimental import pallas as pl
from jax.experimental.pallas import tpu as pltpu
from jax.sharding import PartitionSpec as P

CAP = 2
VMEM = pl.BlockSpec(memory_space=pltpu.VMEM)
RESIDENT = 24 << 20


def run(start, step, end, steps, blocked, table):
    copy = pltpu.make_async_copy(*table)

    def begin():
        copy.start()
        start()
        copy.wait()

    if blocked:
        n = pl.program_id(0)
        pl.when(n == 0)(begin)
        step(n, 0)
        pl.when(n == steps - 1)(end)
        return
    begin()
    lax.fori_loop(0, steps, lambda n, carry: step(n, n), None)
    end()


def group_of(owners):
    for size in (32, 16, 8, 4, 2):
        if owners % size == 0:
            return size
    return 1


def fill_table(table, wide, pieces, tiles, flip, fill):
    for n, piece in enumerate(pieces):
        x = piece[...].astype(jnp.float32)
        samples = x.shape[2]
        lane = lax.broadcasted_iota(jnp.int32, x.shape, 2)
        before = jnp.where(lane == 0, 0.0, pltpu.roll(x, 1, 2))
        after = jnp.where(lane == samples - 1, 0.0, pltpu.roll(x, samples - 1, 2))
        at = pl.ds(n * tiles, tiles)
        wide[at, 0:4, :] = after if flip else before
        wide[at, 4:8, :] = x
        wide[at, 8:12, :] = before if flip else after
    last = len(pieces) * tiles
    wide[pl.ds(last, 2), 0:12, :] = jnp.zeros((2, 12, wide.shape[2]), jnp.float32)
    wide[:, 12:16, :] = jnp.full((last + 2, 4, wide.shape[2]), fill, jnp.float32)
    table[...] = wide[...].astype(jnp.bfloat16)


def act(y):
    t = jnp.tanh(y)
    q = 1.0 + t
    a = y * q
    return t, q, a


def lines_of(idx, own, halo, owners):
    lines = []
    for e in owners:
        line = []
        for r in range(4):
            held = own if r in (1, 2) else halo
            line += [None, None] if held is None else [held[idx[r, e]], held[idx[r, e] + 1]]
        lines.append(line)
    return lines


def stack(lines, traces, flip):
    return jnp.concatenate(
        [
            jnp.concatenate(
                [line[h + 1 + (2 - i if flip else i)] for line in lines for h in traces], axis=1
            )
            for i in range(3)
        ],
        axis=0,
    )


def layers(inputs, w1, w2):
    y1 = jnp.dot(w1[...], inputs, preferred_element_type=jnp.float32)
    t, q, a = act(y1)
    d1 = q + a * (1.0 - t)
    a1 = a.astype(jnp.bfloat16)
    ones = jnp.ones((16, a1.shape[1]), jnp.bfloat16)
    y2 = jnp.dot(w2[...], jnp.concatenate([a1, ones], axis=0), preferred_element_type=jnp.float32)
    t, q, a = act(y2)
    return a1, d1, a, q + a * (1.0 - t)


def forward_inner(
    group, blocked, slots, mine, w1, w2, own, a1_ref, a2_ref, d1_ref, d2_ref, wide, idx, sem,
):
    owners = lax.axis_size("rec")

    def start():
        fill_table(own, wide, (mine,), mine.shape[0], False, 1.0)

    def step(n, block):
        lines = lines_of(idx, own, None, [n * group + u for u in range(group)])
        a1, d1, a2, d2 = layers(stack(lines, (1, 2), False), w1, w2)
        a1_ref[block] = a1
        d1_ref[block] = d1
        a2_ref[block] = a2.astype(jnp.bfloat16)
        d2_ref[block] = d2

    run(start, step, lambda: None, owners // group, blocked, (slots, idx, sem))


def forward_outer(
    group, blocked, slots, near, mine, far, own, w1, w2, w3, inner,
    res, g, halo, a1_ref, a2_ref, d1_ref, d2_ref, wide, est, idx, sem,
):
    tiles, parts, samples = mine.shape
    count = lax.axis_size("rec")
    me = lax.axis_index("rec")
    has_left = (me > 0).astype(jnp.float32)
    has_right = (me < count - 1).astype(jnp.float32)
    lane = lax.broadcasted_iota(jnp.int32, (8, samples), 1)
    low = (lane > 0).astype(jnp.float32)
    high = (lane < samples - 1).astype(jnp.float32)

    def start():
        fill_table(halo, wide, (near, far), tiles, False, 1.0)

    def step(n, block):
        lines = lines_of(idx, own, halo, [n * group + u for u in range(group)])
        a1, d1, a2, d2 = layers(stack(lines, (-1, 0, 3, 4), False), w1, w2)
        cut = lambda x, u, k: x[:, (u * 4 + k) * samples : (u * 4 + k + 1) * samples]
        middle = lambda x: jnp.concatenate(
            [cut(x, u, k) for u in range(group) for k in (1, 2)], axis=1
        )
        a1_ref[block] = middle(a1)
        d1_ref[block] = middle(d1)
        d2_ref[block] = middle(d2)
        rows = []
        for u in range(group):
            row = [cut(a2, u, 0) * has_left, cut(a2, u, 1), cut(a2, u, 2), cut(a2, u, 3) * has_right]
            row = [part.astype(jnp.bfloat16) for part in row]
            within = [
                inner[block, :, (u * 2 + k) * samples : (u * 2 + k + 1) * samples] for k in range(2)
            ]
            rows.append(row[0:2] + within + row[2:4])
        a2_ref[block] = jnp.concatenate([row[k] for row in rows for k in (1, 4)], axis=1)
        rhs = jnp.concatenate(
            [
                jnp.concatenate([row[h + i] for row in rows for h in range(4)], axis=1)
                for i in range(3)
            ],
            axis=0,
        )
        terms = jnp.dot(w3[...], rhs, preferred_element_type=jnp.float32)
        for k in range(group * 4):
            part = terms[:, k * samples : (k + 1) * samples]
            total = (
                part[8:16]
                + pltpu.roll(part[0:8], 1, 1) * low
                + pltpu.roll(part[16:24], samples - 1, 1) * high
            )
            est[n * group * 4 + k] = total.astype(jnp.bfloat16).astype(jnp.float32)

    def end():
        for c in range(tiles // 2):
            at = [idx[4 + v, tiles // 2 + c] for v in range(4)]
            for k in range(2):
                total = (est[at[0] + k] + est[at[1] + k]) + (est[at[2] + k] + est[at[3] + k])
                value = total[0:parts] - mine[c * 2 + k].astype(jnp.float32)
                for o in range(parts):
                    res[o, c, k : k + 1, :] = value[o : o + 1]
                g[c * 2 + k] = value.astype(jnp.bfloat16)

    run(start, step, end, count // group, blocked, (slots, idx, sem))


def weight_terms(acc, fields, inputs, wo, wm, a1, a2, d1, d2):
    channels = wm.shape[0]
    da2 = jnp.dot(wo[...], fields, preferred_element_type=jnp.float32)
    dz2 = (da2 * d2).astype(jnp.bfloat16)
    acc[0:48, :] += product(fields, a2, (1, 1))
    da1 = jnp.dot(wm[...], dz2, preferred_element_type=jnp.float32)
    ones = jnp.ones((16, dz2.shape[1]), jnp.bfloat16)
    acc[48 : 64 + channels, :] += product(jnp.concatenate([a1, ones], axis=0), dz2, (1, 1))
    dz1 = (da1 * d1).astype(jnp.bfloat16)
    acc[64 + channels : 112 + channels, :] += product(inputs, dz1, (1, 1))


def backward_inner(
    group, blocked, slots, mine, wo, wm, own, a1_ref, a2_ref, d1_ref, d2_ref, gown, acc, wide,
    idx, sem,
):
    owners = lax.axis_size("rec")

    def start():
        fill_table(gown, wide, (mine,), mine.shape[0], True, 0.0)
        acc[...] = jnp.zeros_like(acc)

    def step(n, block):
        es = [n * group + u for u in range(group)]
        fields = stack(lines_of(idx, gown, None, es), (1, 2), True)
        inputs = stack(lines_of(idx, own, None, es), (1, 2), False)
        saved = a1_ref[block], a2_ref[block], d1_ref[block], d2_ref[block]
        weight_terms(acc, fields, inputs, wo, wm, *saved)

    run(start, step, lambda: None, owners // group, blocked, (slots, idx, sem))


def backward_outer(
    group, blocked, slots, near, far, wo, wm, own, halo, gown, sums, a1_ref, a2_ref, d1_ref, d2_ref,
    out, ghalo, wide, acc, idx, sem,
):
    owners = lax.axis_size("rec")
    channels = wm.shape[0]
    taps = 9 * near.shape[1]

    def start():
        fill_table(ghalo, wide, (near, far), near.shape[0], True, 0.0)
        acc[...] = sums[...]

    def step(n, block):
        es = [n * group + u for u in range(group)]
        fields = stack(lines_of(idx, gown, ghalo, es), (0, 3), True)
        inputs = stack(lines_of(idx, own, halo, es), (0, 3), False)
        saved = a1_ref[block], a2_ref[block], d1_ref[block], d2_ref[block]
        weight_terms(acc, fields, inputs, wo, wm, *saved)

    def end():
        first, half = 64 + channels, channels // 2
        low, high = slice(0, channels), slice(channels, 2 * channels)
        for k in range(taps):
            at = k % 9 // 3 * 16 + k % 3 * 4 + k // 9
            out[half + k : half + k + 1, low] = acc[first + at : first + at + 1, :]
            out[half + k : half + k + 1, high] = acc[at : at + 1, :]
        middle = acc[48 : 48 + channels, :].T
        out[0:half, low] = middle[0:half]
        out[0:half, high] = middle[half:channels]
        out[half + taps : half + taps + 1, low] = acc[first + 28 : first + 29, :]
        out[half + taps : half + taps + 1, high] = acc[48 + channels : 49 + channels, :]
        rest = out.shape[0] - half - taps - 1
        out[half + taps + 1 :, :] = jnp.zeros((rest, 2 * channels), jnp.float32)

    run(start, step, end, owners // group, blocked, (slots, idx, sem))


def finish_kernel(scale, *refs):
    terms, (g_in, g_bin, g_mid, g_bmid, g_out, held) = refs[:-6], refs[-6:]
    values = [ref[...] for ref in terms]
    while len(values) > 1:
        values = [values[k] + values[k + 1] for k in range(0, len(values), 2)]
    held[...] = values[0] * scale
    channels = g_mid.shape[0]
    half, taps = channels // 2, g_in.shape[0]
    low, high = slice(0, channels), slice(channels, 2 * channels)
    g_mid[0:half] = held[0:half, low]
    g_mid[half:channels] = held[0:half, high]
    g_in[...] = held[half : half + taps, low]
    g_out[...] = held[half : half + taps, high]
    g_bin[...] = held[half + taps : half + taps + 1, low]
    g_bmid[...] = held[half + taps : half + taps + 1, high]


def halves(b):
    high = b.astype(jnp.bfloat16).astype(jnp.float32)
    rest = b - high
    mid = rest.astype(jnp.bfloat16).astype(jnp.float32)
    return [high, mid, rest - mid]


def one_hot(a, b):
    return (a == b).astype(jnp.float32).astype(jnp.bfloat16)


def iota(shape, dim):
    return lax.broadcasted_iota(jnp.int32, shape, dim)


def product(a, b, over):
    return lax.dot_general(
        a, b, dimension_numbers=(((over[0],), (over[1],)), ((), ())),
        preferred_element_type=jnp.float32,
    )


def prep_kernel(blocks, *refs):
    args, (idx, w1, w2, w3, wo, wm, rows), held, sems = refs[:6], refs[6:13], refs[13:19], refs[19]
    copies = [
        pltpu.make_async_copy(src, dst, sems.at[n]) for n, (src, dst) in enumerate(zip(args, held))
    ]
    for copy in copies:
        copy.start()
    for copy in copies:
        copy.wait()
    dest, w_in, b_in, w_mid, b_mid, w_out = held
    count = lax.axis_size("rec")
    me = lax.axis_index("rec")
    ves, total = dest.shape
    channels = w_mid.shape[0]
    at = lax.rem((count + 1 - me) * blocks, total)
    wide = jnp.concatenate([dest[...], jnp.zeros((8 - ves, total), jnp.int32)], axis=0)
    near = pltpu.roll(wide, at, 1)[:, 0:128]
    lane = iota((8, 128), 1)
    low = jnp.where(me > 0, 0, blocks)
    high = jnp.where(me < count - 1, 3 * blocks, 2 * blocks)
    near = jnp.where((lane >= low) & (lane < high), near, -1)
    owner = iota((count, 128), 0)
    hits = [(near[v : v + 1] == owner).astype(jnp.float32) for v in range(ves)]
    before = iota((128, 128), 0)
    after = iota((128, 128), 1)
    segment = (after >= blocks).astype(jnp.int32) + (after >= 2 * blocks).astype(jnp.int32)
    tri = ((before < after) & (before >= segment * blocks)).astype(jnp.float32).astype(jnp.bfloat16)
    rank = product((hits[0] + hits[1] + hits[2] + hits[3]).astype(jnp.bfloat16), tri, (1, 0))
    zeroth = jnp.zeros((count, 128), jnp.float32)
    first = jnp.zeros((count, 128), jnp.float32)
    for v in range(ves):
        zeroth += hits[v] * (rank == 0.0).astype(jnp.float32)
        first += hits[v] * (rank == 1.0).astype(jnp.float32)
        item = jnp.sum(hits[v] * rank, axis=0, keepdims=True)
        idx[4 + v : 5 + v, 0:128] = near[v : v + 1] * 4 + item.astype(jnp.int32) * 2
        rank = rank + hits[v]
    line = iota((8, 128), 0)
    inside = lambda k: (lane >= k * blocks) & (lane < (k + 1) * blocks)
    odd = lax.rem(me, 2)
    left = 2 * lane + 2 * blocks * (1 - odd) - 4 * blocks
    middle = 2 * (lane - blocks) - 2 * blocks
    right = 2 * (lane - 2 * blocks) + 2 * blocks * odd - 4 * blocks
    put = lambda r, k, place: jnp.where((line == r) & inside(k), place, 0)
    pick = product(
        (put(0, 0, left) + put(2, 1, middle)).astype(jnp.float32).astype(jnp.bfloat16),
        first.astype(jnp.bfloat16),
        (1, 1),
    ) + product(
        (put(1, 1, middle) + put(3, 2, right)).astype(jnp.float32).astype(jnp.bfloat16),
        zeroth.astype(jnp.bfloat16),
        (1, 1),
    )
    empty = jnp.where((line == 0) | (line == 3), 4 * blocks, 2 * blocks)[0:4, 0:1]
    idx[0:4, 0:count] = pick[0:4].astype(jnp.int32) + empty

    taps = w_in.shape[0]
    row, col = iota((48, 40), 0), iota((48, 40), 1)
    tap, extra = row & 15, (row & 15) - 12
    target = (row & 3) * 9 + 3 * (row >> 4) + ((row >> 2) & 3)
    target = jnp.where(tap < 12, target, jnp.where((row >> 4) == 1, taps + extra, -1))
    order = one_hot(col, target)
    rows[...] = jnp.zeros_like(rows)
    rows[0:taps, :] = w_in[...].astype(jnp.float32)
    for n, part in enumerate(halves(b_in[...])):
        rows[taps + n : taps + n + 1, :] = part
    w1[...] = (0.5 * product(rows[...].astype(jnp.bfloat16), order, (0, 1))).astype(jnp.bfloat16)
    rows[...] = jnp.zeros_like(rows)
    for n, part in enumerate(halves(b_mid[...])):
        rows[n : n + 1, :] = part
    row, col = iota((40, channels + 16), 0), iota((40, channels + 16), 1)
    bias = product(rows[...].astype(jnp.bfloat16), one_hot(col, row + channels), (0, 0))
    row, col = iota((channels, channels + 16), 0), iota((channels, channels + 16), 1)
    w2[...] = (0.5 * (product(w_mid[...], one_hot(row, col), (1, 0)) + bias)).astype(jnp.bfloat16)
    rows[...] = jnp.zeros_like(rows)
    rows[0:taps, :] = w_out[...].astype(jnp.float32)
    outs = rows[...].astype(jnp.bfloat16)
    wo[...] = (0.5 * product(outs, order, (0, 1))).astype(jnp.bfloat16)
    row, col = iota((24, 40), 0), iota((24, 40), 1)
    for i in range(3):
        target = jnp.where((row & 7) < 4, (row & 3) * 9 + 3 * i + (row >> 3), -1)
        part = product(one_hot(col, target), outs, (1, 0))
        w3[:, i * channels : (i + 1) * channels] = part.astype(jnp.bfloat16)
    eye = one_hot(iota((channels, channels), 0), iota((channels, channels), 1))
    wm[...] = (0.5 * product(w_mid[...], eye, (0, 0))).astype(jnp.bfloat16)


def local(records, dest, w_in, b_in, w_mid, b_mid, w_out):
    count = lax.axis_size("rec")
    me = lax.axis_index("rec")
    parts, blocks, traces, samples = records.shape
    ves = dest.shape[1]
    tiles = blocks * traces
    channels = w_in.shape[0]
    group = group_of(count)
    steps = count // group
    width = group * 2 * samples
    far = [(s, s + 1) for s in range(1, count - 1, 2)]
    far += [(b, a) for a, b in far]
    near = [(s, s + 1) for s in range(0, count - 1, 2)]
    near += [(b, a) for a, b in near]

    flat = records.transpose(1, 2, 0, 3).reshape(tiles, parts, samples)
    from_far = lax.ppermute(flat, "rec", far)
    from_near = lax.ppermute(flat, "rec", near)

    f32, bf16 = jnp.float32, jnp.bfloat16
    shape = (steps, channels, width)
    blocked = 24 * math.prod(shape) > RESIDENT
    saved = [
        jax.ShapeDtypeStruct(shape, kind) if blocked else pltpu.VMEM(shape, kind)
        for kind in (bf16, bf16, f32, f32)
    ]
    held = [VMEM] * 4
    if blocked:
        held = [pl.BlockSpec((1, channels, width), lambda n: (n, 0, 0))] * 4
    grid = (steps,) if blocked else ()
    params = pltpu.CompilerParams(vmem_limit_bytes=16 << 20)
    args = (
        dest.T, w_in.T, b_in.reshape(1, channels), w_mid, b_mid.reshape(1, channels), w_out.T
    )
    idx, w1, w2, w3, wo, wm = pl.pallas_call(
        functools.partial(prep_kernel, blocks),
        out_shape=[jax.ShapeDtypeStruct((8, max(128, count)), jnp.int32)]
        + [
            jax.ShapeDtypeStruct(size, bf16)
            for size in (
                (channels, 48), (channels, channels + 16), (24, 3 * channels), (channels, 48),
                (channels, channels),
            )
        ],
        in_specs=[pl.BlockSpec(memory_space=pltpu.HBM)] * 6,
        out_specs=[VMEM] * 6,
        scratch_shapes=[pltpu.VMEM((40, channels), f32)]
        + [pltpu.VMEM(arg.shape, arg.dtype) for arg in args]
        + [pltpu.SemaphoreType.DMA((6,))],
        compiler_params=params,
        name="prepare",
    )(*[pltpu.with_memory_space_constraint(arg, pltpu.HBM) for arg in args])
    def table(pieces, kind):
        return pltpu.VMEM((pieces * tiles + 2, 16, samples), kind)

    def call(kernel, ins, outs, scratch, args, name, owned):
        return pl.pallas_call(
            functools.partial(kernel, group, blocked),
            grid=grid,
            out_shape=outs[0] + saved * outs[1],
            in_specs=[VMEM] * (1 + ins[0]) + held[:1] * ins[1],
            out_specs=[VMEM] * len(outs[0]) + held * outs[1],
            scratch_shapes=scratch + [pltpu.SMEM(idx.shape, idx.dtype), pltpu.SemaphoreType.DMA],
            compiler_params=params,
            cost_estimate=pl.CostEstimate(
                flops=2 * owned * count * samples * channels * (3 * channels),
                bytes_accessed=owned * count * samples * channels * 12,
                transcendentals=0,
            ),
            name=name,
        )(*args)

    total = (112 + channels, channels)
    rows = (channels // 2 + 9 * parts + 1 + 7) // 8 * 8
    own, *inner = call(
        forward_inner, (3, 0), ([table(1, bf16)], 1), [table(1, f32)],
        (idx, flat, w1, w2), "forward_inner", 2,
    )
    res, g, halo, *outer = call(
        forward_outer, (7, 1),
        (
            [
                jax.ShapeDtypeStruct(records.shape, f32),
                jax.ShapeDtypeStruct((tiles, parts, samples), bf16),
                table(2, bf16),
            ],
            1,
        ),
        [table(2, f32), pltpu.VMEM((count * 4, 8, samples), f32)],
        (idx, from_near, flat, from_far, own, w1, w2, w3, inner[1]), "forward_outer", 4,
    )
    g_far = lax.ppermute(g, "rec", far)
    g_near = lax.ppermute(g, "rec", near)
    gown, part = call(
        backward_inner, (4, 4), ([table(1, bf16), pltpu.VMEM(total, f32)], 0), [table(1, f32)],
        (idx, g, wo, wm, own, *inner), "backward_inner", 2,
    )
    (sums,) = call(
        backward_outer, (8, 4), ([jax.ShapeDtypeStruct((rows, 2 * channels), f32)], 0),
        [table(2, bf16), table(2, f32), pltpu.VMEM(total, f32)],
        (idx, g_near, g_far, wo, wm, own, halo, gown, part, *outer), "backward_outer", 2,
    )

    if count & (count - 1):
        terms = [lax.psum(sums, "rec")]
    else:
        terms = [sums]
        at = 1
        while at < count:
            wide = 4 if at > 1 and 4 * at <= count else 2
            value = terms[0]
            if len(terms) == 2:
                value = terms[0] + terms[1]
            if len(terms) == 4:
                value = (terms[0] + terms[1]) + (terms[2] + terms[3])
            terms = [value] + [
                lax.ppermute(value, "rec", [(s, s ^ (k * at)) for s in range(count)])
                for k in range(1, wide)
            ]
            at *= wide

    scale = 1.0 / math.sqrt(parts * blocks * count * traces * samples)
    g_in, g_bin, g_mid, g_bmid, g_out = pl.pallas_call(
        functools.partial(finish_kernel, scale),
        out_shape=[
            jax.ShapeDtypeStruct(shape, f32)
            for shape in (
                (parts * 9, channels), (1, channels), (channels, channels), (1, channels),
                (parts * 9, channels),
            )
        ],
        in_specs=[VMEM] * len(terms),
        out_specs=[VMEM] * 5,
        scratch_shapes=[pltpu.VMEM(sums.shape, f32)],
        compiler_params=params,
        name="finish",
    )(*terms)
    return (
        res,
        g_in.T,
        g_bin.reshape(channels),
        g_mid,
        g_bmid.reshape(channels),
        g_out.T,
    )


def solution(mesh):
    return jax.shard_map(
        local,
        mesh=mesh,
        in_specs=(
            P(None, ("groups", "rec"), None, None),
            P("groups", None),
            P(),
            P(),
            P(),
            P(),
            P(),
        ),
        out_specs=(
            P(None, ("groups", "rec"), None, None),
            P("groups", None),
            P("groups"),
            P("groups", None),
            P("groups"),
            P("groups", None),
        ),
        check_vma=False,
    )
```

```python
import functools
import math

import jax
import jax.numpy as jnp
from jax import lax
from jax.experimental import pallas as pl
from jax.experimental.pallas import tpu as pltpu
from jax.sharding import PartitionSpec as P

CAP = 2
VMEM = pl.BlockSpec(memory_space=pltpu.VMEM)
RESIDENT = 24 << 20


def run(start, step, end, steps, blocked, table):
    copy = pltpu.make_async_copy(*table)

    def begin():
        copy.start()
        start()
        copy.wait()

    if blocked:
        n = pl.program_id(0)
        pl.when(n == 0)(begin)
        step(n, 0)
        pl.when(n == steps - 1)(end)
        return
    begin()
    lax.fori_loop(0, steps, lambda n, carry: step(n, n), None)
    end()


def group_of(owners):
    for size in (32, 16, 8, 4, 2):
        if owners % size == 0:
            return size
    return 1


def fill_table(table, wide, pieces, tiles, flip, fill):
    for n, piece in enumerate(pieces):
        x = piece[...].astype(jnp.float32)
        samples = x.shape[2]
        lane = lax.broadcasted_iota(jnp.int32, x.shape, 2)
        before = jnp.where(lane == 0, 0.0, pltpu.roll(x, 1, 2))
        after = jnp.where(lane == samples - 1, 0.0, pltpu.roll(x, samples - 1, 2))
        at = pl.ds(n * tiles, tiles)
        wide[at, 0:4, :] = after if flip else before
        wide[at, 4:8, :] = x
        wide[at, 8:12, :] = before if flip else after
    last = len(pieces) * tiles
    wide[pl.ds(last, 2), 0:12, :] = jnp.zeros((2, 12, wide.shape[2]), jnp.float32)
    wide[:, 12:16, :] = jnp.full((last + 2, 4, wide.shape[2]), fill, jnp.float32)
    table[...] = wide[...].astype(jnp.bfloat16)


def act(y):
    t = jnp.tanh(y)
    q = 1.0 + t
    a = y * q
    return t, q, a


def lines_of(idx, own, halo, owners):
    lines = []
    for e in owners:
        line = []
        for r in range(4):
            held = own if r in (1, 2) else halo
            line += [None, None] if held is None else [held[idx[r, e]], held[idx[r, e] + 1]]
        lines.append(line)
    return lines


def stack(lines, traces, flip):
    return jnp.concatenate(
        [
            jnp.concatenate(
                [line[h + 1 + (2 - i if flip else i)] for line in lines for h in traces], axis=1
            )
            for i in range(3)
        ],
        axis=0,
    )


def pipeline(pieces, *stages):
    held = [None] * pieces
    for tick in range(pieces + len(stages) - 1):
        for behind in reversed(range(len(stages))):
            k = tick - behind
            if 0 <= k < pieces:
                held[k] = stages[behind](k, held[k])


def layer(w, inputs):
    t, q, a = act(jnp.dot(w[...], inputs, preferred_element_type=jnp.float32))
    return a, q + a * (1.0 - t)


def with_ones(a1):
    return jnp.concatenate([a1, jnp.ones((16, a1.shape[1]), jnp.bfloat16)], axis=0)


def forward_inner(
    group, blocked, slots, mine, w1, w2, own, a1_ref, a2_ref, d1_ref, d2_ref, wide, idx, sem,
):
    owners = lax.axis_size("rec")

    def start():
        fill_table(own, wide, (mine,), mine.shape[0], False, 1.0)

    def step(n, block):
        sub = min(2, group)
        width = sub * 2 * mine.shape[2]

        def first(k, _):
            es = [n * group + k * sub + u for u in range(sub)]
            at = slice(k * width, (k + 1) * width)
            a, d = layer(w1, stack(lines_of(idx, own, None, es), (1, 2), False))
            a1_ref[block, :, at] = a.astype(jnp.bfloat16)
            d1_ref[block, :, at] = d
            return a.astype(jnp.bfloat16)

        def second(k, a1):
            at = slice(k * width, (k + 1) * width)
            a, d = layer(w2, with_ones(a1))
            a2_ref[block, :, at] = a.astype(jnp.bfloat16)
            d2_ref[block, :, at] = d

        pipeline(group // sub, first, second)

    run(start, step, lambda: None, owners // group, blocked, (slots, idx, sem))


def forward_outer(
    group, blocked, slots, near, mine, far, own, w1, w2, w3, inner,
    res, g, halo, a1_ref, a2_ref, d1_ref, d2_ref, wide, est, idx, sem,
):
    tiles, parts, samples = mine.shape
    count = lax.axis_size("rec")
    me = lax.axis_index("rec")
    has_left = (me > 0).astype(jnp.float32)
    has_right = (me < count - 1).astype(jnp.float32)
    lane = lax.broadcasted_iota(jnp.int32, (8, samples), 1)
    low = (lane > 0).astype(jnp.float32)
    high = (lane < samples - 1).astype(jnp.float32)

    def start():
        fill_table(halo, wide, (near, far), tiles, False, 1.0)

    def step(n, block):
        cut = lambda x, k: x[:, k * samples : (k + 1) * samples]
        middle = lambda x: x[:, samples : 3 * samples]

        def first(u, _):
            lines = lines_of(idx, own, halo, [n * group + u])
            at = slice(u * 2 * samples, (u + 1) * 2 * samples)
            a, d = layer(w1, stack(lines, (-1, 0, 3, 4), False))
            a1 = a.astype(jnp.bfloat16)
            a1_ref[block, :, at] = middle(a1)
            d1_ref[block, :, at] = middle(d)
            return a1

        def second(u, a1):
            at = slice(u * 2 * samples, (u + 1) * 2 * samples)
            a, d = layer(w2, with_ones(a1))
            d2_ref[block, :, at] = middle(d)
            a2_ref[block, :, at] = middle(a).astype(jnp.bfloat16)
            row = [cut(a, 0) * has_left, cut(a, 1), cut(a, 2), cut(a, 3) * has_right]
            row = [part.astype(jnp.bfloat16) for part in row]
            within = [
                inner[block, :, (u * 2 + k) * samples : (u * 2 + k + 1) * samples] for k in range(2)
            ]
            return row[0:2] + within + row[2:4]

        def third(u, row):
            rhs = [jnp.concatenate(row[i : i + 4], axis=1) for i in range(3)]
            terms = jnp.dot(
                w3[...], jnp.concatenate(rhs, axis=0), preferred_element_type=jnp.float32
            )
            for h in range(4):
                part = cut(terms, h)
                total = (
                    part[8:16]
                    + pltpu.roll(part[0:8], 1, 1) * low
                    + pltpu.roll(part[16:24], samples - 1, 1) * high
                )
                est[(n * group + u) * 4 + h] = total.astype(jnp.bfloat16).astype(jnp.float32)

        pipeline(group, first, second, third)

    def end():
        for c in range(tiles // 2):
            at = [idx[4 + v, tiles // 2 + c] for v in range(4)]
            for k in range(2):
                total = (est[at[0] + k] + est[at[1] + k]) + (est[at[2] + k] + est[at[3] + k])
                value = total[0:parts] - mine[c * 2 + k].astype(jnp.float32)
                for o in range(parts):
                    res[o, c, k : k + 1, :] = value[o : o + 1]
                g[c * 2 + k] = value.astype(jnp.bfloat16)

    run(start, step, end, count // group, blocked, (slots, idx, sem))


def weight_terms(acc, pieces, width, fields_of, inputs_of, wo, wm, saved):
    channels = wm.shape[0]
    a1, a2, d1, d2 = saved
    of = lambda ref, k: ref[:, k * width : (k + 1) * width]

    def first(k, _):
        fields = fields_of(k)
        da2 = jnp.dot(wo[...], fields, preferred_element_type=jnp.float32)
        acc[0:48, :] += product(fields, of(a2, k), (1, 1))
        return (da2 * of(d2, k)).astype(jnp.bfloat16)

    def second(k, dz2):
        da1 = jnp.dot(wm[...], dz2, preferred_element_type=jnp.float32)
        acc[48 : 64 + channels, :] += product(with_ones(of(a1, k)), dz2, (1, 1))
        return (da1 * of(d1, k)).astype(jnp.bfloat16)

    def third(k, dz1):
        acc[64 + channels : 112 + channels, :] += product(inputs_of(k), dz1, (1, 1))

    pipeline(pieces, first, second, third)


def backward_inner(
    group, blocked, slots, mine, wo, wm, own, a1_ref, a2_ref, d1_ref, d2_ref, gown, acc, wide,
    idx, sem,
):
    owners = lax.axis_size("rec")

    def start():
        fill_table(gown, wide, (mine,), mine.shape[0], True, 0.0)
        acc[...] = jnp.zeros_like(acc)

    def step(n, block):
        sub = min(2, group)
        es = lambda k: [n * group + k * sub + u for u in range(sub)]
        weight_terms(
            acc, group // sub, sub * 2 * mine.shape[2],
            lambda k: stack(lines_of(idx, gown, None, es(k)), (1, 2), True),
            lambda k: stack(lines_of(idx, own, None, es(k)), (1, 2), False),
            wo, wm, [ref.at[block] for ref in (a1_ref, a2_ref, d1_ref, d2_ref)],
        )

    run(start, step, lambda: None, owners // group, blocked, (slots, idx, sem))


def backward_outer(
    group, blocked, slots, near, far, wo, wm, own, halo, gown, sums, a1_ref, a2_ref, d1_ref, d2_ref,
    out, ghalo, wide, acc, idx, sem,
):
    owners = lax.axis_size("rec")
    channels = wm.shape[0]
    taps = 9 * near.shape[1]

    def start():
        fill_table(ghalo, wide, (near, far), near.shape[0], True, 0.0)
        acc[...] = sums[...]

    def step(n, block):
        sub = min(2, group)
        es = lambda k: [n * group + k * sub + u for u in range(sub)]
        weight_terms(
            acc, group // sub, sub * 2 * near.shape[2],
            lambda k: stack(lines_of(idx, gown, ghalo, es(k)), (0, 3), True),
            lambda k: stack(lines_of(idx, own, halo, es(k)), (0, 3), False),
            wo, wm, [ref.at[block] for ref in (a1_ref, a2_ref, d1_ref, d2_ref)],
        )

    def end():
        first, half = 64 + channels, channels // 2
        low, high = slice(0, channels), slice(channels, 2 * channels)
        for k in range(taps):
            at = k % 9 // 3 * 16 + k % 3 * 4 + k // 9
            out[half + k : half + k + 1, low] = acc[first + at : first + at + 1, :]
            out[half + k : half + k + 1, high] = acc[at : at + 1, :]
        middle = acc[48 : 48 + channels, :].T
        out[0:half, low] = middle[0:half]
        out[0:half, high] = middle[half:channels]
        out[half + taps : half + taps + 1, low] = acc[first + 28 : first + 29, :]
        out[half + taps : half + taps + 1, high] = acc[48 + channels : 49 + channels, :]
        rest = out.shape[0] - half - taps - 1
        out[half + taps + 1 :, :] = jnp.zeros((rest, 2 * channels), jnp.float32)

    run(start, step, end, owners // group, blocked, (slots, idx, sem))


def finish_kernel(scale, *refs):
    terms, (g_in, g_bin, g_mid, g_bmid, g_out, held) = refs[:-6], refs[-6:]
    values = [ref[...] for ref in terms]
    while len(values) > 1:
        values = [values[k] + values[k + 1] for k in range(0, len(values), 2)]
    held[...] = values[0] * scale
    channels = g_mid.shape[0]
    half, taps = channels // 2, g_in.shape[0]
    low, high = slice(0, channels), slice(channels, 2 * channels)
    g_mid[0:half] = held[0:half, low]
    g_mid[half:channels] = held[0:half, high]
    g_in[...] = held[half : half + taps, low]
    g_out[...] = held[half : half + taps, high]
    g_bin[...] = held[half + taps : half + taps + 1, low]
    g_bmid[...] = held[half + taps : half + taps + 1, high]


def halves(b):
    high = b.astype(jnp.bfloat16).astype(jnp.float32)
    rest = b - high
    mid = rest.astype(jnp.bfloat16).astype(jnp.float32)
    return [high, mid, rest - mid]


def one_hot(a, b):
    return (a == b).astype(jnp.float32).astype(jnp.bfloat16)


def iota(shape, dim):
    return lax.broadcasted_iota(jnp.int32, shape, dim)


def product(a, b, over):
    return lax.dot_general(
        a, b, dimension_numbers=(((over[0],), (over[1],)), ((), ())),
        preferred_element_type=jnp.float32,
    )


def prep_kernel(blocks, *refs):
    args, (idx, w1, w2, w3, wo, wm, rows), held, sems = refs[:6], refs[6:13], refs[13:19], refs[19]
    copies = [
        pltpu.make_async_copy(src, dst, sems.at[n]) for n, (src, dst) in enumerate(zip(args, held))
    ]
    for copy in copies:
        copy.start()
    for copy in copies:
        copy.wait()
    dest, w_in, b_in, w_mid, b_mid, w_out = held
    count = lax.axis_size("rec")
    me = lax.axis_index("rec")
    ves, total = dest.shape
    channels = w_mid.shape[0]
    at = lax.rem((count + 1 - me) * blocks, total)
    wide = jnp.concatenate([dest[...], jnp.zeros((8 - ves, total), jnp.int32)], axis=0)
    near = pltpu.roll(wide, at, 1)[:, 0:128]
    lane = iota((8, 128), 1)
    low = jnp.where(me > 0, 0, blocks)
    high = jnp.where(me < count - 1, 3 * blocks, 2 * blocks)
    near = jnp.where((lane >= low) & (lane < high), near, -1)
    owner = iota((count, 128), 0)
    hits = [(near[v : v + 1] == owner).astype(jnp.float32) for v in range(ves)]
    before = iota((128, 128), 0)
    after = iota((128, 128), 1)
    segment = (after >= blocks).astype(jnp.int32) + (after >= 2 * blocks).astype(jnp.int32)
    tri = ((before < after) & (before >= segment * blocks)).astype(jnp.float32).astype(jnp.bfloat16)
    rank = product((hits[0] + hits[1] + hits[2] + hits[3]).astype(jnp.bfloat16), tri, (1, 0))
    zeroth = jnp.zeros((count, 128), jnp.float32)
    first = jnp.zeros((count, 128), jnp.float32)
    for v in range(ves):
        zeroth += hits[v] * (rank == 0.0).astype(jnp.float32)
        first += hits[v] * (rank == 1.0).astype(jnp.float32)
        item = jnp.sum(hits[v] * rank, axis=0, keepdims=True)
        idx[4 + v : 5 + v, 0:128] = near[v : v + 1] * 4 + item.astype(jnp.int32) * 2
        rank = rank + hits[v]
    line = iota((8, 128), 0)
    inside = lambda k: (lane >= k * blocks) & (lane < (k + 1) * blocks)
    odd = lax.rem(me, 2)
    left = 2 * lane + 2 * blocks * (1 - odd) - 4 * blocks
    middle = 2 * (lane - blocks) - 2 * blocks
    right = 2 * (lane - 2 * blocks) + 2 * blocks * odd - 4 * blocks
    put = lambda r, k, place: jnp.where((line == r) & inside(k), place, 0)
    pick = product(
        (put(0, 0, left) + put(2, 1, middle)).astype(jnp.float32).astype(jnp.bfloat16),
        first.astype(jnp.bfloat16),
        (1, 1),
    ) + product(
        (put(1, 1, middle) + put(3, 2, right)).astype(jnp.float32).astype(jnp.bfloat16),
        zeroth.astype(jnp.bfloat16),
        (1, 1),
    )
    empty = jnp.where((line == 0) | (line == 3), 4 * blocks, 2 * blocks)[0:4, 0:1]
    idx[0:4, 0:count] = pick[0:4].astype(jnp.int32) + empty

    taps = w_in.shape[0]
    row, col = iota((48, 40), 0), iota((48, 40), 1)
    tap, extra = row & 15, (row & 15) - 12
    target = (row & 3) * 9 + 3 * (row >> 4) + ((row >> 2) & 3)
    target = jnp.where(tap < 12, target, jnp.where((row >> 4) == 1, taps + extra, -1))
    order = one_hot(col, target)
    rows[...] = jnp.zeros_like(rows)
    rows[0:taps, :] = w_in[...].astype(jnp.float32)
    for n, part in enumerate(halves(b_in[...])):
        rows[taps + n : taps + n + 1, :] = part
    w1[...] = (0.5 * product(rows[...].astype(jnp.bfloat16), order, (0, 1))).astype(jnp.bfloat16)
    rows[...] = jnp.zeros_like(rows)
    for n, part in enumerate(halves(b_mid[...])):
        rows[n : n + 1, :] = part
    row, col = iota((40, channels + 16), 0), iota((40, channels + 16), 1)
    bias = product(rows[...].astype(jnp.bfloat16), one_hot(col, row + channels), (0, 0))
    row, col = iota((channels, channels + 16), 0), iota((channels, channels + 16), 1)
    w2[...] = (0.5 * (product(w_mid[...], one_hot(row, col), (1, 0)) + bias)).astype(jnp.bfloat16)
    rows[...] = jnp.zeros_like(rows)
    rows[0:taps, :] = w_out[...].astype(jnp.float32)
    outs = rows[...].astype(jnp.bfloat16)
    wo[...] = (0.5 * product(outs, order, (0, 1))).astype(jnp.bfloat16)
    row, col = iota((24, 40), 0), iota((24, 40), 1)
    for i in range(3):
        target = jnp.where((row & 7) < 4, (row & 3) * 9 + 3 * i + (row >> 3), -1)
        part = product(one_hot(col, target), outs, (1, 0))
        w3[:, i * channels : (i + 1) * channels] = part.astype(jnp.bfloat16)
    eye = one_hot(iota((channels, channels), 0), iota((channels, channels), 1))
    wm[...] = (0.5 * product(w_mid[...], eye, (0, 0))).astype(jnp.bfloat16)


def local(records, dest, w_in, b_in, w_mid, b_mid, w_out):
    count = lax.axis_size("rec")
    me = lax.axis_index("rec")
    parts, blocks, traces, samples = records.shape
    ves = dest.shape[1]
    tiles = blocks * traces
    channels = w_in.shape[0]
    group = group_of(count)
    steps = count // group
    width = group * 2 * samples
    far = [(s, s + 1) for s in range(1, count - 1, 2)]
    far += [(b, a) for a, b in far]
    near = [(s, s + 1) for s in range(0, count - 1, 2)]
    near += [(b, a) for a, b in near]

    flat = records.transpose(1, 2, 0, 3).reshape(tiles, parts, samples)
    from_far = lax.ppermute(flat, "rec", far)
    from_near = lax.ppermute(flat, "rec", near)

    f32, bf16 = jnp.float32, jnp.bfloat16
    shape = (steps, channels, width)
    blocked = 24 * math.prod(shape) > RESIDENT
    saved = [
        jax.ShapeDtypeStruct(shape, kind) if blocked else pltpu.VMEM(shape, kind)
        for kind in (bf16, bf16, f32, f32)
    ]
    held = [VMEM] * 4
    if blocked:
        held = [pl.BlockSpec((1, channels, width), lambda n: (n, 0, 0))] * 4
    grid = (steps,) if blocked else ()
    params = pltpu.CompilerParams(vmem_limit_bytes=16 << 20)
    args = (
        dest.T, w_in.T, b_in.reshape(1, channels), w_mid, b_mid.reshape(1, channels), w_out.T
    )
    idx, w1, w2, w3, wo, wm = pl.pallas_call(
        functools.partial(prep_kernel, blocks),
        out_shape=[jax.ShapeDtypeStruct((8, max(128, count)), jnp.int32)]
        + [
            jax.ShapeDtypeStruct(size, bf16)
            for size in (
                (channels, 48), (channels, channels + 16), (24, 3 * channels), (channels, 48),
                (channels, channels),
            )
        ],
        in_specs=[pl.BlockSpec(memory_space=pltpu.HBM)] * 6,
        out_specs=[VMEM] * 6,
        scratch_shapes=[pltpu.VMEM((40, channels), f32)]
        + [pltpu.VMEM(arg.shape, arg.dtype) for arg in args]
        + [pltpu.SemaphoreType.DMA((6,))],
        compiler_params=params,
        name="prepare",
    )(*[pltpu.with_memory_space_constraint(arg, pltpu.HBM) for arg in args])
    def table(pieces, kind):
        return pltpu.VMEM((pieces * tiles + 2, 16, samples), kind)

    def call(kernel, ins, outs, scratch, args, name, owned):
        return pl.pallas_call(
            functools.partial(kernel, group, blocked),
            grid=grid,
            out_shape=outs[0] + saved * outs[1],
            in_specs=[VMEM] * (1 + ins[0]) + held[:1] * ins[1],
            out_specs=[VMEM] * len(outs[0]) + held * outs[1],
            scratch_shapes=scratch + [pltpu.SMEM(idx.shape, idx.dtype), pltpu.SemaphoreType.DMA],
            compiler_params=params,
            cost_estimate=pl.CostEstimate(
                flops=2 * owned * count * samples * channels * (3 * channels),
                bytes_accessed=owned * count * samples * channels * 12,
                transcendentals=0,
            ),
            name=name,
        )(*args)

    total = (112 + channels, channels)
    rows = (channels // 2 + 9 * parts + 1 + 7) // 8 * 8
    own, *inner = call(
        forward_inner, (3, 0), ([table(1, bf16)], 1), [table(1, f32)],
        (idx, flat, w1, w2), "forward_inner", 2,
    )
    res, g, halo, *outer = call(
        forward_outer, (7, 1),
        (
            [
                jax.ShapeDtypeStruct(records.shape, f32),
                jax.ShapeDtypeStruct((tiles, parts, samples), bf16),
                table(2, bf16),
            ],
            1,
        ),
        [table(2, f32), pltpu.VMEM((count * 4, 8, samples), f32)],
        (idx, from_near, flat, from_far, own, w1, w2, w3, inner[1]), "forward_outer", 4,
    )
    g_far = lax.ppermute(g, "rec", far)
    g_near = lax.ppermute(g, "rec", near)
    gown, part = call(
        backward_inner, (4, 4), ([table(1, bf16), pltpu.VMEM(total, f32)], 0), [table(1, f32)],
        (idx, g, wo, wm, own, *inner), "backward_inner", 2,
    )
    (sums,) = call(
        backward_outer, (8, 4), ([jax.ShapeDtypeStruct((rows, 2 * channels), f32)], 0),
        [table(2, bf16), table(2, f32), pltpu.VMEM(total, f32)],
        (idx, g_near, g_far, wo, wm, own, halo, gown, part, *outer), "backward_outer", 2,
    )

    if count & (count - 1):
        terms = [lax.psum(sums, "rec")]
    else:
        terms = [sums]
        at = 1
        while at < count:
            wide = 4 if at > 1 and 4 * at <= count else 2
            value = terms[0]
            if len(terms) == 2:
                value = terms[0] + terms[1]
            if len(terms) == 4:
                value = (terms[0] + terms[1]) + (terms[2] + terms[3])
            terms = [value] + [
                lax.ppermute(value, "rec", [(s, s ^ (k * at)) for s in range(count)])
                for k in range(1, wide)
            ]
            at *= wide

    scale = 1.0 / math.sqrt(parts * blocks * count * traces * samples)
    g_in, g_bin, g_mid, g_bmid, g_out = pl.pallas_call(
        functools.partial(finish_kernel, scale),
        out_shape=[
            jax.ShapeDtypeStruct(shape, f32)
            for shape in (
                (parts * 9, channels), (1, channels), (channels, channels), (1, channels),
                (parts * 9, channels),
            )
        ],
        in_specs=[VMEM] * len(terms),
        out_specs=[VMEM] * 5,
        scratch_shapes=[pltpu.VMEM(sums.shape, f32)],
        compiler_params=params,
        name="finish",
    )(*terms)
    return (
        res,
        g_in.T,
        g_bin.reshape(channels),
        g_mid,
        g_bmid.reshape(channels),
        g_out.T,
    )


def solution(mesh):
    return jax.shard_map(
        local,
        mesh=mesh,
        in_specs=(
            P(None, ("groups", "rec"), None, None),
            P("groups", None),
            P(),
            P(),
            P(),
            P(),
            P(),
        ),
        out_specs=(
            P(None, ("groups", "rec"), None, None),
            P("groups", None),
            P("groups"),
            P("groups", None),
            P("groups"),
            P("groups", None),
        ),
        check_vma=False,
    )
```

```python
import functools
import math

import jax
import jax.numpy as jnp
from jax import lax
from jax.experimental import pallas as pl
from jax.experimental.pallas import tpu as pltpu
from jax.sharding import PartitionSpec as P

CAP = 2
VMEM = pl.BlockSpec(memory_space=pltpu.VMEM)
RESIDENT = 24 << 20


def run(start, step, end, steps, blocked, table):
    copy = pltpu.make_async_copy(*table)

    def begin():
        copy.start()
        start()
        copy.wait()

    if blocked:
        n = pl.program_id(0)
        pl.when(n == 0)(begin)
        step(n, 0)
        pl.when(n == steps - 1)(end)
        return
    begin()
    lax.fori_loop(0, steps, lambda n, carry: step(n, n), None)
    end()


def group_of(owners):
    for size in (32, 16, 8, 4, 2):
        if owners % size == 0:
            return size
    return 1


def fill_table(table, wide, pieces, tiles, flip, fill):
    for n, piece in enumerate(pieces):
        x = piece[...].astype(jnp.float32)
        samples = x.shape[2]
        lane = lax.broadcasted_iota(jnp.int32, x.shape, 2)
        before = jnp.where(lane == 0, 0.0, pltpu.roll(x, 1, 2))
        after = jnp.where(lane == samples - 1, 0.0, pltpu.roll(x, samples - 1, 2))
        at = pl.ds(n * tiles, tiles)
        wide[at, 0:4, :] = after if flip else before
        wide[at, 4:8, :] = x
        wide[at, 8:12, :] = before if flip else after
    last = len(pieces) * tiles
    wide[pl.ds(last, 2), 0:12, :] = jnp.zeros((2, 12, wide.shape[2]), jnp.float32)
    wide[:, 12:16, :] = jnp.full((last + 2, 4, wide.shape[2]), fill, jnp.float32)
    table[...] = wide[...].astype(jnp.bfloat16)


def act(y):
    t = jnp.tanh(y)
    q = 1.0 + t
    a = y * q
    return t, q, a


def lines_of(idx, own, halo, owners):
    lines = []
    for e in owners:
        line = []
        for r in range(4):
            held = own if r in (1, 2) else halo
            line += [None, None] if held is None else [held[idx[r, e]], held[idx[r, e] + 1]]
        lines.append(line)
    return lines


def stack(lines, traces, flip):
    return jnp.concatenate(
        [
            jnp.concatenate(
                [line[h + 1 + (2 - i if flip else i)] for line in lines for h in traces], axis=1
            )
            for i in range(3)
        ],
        axis=0,
    )


def pipeline(pieces, *stages):
    held = [None] * pieces
    for tick in range(pieces + len(stages) - 1):
        for behind in reversed(range(len(stages))):
            k = tick - behind
            if 0 <= k < pieces:
                held[k] = stages[behind](k, held[k])


def layer(w, inputs):
    t, q, a = act(jnp.dot(w[...], inputs, preferred_element_type=jnp.float32))
    return a, q + a * (1.0 - t)


def with_ones(a1):
    return jnp.concatenate([a1, jnp.ones((16, a1.shape[1]), jnp.bfloat16)], axis=0)


def forward_inner(
    group, blocked, slots, mine, w1, w2, own, a1_ref, a2_ref, d1_ref, d2_ref, wide, idx, sem,
):
    owners = lax.axis_size("rec")

    def start():
        fill_table(own, wide, (mine,), mine.shape[0], False, 1.0)

    def step(n, block):
        sub = min(16, group)
        width = sub * 2 * mine.shape[2]

        def first(k, _):
            es = [n * group + k * sub + u for u in range(sub)]
            at = slice(k * width, (k + 1) * width)
            a, d = layer(w1, stack(lines_of(idx, own, None, es), (1, 2), False))
            a1_ref[block, :, at] = a.astype(jnp.bfloat16)
            d1_ref[block, :, at] = d
            return a.astype(jnp.bfloat16)

        def second(k, a1):
            at = slice(k * width, (k + 1) * width)
            a, d = layer(w2, with_ones(a1))
            a2_ref[block, :, at] = a.astype(jnp.bfloat16)
            d2_ref[block, :, at] = d

        pipeline(group // sub, first, second)

    run(start, step, lambda: None, owners // group, blocked, (slots, idx, sem))


def forward_outer(
    group, blocked, slots, near, mine, far, own, w1, w2, w3, inner,
    res, g, halo, a1_ref, a2_ref, d1_ref, d2_ref, wide, est, idx, sem,
):
    tiles, parts, samples = mine.shape
    count = lax.axis_size("rec")
    me = lax.axis_index("rec")
    has_left = (me > 0).astype(jnp.float32)
    has_right = (me < count - 1).astype(jnp.float32)
    lane = lax.broadcasted_iota(jnp.int32, (8, samples), 1)
    low = (lane > 0).astype(jnp.float32)
    high = (lane < samples - 1).astype(jnp.float32)

    def start():
        fill_table(halo, wide, (near, far), tiles, False, 1.0)

    def step(n, block):
        cut = lambda x, k: x[:, k * samples : (k + 1) * samples]

        sub = min(8, group)
        own_part = lambda x: jnp.concatenate(
            [x[:, (u * 4 + 1) * samples : (u * 4 + 3) * samples] for u in range(sub)], axis=1
        )
        width = sub * 2 * samples

        def first(k, _):
            lines = lines_of(idx, own, halo, [n * group + k * sub + u for u in range(sub)])
            at = slice(k * width, (k + 1) * width)
            a, d = layer(w1, stack(lines, (-1, 0, 3, 4), False))
            a1 = a.astype(jnp.bfloat16)
            a1_ref[block, :, at] = own_part(a1)
            d1_ref[block, :, at] = own_part(d)
            return a1

        def second(k, a1):
            at = slice(k * width, (k + 1) * width)
            a, d = layer(w2, with_ones(a1))
            d2_ref[block, :, at] = own_part(d)
            a2_ref[block, :, at] = own_part(a).astype(jnp.bfloat16)
            rows = []
            for u in range(sub):
                row = [cut(a, u * 4 + h) for h in range(4)]
                row = [row[0] * has_left, row[1], row[2], row[3] * has_right]
                row = [part.astype(jnp.bfloat16) for part in row]
                within = [cut(inner.at[block], (k * sub + u) * 2 + h) for h in range(2)]
                rows.append(row[0:2] + within + row[2:4])
            return rows

        def third(k, rows):
            rhs = [
                jnp.concatenate([part for row in rows for part in row[i : i + 4]], axis=1)
                for i in range(3)
            ]
            terms = jnp.dot(
                w3[...], jnp.concatenate(rhs, axis=0), preferred_element_type=jnp.float32
            )
            for h in range(sub * 4):
                part = cut(terms, h)
                total = (
                    part[8:16]
                    + pltpu.roll(part[0:8], 1, 1) * low
                    + pltpu.roll(part[16:24], samples - 1, 1) * high
                )
                at = (n * group + k * sub) * 4 + h
                est[at] = total.astype(jnp.bfloat16).astype(jnp.float32)

        pipeline(group // sub, first, second, third)

    def end():
        for c in range(tiles // 2):
            at = [idx[4 + v, tiles // 2 + c] for v in range(4)]
            for k in range(2):
                total = (est[at[0] + k] + est[at[1] + k]) + (est[at[2] + k] + est[at[3] + k])
                value = total[0:parts] - mine[c * 2 + k].astype(jnp.float32)
                for o in range(parts):
                    res[o, c, k : k + 1, :] = value[o : o + 1]
                g[c * 2 + k] = value.astype(jnp.bfloat16)

    run(start, step, end, count // group, blocked, (slots, idx, sem))


def weight_terms(acc, pieces, width, fields_of, inputs_of, wo, wm, saved):
    channels = wm.shape[0]
    a1, a2, d1, d2 = saved
    of = lambda ref, k: ref[:, k * width : (k + 1) * width]

    def first(k, _):
        fields = fields_of(k)
        da2 = jnp.dot(wo[...], fields, preferred_element_type=jnp.float32)
        acc[0:48, :] += product(fields, of(a2, k), (1, 1))
        return (da2 * of(d2, k)).astype(jnp.bfloat16)

    def second(k, dz2):
        da1 = jnp.dot(wm[...], dz2, preferred_element_type=jnp.float32)
        acc[48 : 64 + channels, :] += product(with_ones(of(a1, k)), dz2, (1, 1))
        return (da1 * of(d1, k)).astype(jnp.bfloat16)

    def third(k, dz1):
        acc[64 + channels : 112 + channels, :] += product(inputs_of(k), dz1, (1, 1))

    pipeline(pieces, first, second, third)


def backward_inner(
    group, blocked, slots, mine, wo, wm, own, a1_ref, a2_ref, d1_ref, d2_ref, gown, acc, wide,
    idx, sem,
):
    owners = lax.axis_size("rec")

    def start():
        fill_table(gown, wide, (mine,), mine.shape[0], True, 0.0)
        acc[...] = jnp.zeros_like(acc)

    def step(n, block):
        sub = min(16, group)
        es = lambda k: [n * group + k * sub + u for u in range(sub)]
        weight_terms(
            acc, group // sub, sub * 2 * mine.shape[2],
            lambda k: stack(lines_of(idx, gown, None, es(k)), (1, 2), True),
            lambda k: stack(lines_of(idx, own, None, es(k)), (1, 2), False),
            wo, wm, [ref.at[block] for ref in (a1_ref, a2_ref, d1_ref, d2_ref)],
        )

    run(start, step, lambda: None, owners // group, blocked, (slots, idx, sem))


def backward_outer(
    group, blocked, slots, near, far, wo, wm, own, halo, gown, sums, a1_ref, a2_ref, d1_ref, d2_ref,
    out, ghalo, wide, acc, idx, sem,
):
    owners = lax.axis_size("rec")
    channels = wm.shape[0]
    taps = 9 * near.shape[1]

    def start():
        fill_table(ghalo, wide, (near, far), near.shape[0], True, 0.0)
        acc[...] = sums[...]

    def step(n, block):
        sub = min(16, group)
        es = lambda k: [n * group + k * sub + u for u in range(sub)]
        weight_terms(
            acc, group // sub, sub * 2 * near.shape[2],
            lambda k: stack(lines_of(idx, gown, ghalo, es(k)), (0, 3), True),
            lambda k: stack(lines_of(idx, own, halo, es(k)), (0, 3), False),
            wo, wm, [ref.at[block] for ref in (a1_ref, a2_ref, d1_ref, d2_ref)],
        )

    def end():
        first, half = 64 + channels, channels // 2
        low, high = slice(0, channels), slice(channels, 2 * channels)
        for k in range(taps):
            at = k % 9 // 3 * 16 + k % 3 * 4 + k // 9
            out[half + k : half + k + 1, low] = acc[first + at : first + at + 1, :]
            out[half + k : half + k + 1, high] = acc[at : at + 1, :]
        middle = acc[48 : 48 + channels, :].T
        out[0:half, low] = middle[0:half]
        out[0:half, high] = middle[half:channels]
        out[half + taps : half + taps + 1, low] = acc[first + 28 : first + 29, :]
        out[half + taps : half + taps + 1, high] = acc[48 + channels : 49 + channels, :]
        rest = out.shape[0] - half - taps - 1
        out[half + taps + 1 :, :] = jnp.zeros((rest, 2 * channels), jnp.float32)

    run(start, step, end, owners // group, blocked, (slots, idx, sem))


def finish_kernel(scale, *refs):
    terms, (g_in, g_bin, g_mid, g_bmid, g_out, held) = refs[:-6], refs[-6:]
    values = [ref[...] for ref in terms]
    while len(values) > 1:
        values = [values[k] + values[k + 1] for k in range(0, len(values), 2)]
    held[...] = values[0] * scale
    channels = g_mid.shape[0]
    half, taps = channels // 2, g_in.shape[0]
    low, high = slice(0, channels), slice(channels, 2 * channels)
    g_mid[0:half] = held[0:half, low]
    g_mid[half:channels] = held[0:half, high]
    g_in[...] = held[half : half + taps, low]
    g_out[...] = held[half : half + taps, high]
    g_bin[...] = held[half + taps : half + taps + 1, low]
    g_bmid[...] = held[half + taps : half + taps + 1, high]


def halves(b):
    high = b.astype(jnp.bfloat16).astype(jnp.float32)
    rest = b - high
    mid = rest.astype(jnp.bfloat16).astype(jnp.float32)
    return [high, mid, rest - mid]


def one_hot(a, b):
    return (a == b).astype(jnp.float32).astype(jnp.bfloat16)


def iota(shape, dim):
    return lax.broadcasted_iota(jnp.int32, shape, dim)


def product(a, b, over):
    return lax.dot_general(
        a, b, dimension_numbers=(((over[0],), (over[1],)), ((), ())),
        preferred_element_type=jnp.float32,
    )


def prep_kernel(blocks, *refs):
    args, (idx, w1, w2, w3, wo, wm, rows), held, sems = refs[:6], refs[6:13], refs[13:19], refs[19]
    copies = [
        pltpu.make_async_copy(src, dst, sems.at[n]) for n, (src, dst) in enumerate(zip(args, held))
    ]
    for copy in copies:
        copy.start()
    for copy in copies:
        copy.wait()
    dest, w_in, b_in, w_mid, b_mid, w_out = held
    count = lax.axis_size("rec")
    me = lax.axis_index("rec")
    ves, total = dest.shape
    channels = w_mid.shape[0]
    at = lax.rem((count + 1 - me) * blocks, total)
    wide = jnp.concatenate([dest[...], jnp.zeros((8 - ves, total), jnp.int32)], axis=0)
    near = pltpu.roll(wide, at, 1)[:, 0:128]
    lane = iota((8, 128), 1)
    low = jnp.where(me > 0, 0, blocks)
    high = jnp.where(me < count - 1, 3 * blocks, 2 * blocks)
    near = jnp.where((lane >= low) & (lane < high), near, -1)
    owner = iota((count, 128), 0)
    hits = [(near[v : v + 1] == owner).astype(jnp.float32) for v in range(ves)]
    before = iota((128, 128), 0)
    after = iota((128, 128), 1)
    segment = (after >= blocks).astype(jnp.int32) + (after >= 2 * blocks).astype(jnp.int32)
    tri = ((before < after) & (before >= segment * blocks)).astype(jnp.float32).astype(jnp.bfloat16)
    rank = product((hits[0] + hits[1] + hits[2] + hits[3]).astype(jnp.bfloat16), tri, (1, 0))
    zeroth = jnp.zeros((count, 128), jnp.float32)
    first = jnp.zeros((count, 128), jnp.float32)
    for v in range(ves):
        zeroth += hits[v] * (rank == 0.0).astype(jnp.float32)
        first += hits[v] * (rank == 1.0).astype(jnp.float32)
        item = jnp.sum(hits[v] * rank, axis=0, keepdims=True)
        idx[4 + v : 5 + v, 0:128] = near[v : v + 1] * 4 + item.astype(jnp.int32) * 2
        rank = rank + hits[v]
    line = iota((8, 128), 0)
    inside = lambda k: (lane >= k * blocks) & (lane < (k + 1) * blocks)
    odd = lax.rem(me, 2)
    left = 2 * lane + 2 * blocks * (1 - odd) - 4 * blocks
    middle = 2 * (lane - blocks) - 2 * blocks
    right = 2 * (lane - 2 * blocks) + 2 * blocks * odd - 4 * blocks
    put = lambda r, k, place: jnp.where((line == r) & inside(k), place, 0)
    pick = product(
        (put(0, 0, left) + put(2, 1, middle)).astype(jnp.float32).astype(jnp.bfloat16),
        first.astype(jnp.bfloat16),
        (1, 1),
    ) + product(
        (put(1, 1, middle) + put(3, 2, right)).astype(jnp.float32).astype(jnp.bfloat16),
        zeroth.astype(jnp.bfloat16),
        (1, 1),
    )
    empty = jnp.where((line == 0) | (line == 3), 4 * blocks, 2 * blocks)[0:4, 0:1]
    idx[0:4, 0:count] = pick[0:4].astype(jnp.int32) + empty

    taps = w_in.shape[0]
    row, col = iota((48, 40), 0), iota((48, 40), 1)
    tap, extra = row & 15, (row & 15) - 12
    target = (row & 3) * 9 + 3 * (row >> 4) + ((row >> 2) & 3)
    target = jnp.where(tap < 12, target, jnp.where((row >> 4) == 1, taps + extra, -1))
    order = one_hot(col, target)
    rows[...] = jnp.zeros_like(rows)
    rows[0:taps, :] = w_in[...].astype(jnp.float32)
    for n, part in enumerate(halves(b_in[...])):
        rows[taps + n : taps + n + 1, :] = part
    w1[...] = (0.5 * product(rows[...].astype(jnp.bfloat16), order, (0, 1))).astype(jnp.bfloat16)
    rows[...] = jnp.zeros_like(rows)
    for n, part in enumerate(halves(b_mid[...])):
        rows[n : n + 1, :] = part
    row, col = iota((40, channels + 16), 0), iota((40, channels + 16), 1)
    bias = product(rows[...].astype(jnp.bfloat16), one_hot(col, row + channels), (0, 0))
    row, col = iota((channels, channels + 16), 0), iota((channels, channels + 16), 1)
    w2[...] = (0.5 * (product(w_mid[...], one_hot(row, col), (1, 0)) + bias)).astype(jnp.bfloat16)
    rows[...] = jnp.zeros_like(rows)
    rows[0:taps, :] = w_out[...].astype(jnp.float32)
    outs = rows[...].astype(jnp.bfloat16)
    wo[...] = (0.5 * product(outs, order, (0, 1))).astype(jnp.bfloat16)
    row, col = iota((24, 40), 0), iota((24, 40), 1)
    for i in range(3):
        target = jnp.where((row & 7) < 4, (row & 3) * 9 + 3 * i + (row >> 3), -1)
        part = product(one_hot(col, target), outs, (1, 0))
        w3[:, i * channels : (i + 1) * channels] = part.astype(jnp.bfloat16)
    eye = one_hot(iota((channels, channels), 0), iota((channels, channels), 1))
    wm[...] = (0.5 * product(w_mid[...], eye, (0, 0))).astype(jnp.bfloat16)


def local(records, dest, w_in, b_in, w_mid, b_mid, w_out):
    count = lax.axis_size("rec")
    me = lax.axis_index("rec")
    parts, blocks, traces, samples = records.shape
    ves = dest.shape[1]
    tiles = blocks * traces
    channels = w_in.shape[0]
    group = group_of(count)
    steps = count // group
    width = group * 2 * samples
    far = [(s, s + 1) for s in range(1, count - 1, 2)]
    far += [(b, a) for a, b in far]
    near = [(s, s + 1) for s in range(0, count - 1, 2)]
    near += [(b, a) for a, b in near]

    flat = records.transpose(1, 2, 0, 3).reshape(tiles, parts, samples)
    from_far = lax.ppermute(flat, "rec", far)
    from_near = lax.ppermute(flat, "rec", near)

    f32, bf16 = jnp.float32, jnp.bfloat16
    shape = (steps, channels, width)
    blocked = 24 * math.prod(shape) > RESIDENT
    saved = [
        jax.ShapeDtypeStruct(shape, kind) if blocked else pltpu.VMEM(shape, kind)
        for kind in (bf16, bf16, f32, f32)
    ]
    held = [VMEM] * 4
    if blocked:
        held = [pl.BlockSpec((1, channels, width), lambda n: (n, 0, 0))] * 4
    grid = (steps,) if blocked else ()
    params = pltpu.CompilerParams(vmem_limit_bytes=16 << 20)
    args = (
        dest.T, w_in.T, b_in.reshape(1, channels), w_mid, b_mid.reshape(1, channels), w_out.T
    )
    idx, w1, w2, w3, wo, wm = pl.pallas_call(
        functools.partial(prep_kernel, blocks),
        out_shape=[jax.ShapeDtypeStruct((8, max(128, count)), jnp.int32)]
        + [
            jax.ShapeDtypeStruct(size, bf16)
            for size in (
                (channels, 48), (channels, channels + 16), (24, 3 * channels), (channels, 48),
                (channels, channels),
            )
        ],
        in_specs=[pl.BlockSpec(memory_space=pltpu.HBM)] * 6,
        out_specs=[VMEM] * 6,
        scratch_shapes=[pltpu.VMEM((40, channels), f32)]
        + [pltpu.VMEM(arg.shape, arg.dtype) for arg in args]
        + [pltpu.SemaphoreType.DMA((6,))],
        compiler_params=params,
        name="prepare",
    )(*[pltpu.with_memory_space_constraint(arg, pltpu.HBM) for arg in args])
    def table(pieces, kind):
        return pltpu.VMEM((pieces * tiles + 2, 16, samples), kind)

    def call(kernel, ins, outs, scratch, args, name, owned):
        return pl.pallas_call(
            functools.partial(kernel, group, blocked),
            grid=grid,
            out_shape=outs[0] + saved * outs[1],
            in_specs=[VMEM] * (1 + ins[0]) + held[:1] * ins[1],
            out_specs=[VMEM] * len(outs[0]) + held * outs[1],
            scratch_shapes=scratch + [pltpu.SMEM(idx.shape, idx.dtype), pltpu.SemaphoreType.DMA],
            compiler_params=params,
            cost_estimate=pl.CostEstimate(
                flops=2 * owned * count * samples * channels * (3 * channels),
                bytes_accessed=owned * count * samples * channels * 12,
                transcendentals=0,
            ),
            name=name,
        )(*args)

    total = (112 + channels, channels)
    rows = (channels // 2 + 9 * parts + 1 + 7) // 8 * 8
    own, *inner = call(
        forward_inner, (3, 0), ([table(1, bf16)], 1), [table(1, f32)],
        (idx, flat, w1, w2), "forward_inner", 2,
    )
    res, g, halo, *outer = call(
        forward_outer, (7, 1),
        (
            [
                jax.ShapeDtypeStruct(records.shape, f32),
                jax.ShapeDtypeStruct((tiles, parts, samples), bf16),
                table(2, bf16),
            ],
            1,
        ),
        [table(2, f32), pltpu.VMEM((count * 4, 8, samples), f32)],
        (idx, from_near, flat, from_far, own, w1, w2, w3, inner[1]), "forward_outer", 4,
    )
    g_far = lax.ppermute(g, "rec", far)
    g_near = lax.ppermute(g, "rec", near)
    gown, part = call(
        backward_inner, (4, 4), ([table(1, bf16), pltpu.VMEM(total, f32)], 0), [table(1, f32)],
        (idx, g, wo, wm, own, *inner), "backward_inner", 2,
    )
    (sums,) = call(
        backward_outer, (8, 4), ([jax.ShapeDtypeStruct((rows, 2 * channels), f32)], 0),
        [table(2, bf16), table(2, f32), pltpu.VMEM(total, f32)],
        (idx, g_near, g_far, wo, wm, own, halo, gown, part, *outer), "backward_outer", 2,
    )

    if count & (count - 1):
        terms = [lax.psum(sums, "rec")]
    else:
        terms = [sums]
        at = 1
        while at < count:
            wide = 4 if at > 1 and 4 * at <= count else 2
            value = terms[0]
            if len(terms) == 2:
                value = terms[0] + terms[1]
            if len(terms) == 4:
                value = (terms[0] + terms[1]) + (terms[2] + terms[3])
            terms = [value] + [
                lax.ppermute(value, "rec", [(s, s ^ (k * at)) for s in range(count)])
                for k in range(1, wide)
            ]
            at *= wide

    scale = 1.0 / math.sqrt(parts * blocks * count * traces * samples)
    g_in, g_bin, g_mid, g_bmid, g_out = pl.pallas_call(
        functools.partial(finish_kernel, scale),
        out_shape=[
            jax.ShapeDtypeStruct(shape, f32)
            for shape in (
                (parts * 9, channels), (1, channels), (channels, channels), (1, channels),
                (parts * 9, channels),
            )
        ],
        in_specs=[VMEM] * len(terms),
        out_specs=[VMEM] * 5,
        scratch_shapes=[pltpu.VMEM(sums.shape, f32)],
        compiler_params=params,
        name="finish",
    )(*terms)
    return (
        res,
        g_in.T,
        g_bin.reshape(channels),
        g_mid,
        g_bmid.reshape(channels),
        g_out.T,
    )


def solution(mesh):
    return jax.shard_map(
        local,
        mesh=mesh,
        in_specs=(
            P(None, ("groups", "rec"), None, None),
            P("groups", None),
            P(),
            P(),
            P(),
            P(),
            P(),
        ),
        out_specs=(
            P(None, ("groups", "rec"), None, None),
            P("groups", None),
            P("groups"),
            P("groups", None),
            P("groups"),
            P("groups", None),
        ),
        check_vma=False,
    )
```

```python
import functools
import math

import jax
import jax.numpy as jnp
from jax import lax
from jax.experimental import pallas as pl
from jax.experimental.pallas import tpu as pltpu
from jax.sharding import PartitionSpec as P

CAP = 2
VMEM = pl.BlockSpec(memory_space=pltpu.VMEM)
RESIDENT = 24 << 20


def run(start, step, end, steps, blocked, table):
    copy = pltpu.make_async_copy(*table)

    def begin():
        copy.start()
        start()
        copy.wait()

    if blocked:
        n = pl.program_id(0)
        pl.when(n == 0)(begin)
        step(n, 0)
        pl.when(n == steps - 1)(end)
        return
    begin()
    lax.fori_loop(0, steps, lambda n, carry: step(n, n), None)
    end()


def group_of(owners):
    for size in (32, 16, 8, 4, 2):
        if owners % size == 0:
            return size
    return 1


def fill_table(table, wide, pieces, tiles, flip, fill):
    for n, piece in enumerate(pieces):
        x = piece[...].astype(jnp.float32)
        samples = x.shape[2]
        lane = lax.broadcasted_iota(jnp.int32, x.shape, 2)
        before = jnp.where(lane == 0, 0.0, pltpu.roll(x, 1, 2))
        after = jnp.where(lane == samples - 1, 0.0, pltpu.roll(x, samples - 1, 2))
        at = pl.ds(n * tiles, tiles)
        wide[at, 0:4, :] = after if flip else before
        wide[at, 4:8, :] = x
        wide[at, 8:12, :] = before if flip else after
    last = len(pieces) * tiles
    wide[pl.ds(last, 2), 0:12, :] = jnp.zeros((2, 12, wide.shape[2]), jnp.float32)
    wide[:, 12:16, :] = jnp.full((last + 2, 4, wide.shape[2]), fill, jnp.float32)
    table[...] = wide[...].astype(jnp.bfloat16)


def act(y):
    t = jnp.tanh(y)
    q = 1.0 + t
    a = y * q
    return t, q, a


def lines_of(idx, own, halo, owners):
    lines = []
    for e in owners:
        line = []
        for r in range(4):
            held = own if r in (1, 2) else halo
            line += [None, None] if held is None else [held[idx[r, e]], held[idx[r, e] + 1]]
        lines.append(line)
    return lines


def stack(lines, traces, flip):
    return jnp.concatenate(
        [
            jnp.concatenate(
                [line[h + 1 + (2 - i if flip else i)] for line in lines for h in traces], axis=1
            )
            for i in range(3)
        ],
        axis=0,
    )


def pipeline(pieces, *stages):
    held = [None] * pieces
    for tick in range(pieces + len(stages) - 1):
        for behind in reversed(range(len(stages))):
            k = tick - behind
            if 0 <= k < pieces:
                held[k] = stages[behind](k, held[k])


def layer(w, inputs):
    t, q, a = act(jnp.dot(w[...], inputs, preferred_element_type=jnp.float32))
    return a, q + a * (1.0 - t)


def with_ones(a1):
    return jnp.concatenate([a1, jnp.ones((16, a1.shape[1]), jnp.bfloat16)], axis=0)


def forward_inner(
    group, blocked, slots, mine, w1, w2, own, a1_ref, a2_ref, d1_ref, d2_ref, wide, idx, sem,
):
    owners = lax.axis_size("rec")

    def start():
        fill_table(own, wide, (mine,), mine.shape[0], False, 1.0)

    def step(n, block):
        sub = group
        width = sub * 2 * mine.shape[2]

        def first(k, _):
            es = [n * group + k * sub + u for u in range(sub)]
            at = slice(k * width, (k + 1) * width)
            a, d = layer(w1, stack(lines_of(idx, own, None, es), (1, 2), False))
            a1_ref[block, :, at] = a.astype(jnp.bfloat16)
            d1_ref[block, :, at] = d
            return a.astype(jnp.bfloat16)

        def second(k, a1):
            at = slice(k * width, (k + 1) * width)
            a, d = layer(w2, with_ones(a1))
            a2_ref[block, :, at] = a.astype(jnp.bfloat16)
            d2_ref[block, :, at] = d

        pipeline(group // sub, first, second)

    run(start, step, lambda: None, owners // group, blocked, (slots, idx, sem))


def forward_outer(
    group, blocked, slots, near, mine, far, own, w1, w2, w3, inner,
    res, g, halo, a1_ref, a2_ref, d1_ref, d2_ref, wide, est, idx, sem,
):
    tiles, parts, samples = mine.shape
    count = lax.axis_size("rec")
    me = lax.axis_index("rec")
    odd = lax.rem(me, 2)
    has_left = (me > 0).astype(jnp.float32)
    has_right = (me < count - 1).astype(jnp.float32)
    lane = lax.broadcasted_iota(jnp.int32, (8, samples), 1)
    low = (lane > 0).astype(jnp.float32)
    high = (lane < samples - 1).astype(jnp.float32)

    def start():
        fill_table(halo, wide, (near, far), tiles, False, 1.0)

    def step(n, block):
        cut = lambda x, k: x[:, k * samples : (k + 1) * samples]

        sub = min(8, group)
        width = sub * samples

        def save(ref, k, x):
            for h, side in ((1, 1 - odd), (2, odd)):
                ref[block, side, :, k * width : (k + 1) * width] = jnp.concatenate(
                    [cut(x, u * 4 + h) for u in range(sub)], axis=1
                )

        def first(k, _):
            lines = lines_of(idx, own, halo, [n * group + k * sub + u for u in range(sub)])
            a, d = layer(w1, stack(lines, (-1, 0, 3, 4), False))
            a1 = a.astype(jnp.bfloat16)
            save(a1_ref, k, a1)
            save(d1_ref, k, d)
            return a1

        def second(k, a1):
            a, d = layer(w2, with_ones(a1))
            save(d2_ref, k, d)
            save(a2_ref, k, a.astype(jnp.bfloat16))
            rows = []
            for u in range(sub):
                row = [cut(a, u * 4 + h) for h in range(4)]
                row = [row[0] * has_left, row[1], row[2], row[3] * has_right]
                row = [part.astype(jnp.bfloat16) for part in row]
                within = [cut(inner.at[block], (k * sub + u) * 2 + h) for h in range(2)]
                rows.append(row[0:2] + within + row[2:4])
            return rows

        def third(k, rows):
            rhs = [
                jnp.concatenate([part for row in rows for part in row[i : i + 4]], axis=1)
                for i in range(3)
            ]
            terms = jnp.dot(
                w3[...], jnp.concatenate(rhs, axis=0), preferred_element_type=jnp.float32
            )
            for h in range(sub * 4):
                part = cut(terms, h)
                total = (
                    part[8:16]
                    + pltpu.roll(part[0:8], 1, 1) * low
                    + pltpu.roll(part[16:24], samples - 1, 1) * high
                )
                at = (n * group + k * sub) * 4 + h
                est[at] = total.astype(jnp.bfloat16).astype(jnp.float32)

        pipeline(group // sub, first, second, third)

    def end():
        for c in range(tiles // 2):
            at = [idx[4 + v, tiles // 2 + c] for v in range(4)]
            for k in range(2):
                total = (est[at[0] + k] + est[at[1] + k]) + (est[at[2] + k] + est[at[3] + k])
                value = total[0:parts] - mine[c * 2 + k].astype(jnp.float32)
                for o in range(parts):
                    res[o, c, k : k + 1, :] = value[o : o + 1]
                g[c * 2 + k] = value.astype(jnp.bfloat16)

    run(start, step, end, count // group, blocked, (slots, idx, sem))


def weight_terms(acc, pieces, width, fields_of, inputs_of, wo, wm, saved):
    channels = wm.shape[0]
    a1, a2, d1, d2 = saved
    of = lambda ref, k: ref[:, k * width : (k + 1) * width]

    def first(k, _):
        fields = fields_of(k)
        da2 = jnp.dot(wo[...], fields, preferred_element_type=jnp.float32)
        acc[0:48, :] += product(fields, of(a2, k), (1, 1))
        return (da2 * of(d2, k)).astype(jnp.bfloat16)

    def second(k, dz2):
        da1 = jnp.dot(wm[...], dz2, preferred_element_type=jnp.float32)
        acc[48 : 64 + channels, :] += product(with_ones(of(a1, k)), dz2, (1, 1))
        return (da1 * of(d1, k)).astype(jnp.bfloat16)

    def third(k, dz1):
        acc[64 + channels : 112 + channels, :] += product(inputs_of(k), dz1, (1, 1))

    pipeline(pieces, first, second, third)


def backward_inner(
    group, blocked, slots, mine, wo, wm, own, a1_ref, a2_ref, d1_ref, d2_ref, gown, acc, wide,
    idx, sem,
):
    owners = lax.axis_size("rec")

    def start():
        fill_table(gown, wide, (mine,), mine.shape[0], True, 0.0)
        acc[...] = jnp.zeros_like(acc)

    def step(n, block):
        sub = group
        es = lambda k: [n * group + k * sub + u for u in range(sub)]
        weight_terms(
            acc, group // sub, sub * 2 * mine.shape[2],
            lambda k: stack(lines_of(idx, gown, None, es(k)), (1, 2), True),
            lambda k: stack(lines_of(idx, own, None, es(k)), (1, 2), False),
            wo, wm, [ref.at[block] for ref in (a1_ref, a2_ref, d1_ref, d2_ref)],
        )

    run(start, step, lambda: None, owners // group, blocked, (slots, idx, sem))


def pack_terms(acc, out, taps, channels):
    first, half = 64 + channels, channels // 2
    low, high = slice(0, channels), slice(channels, 2 * channels)
    for k in range(taps):
        at = k % 9 // 3 * 16 + k % 3 * 4 + k // 9
        out[half + k : half + k + 1, low] = acc[first + at : first + at + 1, :]
        out[half + k : half + k + 1, high] = acc[at : at + 1, :]
    middle = acc[48 : 48 + channels, :].T
    out[0:half, low] = middle[0:half]
    out[0:half, high] = middle[half:channels]
    out[half + taps : half + taps + 1, low] = acc[first + 28 : first + 29, :]
    out[half + taps : half + taps + 1, high] = acc[48 + channels : 49 + channels, :]
    rest = out.shape[0] - half - taps - 1
    out[half + taps + 1 :, :] = jnp.zeros((rest, 2 * channels), jnp.float32)


def backward_edge(
    group, blocked, slots, piece, wo, wm, own, halo, gown, sums, a1_ref, a2_ref, d1_ref, d2_ref,
    out, ghalo, wide, acc, idx, sem, *, far,
):
    tiles, parts, _ = piece.shape
    owners = lax.axis_size("rec")
    channels = wm.shape[0]
    side = 1 if far else 0
    left = lax.rem(lax.axis_index("rec"), 2) == (0 if far else 1)

    def start():
        fill_table(ghalo, wide, (piece,), tiles, True, 0.0)
        acc[...] = sums[...]

    def tiles_of(e, table, outer, g):
        at = jnp.where(left, idx[0, e], idx[3, e])
        if g:
            at = at - tiles if far else jnp.minimum(at, tiles)
        beyond = outer[at + jnp.where(left, 1, 0)]
        here = table[jnp.where(left, idx[1, e], idx[2, e] + 1)]
        within = table[jnp.where(left, idx[1, e] + 1, idx[2, e])]
        return [lax.select_n(left, within, beyond), here, lax.select_n(left, beyond, within)]

    def step(n, block):
        def of(table, outer, g):
            lines = [tiles_of(n * group + u, table, outer, g) for u in range(group)]
            order = (2, 1, 0) if g else (0, 1, 2)
            return jnp.concatenate(
                [jnp.concatenate([line[i] for line in lines], axis=1) for i in order], axis=0
            )

        weight_terms(
            acc, 1, group * piece.shape[2], lambda k: of(gown, ghalo, True),
            lambda k: of(own, halo, False), wo, wm,
            [ref.at[block, 0 if blocked else side] for ref in (a1_ref, a2_ref, d1_ref, d2_ref)],
        )

    def end():
        if far:
            pack_terms(acc, out, 9 * parts, channels)
        else:
            out[...] = acc[...]

    run(start, step, end, owners // group, blocked, (slots, idx, sem))


def finish_kernel(scale, *refs):
    terms, (g_in, g_bin, g_mid, g_bmid, g_out, held) = refs[:-6], refs[-6:]
    values = [ref[...] for ref in terms]
    while len(values) > 1:
        values = [values[k] + values[k + 1] for k in range(0, len(values), 2)]
    held[...] = values[0] * scale
    channels = g_mid.shape[0]
    half, taps = channels // 2, g_in.shape[0]
    low, high = slice(0, channels), slice(channels, 2 * channels)
    g_mid[0:half] = held[0:half, low]
    g_mid[half:channels] = held[0:half, high]
    g_in[...] = held[half : half + taps, low]
    g_out[...] = held[half : half + taps, high]
    g_bin[...] = held[half + taps : half + taps + 1, low]
    g_bmid[...] = held[half + taps : half + taps + 1, high]


def halves(b):
    high = b.astype(jnp.bfloat16).astype(jnp.float32)
    rest = b - high
    mid = rest.astype(jnp.bfloat16).astype(jnp.float32)
    return [high, mid, rest - mid]


def one_hot(a, b):
    return (a == b).astype(jnp.float32).astype(jnp.bfloat16)


def iota(shape, dim):
    return lax.broadcasted_iota(jnp.int32, shape, dim)


def product(a, b, over):
    return lax.dot_general(
        a, b, dimension_numbers=(((over[0],), (over[1],)), ((), ())),
        preferred_element_type=jnp.float32,
    )


def prep_kernel(blocks, *refs):
    args, (idx, w1, w2, w3, wo, wm, rows), held, sems = refs[:6], refs[6:13], refs[13:19], refs[19]
    copies = [
        pltpu.make_async_copy(src, dst, sems.at[n]) for n, (src, dst) in enumerate(zip(args, held))
    ]
    for copy in copies:
        copy.start()
    for copy in copies:
        copy.wait()
    dest, w_in, b_in, w_mid, b_mid, w_out = held
    count = lax.axis_size("rec")
    me = lax.axis_index("rec")
    ves, total = dest.shape
    channels = w_mid.shape[0]
    at = lax.rem((count + 1 - me) * blocks, total)
    wide = jnp.concatenate([dest[...], jnp.zeros((8 - ves, total), jnp.int32)], axis=0)
    near = pltpu.roll(wide, at, 1)[:, 0:128]
    lane = iota((8, 128), 1)
    low = jnp.where(me > 0, 0, blocks)
    high = jnp.where(me < count - 1, 3 * blocks, 2 * blocks)
    near = jnp.where((lane >= low) & (lane < high), near, -1)
    owner = iota((count, 128), 0)
    hits = [(near[v : v + 1] == owner).astype(jnp.float32) for v in range(ves)]
    before = iota((128, 128), 0)
    after = iota((128, 128), 1)
    segment = (after >= blocks).astype(jnp.int32) + (after >= 2 * blocks).astype(jnp.int32)
    tri = ((before < after) & (before >= segment * blocks)).astype(jnp.float32).astype(jnp.bfloat16)
    rank = product((hits[0] + hits[1] + hits[2] + hits[3]).astype(jnp.bfloat16), tri, (1, 0))
    zeroth = jnp.zeros((count, 128), jnp.float32)
    first = jnp.zeros((count, 128), jnp.float32)
    for v in range(ves):
        zeroth += hits[v] * (rank == 0.0).astype(jnp.float32)
        first += hits[v] * (rank == 1.0).astype(jnp.float32)
        item = jnp.sum(hits[v] * rank, axis=0, keepdims=True)
        idx[4 + v : 5 + v, 0:128] = near[v : v + 1] * 4 + item.astype(jnp.int32) * 2
        rank = rank + hits[v]
    line = iota((8, 128), 0)
    inside = lambda k: (lane >= k * blocks) & (lane < (k + 1) * blocks)
    odd = lax.rem(me, 2)
    left = 2 * lane + 2 * blocks * (1 - odd) - 4 * blocks
    middle = 2 * (lane - blocks) - 2 * blocks
    right = 2 * (lane - 2 * blocks) + 2 * blocks * odd - 4 * blocks
    put = lambda r, k, place: jnp.where((line == r) & inside(k), place, 0)
    pick = product(
        (put(0, 0, left) + put(2, 1, middle)).astype(jnp.float32).astype(jnp.bfloat16),
        first.astype(jnp.bfloat16),
        (1, 1),
    ) + product(
        (put(1, 1, middle) + put(3, 2, right)).astype(jnp.float32).astype(jnp.bfloat16),
        zeroth.astype(jnp.bfloat16),
        (1, 1),
    )
    empty = jnp.where((line == 0) | (line == 3), 4 * blocks, 2 * blocks)[0:4, 0:1]
    idx[0:4, 0:count] = pick[0:4].astype(jnp.int32) + empty

    taps = w_in.shape[0]
    row, col = iota((48, 40), 0), iota((48, 40), 1)
    tap, extra = row & 15, (row & 15) - 12
    target = (row & 3) * 9 + 3 * (row >> 4) + ((row >> 2) & 3)
    target = jnp.where(tap < 12, target, jnp.where((row >> 4) == 1, taps + extra, -1))
    order = one_hot(col, target)
    rows[...] = jnp.zeros_like(rows)
    rows[0:taps, :] = w_in[...].astype(jnp.float32)
    for n, part in enumerate(halves(b_in[...])):
        rows[taps + n : taps + n + 1, :] = part
    w1[...] = (0.5 * product(rows[...].astype(jnp.bfloat16), order, (0, 1))).astype(jnp.bfloat16)
    rows[...] = jnp.zeros_like(rows)
    for n, part in enumerate(halves(b_mid[...])):
        rows[n : n + 1, :] = part
    row, col = iota((40, channels + 16), 0), iota((40, channels + 16), 1)
    bias = product(rows[...].astype(jnp.bfloat16), one_hot(col, row + channels), (0, 0))
    row, col = iota((channels, channels + 16), 0), iota((channels, channels + 16), 1)
    w2[...] = (0.5 * (product(w_mid[...], one_hot(row, col), (1, 0)) + bias)).astype(jnp.bfloat16)
    rows[...] = jnp.zeros_like(rows)
    rows[0:taps, :] = w_out[...].astype(jnp.float32)
    outs = rows[...].astype(jnp.bfloat16)
    wo[...] = (0.5 * product(outs, order, (0, 1))).astype(jnp.bfloat16)
    row, col = iota((24, 40), 0), iota((24, 40), 1)
    for i in range(3):
        target = jnp.where((row & 7) < 4, (row & 3) * 9 + 3 * i + (row >> 3), -1)
        part = product(one_hot(col, target), outs, (1, 0))
        w3[:, i * channels : (i + 1) * channels] = part.astype(jnp.bfloat16)
    eye = one_hot(iota((channels, channels), 0), iota((channels, channels), 1))
    wm[...] = (0.5 * product(w_mid[...], eye, (0, 0))).astype(jnp.bfloat16)


def local(records, dest, w_in, b_in, w_mid, b_mid, w_out):
    count = lax.axis_size("rec")
    me = lax.axis_index("rec")
    parts, blocks, traces, samples = records.shape
    ves = dest.shape[1]
    tiles = blocks * traces
    channels = w_in.shape[0]
    group = group_of(count)
    steps = count // group
    width = group * 2 * samples
    far = [(s, s + 1) for s in range(1, count - 1, 2)]
    far += [(b, a) for a, b in far]
    near = [(s, s + 1) for s in range(0, count - 1, 2)]
    near += [(b, a) for a, b in near]

    flat = records.transpose(1, 2, 0, 3).reshape(tiles, parts, samples)
    from_far = lax.ppermute(flat, "rec", far)
    from_near = lax.ppermute(flat, "rec", near)

    f32, bf16 = jnp.float32, jnp.bfloat16
    shape = (steps, channels, width)
    blocked = 24 * math.prod(shape) > RESIDENT
    saved = [
        jax.ShapeDtypeStruct(shape, kind) if blocked else pltpu.VMEM(shape, kind)
        for kind in (bf16, bf16, f32, f32)
    ]
    edge_shape = (steps, 2, channels, group * samples)
    saved_edge = [
        jax.ShapeDtypeStruct(edge_shape, kind) if blocked else pltpu.VMEM(edge_shape, kind)
        for kind in (bf16, bf16, f32, f32)
    ]
    held = [VMEM] * 4
    held_edge = held_sides = [held, held]
    if blocked:
        held = [pl.BlockSpec((1, channels, width), lambda n: (n, 0, 0))] * 4
        whole_edge = pl.BlockSpec((1, *edge_shape[1:]), lambda n: (n, 0, 0, 0))
        sides = [
            pl.BlockSpec((1, 1, *edge_shape[2:]), lambda n, side=side: (n, side, 0, 0))
            for side in range(2)
        ]
        held_edge, held_sides = [[whole_edge] * 4] * 2, [[side] * 4 for side in sides]
    grid = (steps,) if blocked else ()
    params = pltpu.CompilerParams(vmem_limit_bytes=16 << 20)
    args = (
        dest.T, w_in.T, b_in.reshape(1, channels), w_mid, b_mid.reshape(1, channels), w_out.T
    )
    idx, w1, w2, w3, wo, wm = pl.pallas_call(
        functools.partial(prep_kernel, blocks),
        out_shape=[jax.ShapeDtypeStruct((8, max(128, count)), jnp.int32)]
        + [
            jax.ShapeDtypeStruct(size, bf16)
            for size in (
                (channels, 48), (channels, channels + 16), (24, 3 * channels), (channels, 48),
                (channels, channels),
            )
        ],
        in_specs=[pl.BlockSpec(memory_space=pltpu.HBM)] * 6,
        out_specs=[VMEM] * 6,
        scratch_shapes=[pltpu.VMEM((40, channels), f32)]
        + [pltpu.VMEM(arg.shape, arg.dtype) for arg in args]
        + [pltpu.SemaphoreType.DMA((6,))],
        compiler_params=params,
        name="prepare",
    )(*[pltpu.with_memory_space_constraint(arg, pltpu.HBM) for arg in args])
    def table(pieces, kind):
        return pltpu.VMEM((pieces * tiles + 2, 16, samples), kind)

    def call(kernel, ins, outs, scratch, args, name, owned):
        return pl.pallas_call(
            functools.partial(kernel, group, blocked),
            grid=grid,
            out_shape=outs[0] + outs[1],
            in_specs=[VMEM] * (1 + ins[0]) + ins[1],
            out_specs=[VMEM] * len(outs[0]) + outs[2],
            scratch_shapes=scratch + [pltpu.SMEM(idx.shape, idx.dtype), pltpu.SemaphoreType.DMA],
            compiler_params=params,
            cost_estimate=pl.CostEstimate(
                flops=2 * owned * count * samples * channels * (3 * channels),
                bytes_accessed=owned * count * samples * channels * 12,
                transcendentals=0,
            ),
            name=name,
        )(*args)

    total = (112 + channels, channels)
    rows = (channels // 2 + 9 * parts + 1 + 7) // 8 * 8
    own, *inner = call(
        forward_inner, (3, []), ([table(1, bf16)], saved, held), [table(1, f32)],
        (idx, flat, w1, w2), "forward_inner", 2,
    )
    res, g, halo, *outer = call(
        forward_outer, (7, held[:1]),
        (
            [
                jax.ShapeDtypeStruct(records.shape, f32),
                jax.ShapeDtypeStruct((tiles, parts, samples), bf16),
                table(2, bf16),
            ],
            saved_edge,
            held_edge[0],
        ),
        [table(2, f32), pltpu.VMEM((count * 4, 8, samples), f32)],
        (idx, from_near, flat, from_far, own, w1, w2, w3, inner[1]), "forward_outer", 4,
    )
    g_far = lax.ppermute(g, "rec", far)
    g_near = lax.ppermute(g, "rec", near)
    gown, part = call(
        backward_inner, (4, held), ([table(1, bf16), pltpu.VMEM(total, f32)], [], []),
        [table(1, f32)], (idx, g, wo, wm, own, *inner), "backward_inner", 2,
    )

    def edge(piece, part, out, far):
        return call(
            functools.partial(backward_edge, far=far), (7, held_sides[1 if far else 0]), ([out], [], []),
            [table(1, bf16), table(1, f32), pltpu.VMEM(total, f32)],
            (idx, piece, wo, wm, own, halo, gown, part, *outer),
            "backward_far" if far else "backward_near", 1,
        )[0]

    part = edge(g_near, part, pltpu.VMEM(total, f32), False)
    sums = edge(g_far, part, jax.ShapeDtypeStruct((rows, 2 * channels), f32), True)

    if count & (count - 1):
        terms = [lax.psum(sums, "rec")]
    else:
        terms = [sums]
        at = 1
        while at < count:
            wide = 4 if at > 1 and 4 * at <= count else 2
            value = terms[0]
            if len(terms) == 2:
                value = terms[0] + terms[1]
            if len(terms) == 4:
                value = (terms[0] + terms[1]) + (terms[2] + terms[3])
            terms = [value] + [
                lax.ppermute(value, "rec", [(s, s ^ (k * at)) for s in range(count)])
                for k in range(1, wide)
            ]
            at *= wide

    scale = 1.0 / math.sqrt(parts * blocks * count * traces * samples)
    g_in, g_bin, g_mid, g_bmid, g_out = pl.pallas_call(
        functools.partial(finish_kernel, scale),
        out_shape=[
            jax.ShapeDtypeStruct(shape, f32)
            for shape in (
                (parts * 9, channels), (1, channels), (channels, channels), (1, channels),
                (parts * 9, channels),
            )
        ],
        in_specs=[VMEM] * len(terms),
        out_specs=[VMEM] * 5,
        scratch_shapes=[pltpu.VMEM(sums.shape, f32)],
        compiler_params=params,
        name="finish",
    )(*terms)
    return (
        res,
        g_in.T,
        g_bin.reshape(channels),
        g_mid,
        g_bmid.reshape(channels),
        g_out.T,
    )


def solution(mesh):
    return jax.shard_map(
        local,
        mesh=mesh,
        in_specs=(
            P(None, ("groups", "rec"), None, None),
            P("groups", None),
            P(),
            P(),
            P(),
            P(),
            P(),
        ),
        out_specs=(
            P(None, ("groups", "rec"), None, None),
            P("groups", None),
            P("groups"),
            P("groups", None),
            P("groups"),
            P("groups", None),
        ),
        check_vma=False,
    )
```

```python
import functools
import math

import jax
import jax.numpy as jnp
from jax import lax
from jax.experimental import pallas as pl
from jax.experimental.pallas import tpu as pltpu
from jax.sharding import PartitionSpec as P

CAP = 2
VMEM = pl.BlockSpec(memory_space=pltpu.VMEM)
RESIDENT = 24 << 20


def run(start, step, end, steps, blocked, table):
    copy = pltpu.make_async_copy(*table)

    def begin():
        copy.start()
        start()
        copy.wait()

    if blocked:
        n = pl.program_id(0)
        pl.when(n == 0)(begin)
        step(n, 0)
        pl.when(n == steps - 1)(end)
        return
    begin()
    lax.fori_loop(0, steps, lambda n, carry: step(n, n), None)
    end()


def group_of(owners):
    for size in (32, 16, 8, 4, 2):
        if owners % size == 0:
            return size
    return 1


def fill_table(table, pieces, tiles, flip, fill):
    for n, piece in enumerate(pieces):
        x = piece[...].astype(jnp.float32)
        x = jnp.concatenate([x, x], axis=1)
        samples = x.shape[2]
        row = lax.broadcasted_iota(jnp.int32, x.shape, 1)
        lane = lax.broadcasted_iota(jnp.int32, x.shape, 2)
        earlier = row >= 4 if flip else row < 4
        sides = jnp.where(earlier, pltpu.roll(x, 1, 2), pltpu.roll(x, samples - 1, 2))
        sides = jnp.where(lane == jnp.where(earlier, 0, samples - 1), 0.0, sides)
        rest = jnp.where(row < 4, x, fill)
        table[pl.ds(n * tiles, tiles)] = jnp.concatenate([sides, rest], axis=1).astype(jnp.bfloat16)
    last, count = len(pieces) * tiles, table.shape[0]
    row = lax.broadcasted_iota(jnp.int32, (count - last, *table.shape[1:]), 1)
    table[pl.ds(last, count - last)] = jnp.where(row < 12, 0.0, fill).astype(jnp.bfloat16)


def act(y):
    t = jnp.tanh(y)
    q = 1.0 + t
    a = y * q
    return t, q, a


def lines_of(idx, own, halo, owners):
    lines = []
    for e in owners:
        line = []
        for r in range(4):
            held = own if r in (1, 2) else halo
            line += [None, None] if held is None else [held[idx[r, e]], held[idx[r, e] + 1]]
        lines.append(line)
    return lines


def stack(lines, traces, flip):
    return jnp.concatenate(
        [
            jnp.concatenate(
                [line[h + 1 + (2 - i if flip else i)] for line in lines for h in traces], axis=1
            )
            for i in range(3)
        ],
        axis=0,
    )


def pipeline(pieces, *stages):
    held = [None] * pieces
    for tick in range(pieces + len(stages) - 1):
        for behind in reversed(range(len(stages))):
            k = tick - behind
            if 0 <= k < pieces:
                held[k] = stages[behind](k, held[k])


def layer(w, inputs):
    t, q, a = act(jnp.dot(w[...], inputs, preferred_element_type=jnp.float32))
    return a, q + a * (1.0 - t)


def with_ones(a1):
    return jnp.concatenate([a1, jnp.ones((16, a1.shape[1]), jnp.bfloat16)], axis=0)


def forward_inner(
    group, blocked, slots, mine, w1, w2, own, a1_ref, a2_ref, d1_ref, d2_ref, idx, sem,
):
    owners = lax.axis_size("rec")

    def start():
        fill_table(own, (mine,), mine.shape[0], False, 1.0)

    def step(n, block):
        sub = group
        width = sub * 2 * mine.shape[2]

        def first(k, _):
            es = [n * group + k * sub + u for u in range(sub)]
            at = slice(k * width, (k + 1) * width)
            a, d = layer(w1, stack(lines_of(idx, own, None, es), (1, 2), False))
            a1_ref[block, :, at] = a.astype(jnp.bfloat16)
            d1_ref[block, :, at] = d
            return a.astype(jnp.bfloat16)

        def second(k, a1):
            at = slice(k * width, (k + 1) * width)
            a, d = layer(w2, with_ones(a1))
            a2_ref[block, :, at] = a.astype(jnp.bfloat16)
            d2_ref[block, :, at] = d

        pipeline(group // sub, first, second)

    run(start, step, lambda: None, owners // group, blocked, (slots, idx, sem))


def forward_outer(
    group, blocked, slots, near, mine, far, own, w1, w2, w3, inner,
    res, g, halo, a1_ref, a2_ref, d1_ref, d2_ref, est, idx, sem,
):
    tiles, parts, samples = mine.shape
    count = lax.axis_size("rec")
    me = lax.axis_index("rec")
    has_left = (me > 0).astype(jnp.float32)
    has_right = (me < count - 1).astype(jnp.float32)
    lane = lax.broadcasted_iota(jnp.int32, (8, samples), 1)
    low = (lane > 0).astype(jnp.float32)
    high = (lane < samples - 1).astype(jnp.float32)

    def start():
        fill_table(halo, (near, far), tiles, False, 1.0)

    def step(n, block):
        cut = lambda x, k: x[:, k * samples : (k + 1) * samples]

        sub = min(8, group)
        own_part = lambda x: jnp.concatenate(
            [x[:, (u * 4 + 1) * samples : (u * 4 + 3) * samples] for u in range(sub)], axis=1
        )
        width = sub * 2 * samples

        def first(k, _):
            lines = lines_of(idx, own, halo, [n * group + k * sub + u for u in range(sub)])
            at = slice(k * width, (k + 1) * width)
            a, d = layer(w1, stack(lines, (-1, 0, 3, 4), False))
            a1 = a.astype(jnp.bfloat16)
            a1_ref[block, :, at] = own_part(a1)
            d1_ref[block, :, at] = own_part(d)
            return a1

        def second(k, a1):
            at = slice(k * width, (k + 1) * width)
            a, d = layer(w2, with_ones(a1))
            d2_ref[block, :, at] = own_part(d)
            a2_ref[block, :, at] = own_part(a).astype(jnp.bfloat16)
            rows = []
            for u in range(sub):
                row = [cut(a, u * 4 + h) for h in range(4)]
                row = [row[0] * has_left, row[1], row[2], row[3] * has_right]
                row = [part.astype(jnp.bfloat16) for part in row]
                within = [cut(inner.at[block], (k * sub + u) * 2 + h) for h in range(2)]
                rows.append(row[0:2] + within + row[2:4])
            return rows

        def third(k, rows):
            rhs = [
                jnp.concatenate([part for row in rows for part in row[i : i + 4]], axis=1)
                for i in range(3)
            ]
            terms = jnp.dot(
                w3[...], jnp.concatenate(rhs, axis=0), preferred_element_type=jnp.float32
            )
            for h in range(sub * 4):
                part = cut(terms, h)
                total = (
                    part[8:16]
                    + pltpu.roll(part[0:8], 1, 1) * low
                    + pltpu.roll(part[16:24], samples - 1, 1) * high
                )
                at = (n * group + k * sub) * 4 + h
                est[at] = total.astype(jnp.bfloat16).astype(jnp.float32)

        pipeline(group // sub, first, second, third)

    def end():
        for c in range(tiles // 2):
            at = [idx[4 + v, tiles // 2 + c] for v in range(4)]
            for k in range(2):
                total = (est[at[0] + k] + est[at[1] + k]) + (est[at[2] + k] + est[at[3] + k])
                value = total[0:parts] - mine[c * 2 + k].astype(jnp.float32)
                for o in range(parts):
                    res[o, c, k : k + 1, :] = value[o : o + 1]
                g[c * 2 + k] = value.astype(jnp.bfloat16)

    run(start, step, end, count // group, blocked, (slots, idx, sem))


def weight_terms(acc, pieces, width, fields_of, inputs_of, wo, wm, saved):
    channels = wm.shape[0]
    a1, a2, d1, d2 = saved
    of = lambda ref, k: ref[:, k * width : (k + 1) * width]

    def first(k, _):
        fields = fields_of(k)
        da2 = jnp.dot(wo[...], fields, preferred_element_type=jnp.float32)
        acc[0:48, :] += product(fields, of(a2, k), (1, 1))
        return (da2 * of(d2, k)).astype(jnp.bfloat16)

    def second(k, dz2):
        da1 = jnp.dot(wm[...], dz2, preferred_element_type=jnp.float32)
        acc[48 : 64 + channels, :] += product(with_ones(of(a1, k)), dz2, (1, 1))
        return (da1 * of(d1, k)).astype(jnp.bfloat16)

    def third(k, dz1):
        acc[64 + channels : 112 + channels, :] += product(inputs_of(k), dz1, (1, 1))

    pipeline(pieces, first, second, third)


def backward_inner(
    group, blocked, slots, mine, wo, wm, own, a1_ref, a2_ref, d1_ref, d2_ref, gown, acc,
    idx, sem,
):
    owners = lax.axis_size("rec")

    def start():
        fill_table(gown, (mine,), mine.shape[0], True, 0.0)
        acc[...] = jnp.zeros_like(acc)

    def step(n, block):
        sub = group
        es = lambda k: [n * group + k * sub + u for u in range(sub)]
        weight_terms(
            acc, group // sub, sub * 2 * mine.shape[2],
            lambda k: stack(lines_of(idx, gown, None, es(k)), (1, 2), True),
            lambda k: stack(lines_of(idx, own, None, es(k)), (1, 2), False),
            wo, wm, [ref.at[block] for ref in (a1_ref, a2_ref, d1_ref, d2_ref)],
        )

    run(start, step, lambda: None, owners // group, blocked, (slots, idx, sem))


def backward_outer(
    group, blocked, slots, near, far, wo, wm, own, halo, gown, sums, a1_ref, a2_ref, d1_ref, d2_ref,
    out, ghalo, acc, idx, sem,
):
    owners = lax.axis_size("rec")
    channels = wm.shape[0]
    taps = 9 * near.shape[1]

    def start():
        fill_table(ghalo, (near, far), near.shape[0], True, 0.0)
        acc[...] = sums[...]

    def step(n, block):
        sub = group
        es = lambda k: [n * group + k * sub + u for u in range(sub)]
        weight_terms(
            acc, group // sub, sub * 2 * near.shape[2],
            lambda k: stack(lines_of(idx, gown, ghalo, es(k)), (0, 3), True),
            lambda k: stack(lines_of(idx, own, halo, es(k)), (0, 3), False),
            wo, wm, [ref.at[block] for ref in (a1_ref, a2_ref, d1_ref, d2_ref)],
        )

    def end():
        first, half = 64 + channels, channels // 2
        low, high = slice(0, channels), slice(channels, 2 * channels)
        for k in range(taps):
            at = k % 9 // 3 * 16 + k % 3 * 2 % 3 * 4 + k // 9
            out[half + k : half + k + 1, low] = acc[first + at : first + at + 1, :]
            out[half + k : half + k + 1, high] = acc[at : at + 1, :]
        middle = acc[48 : 48 + channels, :].T
        out[0:half, low] = middle[0:half]
        out[0:half, high] = middle[half:channels]
        out[half + taps : half + taps + 1, low] = acc[first + 28 : first + 29, :]
        out[half + taps : half + taps + 1, high] = acc[48 + channels : 49 + channels, :]
        rest = out.shape[0] - half - taps - 1
        out[half + taps + 1 :, :] = jnp.zeros((rest, 2 * channels), jnp.float32)

    run(start, step, end, owners // group, blocked, (slots, idx, sem))


def finish_kernel(scale, *refs):
    terms, (g_in, g_bin, g_mid, g_bmid, g_out, held) = refs[:-6], refs[-6:]
    values = [ref[...] for ref in terms]
    while len(values) > 1:
        values = [values[k] + values[k + 1] for k in range(0, len(values), 2)]
    held[...] = values[0] * scale
    channels = g_mid.shape[0]
    half, taps = channels // 2, g_in.shape[0]
    low, high = slice(0, channels), slice(channels, 2 * channels)
    g_mid[0:half] = held[0:half, low]
    g_mid[half:channels] = held[0:half, high]
    g_in[...] = held[half : half + taps, low]
    g_out[...] = held[half : half + taps, high]
    g_bin[...] = held[half + taps : half + taps + 1, low]
    g_bmid[...] = held[half + taps : half + taps + 1, high]


def halves(b):
    high = b.astype(jnp.bfloat16).astype(jnp.float32)
    rest = b - high
    mid = rest.astype(jnp.bfloat16).astype(jnp.float32)
    return [high, mid, rest - mid]


def one_hot(a, b):
    return (a == b).astype(jnp.float32).astype(jnp.bfloat16)


def iota(shape, dim):
    return lax.broadcasted_iota(jnp.int32, shape, dim)


def product(a, b, over):
    return lax.dot_general(
        a, b, dimension_numbers=(((over[0],), (over[1],)), ((), ())),
        preferred_element_type=jnp.float32,
    )


def prep_kernel(blocks, *refs):
    args, (idx, w1, w2, w3, wo, wm, rows), held, sems = refs[:6], refs[6:13], refs[13:19], refs[19]
    copies = [
        pltpu.make_async_copy(src, dst, sems.at[n]) for n, (src, dst) in enumerate(zip(args, held))
    ]
    for copy in copies:
        copy.start()
    for copy in copies:
        copy.wait()
    dest, w_in, b_in, w_mid, b_mid, w_out = held
    count = lax.axis_size("rec")
    me = lax.axis_index("rec")
    ves, total = dest.shape
    channels = w_mid.shape[0]
    at = lax.rem((count + 1 - me) * blocks, total)
    wide = jnp.concatenate([dest[...], jnp.zeros((8 - ves, total), jnp.int32)], axis=0)
    near = pltpu.roll(wide, at, 1)[:, 0:128]
    lane = iota((8, 128), 1)
    low = jnp.where(me > 0, 0, blocks)
    high = jnp.where(me < count - 1, 3 * blocks, 2 * blocks)
    near = jnp.where((lane >= low) & (lane < high), near, -1)
    owner = iota((count, 128), 0)
    hits = [(near[v : v + 1] == owner).astype(jnp.float32) for v in range(ves)]
    before = iota((128, 128), 0)
    after = iota((128, 128), 1)
    segment = (after >= blocks).astype(jnp.int32) + (after >= 2 * blocks).astype(jnp.int32)
    tri = ((before < after) & (before >= segment * blocks)).astype(jnp.float32).astype(jnp.bfloat16)
    rank = product((hits[0] + hits[1] + hits[2] + hits[3]).astype(jnp.bfloat16), tri, (1, 0))
    zeroth = jnp.zeros((count, 128), jnp.float32)
    first = jnp.zeros((count, 128), jnp.float32)
    for v in range(ves):
        zeroth += hits[v] * (rank == 0.0).astype(jnp.float32)
        first += hits[v] * (rank == 1.0).astype(jnp.float32)
        item = jnp.sum(hits[v] * rank, axis=0, keepdims=True)
        idx[4 + v : 5 + v, 0:128] = near[v : v + 1] * 4 + item.astype(jnp.int32) * 2
        rank = rank + hits[v]
    line = iota((8, 128), 0)
    inside = lambda k: (lane >= k * blocks) & (lane < (k + 1) * blocks)
    odd = lax.rem(me, 2)
    left = 2 * lane + 2 * blocks * (1 - odd) - 4 * blocks
    middle = 2 * (lane - blocks) - 2 * blocks
    right = 2 * (lane - 2 * blocks) + 2 * blocks * odd - 4 * blocks
    put = lambda r, k, place: jnp.where((line == r) & inside(k), place, 0)
    pick = product(
        (put(0, 0, left) + put(2, 1, middle)).astype(jnp.float32).astype(jnp.bfloat16),
        first.astype(jnp.bfloat16),
        (1, 1),
    ) + product(
        (put(1, 1, middle) + put(3, 2, right)).astype(jnp.float32).astype(jnp.bfloat16),
        zeroth.astype(jnp.bfloat16),
        (1, 1),
    )
    empty = jnp.where((line == 0) | (line == 3), 4 * blocks, 2 * blocks)[0:4, 0:1]
    idx[0:4, 0:count] = pick[0:4].astype(jnp.int32) + empty

    taps = w_in.shape[0]
    row, col = iota((48, 40), 0), iota((48, 40), 1)
    tap, extra = row & 15, (row & 15) - 12
    place = (row >> 2) & 3
    target = (row & 3) * 9 + 3 * (row >> 4) + jnp.where(place == 0, 0, 3 - place)
    target = jnp.where(tap < 12, target, jnp.where((row >> 4) == 1, taps + extra, -1))
    order = one_hot(col, target)
    rows[...] = jnp.zeros_like(rows)
    rows[0:taps, :] = w_in[...].astype(jnp.float32)
    for n, part in enumerate(halves(b_in[...])):
        rows[taps + n : taps + n + 1, :] = part
    w1[...] = (0.5 * product(rows[...].astype(jnp.bfloat16), order, (0, 1))).astype(jnp.bfloat16)
    rows[...] = jnp.zeros_like(rows)
    for n, part in enumerate(halves(b_mid[...])):
        rows[n : n + 1, :] = part
    row, col = iota((40, channels + 16), 0), iota((40, channels + 16), 1)
    bias = product(rows[...].astype(jnp.bfloat16), one_hot(col, row + channels), (0, 0))
    row, col = iota((channels, channels + 16), 0), iota((channels, channels + 16), 1)
    w2[...] = (0.5 * (product(w_mid[...], one_hot(row, col), (1, 0)) + bias)).astype(jnp.bfloat16)
    rows[...] = jnp.zeros_like(rows)
    rows[0:taps, :] = w_out[...].astype(jnp.float32)
    outs = rows[...].astype(jnp.bfloat16)
    wo[...] = (0.5 * product(outs, order, (0, 1))).astype(jnp.bfloat16)
    row, col = iota((24, 40), 0), iota((24, 40), 1)
    for i in range(3):
        target = jnp.where((row & 7) < 4, (row & 3) * 9 + 3 * i + (row >> 3), -1)
        part = product(one_hot(col, target), outs, (1, 0))
        w3[:, i * channels : (i + 1) * channels] = part.astype(jnp.bfloat16)
    eye = one_hot(iota((channels, channels), 0), iota((channels, channels), 1))
    wm[...] = (0.5 * product(w_mid[...], eye, (0, 0))).astype(jnp.bfloat16)


def local(records, dest, w_in, b_in, w_mid, b_mid, w_out):
    count = lax.axis_size("rec")
    me = lax.axis_index("rec")
    parts, blocks, traces, samples = records.shape
    ves = dest.shape[1]
    tiles = blocks * traces
    channels = w_in.shape[0]
    group = group_of(count)
    steps = count // group
    width = group * 2 * samples
    far = [(s, s + 1) for s in range(1, count - 1, 2)]
    far += [(b, a) for a, b in far]
    near = [(s, s + 1) for s in range(0, count - 1, 2)]
    near += [(b, a) for a, b in near]

    flat = records.transpose(1, 2, 0, 3).reshape(tiles, parts, samples)
    from_far = lax.ppermute(flat, "rec", far)
    from_near = lax.ppermute(flat, "rec", near)

    f32, bf16 = jnp.float32, jnp.bfloat16
    shape = (steps, channels, width)
    blocked = 24 * math.prod(shape) > RESIDENT
    saved = [
        jax.ShapeDtypeStruct(shape, kind) if blocked else pltpu.VMEM(shape, kind)
        for kind in (bf16, bf16, f32, f32)
    ]
    held = [VMEM] * 4
    if blocked:
        held = [pl.BlockSpec((1, channels, width), lambda n: (n, 0, 0))] * 4
    grid = (steps,) if blocked else ()
    params = pltpu.CompilerParams(vmem_limit_bytes=16 << 20)
    args = (
        dest.T, w_in.T, b_in.reshape(1, channels), w_mid, b_mid.reshape(1, channels), w_out.T
    )
    idx, w1, w2, w3, wo, wm = pl.pallas_call(
        functools.partial(prep_kernel, blocks),
        out_shape=[jax.ShapeDtypeStruct((8, max(128, count)), jnp.int32)]
        + [
            jax.ShapeDtypeStruct(size, bf16)
            for size in (
                (channels, 48), (channels, channels + 16), (24, 3 * channels), (channels, 48),
                (channels, channels),
            )
        ],
        in_specs=[pl.BlockSpec(memory_space=pltpu.HBM)] * 6,
        out_specs=[VMEM] * 6,
        scratch_shapes=[pltpu.VMEM((40, channels), f32)]
        + [pltpu.VMEM(arg.shape, arg.dtype) for arg in args]
        + [pltpu.SemaphoreType.DMA((6,))],
        compiler_params=params,
        name="prepare",
    )(*[pltpu.with_memory_space_constraint(arg, pltpu.HBM) for arg in args])
    def table(pieces, kind):
        return pltpu.VMEM((pieces * tiles + 2, 16, samples), kind)

    def call(kernel, ins, outs, scratch, args, name, owned):
        return pl.pallas_call(
            functools.partial(kernel, group, blocked),
            grid=grid,
            out_shape=outs[0] + saved * outs[1],
            in_specs=[VMEM] * (1 + ins[0]) + held[:1] * ins[1],
            out_specs=[VMEM] * len(outs[0]) + held * outs[1],
            scratch_shapes=scratch + [pltpu.SMEM(idx.shape, idx.dtype), pltpu.SemaphoreType.DMA],
            compiler_params=params,
            cost_estimate=pl.CostEstimate(
                flops=2 * owned * count * samples * channels * (3 * channels),
                bytes_accessed=owned * count * samples * channels * 12,
                transcendentals=0,
            ),
            name=name,
        )(*args)

    total = (112 + channels, channels)
    rows = (channels // 2 + 9 * parts + 1 + 7) // 8 * 8
    own, *inner = call(
        forward_inner, (3, 0), ([table(1, bf16)], 1), [],
        (idx, flat, w1, w2), "forward_inner", 2,
    )
    res, g, halo, *outer = call(
        forward_outer, (7, 1),
        (
            [
                jax.ShapeDtypeStruct(records.shape, f32),
                jax.ShapeDtypeStruct((tiles, parts, samples), bf16),
                table(2, bf16),
            ],
            1,
        ),
        [pltpu.VMEM((count * 4, 8, samples), f32)],
        (idx, from_near, flat, from_far, own, w1, w2, w3, inner[1]), "forward_outer", 4,
    )
    g_far = lax.ppermute(g, "rec", far)
    g_near = lax.ppermute(g, "rec", near)
    gown, part = call(
        backward_inner, (4, 4), ([table(1, bf16), pltpu.VMEM(total, f32)], 0), [],
        (idx, g, wo, wm, own, *inner), "backward_inner", 2,
    )
    (sums,) = call(
        backward_outer, (8, 4), ([jax.ShapeDtypeStruct((rows, 2 * channels), f32)], 0),
        [table(2, bf16), pltpu.VMEM(total, f32)],
        (idx, g_near, g_far, wo, wm, own, halo, gown, part, *outer), "backward_outer", 2,
    )

    if count & (count - 1):
        terms = [lax.psum(sums, "rec")]
    else:
        terms = [sums]
        at = 1
        while at < count:
            wide = 4 if at > 1 and 4 * at <= count else 2
            value = terms[0]
            if len(terms) == 2:
                value = terms[0] + terms[1]
            if len(terms) == 4:
                value = (terms[0] + terms[1]) + (terms[2] + terms[3])
            terms = [value] + [
                lax.ppermute(value, "rec", [(s, s ^ (k * at)) for s in range(count)])
                for k in range(1, wide)
            ]
            at *= wide

    scale = 1.0 / math.sqrt(parts * blocks * count * traces * samples)
    g_in, g_bin, g_mid, g_bmid, g_out = pl.pallas_call(
        functools.partial(finish_kernel, scale),
        out_shape=[
            jax.ShapeDtypeStruct(shape, f32)
            for shape in (
                (parts * 9, channels), (1, channels), (channels, channels), (1, channels),
                (parts * 9, channels),
            )
        ],
        in_specs=[VMEM] * len(terms),
        out_specs=[VMEM] * 5,
        scratch_shapes=[pltpu.VMEM(sums.shape, f32)],
        compiler_params=params,
        name="finish",
    )(*terms)
    return (
        res,
        g_in.T,
        g_bin.reshape(channels),
        g_mid,
        g_bmid.reshape(channels),
        g_out.T,
    )


def solution(mesh):
    return jax.shard_map(
        local,
        mesh=mesh,
        in_specs=(
            P(None, ("groups", "rec"), None, None),
            P("groups", None),
            P(),
            P(),
            P(),
            P(),
            P(),
        ),
        out_specs=(
            P(None, ("groups", "rec"), None, None),
            P("groups", None),
            P("groups"),
            P("groups", None),
            P("groups"),
            P("groups", None),
        ),
        check_vma=False,
    )
```

```python
import functools
import math

import jax
import jax.numpy as jnp
from jax import lax
from jax.experimental import pallas as pl
from jax.experimental.pallas import tpu as pltpu
from jax.sharding import PartitionSpec as P

CAP = 2
VMEM = pl.BlockSpec(memory_space=pltpu.VMEM)
RESIDENT = 24 << 20


def run(start, step, end, steps, blocked, table):
    copy = pltpu.make_async_copy(*table)

    def begin():
        copy.start()
        start()
        copy.wait()

    if blocked:
        n = pl.program_id(0)
        pl.when(n == 0)(begin)
        step(n, 0)
        pl.when(n == steps - 1)(end)
        return
    begin()
    lax.fori_loop(0, steps, lambda n, carry: step(n, n), None)
    end()


def group_of(owners):
    for size in (32, 16, 8, 4, 2):
        if owners % size == 0:
            return size
    return 1


def fill_table(table, pieces, tiles, flip, fill):
    for n, piece in enumerate(pieces):
        x = piece[...].astype(jnp.float32)
        x = jnp.concatenate([x, x], axis=1)
        samples = x.shape[2]
        row = lax.broadcasted_iota(jnp.int32, x.shape, 1)
        lane = lax.broadcasted_iota(jnp.int32, x.shape, 2)
        earlier = row >= 4 if flip else row < 4
        sides = jnp.where(earlier, pltpu.roll(x, 1, 2), pltpu.roll(x, samples - 1, 2))
        sides = jnp.where(lane == jnp.where(earlier, 0, samples - 1), 0.0, sides)
        rest = jnp.where(row < 4, x, fill)
        table[pl.ds(n * tiles, tiles)] = jnp.concatenate([sides, rest], axis=1).astype(jnp.bfloat16)
    last, count = len(pieces) * tiles, table.shape[0]
    row = lax.broadcasted_iota(jnp.int32, (count - last, *table.shape[1:]), 1)
    table[pl.ds(last, count - last)] = jnp.where(row < 12, 0.0, fill).astype(jnp.bfloat16)


def act(y):
    t = jnp.tanh(y)
    q = 1.0 + t
    a = y * q
    return t, q, a


def lines_of(idx, own, halo, owners):
    lines = []
    for e in owners:
        line = []
        for r in range(4):
            held = own if r in (1, 2) else halo
            line += [None, None] if held is None else [held[idx[r, e]], held[idx[r, e] + 1]]
        lines.append(line)
    return lines


def stack(lines, traces, flip):
    return jnp.concatenate(
        [
            jnp.concatenate(
                [line[h + 1 + (2 - i if flip else i)] for line in lines for h in traces], axis=1
            )
            for i in range(3)
        ],
        axis=0,
    )


def pipeline(pieces, *stages):
    held = [None] * pieces
    for tick in range(pieces + len(stages) - 1):
        for behind in reversed(range(len(stages))):
            k = tick - behind
            if 0 <= k < pieces:
                held[k] = stages[behind](k, held[k])


def layer(w, inputs):
    t, q, a = act(jnp.dot(w[...], inputs, preferred_element_type=jnp.float32))
    return a, q + a * (1.0 - t)


def with_ones(a1):
    return jnp.concatenate([a1, jnp.ones((16, a1.shape[1]), jnp.bfloat16)], axis=0)


def forward_inner(
    group, blocked, slots, mine, w1, w2, own, a1_ref, a2_ref, d1_ref, d2_ref, idx, sem,
):
    owners = lax.axis_size("rec")

    def start():
        fill_table(own, (mine,), mine.shape[0], False, 1.0)

    def step(n, block):
        sub = group
        width = sub * 2 * mine.shape[2]

        def first(k, _):
            es = [n * group + k * sub + u for u in range(sub)]
            at = slice(k * width, (k + 1) * width)
            a, d = layer(w1, stack(lines_of(idx, own, None, es), (1, 2), False))
            a1_ref[block, :, at] = a.astype(jnp.bfloat16)
            d1_ref[block, :, at] = d
            return a.astype(jnp.bfloat16)

        def second(k, a1):
            at = slice(k * width, (k + 1) * width)
            a, d = layer(w2, with_ones(a1))
            a2_ref[block, :, at] = a.astype(jnp.bfloat16)
            d2_ref[block, :, at] = d

        pipeline(group // sub, first, second)

    run(start, step, lambda: None, owners // group, blocked, (slots, idx, sem))


def forward_outer(
    group, blocked, slots, left, mine, right, own, w1, w2, w3, inner,
    res, g, halo, a1_ref, a2_ref, d1_ref, d2_ref, est, idx, sem,
):
    tiles, parts, samples = mine.shape
    count = lax.axis_size("rec")
    me = lax.axis_index("rec")
    has_left = (me > 0).astype(jnp.float32)
    has_right = (me < count - 1).astype(jnp.float32)
    lane = lax.broadcasted_iota(jnp.int32, (8, samples), 1)
    low = (lane > 0).astype(jnp.float32)
    high = (lane < samples - 1).astype(jnp.float32)

    def start():
        fill_table(halo, (left, right), tiles, False, 1.0)

    def step(n, block):
        cut = lambda x, k: x[:, k * samples : (k + 1) * samples]

        sub = min(8, group)
        own_part = lambda x: jnp.concatenate(
            [x[:, (u * 4 + 1) * samples : (u * 4 + 3) * samples] for u in range(sub)], axis=1
        )
        width = sub * 2 * samples

        def first(k, _):
            lines = lines_of(idx, own, halo, [n * group + k * sub + u for u in range(sub)])
            at = slice(k * width, (k + 1) * width)
            a, d = layer(w1, stack(lines, (-1, 0, 3, 4), False))
            a1 = a.astype(jnp.bfloat16)
            a1_ref[block, :, at] = own_part(a1)
            d1_ref[block, :, at] = own_part(d)
            return a1

        def second(k, a1):
            at = slice(k * width, (k + 1) * width)
            a, d = layer(w2, with_ones(a1))
            d2_ref[block, :, at] = own_part(d)
            a2_ref[block, :, at] = own_part(a).astype(jnp.bfloat16)
            rows = []
            for u in range(sub):
                row = [cut(a, u * 4 + h) for h in range(4)]
                row = [row[0] * has_left, row[1], row[2], row[3] * has_right]
                row = [part.astype(jnp.bfloat16) for part in row]
                within = [cut(inner.at[block], (k * sub + u) * 2 + h) for h in range(2)]
                rows.append(row[0:2] + within + row[2:4])
            return rows

        def third(k, rows):
            rhs = [
                jnp.concatenate([part for row in rows for part in row[i : i + 4]], axis=1)
                for i in range(3)
            ]
            terms = jnp.dot(
                w3[...], jnp.concatenate(rhs, axis=0), preferred_element_type=jnp.float32
            )
            for h in range(sub * 4):
                part = cut(terms, h)
                total = (
                    part[8:16]
                    + pltpu.roll(part[0:8], 1, 1) * low
                    + pltpu.roll(part[16:24], samples - 1, 1) * high
                )
                at = (n * group + k * sub) * 4 + h
                est[at] = total.astype(jnp.bfloat16).astype(jnp.float32)

        pipeline(group // sub, first, second, third)

    def end():
        for c in range(tiles // 2):
            at = [idx[4 + v, tiles // 2 + c] for v in range(4)]
            for k in range(2):
                total = (est[at[0] + k] + est[at[1] + k]) + (est[at[2] + k] + est[at[3] + k])
                value = total[0:parts] - mine[c * 2 + k].astype(jnp.float32)
                for o in range(parts):
                    res[o, c, k : k + 1, :] = value[o : o + 1]
                g[c * 2 + k] = value.astype(jnp.bfloat16)

    run(start, step, end, count // group, blocked, (slots, idx, sem))


def weight_terms(acc, pieces, width, fields_of, inputs_of, wo, wm, saved):
    channels = wm.shape[0]
    a1, a2, d1, d2 = saved
    of = lambda ref, k: ref[:, k * width : (k + 1) * width]

    def first(k, _):
        fields = fields_of(k)
        da2 = jnp.dot(wo[...], fields, preferred_element_type=jnp.float32)
        acc[0:48, :] += product(fields, of(a2, k), (1, 1))
        return (da2 * of(d2, k)).astype(jnp.bfloat16)

    def second(k, dz2):
        da1 = jnp.dot(wm[...], dz2, preferred_element_type=jnp.float32)
        acc[48 : 64 + channels, :] += product(with_ones(of(a1, k)), dz2, (1, 1))
        return (da1 * of(d1, k)).astype(jnp.bfloat16)

    def third(k, dz1):
        acc[64 + channels : 112 + channels, :] += product(inputs_of(k), dz1, (1, 1))

    pipeline(pieces, first, second, third)


def backward_inner(
    group, blocked, slots, mine, wo, wm, own, a1_ref, a2_ref, d1_ref, d2_ref, gown, acc,
    idx, sem,
):
    owners = lax.axis_size("rec")

    def start():
        fill_table(gown, (mine,), mine.shape[0], True, 0.0)
        acc[...] = jnp.zeros_like(acc)

    def step(n, block):
        sub = group
        es = lambda k: [n * group + k * sub + u for u in range(sub)]
        weight_terms(
            acc, group // sub, sub * 2 * mine.shape[2],
            lambda k: stack(lines_of(idx, gown, None, es(k)), (1, 2), True),
            lambda k: stack(lines_of(idx, own, None, es(k)), (1, 2), False),
            wo, wm, [ref.at[block] for ref in (a1_ref, a2_ref, d1_ref, d2_ref)],
        )

    run(start, step, lambda: None, owners // group, blocked, (slots, idx, sem))


def backward_outer(
    group, blocked, slots, left, right, wo, wm, own, halo, gown, sums, a1_ref, a2_ref, d1_ref, d2_ref,
    out, ghalo, acc, idx, sem,
):
    owners = lax.axis_size("rec")
    channels = wm.shape[0]
    taps = 9 * left.shape[1]

    def start():
        fill_table(ghalo, (left, right), left.shape[0], True, 0.0)
        acc[...] = sums[...]

    def step(n, block):
        sub = group
        es = lambda k: [n * group + k * sub + u for u in range(sub)]
        weight_terms(
            acc, group // sub, sub * 2 * left.shape[2],
            lambda k: stack(lines_of(idx, gown, ghalo, es(k)), (0, 3), True),
            lambda k: stack(lines_of(idx, own, halo, es(k)), (0, 3), False),
            wo, wm, [ref.at[block] for ref in (a1_ref, a2_ref, d1_ref, d2_ref)],
        )

    def end():
        first, half = 64 + channels, channels // 2
        low, high = slice(0, channels), slice(channels, 2 * channels)
        for k in range(taps):
            at = k % 9 // 3 * 16 + k % 3 * 2 % 3 * 4 + k // 9
            out[half + k : half + k + 1, low] = acc[first + at : first + at + 1, :]
            out[half + k : half + k + 1, high] = acc[at : at + 1, :]
        middle = acc[48 : 48 + channels, :].T
        out[0:half, low] = middle[0:half]
        out[0:half, high] = middle[half:channels]
        out[half + taps : half + taps + 1, low] = acc[first + 28 : first + 29, :]
        out[half + taps : half + taps + 1, high] = acc[48 + channels : 49 + channels, :]
        rest = out.shape[0] - half - taps - 1
        out[half + taps + 1 :, :] = jnp.zeros((rest, 2 * channels), jnp.float32)

    run(start, step, end, owners // group, blocked, (slots, idx, sem))


def finish_kernel(scale, *refs):
    terms, (g_in, g_bin, g_mid, g_bmid, g_out, held) = refs[:-6], refs[-6:]
    values = [ref[...] for ref in terms]
    while len(values) > 1:
        values = [values[k] + values[k + 1] for k in range(0, len(values), 2)]
    held[...] = values[0] * scale
    channels = g_mid.shape[0]
    half, taps = channels // 2, g_in.shape[0]
    low, high = slice(0, channels), slice(channels, 2 * channels)
    g_mid[0:half] = held[0:half, low]
    g_mid[half:channels] = held[0:half, high]
    g_in[...] = held[half : half + taps, low]
    g_out[...] = held[half : half + taps, high]
    g_bin[...] = held[half + taps : half + taps + 1, low]
    g_bmid[...] = held[half + taps : half + taps + 1, high]


def halves(b):
    high = b.astype(jnp.bfloat16).astype(jnp.float32)
    rest = b - high
    mid = rest.astype(jnp.bfloat16).astype(jnp.float32)
    return [high, mid, rest - mid]


def one_hot(a, b):
    return (a == b).astype(jnp.float32).astype(jnp.bfloat16)


def iota(shape, dim):
    return lax.broadcasted_iota(jnp.int32, shape, dim)


def product(a, b, over):
    return lax.dot_general(
        a, b, dimension_numbers=(((over[0],), (over[1],)), ((), ())),
        preferred_element_type=jnp.float32,
    )


def prep_kernel(blocks, *refs):
    args, (idx, w1, w2, w3, wo, wm, rows), held, sems = refs[:6], refs[6:13], refs[13:19], refs[19]
    copies = [
        pltpu.make_async_copy(src, dst, sems.at[n]) for n, (src, dst) in enumerate(zip(args, held))
    ]
    for copy in copies:
        copy.start()
    for copy in copies:
        copy.wait()
    dest, w_in, b_in, w_mid, b_mid, w_out = held
    count = lax.axis_size("rec")
    me = lax.axis_index("rec")
    ves, total = dest.shape
    channels = w_mid.shape[0]
    at = lax.rem((count + 1 - me) * blocks, total)
    wide = jnp.concatenate([dest[...], jnp.zeros((8 - ves, total), jnp.int32)], axis=0)
    near = pltpu.roll(wide, at, 1)[:, 0:128]
    lane = iota((8, 128), 1)
    low = jnp.where(me > 0, 0, blocks)
    high = jnp.where(me < count - 1, 3 * blocks, 2 * blocks)
    near = jnp.where((lane >= low) & (lane < high), near, -1)
    owner = iota((count, 128), 0)
    hits = [(near[v : v + 1] == owner).astype(jnp.float32) for v in range(ves)]
    before = iota((128, 128), 0)
    after = iota((128, 128), 1)
    segment = (after >= blocks).astype(jnp.int32) + (after >= 2 * blocks).astype(jnp.int32)
    tri = ((before < after) & (before >= segment * blocks)).astype(jnp.float32).astype(jnp.bfloat16)
    rank = product((hits[0] + hits[1] + hits[2] + hits[3]).astype(jnp.bfloat16), tri, (1, 0))
    zeroth = jnp.zeros((count, 128), jnp.float32)
    first = jnp.zeros((count, 128), jnp.float32)
    for v in range(ves):
        zeroth += hits[v] * (rank == 0.0).astype(jnp.float32)
        first += hits[v] * (rank == 1.0).astype(jnp.float32)
        item = jnp.sum(hits[v] * rank, axis=0, keepdims=True)
        idx[4 + v : 5 + v, 0:128] = near[v : v + 1] * 4 + item.astype(jnp.int32) * 2
        rank = rank + hits[v]
    line = iota((8, 128), 0)
    inside = lambda k: (lane >= k * blocks) & (lane < (k + 1) * blocks)
    left = 2 * lane - 4 * blocks
    middle = 2 * (lane - blocks) - 2 * blocks
    right = 2 * (lane - blocks) - 4 * blocks
    put = lambda r, k, place: jnp.where((line == r) & inside(k), place, 0)
    pick = product(
        (put(0, 0, left) + put(2, 1, middle)).astype(jnp.float32).astype(jnp.bfloat16),
        first.astype(jnp.bfloat16),
        (1, 1),
    ) + product(
        (put(1, 1, middle) + put(3, 2, right)).astype(jnp.float32).astype(jnp.bfloat16),
        zeroth.astype(jnp.bfloat16),
        (1, 1),
    )
    empty = jnp.where((line == 0) | (line == 3), 4 * blocks, 2 * blocks)[0:4, 0:1]
    idx[0:4, 0:count] = pick[0:4].astype(jnp.int32) + empty

    taps = w_in.shape[0]
    row, col = iota((48, 40), 0), iota((48, 40), 1)
    tap, extra = row & 15, (row & 15) - 12
    place = (row >> 2) & 3
    target = (row & 3) * 9 + 3 * (row >> 4) + jnp.where(place == 0, 0, 3 - place)
    target = jnp.where(tap < 12, target, jnp.where((row >> 4) == 1, taps + extra, -1))
    order = one_hot(col, target)
    rows[...] = jnp.zeros_like(rows)
    rows[0:taps, :] = w_in[...].astype(jnp.float32)
    for n, part in enumerate(halves(b_in[...])):
        rows[taps + n : taps + n + 1, :] = part
    w1[...] = (0.5 * product(rows[...].astype(jnp.bfloat16), order, (0, 1))).astype(jnp.bfloat16)
    rows[...] = jnp.zeros_like(rows)
    for n, part in enumerate(halves(b_mid[...])):
        rows[n : n + 1, :] = part
    row, col = iota((40, channels + 16), 0), iota((40, channels + 16), 1)
    bias = product(rows[...].astype(jnp.bfloat16), one_hot(col, row + channels), (0, 0))
    row, col = iota((channels, channels + 16), 0), iota((channels, channels + 16), 1)
    w2[...] = (0.5 * (product(w_mid[...], one_hot(row, col), (1, 0)) + bias)).astype(jnp.bfloat16)
    rows[...] = jnp.zeros_like(rows)
    rows[0:taps, :] = w_out[...].astype(jnp.float32)
    outs = rows[...].astype(jnp.bfloat16)
    wo[...] = (0.5 * product(outs, order, (0, 1))).astype(jnp.bfloat16)
    row, col = iota((24, 40), 0), iota((24, 40), 1)
    for i in range(3):
        target = jnp.where((row & 7) < 4, (row & 3) * 9 + 3 * i + (row >> 3), -1)
        part = product(one_hot(col, target), outs, (1, 0))
        w3[:, i * channels : (i + 1) * channels] = part.astype(jnp.bfloat16)
    eye = one_hot(iota((channels, channels), 0), iota((channels, channels), 1))
    wm[...] = (0.5 * product(w_mid[...], eye, (0, 0))).astype(jnp.bfloat16)


def local(records, dest, w_in, b_in, w_mid, b_mid, w_out):
    count = lax.axis_size("rec")
    me = lax.axis_index("rec")
    parts, blocks, traces, samples = records.shape
    ves = dest.shape[1]
    tiles = blocks * traces
    channels = w_in.shape[0]
    group = group_of(count)
    steps = count // group
    width = group * 2 * samples
    up = [(s, (s + 1) % count) for s in range(count)]
    down = [(s, (s - 1) % count) for s in range(count)]

    flat = records.transpose(1, 2, 0, 3).reshape(tiles, parts, samples)
    from_left = lax.ppermute(flat, "rec", up)
    from_right = lax.ppermute(flat, "rec", down)

    f32, bf16 = jnp.float32, jnp.bfloat16
    shape = (steps, channels, width)
    blocked = 24 * math.prod(shape) > RESIDENT
    saved = [
        jax.ShapeDtypeStruct(shape, kind) if blocked else pltpu.VMEM(shape, kind)
        for kind in (bf16, bf16, f32, f32)
    ]
    held = [VMEM] * 4
    if blocked:
        held = [pl.BlockSpec((1, channels, width), lambda n: (n, 0, 0))] * 4
    grid = (steps,) if blocked else ()
    params = pltpu.CompilerParams(vmem_limit_bytes=16 << 20)
    args = (
        dest.T, w_in.T, b_in.reshape(1, channels), w_mid, b_mid.reshape(1, channels), w_out.T
    )
    idx, w1, w2, w3, wo, wm = pl.pallas_call(
        functools.partial(prep_kernel, blocks),
        out_shape=[jax.ShapeDtypeStruct((8, max(128, count)), jnp.int32)]
        + [
            jax.ShapeDtypeStruct(size, bf16)
            for size in (
                (channels, 48), (channels, channels + 16), (24, 3 * channels), (channels, 48),
                (channels, channels),
            )
        ],
        in_specs=[pl.BlockSpec(memory_space=pltpu.HBM)] * 6,
        out_specs=[VMEM] * 6,
        scratch_shapes=[pltpu.VMEM((40, channels), f32)]
        + [pltpu.VMEM(arg.shape, arg.dtype) for arg in args]
        + [pltpu.SemaphoreType.DMA((6,))],
        compiler_params=params,
        name="prepare",
    )(*[pltpu.with_memory_space_constraint(arg, pltpu.HBM) for arg in args])
    def table(pieces, kind):
        return pltpu.VMEM((pieces * tiles + 2, 16, samples), kind)

    def call(kernel, ins, outs, scratch, args, name, owned):
        return pl.pallas_call(
            functools.partial(kernel, group, blocked),
            grid=grid,
            out_shape=outs[0] + saved * outs[1],
            in_specs=[VMEM] * (1 + ins[0]) + held[:1] * ins[1],
            out_specs=[VMEM] * len(outs[0]) + held * outs[1],
            scratch_shapes=scratch + [pltpu.SMEM(idx.shape, idx.dtype), pltpu.SemaphoreType.DMA],
            compiler_params=params,
            cost_estimate=pl.CostEstimate(
                flops=2 * owned * count * samples * channels * (3 * channels),
                bytes_accessed=owned * count * samples * channels * 12,
                transcendentals=0,
            ),
            name=name,
        )(*args)

    total = (112 + channels, channels)
    rows = (channels // 2 + 9 * parts + 1 + 7) // 8 * 8
    own, *inner = call(
        forward_inner, (3, 0), ([table(1, bf16)], 1), [],
        (idx, flat, w1, w2), "forward_inner", 2,
    )
    res, g, halo, *outer = call(
        forward_outer, (7, 1),
        (
            [
                jax.ShapeDtypeStruct(records.shape, f32),
                jax.ShapeDtypeStruct((tiles, parts, samples), bf16),
                table(2, bf16),
            ],
            1,
        ),
        [pltpu.VMEM((count * 4, 8, samples), f32)],
        (idx, from_left, flat, from_right, own, w1, w2, w3, inner[1]), "forward_outer", 4,
    )
    g_left = lax.ppermute(g, "rec", up)
    g_right = lax.ppermute(g, "rec", down)
    gown, part = call(
        backward_inner, (4, 4), ([table(1, bf16), pltpu.VMEM(total, f32)], 0), [],
        (idx, g, wo, wm, own, *inner), "backward_inner", 2,
    )
    (sums,) = call(
        backward_outer, (8, 4), ([jax.ShapeDtypeStruct((rows, 2 * channels), f32)], 0),
        [table(2, bf16), pltpu.VMEM(total, f32)],
        (idx, g_left, g_right, wo, wm, own, halo, gown, part, *outer), "backward_outer", 2,
    )

    if count & (count - 1):
        terms = [lax.psum(sums, "rec")]
    else:
        terms = [sums]
        at = 1
        while at < count:
            wide = 4 if at > 1 and 4 * at <= count else 2
            value = terms[0]
            if len(terms) == 2:
                value = terms[0] + terms[1]
            if len(terms) == 4:
                value = (terms[0] + terms[1]) + (terms[2] + terms[3])
            terms = [value] + [
                lax.ppermute(value, "rec", [(s, s ^ (k * at)) for s in range(count)])
                for k in range(1, wide)
            ]
            at *= wide

    scale = 1.0 / math.sqrt(parts * blocks * count * traces * samples)
    g_in, g_bin, g_mid, g_bmid, g_out = pl.pallas_call(
        functools.partial(finish_kernel, scale),
        out_shape=[
            jax.ShapeDtypeStruct(shape, f32)
            for shape in (
                (parts * 9, channels), (1, channels), (channels, channels), (1, channels),
                (parts * 9, channels),
            )
        ],
        in_specs=[VMEM] * len(terms),
        out_specs=[VMEM] * 5,
        scratch_shapes=[pltpu.VMEM(sums.shape, f32)],
        compiler_params=params,
        name="finish",
    )(*terms)
    return (
        res,
        g_in.T,
        g_bin.reshape(channels),
        g_mid,
        g_bmid.reshape(channels),
        g_out.T,
    )


def solution(mesh):
    return jax.shard_map(
        local,
        mesh=mesh,
        in_specs=(
            P(None, ("groups", "rec"), None, None),
            P("groups", None),
            P(),
            P(),
            P(),
            P(),
            P(),
        ),
        out_specs=(
            P(None, ("groups", "rec"), None, None),
            P("groups", None),
            P("groups"),
            P("groups", None),
            P("groups"),
            P("groups", None),
        ),
        check_vma=False,
    )
```

```python
import functools
import math

import jax
import jax.numpy as jnp
from jax import lax
from jax.experimental import pallas as pl
from jax.experimental.pallas import tpu as pltpu
from jax.sharding import PartitionSpec as P

CAP = 2
VMEM = pl.BlockSpec(memory_space=pltpu.VMEM)
RESIDENT = 24 << 20


def run(start, step, end, steps, blocked, table):
    copy = pltpu.make_async_copy(*table)

    def begin():
        copy.start()
        start()
        copy.wait()

    if blocked:
        n = pl.program_id(0)
        pl.when(n == 0)(begin)
        step(n, 0)
        pl.when(n == steps - 1)(end)
        return
    begin()
    lax.fori_loop(0, steps, lambda n, carry: step(n, n), None)
    end()


def group_of(owners):
    for size in (32, 16, 8, 4, 2):
        if owners % size == 0:
            return size
    return 1


def fill_table(table, pieces, tiles, flip, fill):
    for n, piece in enumerate(pieces):
        x = piece[...].astype(jnp.float32)
        x = jnp.concatenate([x, x], axis=1)
        samples = x.shape[2]
        row = lax.broadcasted_iota(jnp.int32, x.shape, 1)
        lane = lax.broadcasted_iota(jnp.int32, x.shape, 2)
        earlier = row >= 4 if flip else row < 4
        sides = jnp.where(earlier, pltpu.roll(x, 1, 2), pltpu.roll(x, samples - 1, 2))
        sides = jnp.where(lane == jnp.where(earlier, 0, samples - 1), 0.0, sides)
        rest = jnp.where(row < 4, x, fill)
        table[pl.ds(n * tiles, tiles)] = jnp.concatenate([sides, rest], axis=1).astype(jnp.bfloat16)
    last, count = len(pieces) * tiles, table.shape[0]
    row = lax.broadcasted_iota(jnp.int32, (count - last, *table.shape[1:]), 1)
    table[pl.ds(last, count - last)] = jnp.where(row < 12, 0.0, fill).astype(jnp.bfloat16)


def act(y):
    t = jnp.tanh(y)
    q = 1.0 + t
    a = y * q
    return t, q, a


def lines_of(idx, own, halo, owners):
    lines = []
    for e in owners:
        line = []
        for r in range(4):
            held = own if r in (1, 2) else halo
            line += [None, None] if held is None else [held[idx[r, e]], held[idx[r, e] + 1]]
        lines.append(line)
    return lines


def stack(lines, traces, flip):
    return jnp.concatenate(
        [
            jnp.concatenate(
                [line[h + 1 + (2 - i if flip else i)] for line in lines for h in traces], axis=1
            )
            for i in range(3)
        ],
        axis=0,
    )


def pipeline(pieces, *stages):
    held = [None] * pieces
    for tick in range(pieces + len(stages) - 1):
        for behind in reversed(range(len(stages))):
            k = tick - behind
            if 0 <= k < pieces:
                held[k] = stages[behind](k, held[k])


def layer(w, inputs):
    t, q, a = act(jnp.dot(w[...], inputs, preferred_element_type=jnp.float32))
    return a, q + a * (1.0 - t)


def with_ones(a1):
    return jnp.concatenate([a1, jnp.ones((16, a1.shape[1]), jnp.bfloat16)], axis=0)


def forward_inner(
    group, blocked, slots, mine, w1, w2, own, a1_ref, a2_ref, d1_ref, d2_ref, idx, sem,
):
    owners = lax.axis_size("rec")

    def start():
        fill_table(own, (mine,), mine.shape[0], False, 1.0)

    def step(n, block):
        sub = group
        width = sub * 2 * mine.shape[2]

        def first(k, _):
            es = [n * group + k * sub + u for u in range(sub)]
            at = slice(k * width, (k + 1) * width)
            a, d = layer(w1, stack(lines_of(idx, own, None, es), (1, 2), False))
            a1_ref[block, :, at] = a.astype(jnp.bfloat16)
            d1_ref[block, :, at] = d
            return a.astype(jnp.bfloat16)

        def second(k, a1):
            at = slice(k * width, (k + 1) * width)
            a, d = layer(w2, with_ones(a1))
            a2_ref[block, :, at] = a.astype(jnp.bfloat16)
            d2_ref[block, :, at] = d

        pipeline(group // sub, first, second)

    run(start, step, lambda: None, owners // group, blocked, (slots, idx, sem))


def forward_outer(
    group, blocked, slots, near, mine, far, own, w1, w2, w3, inner,
    res, g, halo, a1_ref, a2_ref, d1_ref, d2_ref, est, idx, sem,
):
    tiles, parts, samples = mine.shape
    count = lax.axis_size("rec")
    me = lax.axis_index("rec")
    has_left = (me > 0).astype(jnp.float32)
    has_right = (me < count - 1).astype(jnp.float32)
    lane = lax.broadcasted_iota(jnp.int32, (8, samples), 1)
    low = (lane > 0).astype(jnp.float32)
    high = (lane < samples - 1).astype(jnp.float32)

    def start():
        fill_table(halo, (near, far), tiles, False, 1.0)

    def step(n, block):
        cut = lambda x, k: x[:, k * samples : (k + 1) * samples]

        sub = min(8, group)
        own_part = lambda x: jnp.concatenate(
            [x[:, (u * 4 + 1) * samples : (u * 4 + 3) * samples] for u in range(sub)], axis=1
        )
        width = sub * 2 * samples

        def first(k, _):
            lines = lines_of(idx, own, halo, [n * group + k * sub + u for u in range(sub)])
            at = slice(k * width, (k + 1) * width)
            a, d = layer(w1, stack(lines, (-1, 0, 3, 4), False))
            a1 = a.astype(jnp.bfloat16)
            a1_ref[block, :, at] = own_part(a1)
            d1_ref[block, :, at] = own_part(d)
            return a1

        def second(k, a1):
            at = slice(k * width, (k + 1) * width)
            a, d = layer(w2, with_ones(a1))
            d2_ref[block, :, at] = own_part(d)
            a2_ref[block, :, at] = own_part(a).astype(jnp.bfloat16)
            rows = []
            for u in range(sub):
                row = [cut(a, u * 4 + h) for h in range(4)]
                row = [row[0] * has_left, row[1], row[2], row[3] * has_right]
                row = [part.astype(jnp.bfloat16) for part in row]
                within = [cut(inner.at[block], (k * sub + u) * 2 + h) for h in range(2)]
                rows.append(row[0:2] + within + row[2:4])
            return rows

        def third(k, rows):
            rhs = [
                jnp.concatenate([part for row in rows for part in row[i : i + 4]], axis=1)
                for i in range(3)
            ]
            terms = jnp.dot(
                w3[...], jnp.concatenate(rhs, axis=0), preferred_element_type=jnp.float32
            )
            for h in range(sub * 4):
                part = cut(terms, h)
                total = (
                    part[8:16]
                    + pltpu.roll(part[0:8], 1, 1) * low
                    + pltpu.roll(part[16:24], samples - 1, 1) * high
                )
                at = (n * group + k * sub) * 4 + h
                est[at] = total.astype(jnp.bfloat16).astype(jnp.float32)

        pipeline(group // sub, first, second, third)

    def end():
        for c in range(tiles // 2):
            at = [idx[4 + v, tiles // 2 + c] for v in range(4)]
            for k in range(2):
                total = (est[at[0] + k] + est[at[1] + k]) + (est[at[2] + k] + est[at[3] + k])
                value = total[0:parts] - mine[c * 2 + k].astype(jnp.float32)
                for o in range(parts):
                    res[o, c, k : k + 1, :] = value[o : o + 1]
                g[c * 2 + k] = value.astype(jnp.bfloat16)

    run(start, step, end, count // group, blocked, (slots, idx, sem))


def weight_terms(acc, pieces, width, fields_of, inputs_of, wo, wm, saved):
    channels = wm.shape[0]
    a1, a2, d1, d2 = saved
    of = lambda ref, k: ref[:, k * width : (k + 1) * width]

    def first(k, _):
        fields = fields_of(k)
        da2 = jnp.dot(wo[...], fields, preferred_element_type=jnp.float32)
        acc[0:48, :] += product(fields, of(a2, k), (1, 1))
        return (da2 * of(d2, k)).astype(jnp.bfloat16)

    def second(k, dz2):
        da1 = jnp.dot(wm[...], dz2, preferred_element_type=jnp.float32)
        acc[48 : 64 + channels, :] += product(with_ones(of(a1, k)), dz2, (1, 1))
        return (da1 * of(d1, k)).astype(jnp.bfloat16)

    def third(k, dz1):
        acc[64 + channels : 112 + channels, :] += product(inputs_of(k), dz1, (1, 1))

    pipeline(pieces, first, second, third)


def backward_inner(
    group, blocked, slots, mine, wo, wm, own, a1_ref, a2_ref, d1_ref, d2_ref, gown, acc,
    idx, sem,
):
    owners = lax.axis_size("rec")

    def start():
        fill_table(gown, (mine,), mine.shape[0], True, 0.0)
        acc[...] = jnp.zeros_like(acc)

    def step(n, block):
        sub = group
        es = lambda k: [n * group + k * sub + u for u in range(sub)]
        weight_terms(
            acc, group // sub, sub * 2 * mine.shape[2],
            lambda k: stack(lines_of(idx, gown, None, es(k)), (1, 2), True),
            lambda k: stack(lines_of(idx, own, None, es(k)), (1, 2), False),
            wo, wm, [ref.at[block] for ref in (a1_ref, a2_ref, d1_ref, d2_ref)],
        )

    run(start, step, lambda: None, owners // group, blocked, (slots, idx, sem))


def backward_outer(
    group, blocked, slots, near, far, wo, wm, own, halo, gown, sums, a1_ref, a2_ref, d1_ref, d2_ref,
    out, ghalo, acc, idx, sem,
):
    owners = lax.axis_size("rec")
    channels = wm.shape[0]
    taps = 9 * near.shape[1]

    def start():
        fill_table(ghalo, (near, far), near.shape[0], True, 0.0)
        acc[...] = sums[...]

    def step(n, block):
        sub = group
        es = lambda k: [n * group + k * sub + u for u in range(sub)]
        weight_terms(
            acc, group // sub, sub * 2 * near.shape[2],
            lambda k: stack(lines_of(idx, gown, ghalo, es(k)), (0, 3), True),
            lambda k: stack(lines_of(idx, own, halo, es(k)), (0, 3), False),
            wo, wm, [ref.at[block] for ref in (a1_ref, a2_ref, d1_ref, d2_ref)],
        )

    def end():
        first, half = 64 + channels, channels // 2
        low, high = slice(0, channels), slice(channels, 2 * channels)
        for k in range(taps):
            at = k % 9 // 3 * 16 + k % 3 * 2 % 3 * 4 + k // 9
            out[half + k : half + k + 1, low] = acc[first + at : first + at + 1, :]
            out[half + k : half + k + 1, high] = acc[at : at + 1, :]
        middle = acc[48 : 48 + channels, :].T
        out[0:half, low] = middle[0:half]
        out[0:half, high] = middle[half:channels]
        out[half + taps : half + taps + 1, low] = acc[first + 28 : first + 29, :]
        out[half + taps : half + taps + 1, high] = acc[48 + channels : 49 + channels, :]
        rest = out.shape[0] - half - taps - 1
        out[half + taps + 1 :, :] = jnp.zeros((rest, 2 * channels), jnp.float32)

    run(start, step, end, owners // group, blocked, (slots, idx, sem))


def finish_kernel(scale, *refs):
    terms, (g_in, g_bin, g_mid, g_bmid, g_out, held) = refs[:-6], refs[-6:]
    values = [ref[...] for ref in terms]
    while len(values) > 1:
        values = [values[k] + values[k + 1] for k in range(0, len(values), 2)]
    held[...] = values[0] * scale
    channels = g_mid.shape[0]
    half, taps = channels // 2, g_in.shape[0]
    low, high = slice(0, channels), slice(channels, 2 * channels)
    g_mid[0:half] = held[0:half, low]
    g_mid[half:channels] = held[0:half, high]
    g_in[...] = held[half : half + taps, low]
    g_out[...] = held[half : half + taps, high]
    g_bin[...] = held[half + taps : half + taps + 1, low]
    g_bmid[...] = held[half + taps : half + taps + 1, high]


def halves(b):
    high = b.astype(jnp.bfloat16).astype(jnp.float32)
    rest = b - high
    mid = rest.astype(jnp.bfloat16).astype(jnp.float32)
    return [high, mid, rest - mid]


def one_hot(a, b):
    return (a == b).astype(jnp.float32).astype(jnp.bfloat16)


def iota(shape, dim):
    return lax.broadcasted_iota(jnp.int32, shape, dim)


def product(a, b, over):
    return lax.dot_general(
        a, b, dimension_numbers=(((over[0],), (over[1],)), ((), ())),
        preferred_element_type=jnp.float32,
    )


def prep_kernel(blocks, *refs):
    args, (idx, w1, w2, w3, wo, wm, rows), held, sems = refs[:6], refs[6:13], refs[13:19], refs[19]
    copies = [
        pltpu.make_async_copy(src, dst, sems.at[n]) for n, (src, dst) in enumerate(zip(args, held))
    ]
    for copy in copies:
        copy.start()
    for copy in copies:
        copy.wait()
    dest, w_in, b_in, w_mid, b_mid, w_out = held
    count = lax.axis_size("rec")
    me = lax.axis_index("rec")
    ves, total = dest.shape
    channels = w_mid.shape[0]
    at = lax.rem((count + 1 - me) * blocks, total)
    wide = jnp.concatenate([dest[...], jnp.zeros((8 - ves, total), jnp.int32)], axis=0)
    near = pltpu.roll(wide, at, 1)[:, 0:128]
    lane = iota((8, 128), 1)
    low = jnp.where(me > 0, 0, blocks)
    high = jnp.where(me < count - 1, 3 * blocks, 2 * blocks)
    near = jnp.where((lane >= low) & (lane < high), near, -1)
    owner = iota((count, 128), 0)
    hits = [(near[v : v + 1] == owner).astype(jnp.float32) for v in range(ves)]
    before = iota((128, 128), 0)
    after = iota((128, 128), 1)
    segment = (after >= blocks).astype(jnp.int32) + (after >= 2 * blocks).astype(jnp.int32)
    tri = ((before < after) & (before >= segment * blocks)).astype(jnp.float32).astype(jnp.bfloat16)
    rank = product((hits[0] + hits[1] + hits[2] + hits[3]).astype(jnp.bfloat16), tri, (1, 0))
    zeroth = jnp.zeros((count, 128), jnp.float32)
    first = jnp.zeros((count, 128), jnp.float32)
    for v in range(ves):
        zeroth += hits[v] * (rank == 0.0).astype(jnp.float32)
        first += hits[v] * (rank == 1.0).astype(jnp.float32)
        item = jnp.sum(hits[v] * rank, axis=0, keepdims=True)
        idx[4 + v : 5 + v, 0:128] = near[v : v + 1] * 4 + item.astype(jnp.int32) * 2
        rank = rank + hits[v]
    line = iota((8, 128), 0)
    inside = lambda k: (lane >= k * blocks) & (lane < (k + 1) * blocks)
    odd = lax.rem(me, 2)
    left = 2 * lane + 2 * blocks * (1 - odd) - 4 * blocks
    middle = 2 * (lane - blocks) - 2 * blocks
    right = 2 * (lane - 2 * blocks) + 2 * blocks * odd - 4 * blocks
    put = lambda r, k, place: jnp.where((line == r) & inside(k), place, 0)
    pick = product(
        (put(0, 0, left) + put(2, 1, middle)).astype(jnp.float32).astype(jnp.bfloat16),
        first.astype(jnp.bfloat16),
        (1, 1),
    ) + product(
        (put(1, 1, middle) + put(3, 2, right)).astype(jnp.float32).astype(jnp.bfloat16),
        zeroth.astype(jnp.bfloat16),
        (1, 1),
    )
    empty = jnp.where((line == 0) | (line == 3), 4 * blocks, 2 * blocks)[0:4, 0:1]
    idx[0:4, 0:count] = pick[0:4].astype(jnp.int32) + empty

    taps = w_in.shape[0]
    row, col = iota((48, 40), 0), iota((48, 40), 1)
    tap, extra = row & 15, (row & 15) - 12
    place = (row >> 2) & 3
    target = (row & 3) * 9 + 3 * (row >> 4) + jnp.where(place == 0, 0, 3 - place)
    target = jnp.where(tap < 12, target, jnp.where((row >> 4) == 1, taps + extra, -1))
    order = one_hot(col, target)
    rows[...] = jnp.zeros_like(rows)
    rows[0:taps, :] = w_in[...].astype(jnp.float32)
    for n, part in enumerate(halves(b_in[...])):
        rows[taps + n : taps + n + 1, :] = part
    w1[...] = (0.5 * product(rows[...].astype(jnp.bfloat16), order, (0, 1))).astype(jnp.bfloat16)
    rows[...] = jnp.zeros_like(rows)
    for n, part in enumerate(halves(b_mid[...])):
        rows[n : n + 1, :] = part
    row, col = iota((40, channels + 16), 0), iota((40, channels + 16), 1)
    bias = product(rows[...].astype(jnp.bfloat16), one_hot(col, row + channels), (0, 0))
    row, col = iota((channels, channels + 16), 0), iota((channels, channels + 16), 1)
    w2[...] = (0.5 * (product(w_mid[...], one_hot(row, col), (1, 0)) + bias)).astype(jnp.bfloat16)
    rows[...] = jnp.zeros_like(rows)
    rows[0:taps, :] = w_out[...].astype(jnp.float32)
    outs = rows[...].astype(jnp.bfloat16)
    wo[...] = (0.5 * product(outs, order, (0, 1))).astype(jnp.bfloat16)
    row, col = iota((24, 40), 0), iota((24, 40), 1)
    for i in range(3):
        target = jnp.where((row & 7) < 4, (row & 3) * 9 + 3 * i + (row >> 3), -1)
        part = product(one_hot(col, target), outs, (1, 0))
        w3[:, i * channels : (i + 1) * channels] = part.astype(jnp.bfloat16)
    eye = one_hot(iota((channels, channels), 0), iota((channels, channels), 1))
    wm[...] = (0.5 * product(w_mid[...], eye, (0, 0))).astype(jnp.bfloat16)


def local(records, dest, w_in, b_in, w_mid, b_mid, w_out):
    count = lax.axis_size("rec")
    me = lax.axis_index("rec")
    parts, blocks, traces, samples = records.shape
    ves = dest.shape[1]
    tiles = blocks * traces
    channels = w_in.shape[0]
    group = group_of(count)
    steps = count // group
    width = group * 2 * samples
    far = [(s, (s + 1) % count) for s in range(1, count, 2)]
    far += [(b, a) for a, b in far]
    near = [(s, s + 1) for s in range(0, count - 1, 2)]
    near += [(b, a) for a, b in near]

    flat = records.transpose(1, 2, 0, 3).reshape(tiles, parts, samples)
    from_far = lax.ppermute(flat, "rec", far)
    from_near = lax.ppermute(flat, "rec", near)

    f32, bf16 = jnp.float32, jnp.bfloat16
    shape = (steps, channels, width)
    blocked = 24 * math.prod(shape) > RESIDENT
    saved = [
        jax.ShapeDtypeStruct(shape, kind) if blocked else pltpu.VMEM(shape, kind)
        for kind in (bf16, bf16, f32, f32)
    ]
    held = [VMEM] * 4
    if blocked:
        held = [pl.BlockSpec((1, channels, width), lambda n: (n, 0, 0))] * 4
    grid = (steps,) if blocked else ()
    params = pltpu.CompilerParams(vmem_limit_bytes=16 << 20)
    args = (
        dest.T, w_in.T, b_in.reshape(1, channels), w_mid, b_mid.reshape(1, channels), w_out.T
    )
    idx, w1, w2, w3, wo, wm = pl.pallas_call(
        functools.partial(prep_kernel, blocks),
        out_shape=[jax.ShapeDtypeStruct((8, max(128, count)), jnp.int32)]
        + [
            jax.ShapeDtypeStruct(size, bf16)
            for size in (
                (channels, 48), (channels, channels + 16), (24, 3 * channels), (channels, 48),
                (channels, channels),
            )
        ],
        in_specs=[pl.BlockSpec(memory_space=pltpu.HBM)] * 6,
        out_specs=[VMEM] * 6,
        scratch_shapes=[pltpu.VMEM((40, channels), f32)]
        + [pltpu.VMEM(arg.shape, arg.dtype) for arg in args]
        + [pltpu.SemaphoreType.DMA((6,))],
        compiler_params=params,
        name="prepare",
    )(*[pltpu.with_memory_space_constraint(arg, pltpu.HBM) for arg in args])
    def table(pieces, kind):
        return pltpu.VMEM((pieces * tiles + 2, 16, samples), kind)

    def call(kernel, ins, outs, scratch, args, name, owned):
        return pl.pallas_call(
            functools.partial(kernel, group, blocked),
            grid=grid,
            out_shape=outs[0] + saved * outs[1],
            in_specs=[VMEM] * (1 + ins[0]) + held[:1] * ins[1],
            out_specs=[VMEM] * len(outs[0]) + held * outs[1],
            scratch_shapes=scratch + [pltpu.SMEM(idx.shape, idx.dtype), pltpu.SemaphoreType.DMA],
            compiler_params=params,
            cost_estimate=pl.CostEstimate(
                flops=2 * owned * count * samples * channels * (3 * channels),
                bytes_accessed=owned * count * samples * channels * 12,
                transcendentals=0,
            ),
            name=name,
        )(*args)

    total = (112 + channels, channels)
    rows = (channels // 2 + 9 * parts + 1 + 7) // 8 * 8
    own, *inner = call(
        forward_inner, (3, 0), ([table(1, bf16)], 1), [],
        (idx, flat, w1, w2), "forward_inner", 2,
    )
    res, g, halo, *outer = call(
        forward_outer, (7, 1),
        (
            [
                jax.ShapeDtypeStruct(records.shape, f32),
                jax.ShapeDtypeStruct((tiles, parts, samples), bf16),
                table(2, bf16),
            ],
            1,
        ),
        [pltpu.VMEM((count * 4, 8, samples), f32)],
        (idx, from_near, flat, from_far, own, w1, w2, w3, inner[1]), "forward_outer", 4,
    )
    g_far = lax.ppermute(g, "rec", far)
    g_near = lax.ppermute(g, "rec", near)
    gown, part = call(
        backward_inner, (4, 4), ([table(1, bf16), pltpu.VMEM(total, f32)], 0), [],
        (idx, g, wo, wm, own, *inner), "backward_inner", 2,
    )
    (sums,) = call(
        backward_outer, (8, 4), ([jax.ShapeDtypeStruct((rows, 2 * channels), f32)], 0),
        [table(2, bf16), pltpu.VMEM(total, f32)],
        (idx, g_near, g_far, wo, wm, own, halo, gown, part, *outer), "backward_outer", 2,
    )

    if count & (count - 1):
        terms = [lax.psum(sums, "rec")]
    else:
        terms = [sums]
        at = 1
        while at < count:
            wide = 4 if at > 1 and 4 * at <= count else 2
            value = terms[0]
            if len(terms) == 2:
                value = terms[0] + terms[1]
            if len(terms) == 4:
                value = (terms[0] + terms[1]) + (terms[2] + terms[3])
            terms = [value] + [
                lax.ppermute(value, "rec", [(s, s ^ (k * at)) for s in range(count)])
                for k in range(1, wide)
            ]
            at *= wide

    scale = 1.0 / math.sqrt(parts * blocks * count * traces * samples)
    g_in, g_bin, g_mid, g_bmid, g_out = pl.pallas_call(
        functools.partial(finish_kernel, scale),
        out_shape=[
            jax.ShapeDtypeStruct(shape, f32)
            for shape in (
                (parts * 9, channels), (1, channels), (channels, channels), (1, channels),
                (parts * 9, channels),
            )
        ],
        in_specs=[VMEM] * len(terms),
        out_specs=[VMEM] * 5,
        scratch_shapes=[pltpu.VMEM(sums.shape, f32)],
        compiler_params=params,
        name="finish",
    )(*terms)
    return (
        res,
        g_in.T,
        g_bin.reshape(channels),
        g_mid,
        g_bmid.reshape(channels),
        g_out.T,
    )


def solution(mesh):
    return jax.shard_map(
        local,
        mesh=mesh,
        in_specs=(
            P(None, ("groups", "rec"), None, None),
            P("groups", None),
            P(),
            P(),
            P(),
            P(),
            P(),
        ),
        out_specs=(
            P(None, ("groups", "rec"), None, None),
            P("groups", None),
            P("groups"),
            P("groups", None),
            P("groups"),
            P("groups", None),
        ),
        check_vma=False,
    )
```

```python
import functools
import math

import jax
import jax.numpy as jnp
from jax import lax
from jax.experimental import pallas as pl
from jax.experimental.pallas import tpu as pltpu
from jax.sharding import PartitionSpec as P

CAP = 2
VMEM = pl.BlockSpec(memory_space=pltpu.VMEM)
RESIDENT = 24 << 20


def run(start, step, end, steps, blocked, table):
    copy = pltpu.make_async_copy(*table)

    def begin():
        copy.start()
        start()
        copy.wait()

    if blocked:
        n = pl.program_id(0)
        pl.when(n == 0)(begin)
        step(n, 0)
        pl.when(n == steps - 1)(end)
        return
    begin()
    lax.fori_loop(0, steps, lambda n, carry: step(n, n), None)
    end()


def group_of(owners):
    for size in (32, 16, 8, 4, 2):
        if owners % size == 0:
            return size
    return 1


def fill_table(table, pieces, tiles, flip, fill):
    for n, piece in enumerate(pieces):
        x = piece[...].astype(jnp.float32)
        x = jnp.concatenate([x, x], axis=1)
        samples = x.shape[2]
        row = lax.broadcasted_iota(jnp.int32, x.shape, 1)
        lane = lax.broadcasted_iota(jnp.int32, x.shape, 2)
        earlier = row >= 4 if flip else row < 4
        sides = jnp.where(earlier, pltpu.roll(x, 1, 2), pltpu.roll(x, samples - 1, 2))
        sides = jnp.where(lane == jnp.where(earlier, 0, samples - 1), 0.0, sides)
        rest = jnp.where(row < 4, x, fill)
        table[pl.ds(n * tiles, tiles)] = jnp.concatenate([sides, rest], axis=1).astype(jnp.bfloat16)
    last, count = len(pieces) * tiles, table.shape[0]
    row = lax.broadcasted_iota(jnp.int32, (count - last, *table.shape[1:]), 1)
    table[pl.ds(last, count - last)] = jnp.where(row < 12, 0.0, fill).astype(jnp.bfloat16)


def act(y):
    t = jnp.tanh(y)
    q = 1.0 + t
    a = y * q
    return t, q, a


def far_of(within, across):
    size = math.gcd(lax.axis_size("rec"), 8)
    at = lax.rem(lax.axis_index("rec"), size)
    end = ((at == 0) | (at == size - 1)).astype(jnp.float32)
    x, y = within[...].astype(jnp.float32), across[...].astype(jnp.float32)
    return jnp.where(jnp.full(x.shape, end) > 0.0, y, x)


def lines_of(idx, own, halo, owners):
    lines = []
    for e in owners:
        line = []
        for r in range(4):
            held = own if r in (1, 2) else halo
            line += [None, None] if held is None else [held[idx[r, e]], held[idx[r, e] + 1]]
        lines.append(line)
    return lines


def stack(lines, traces, flip):
    return jnp.concatenate(
        [
            jnp.concatenate(
                [line[h + 1 + (2 - i if flip else i)] for line in lines for h in traces], axis=1
            )
            for i in range(3)
        ],
        axis=0,
    )


def pipeline(pieces, *stages):
    held = [None] * pieces
    for tick in range(pieces + len(stages) - 1):
        for behind in reversed(range(len(stages))):
            k = tick - behind
            if 0 <= k < pieces:
                held[k] = stages[behind](k, held[k])


def layer(w, inputs):
    t, q, a = act(jnp.dot(w[...], inputs, preferred_element_type=jnp.float32))
    return a, q + a * (1.0 - t)


def with_ones(a1):
    return jnp.concatenate([a1, jnp.ones((16, a1.shape[1]), jnp.bfloat16)], axis=0)


def forward_inner(
    group, blocked, slots, mine, w1, w2, own, a1_ref, a2_ref, d1_ref, d2_ref, idx, sem,
):
    owners = lax.axis_size("rec")

    def start():
        fill_table(own, (mine,), mine.shape[0], False, 1.0)

    def step(n, block):
        sub = group
        width = sub * 2 * mine.shape[2]

        def first(k, _):
            es = [n * group + k * sub + u for u in range(sub)]
            at = slice(k * width, (k + 1) * width)
            a, d = layer(w1, stack(lines_of(idx, own, None, es), (1, 2), False))
            a1_ref[block, :, at] = a.astype(jnp.bfloat16)
            d1_ref[block, :, at] = d
            return a.astype(jnp.bfloat16)

        def second(k, a1):
            at = slice(k * width, (k + 1) * width)
            a, d = layer(w2, with_ones(a1))
            a2_ref[block, :, at] = a.astype(jnp.bfloat16)
            d2_ref[block, :, at] = d

        pipeline(group // sub, first, second)

    run(start, step, lambda: None, owners // group, blocked, (slots, idx, sem))


def forward_outer(
    group, blocked, slots, near, mine, far, across, own, w1, w2, w3, inner,
    res, g, halo, a1_ref, a2_ref, d1_ref, d2_ref, est, idx, sem,
):
    tiles, parts, samples = mine.shape
    count = lax.axis_size("rec")
    me = lax.axis_index("rec")
    has_left = (me > 0).astype(jnp.float32)
    has_right = (me < count - 1).astype(jnp.float32)
    lane = lax.broadcasted_iota(jnp.int32, (8, samples), 1)
    low = (lane > 0).astype(jnp.float32)
    high = (lane < samples - 1).astype(jnp.float32)

    def start():
        fill_table(halo, (near, far_of(far, across)), tiles, False, 1.0)

    def step(n, block):
        cut = lambda x, k: x[:, k * samples : (k + 1) * samples]

        sub = min(8, group)
        own_part = lambda x: jnp.concatenate(
            [x[:, (u * 4 + 1) * samples : (u * 4 + 3) * samples] for u in range(sub)], axis=1
        )
        width = sub * 2 * samples

        def first(k, _):
            lines = lines_of(idx, own, halo, [n * group + k * sub + u for u in range(sub)])
            at = slice(k * width, (k + 1) * width)
            a, d = layer(w1, stack(lines, (-1, 0, 3, 4), False))
            a1 = a.astype(jnp.bfloat16)
            a1_ref[block, :, at] = own_part(a1)
            d1_ref[block, :, at] = own_part(d)
            return a1

        def second(k, a1):
            at = slice(k * width, (k + 1) * width)
            a, d = layer(w2, with_ones(a1))
            d2_ref[block, :, at] = own_part(d)
            a2_ref[block, :, at] = own_part(a).astype(jnp.bfloat16)
            rows = []
            for u in range(sub):
                row = [cut(a, u * 4 + h) for h in range(4)]
                row = [row[0] * has_left, row[1], row[2], row[3] * has_right]
                row = [part.astype(jnp.bfloat16) for part in row]
                within = [cut(inner.at[block], (k * sub + u) * 2 + h) for h in range(2)]
                rows.append(row[0:2] + within + row[2:4])
            return rows

        def third(k, rows):
            rhs = [
                jnp.concatenate([part for row in rows for part in row[i : i + 4]], axis=1)
                for i in range(3)
            ]
            terms = jnp.dot(
                w3[...], jnp.concatenate(rhs, axis=0), preferred_element_type=jnp.float32
            )
            for h in range(sub * 4):
                part = cut(terms, h)
                total = (
                    part[8:16]
                    + pltpu.roll(part[0:8], 1, 1) * low
                    + pltpu.roll(part[16:24], samples - 1, 1) * high
                )
                at = (n * group + k * sub) * 4 + h
                est[at] = total.astype(jnp.bfloat16).astype(jnp.float32)

        pipeline(group // sub, first, second, third)

    def end():
        for c in range(tiles // 2):
            at = [idx[4 + v, tiles // 2 + c] for v in range(4)]
            for k in range(2):
                total = (est[at[0] + k] + est[at[1] + k]) + (est[at[2] + k] + est[at[3] + k])
                value = total[0:parts] - mine[c * 2 + k].astype(jnp.float32)
                for o in range(parts):
                    res[o, c, k : k + 1, :] = value[o : o + 1]
                g[c * 2 + k] = value.astype(jnp.bfloat16)

    run(start, step, end, count // group, blocked, (slots, idx, sem))


def weight_terms(acc, pieces, width, fields_of, inputs_of, wo, wm, saved):
    channels = wm.shape[0]
    a1, a2, d1, d2 = saved
    of = lambda ref, k: ref[:, k * width : (k + 1) * width]

    def first(k, _):
        fields = fields_of(k)
        da2 = jnp.dot(wo[...], fields, preferred_element_type=jnp.float32)
        acc[0:48, :] += product(fields, of(a2, k), (1, 1))
        return (da2 * of(d2, k)).astype(jnp.bfloat16)

    def second(k, dz2):
        da1 = jnp.dot(wm[...], dz2, preferred_element_type=jnp.float32)
        acc[48 : 64 + channels, :] += product(with_ones(of(a1, k)), dz2, (1, 1))
        return (da1 * of(d1, k)).astype(jnp.bfloat16)

    def third(k, dz1):
        acc[64 + channels : 112 + channels, :] += product(inputs_of(k), dz1, (1, 1))

    pipeline(pieces, first, second, third)


def backward_inner(
    group, blocked, slots, mine, wo, wm, own, a1_ref, a2_ref, d1_ref, d2_ref, gown, acc,
    idx, sem,
):
    owners = lax.axis_size("rec")

    def start():
        fill_table(gown, (mine,), mine.shape[0], True, 0.0)
        acc[...] = jnp.zeros_like(acc)

    def step(n, block):
        sub = group
        es = lambda k: [n * group + k * sub + u for u in range(sub)]
        weight_terms(
            acc, group // sub, sub * 2 * mine.shape[2],
            lambda k: stack(lines_of(idx, gown, None, es(k)), (1, 2), True),
            lambda k: stack(lines_of(idx, own, None, es(k)), (1, 2), False),
            wo, wm, [ref.at[block] for ref in (a1_ref, a2_ref, d1_ref, d2_ref)],
        )

    run(start, step, lambda: None, owners // group, blocked, (slots, idx, sem))


def backward_outer(
    group, blocked, slots, near, far, across, wo, wm, own, halo, gown, sums, a1_ref, a2_ref, d1_ref, d2_ref,
    out, ghalo, acc, idx, sem,
):
    owners = lax.axis_size("rec")
    channels = wm.shape[0]
    taps = 9 * near.shape[1]

    def start():
        fill_table(ghalo, (near, far_of(far, across)), near.shape[0], True, 0.0)
        acc[...] = sums[...]

    def step(n, block):
        sub = group
        es = lambda k: [n * group + k * sub + u for u in range(sub)]
        weight_terms(
            acc, group // sub, sub * 2 * near.shape[2],
            lambda k: stack(lines_of(idx, gown, ghalo, es(k)), (0, 3), True),
            lambda k: stack(lines_of(idx, own, halo, es(k)), (0, 3), False),
            wo, wm, [ref.at[block] for ref in (a1_ref, a2_ref, d1_ref, d2_ref)],
        )

    def end():
        first, half = 64 + channels, channels // 2
        low, high = slice(0, channels), slice(channels, 2 * channels)
        for k in range(taps):
            at = k % 9 // 3 * 16 + k % 3 * 2 % 3 * 4 + k // 9
            out[half + k : half + k + 1, low] = acc[first + at : first + at + 1, :]
            out[half + k : half + k + 1, high] = acc[at : at + 1, :]
        middle = acc[48 : 48 + channels, :].T
        out[0:half, low] = middle[0:half]
        out[0:half, high] = middle[half:channels]
        out[half + taps : half + taps + 1, low] = acc[first + 28 : first + 29, :]
        out[half + taps : half + taps + 1, high] = acc[48 + channels : 49 + channels, :]
        rest = out.shape[0] - half - taps - 1
        out[half + taps + 1 :, :] = jnp.zeros((rest, 2 * channels), jnp.float32)

    run(start, step, end, owners // group, blocked, (slots, idx, sem))


def finish_kernel(scale, *refs):
    terms, (g_in, g_bin, g_mid, g_bmid, g_out, held) = refs[:-6], refs[-6:]
    values = [ref[...] for ref in terms]
    while len(values) > 1:
        values = [values[k] + values[k + 1] for k in range(0, len(values), 2)]
    held[...] = values[0] * scale
    channels = g_mid.shape[0]
    half, taps = channels // 2, g_in.shape[0]
    low, high = slice(0, channels), slice(channels, 2 * channels)
    g_mid[0:half] = held[0:half, low]
    g_mid[half:channels] = held[0:half, high]
    g_in[...] = held[half : half + taps, low]
    g_out[...] = held[half : half + taps, high]
    g_bin[...] = held[half + taps : half + taps + 1, low]
    g_bmid[...] = held[half + taps : half + taps + 1, high]


def halves(b):
    high = b.astype(jnp.bfloat16).astype(jnp.float32)
    rest = b - high
    mid = rest.astype(jnp.bfloat16).astype(jnp.float32)
    return [high, mid, rest - mid]


def one_hot(a, b):
    return (a == b).astype(jnp.float32).astype(jnp.bfloat16)


def iota(shape, dim):
    return lax.broadcasted_iota(jnp.int32, shape, dim)


def product(a, b, over):
    return lax.dot_general(
        a, b, dimension_numbers=(((over[0],), (over[1],)), ((), ())),
        preferred_element_type=jnp.float32,
    )


def prep_kernel(blocks, *refs):
    args, (idx, w1, w2, w3, wo, wm, rows), held, sems = refs[:6], refs[6:13], refs[13:19], refs[19]
    copies = [
        pltpu.make_async_copy(src, dst, sems.at[n]) for n, (src, dst) in enumerate(zip(args, held))
    ]
    for copy in copies:
        copy.start()
    for copy in copies:
        copy.wait()
    dest, w_in, b_in, w_mid, b_mid, w_out = held
    count = lax.axis_size("rec")
    me = lax.axis_index("rec")
    ves, total = dest.shape
    channels = w_mid.shape[0]
    at = lax.rem((count + 1 - me) * blocks, total)
    wide = jnp.concatenate([dest[...], jnp.zeros((8 - ves, total), jnp.int32)], axis=0)
    near = pltpu.roll(wide, at, 1)[:, 0:128]
    lane = iota((8, 128), 1)
    low = jnp.where(me > 0, 0, blocks)
    high = jnp.where(me < count - 1, 3 * blocks, 2 * blocks)
    near = jnp.where((lane >= low) & (lane < high), near, -1)
    owner = iota((count, 128), 0)
    hits = [(near[v : v + 1] == owner).astype(jnp.float32) for v in range(ves)]
    before = iota((128, 128), 0)
    after = iota((128, 128), 1)
    segment = (after >= blocks).astype(jnp.int32) + (after >= 2 * blocks).astype(jnp.int32)
    tri = ((before < after) & (before >= segment * blocks)).astype(jnp.float32).astype(jnp.bfloat16)
    rank = product((hits[0] + hits[1] + hits[2] + hits[3]).astype(jnp.bfloat16), tri, (1, 0))
    zeroth = jnp.zeros((count, 128), jnp.float32)
    first = jnp.zeros((count, 128), jnp.float32)
    for v in range(ves):
        zeroth += hits[v] * (rank == 0.0).astype(jnp.float32)
        first += hits[v] * (rank == 1.0).astype(jnp.float32)
        item = jnp.sum(hits[v] * rank, axis=0, keepdims=True)
        idx[4 + v : 5 + v, 0:128] = near[v : v + 1] * 4 + item.astype(jnp.int32) * 2
        rank = rank + hits[v]
    line = iota((8, 128), 0)
    inside = lambda k: (lane >= k * blocks) & (lane < (k + 1) * blocks)
    odd = lax.rem(me, 2)
    left = 2 * lane + 2 * blocks * (1 - odd) - 4 * blocks
    middle = 2 * (lane - blocks) - 2 * blocks
    right = 2 * (lane - 2 * blocks) + 2 * blocks * odd - 4 * blocks
    put = lambda r, k, place: jnp.where((line == r) & inside(k), place, 0)
    pick = product(
        (put(0, 0, left) + put(2, 1, middle)).astype(jnp.float32).astype(jnp.bfloat16),
        first.astype(jnp.bfloat16),
        (1, 1),
    ) + product(
        (put(1, 1, middle) + put(3, 2, right)).astype(jnp.float32).astype(jnp.bfloat16),
        zeroth.astype(jnp.bfloat16),
        (1, 1),
    )
    empty = jnp.where((line == 0) | (line == 3), 4 * blocks, 2 * blocks)[0:4, 0:1]
    idx[0:4, 0:count] = pick[0:4].astype(jnp.int32) + empty

    taps = w_in.shape[0]
    row, col = iota((48, 40), 0), iota((48, 40), 1)
    tap, extra = row & 15, (row & 15) - 12
    place = (row >> 2) & 3
    target = (row & 3) * 9 + 3 * (row >> 4) + jnp.where(place == 0, 0, 3 - place)
    target = jnp.where(tap < 12, target, jnp.where((row >> 4) == 1, taps + extra, -1))
    order = one_hot(col, target)
    rows[...] = jnp.zeros_like(rows)
    rows[0:taps, :] = w_in[...].astype(jnp.float32)
    for n, part in enumerate(halves(b_in[...])):
        rows[taps + n : taps + n + 1, :] = part
    w1[...] = (0.5 * product(rows[...].astype(jnp.bfloat16), order, (0, 1))).astype(jnp.bfloat16)
    rows[...] = jnp.zeros_like(rows)
    for n, part in enumerate(halves(b_mid[...])):
        rows[n : n + 1, :] = part
    row, col = iota((40, channels + 16), 0), iota((40, channels + 16), 1)
    bias = product(rows[...].astype(jnp.bfloat16), one_hot(col, row + channels), (0, 0))
    row, col = iota((channels, channels + 16), 0), iota((channels, channels + 16), 1)
    w2[...] = (0.5 * (product(w_mid[...], one_hot(row, col), (1, 0)) + bias)).astype(jnp.bfloat16)
    rows[...] = jnp.zeros_like(rows)
    rows[0:taps, :] = w_out[...].astype(jnp.float32)
    outs = rows[...].astype(jnp.bfloat16)
    wo[...] = (0.5 * product(outs, order, (0, 1))).astype(jnp.bfloat16)
    row, col = iota((24, 40), 0), iota((24, 40), 1)
    for i in range(3):
        target = jnp.where((row & 7) < 4, (row & 3) * 9 + 3 * i + (row >> 3), -1)
        part = product(one_hot(col, target), outs, (1, 0))
        w3[:, i * channels : (i + 1) * channels] = part.astype(jnp.bfloat16)
    eye = one_hot(iota((channels, channels), 0), iota((channels, channels), 1))
    wm[...] = (0.5 * product(w_mid[...], eye, (0, 0))).astype(jnp.bfloat16)


def local(records, dest, w_in, b_in, w_mid, b_mid, w_out):
    count = lax.axis_size("rec")
    me = lax.axis_index("rec")
    parts, blocks, traces, samples = records.shape
    ves = dest.shape[1]
    tiles = blocks * traces
    channels = w_in.shape[0]
    group = group_of(count)
    steps = count // group
    width = group * 2 * samples
    size = math.gcd(count, 8)
    within = [(r + k, r + k + 1) for r in range(0, count, size) for k in range(1, size - 1, 2)]
    within += [(r, r + size - 1) for r in range(0, count, size)]
    within += [(b, a) for a, b in within]
    across = [(r - 1 - k, r + k) for r in range(size, count, size) for k in range(2)]
    taken = {s for pair in across for s in pair}
    across += [(s, s + 1) for s in range(0, count, 2) if s not in taken]
    across += [(b, a) for a, b in across]
    near = [(s, s + 1) for s in range(0, count - 1, 2)]
    near += [(b, a) for a, b in near]

    flat = records.transpose(1, 2, 0, 3).reshape(tiles, parts, samples)
    from_across = lax.ppermute(flat, "rec", across)
    from_within = lax.ppermute(flat, "rec", within)
    from_near = lax.ppermute(flat, "rec", near)

    f32, bf16 = jnp.float32, jnp.bfloat16
    shape = (steps, channels, width)
    blocked = 24 * math.prod(shape) > RESIDENT
    saved = [
        jax.ShapeDtypeStruct(shape, kind) if blocked else pltpu.VMEM(shape, kind)
        for kind in (bf16, bf16, f32, f32)
    ]
    held = [VMEM] * 4
    if blocked:
        held = [pl.BlockSpec((1, channels, width), lambda n: (n, 0, 0))] * 4
    grid = (steps,) if blocked else ()
    params = pltpu.CompilerParams(vmem_limit_bytes=16 << 20)
    args = (
        dest.T, w_in.T, b_in.reshape(1, channels), w_mid, b_mid.reshape(1, channels), w_out.T
    )
    idx, w1, w2, w3, wo, wm = pl.pallas_call(
        functools.partial(prep_kernel, blocks),
        out_shape=[jax.ShapeDtypeStruct((8, max(128, count)), jnp.int32)]
        + [
            jax.ShapeDtypeStruct(size, bf16)
            for size in (
                (channels, 48), (channels, channels + 16), (24, 3 * channels), (channels, 48),
                (channels, channels),
            )
        ],
        in_specs=[pl.BlockSpec(memory_space=pltpu.HBM)] * 6,
        out_specs=[VMEM] * 6,
        scratch_shapes=[pltpu.VMEM((40, channels), f32)]
        + [pltpu.VMEM(arg.shape, arg.dtype) for arg in args]
        + [pltpu.SemaphoreType.DMA((6,))],
        compiler_params=params,
        name="prepare",
    )(*[pltpu.with_memory_space_constraint(arg, pltpu.HBM) for arg in args])
    def table(pieces, kind):
        return pltpu.VMEM((pieces * tiles + 2, 16, samples), kind)

    def call(kernel, ins, outs, scratch, args, name, owned):
        return pl.pallas_call(
            functools.partial(kernel, group, blocked),
            grid=grid,
            out_shape=outs[0] + saved * outs[1],
            in_specs=[VMEM] * (1 + ins[0]) + held[:1] * ins[1],
            out_specs=[VMEM] * len(outs[0]) + held * outs[1],
            scratch_shapes=scratch + [pltpu.SMEM(idx.shape, idx.dtype), pltpu.SemaphoreType.DMA],
            compiler_params=params,
            cost_estimate=pl.CostEstimate(
                flops=2 * owned * count * samples * channels * (3 * channels),
                bytes_accessed=owned * count * samples * channels * 12,
                transcendentals=0,
            ),
            name=name,
        )(*args)

    total = (112 + channels, channels)
    rows = (channels // 2 + 9 * parts + 1 + 7) // 8 * 8
    own, *inner = call(
        forward_inner, (3, 0), ([table(1, bf16)], 1), [],
        (idx, flat, w1, w2), "forward_inner", 2,
    )
    res, g, halo, *outer = call(
        forward_outer, (8, 1),
        (
            [
                jax.ShapeDtypeStruct(records.shape, f32),
                jax.ShapeDtypeStruct((tiles, parts, samples), bf16),
                table(2, bf16),
            ],
            1,
        ),
        [pltpu.VMEM((count * 4, 8, samples), f32)],
        (idx, from_near, flat, from_within, from_across, own, w1, w2, w3, inner[1]), "forward_outer", 4,
    )
    g_across = lax.ppermute(g, "rec", across)
    g_within = lax.ppermute(g, "rec", within)
    g_near = lax.ppermute(g, "rec", near)
    gown, part = call(
        backward_inner, (4, 4), ([table(1, bf16), pltpu.VMEM(total, f32)], 0), [],
        (idx, g, wo, wm, own, *inner), "backward_inner", 2,
    )
    (sums,) = call(
        backward_outer, (9, 4), ([jax.ShapeDtypeStruct((rows, 2 * channels), f32)], 0),
        [table(2, bf16), pltpu.VMEM(total, f32)],
        (idx, g_near, g_within, g_across, wo, wm, own, halo, gown, part, *outer), "backward_outer", 2,
    )

    if count & (count - 1):
        terms = [lax.psum(sums, "rec")]
    else:
        terms = [sums]
        at = 1
        while at < count:
            wide = 4 if at > 1 and 4 * at <= count else 2
            value = terms[0]
            if len(terms) == 2:
                value = terms[0] + terms[1]
            if len(terms) == 4:
                value = (terms[0] + terms[1]) + (terms[2] + terms[3])
            terms = [value] + [
                lax.ppermute(value, "rec", [(s, s ^ (k * at)) for s in range(count)])
                for k in range(1, wide)
            ]
            at *= wide

    scale = 1.0 / math.sqrt(parts * blocks * count * traces * samples)
    g_in, g_bin, g_mid, g_bmid, g_out = pl.pallas_call(
        functools.partial(finish_kernel, scale),
        out_shape=[
            jax.ShapeDtypeStruct(shape, f32)
            for shape in (
                (parts * 9, channels), (1, channels), (channels, channels), (1, channels),
                (parts * 9, channels),
            )
        ],
        in_specs=[VMEM] * len(terms),
        out_specs=[VMEM] * 5,
        scratch_shapes=[pltpu.VMEM(sums.shape, f32)],
        compiler_params=params,
        name="finish",
    )(*terms)
    return (
        res,
        g_in.T,
        g_bin.reshape(channels),
        g_mid,
        g_bmid.reshape(channels),
        g_out.T,
    )


def solution(mesh):
    return jax.shard_map(
        local,
        mesh=mesh,
        in_specs=(
            P(None, ("groups", "rec"), None, None),
            P("groups", None),
            P(),
            P(),
            P(),
            P(),
            P(),
        ),
        out_specs=(
            P(None, ("groups", "rec"), None, None),
            P("groups", None),
            P("groups"),
            P("groups", None),
            P("groups"),
            P("groups", None),
        ),
        check_vma=False,
    )
```

```python
import functools
import math

import jax
import jax.numpy as jnp
from jax import lax
from jax.experimental import pallas as pl
from jax.experimental.pallas import tpu as pltpu
from jax.sharding import PartitionSpec as P

CAP = 2
VMEM = pl.BlockSpec(memory_space=pltpu.VMEM)
RESIDENT = 24 << 20


def run(start, step, end, steps, blocked, table):
    copy = pltpu.make_async_copy(*table)

    def begin():
        copy.start()
        start()
        copy.wait()

    if blocked:
        n = pl.program_id(0)
        pl.when(n == 0)(begin)
        step(n, 0)
        pl.when(n == steps - 1)(end)
        return
    begin()
    lax.fori_loop(0, steps, lambda n, carry: step(n, n), None)
    end()


def group_of(owners):
    for size in (32, 16, 8, 4, 2):
        if owners % size == 0:
            return size
    return 1


def fill_table(table, pieces, tiles, flip, fill):
    for n, piece in enumerate(pieces):
        x = piece[...].astype(jnp.float32)
        x = jnp.concatenate([x, x], axis=1)
        samples = x.shape[2]
        row = lax.broadcasted_iota(jnp.int32, x.shape, 1)
        lane = lax.broadcasted_iota(jnp.int32, x.shape, 2)
        earlier = row >= 4 if flip else row < 4
        sides = jnp.where(earlier, pltpu.roll(x, 1, 2), pltpu.roll(x, samples - 1, 2))
        sides = jnp.where(lane == jnp.where(earlier, 0, samples - 1), 0.0, sides)
        rest = jnp.where(row < 4, x, fill)
        table[pl.ds(n * tiles, tiles)] = jnp.concatenate([sides, rest], axis=1).astype(jnp.bfloat16)
    last, count = len(pieces) * tiles, table.shape[0]
    row = lax.broadcasted_iota(jnp.int32, (count - last, *table.shape[1:]), 1)
    table[pl.ds(last, count - last)] = jnp.where(row < 12, 0.0, fill).astype(jnp.bfloat16)


def act(y):
    t = jnp.tanh(y)
    q = 1.0 + t
    a = y * q
    return t, q, a


def far_of(within, across):
    size = math.gcd(lax.axis_size("rec"), 8)
    at = lax.rem(lax.axis_index("rec"), size)
    end = ((at == 0) | (at == size - 1)).astype(jnp.float32)
    x, y = within[...].astype(jnp.float32), across[...].astype(jnp.float32)
    return jnp.where(jnp.full(x.shape, end) > 0.0, y, x)


def lines_of(idx, own, halo, owners):
    lines = []
    for e in owners:
        line = []
        for r in range(4):
            held = own if r in (1, 2) else halo
            line += [None, None] if held is None else [held[idx[r, e]], held[idx[r, e] + 1]]
        lines.append(line)
    return lines


def stack(lines, traces, flip):
    return jnp.concatenate(
        [
            jnp.concatenate(
                [line[h + 1 + (2 - i if flip else i)] for line in lines for h in traces], axis=1
            )
            for i in range(3)
        ],
        axis=0,
    )


def pipeline(pieces, *stages):
    held = [None] * pieces
    for tick in range(pieces + len(stages) - 1):
        for behind in reversed(range(len(stages))):
            k = tick - behind
            if 0 <= k < pieces:
                held[k] = stages[behind](k, held[k])


def layer(w, inputs):
    t, q, a = act(jnp.dot(w[...], inputs, preferred_element_type=jnp.float32))
    return a, q + a * (1.0 - t)


def with_ones(a1):
    return jnp.concatenate([a1, jnp.ones((16, a1.shape[1]), jnp.bfloat16)], axis=0)


def forward_inner(
    group, blocked, slots, mine, w1, w2, own, a1_ref, a2_ref, d1_ref, d2_ref, idx, sem,
):
    owners = lax.axis_size("rec")

    def start():
        fill_table(own, (mine,), mine.shape[0], False, 1.0)

    def step(n, block):
        sub = group
        width = sub * 2 * mine.shape[2]

        def first(k, _):
            es = [n * group + k * sub + u for u in range(sub)]
            at = slice(k * width, (k + 1) * width)
            a, d = layer(w1, stack(lines_of(idx, own, None, es), (1, 2), False))
            a1_ref[block, :, at] = a.astype(jnp.bfloat16)
            d1_ref[block, :, at] = d
            return a.astype(jnp.bfloat16)

        def second(k, a1):
            at = slice(k * width, (k + 1) * width)
            a, d = layer(w2, with_ones(a1))
            a2_ref[block, :, at] = a.astype(jnp.bfloat16)
            d2_ref[block, :, at] = d

        pipeline(group // sub, first, second)

    run(start, step, lambda: None, owners // group, blocked, (slots, idx, sem))


def forward_outer(
    group, blocked, slots, near, mine, far, across, own, w1, w2, w3, inner,
    res, g, halo, a1_ref, a2_ref, d1_ref, d2_ref, est, idx, sem,
):
    tiles, parts, samples = mine.shape
    count = lax.axis_size("rec")
    me = lax.axis_index("rec")
    has_left = (me > 0).astype(jnp.float32)
    has_right = (me < count - 1).astype(jnp.float32)
    lane = lax.broadcasted_iota(jnp.int32, (8, samples), 1)
    low = (lane > 0).astype(jnp.float32)
    high = (lane < samples - 1).astype(jnp.float32)

    def start():
        fill_table(halo, (near, far_of(far, across)), tiles, False, 1.0)

    def step(n, block):
        cut = lambda x, k: x[:, k * samples : (k + 1) * samples]

        sub = min(8, group)
        own_part = lambda x: jnp.concatenate(
            [x[:, (u * 4 + 1) * samples : (u * 4 + 3) * samples] for u in range(sub)], axis=1
        )
        width = sub * 2 * samples

        def first(k, _):
            lines = lines_of(idx, own, halo, [n * group + k * sub + u for u in range(sub)])
            at = slice(k * width, (k + 1) * width)
            a, d = layer(w1, stack(lines, (-1, 0, 3, 4), False))
            a1 = a.astype(jnp.bfloat16)
            a1_ref[block, :, at] = own_part(a1)
            d1_ref[block, :, at] = own_part(d)
            return a1

        def second(k, a1):
            at = slice(k * width, (k + 1) * width)
            a, d = layer(w2, with_ones(a1))
            d2_ref[block, :, at] = own_part(d)
            a2_ref[block, :, at] = own_part(a).astype(jnp.bfloat16)
            rows = []
            for u in range(sub):
                row = [cut(a, u * 4 + h) for h in range(4)]
                row = [row[0] * has_left, row[1], row[2], row[3] * has_right]
                row = [part.astype(jnp.bfloat16) for part in row]
                within = [cut(inner.at[block], (k * sub + u) * 2 + h) for h in range(2)]
                rows.append(row[0:2] + within + row[2:4])
            return rows

        def third(k, rows):
            rhs = [
                jnp.concatenate([part for row in rows for part in row[i : i + 4]], axis=1)
                for i in range(3)
            ]
            terms = jnp.dot(
                w3[...], jnp.concatenate(rhs, axis=0), preferred_element_type=jnp.float32
            )
            for h in range(sub * 4):
                part = cut(terms, h)
                total = (
                    part[8:16]
                    + pltpu.roll(part[0:8], 1, 1) * low
                    + pltpu.roll(part[16:24], samples - 1, 1) * high
                )
                at = (n * group + k * sub) * 4 + h
                est[at] = total.astype(jnp.bfloat16).astype(jnp.float32)

        pipeline(group // sub, first, second, third)

    def end():
        for c in range(tiles // 2):
            at = [idx[4 + v, tiles // 2 + c] for v in range(4)]
            for k in range(2):
                total = (est[at[0] + k] + est[at[1] + k]) + (est[at[2] + k] + est[at[3] + k])
                value = total[0:parts] - mine[c * 2 + k].astype(jnp.float32)
                for o in range(parts):
                    res[o, c, k : k + 1, :] = value[o : o + 1]
                g[c * 2 + k] = value.astype(jnp.bfloat16)

    run(start, step, end, count // group, blocked, (slots, idx, sem))


def weight_terms(acc, pieces, width, fields_of, inputs_of, wo, wm, saved):
    channels = wm.shape[0]
    a1, a2, d1, d2 = saved
    of = lambda ref, k: ref[:, k * width : (k + 1) * width]

    def first(k, _):
        fields = fields_of(k)
        da2 = jnp.dot(wo[...], fields, preferred_element_type=jnp.float32)
        acc[0:48, :] += product(fields, of(a2, k), (1, 1))
        return (da2 * of(d2, k)).astype(jnp.bfloat16)

    def second(k, dz2):
        da1 = jnp.dot(wm[...], dz2, preferred_element_type=jnp.float32)
        acc[48 : 64 + channels, :] += product(with_ones(of(a1, k)), dz2, (1, 1))
        return (da1 * of(d1, k)).astype(jnp.bfloat16)

    def third(k, dz1):
        acc[64 + channels : 112 + channels, :] += product(inputs_of(k), dz1, (1, 1))

    pipeline(pieces, first, second, third)


def backward_inner(
    group, blocked, slots, mine, wo, wm, own, a1_ref, a2_ref, d1_ref, d2_ref, gown, acc,
    idx, sem,
):
    owners = lax.axis_size("rec")

    def start():
        fill_table(gown, (mine,), mine.shape[0], True, 0.0)
        acc[...] = jnp.zeros_like(acc)

    def step(n, block):
        sub = group
        es = lambda k: [n * group + k * sub + u for u in range(sub)]
        weight_terms(
            acc, group // sub, sub * 2 * mine.shape[2],
            lambda k: stack(lines_of(idx, gown, None, es(k)), (1, 2), True),
            lambda k: stack(lines_of(idx, own, None, es(k)), (1, 2), False),
            wo, wm, [ref.at[block] for ref in (a1_ref, a2_ref, d1_ref, d2_ref)],
        )

    run(start, step, lambda: None, owners // group, blocked, (slots, idx, sem))


def backward_outer(
    group, blocked, slots, near, far, across, wo, wm, own, halo, gown, sums, a1_ref, a2_ref, d1_ref, d2_ref,
    out, ghalo, acc, idx, sem,
):
    owners = lax.axis_size("rec")
    channels = wm.shape[0]
    taps = 9 * near.shape[1]

    def start():
        fill_table(ghalo, (near, far_of(far, across)), near.shape[0], True, 0.0)
        acc[...] = sums[...]

    def step(n, block):
        sub = group
        es = lambda k: [n * group + k * sub + u for u in range(sub)]
        weight_terms(
            acc, group // sub, sub * 2 * near.shape[2],
            lambda k: stack(lines_of(idx, gown, ghalo, es(k)), (0, 3), True),
            lambda k: stack(lines_of(idx, own, halo, es(k)), (0, 3), False),
            wo, wm, [ref.at[block] for ref in (a1_ref, a2_ref, d1_ref, d2_ref)],
        )

    def end():
        first, half = 64 + channels, channels // 2
        low, high = slice(0, channels), slice(channels, 2 * channels)
        for k in range(taps):
            at = k % 9 // 3 * 16 + k % 3 * 2 % 3 * 4 + k // 9
            out[half + k : half + k + 1, low] = acc[first + at : first + at + 1, :]
            out[half + k : half + k + 1, high] = acc[at : at + 1, :]
        middle = acc[48 : 48 + channels, :].T
        out[0:half, low] = middle[0:half]
        out[0:half, high] = middle[half:channels]
        out[half + taps : half + taps + 1, low] = acc[first + 28 : first + 29, :]
        out[half + taps : half + taps + 1, high] = acc[48 + channels : 49 + channels, :]
        rest = out.shape[0] - half - taps - 1
        out[half + taps + 1 :, :] = jnp.zeros((rest, 2 * channels), jnp.float32)

    run(start, step, end, owners // group, blocked, (slots, idx, sem))


def finish_kernel(scale, *refs):
    terms, (g_in, g_bin, g_mid, g_bmid, g_out, held) = refs[:-6], refs[-6:]
    values = [ref[...] for ref in terms]
    while len(values) > 1:
        values = [values[k] + values[k + 1] for k in range(0, len(values), 2)]
    held[...] = values[0] * scale
    channels = g_mid.shape[0]
    half, taps = channels // 2, g_in.shape[0]
    low, high = slice(0, channels), slice(channels, 2 * channels)
    g_mid[0:half] = held[0:half, low]
    g_mid[half:channels] = held[0:half, high]
    g_in[...] = held[half : half + taps, low]
    g_out[...] = held[half : half + taps, high]
    g_bin[...] = held[half + taps : half + taps + 1, low]
    g_bmid[...] = held[half + taps : half + taps + 1, high]


def halves(b):
    high = b.astype(jnp.bfloat16).astype(jnp.float32)
    rest = b - high
    mid = rest.astype(jnp.bfloat16).astype(jnp.float32)
    return [high, mid, rest - mid]


def one_hot(a, b):
    return (a == b).astype(jnp.float32).astype(jnp.bfloat16)


def iota(shape, dim):
    return lax.broadcasted_iota(jnp.int32, shape, dim)


def product(a, b, over):
    return lax.dot_general(
        a, b, dimension_numbers=(((over[0],), (over[1],)), ((), ())),
        preferred_element_type=jnp.float32,
    )


def prep_kernel(blocks, *refs):
    args, (idx, w1, w2, w3, wo, wm, rows), held, sems = refs[:6], refs[6:13], refs[13:19], refs[19]
    copies = [
        pltpu.make_async_copy(src, dst, sems.at[n]) for n, (src, dst) in enumerate(zip(args, held))
    ]
    for copy in copies:
        copy.start()
    for copy in copies:
        copy.wait()
    dest, w_in, b_in, w_mid, b_mid, w_out = held
    count = lax.axis_size("rec")
    me = lax.axis_index("rec")
    ves, total = dest.shape
    channels = w_mid.shape[0]
    at = lax.rem((count + 1 - me) * blocks, total)
    wide = jnp.concatenate([dest[...], jnp.zeros((8 - ves, total), jnp.int32)], axis=0)
    near = pltpu.roll(wide, at, 1)[:, 0:128]
    lane = iota((8, 128), 1)
    low = jnp.where(me > 0, 0, blocks)
    high = jnp.where(me < count - 1, 3 * blocks, 2 * blocks)
    near = jnp.where((lane >= low) & (lane < high), near, -1)
    owner = iota((count, 128), 0)
    hits = [(near[v : v + 1] == owner).astype(jnp.float32) for v in range(ves)]
    before = iota((128, 128), 0)
    after = iota((128, 128), 1)
    segment = (after >= blocks).astype(jnp.int32) + (after >= 2 * blocks).astype(jnp.int32)
    tri = ((before < after) & (before >= segment * blocks)).astype(jnp.float32).astype(jnp.bfloat16)
    rank = product((hits[0] + hits[1] + hits[2] + hits[3]).astype(jnp.bfloat16), tri, (1, 0))
    zeroth = jnp.zeros((count, 128), jnp.float32)
    first = jnp.zeros((count, 128), jnp.float32)
    for v in range(ves):
        zeroth += hits[v] * (rank == 0.0).astype(jnp.float32)
        first += hits[v] * (rank == 1.0).astype(jnp.float32)
        item = jnp.sum(hits[v] * rank, axis=0, keepdims=True)
        idx[4 + v : 5 + v, 0:128] = near[v : v + 1] * 4 + item.astype(jnp.int32) * 2
        rank = rank + hits[v]
    line = iota((8, 128), 0)
    inside = lambda k: (lane >= k * blocks) & (lane < (k + 1) * blocks)
    odd = lax.rem(me, 2)
    left = 2 * lane + 2 * blocks * (1 - odd) - 4 * blocks
    middle = 2 * (lane - blocks) - 2 * blocks
    right = 2 * (lane - 2 * blocks) + 2 * blocks * odd - 4 * blocks
    put = lambda r, k, place: jnp.where((line == r) & inside(k), place, 0)
    pick = product(
        (put(0, 0, left) + put(2, 1, middle)).astype(jnp.float32).astype(jnp.bfloat16),
        first.astype(jnp.bfloat16),
        (1, 1),
    ) + product(
        (put(1, 1, middle) + put(3, 2, right)).astype(jnp.float32).astype(jnp.bfloat16),
        zeroth.astype(jnp.bfloat16),
        (1, 1),
    )
    empty = jnp.where((line == 0) | (line == 3), 4 * blocks, 2 * blocks)[0:4, 0:1]
    idx[0:4, 0:count] = pick[0:4].astype(jnp.int32) + empty

    taps = w_in.shape[0]
    row, col = iota((48, 40), 0), iota((48, 40), 1)
    tap, extra = row & 15, (row & 15) - 12
    place = (row >> 2) & 3
    target = (row & 3) * 9 + 3 * (row >> 4) + jnp.where(place == 0, 0, 3 - place)
    target = jnp.where(tap < 12, target, jnp.where((row >> 4) == 1, taps + extra, -1))
    order = one_hot(col, target)
    rows[...] = jnp.zeros_like(rows)
    rows[0:taps, :] = w_in[...].astype(jnp.float32)
    for n, part in enumerate(halves(b_in[...])):
        rows[taps + n : taps + n + 1, :] = part
    w1[...] = (0.5 * product(rows[...].astype(jnp.bfloat16), order, (0, 1))).astype(jnp.bfloat16)
    rows[...] = jnp.zeros_like(rows)
    for n, part in enumerate(halves(b_mid[...])):
        rows[n : n + 1, :] = part
    row, col = iota((40, channels + 16), 0), iota((40, channels + 16), 1)
    bias = product(rows[...].astype(jnp.bfloat16), one_hot(col, row + channels), (0, 0))
    row, col = iota((channels, channels + 16), 0), iota((channels, channels + 16), 1)
    w2[...] = (0.5 * (product(w_mid[...], one_hot(row, col), (1, 0)) + bias)).astype(jnp.bfloat16)
    rows[...] = jnp.zeros_like(rows)
    rows[0:taps, :] = w_out[...].astype(jnp.float32)
    outs = rows[...].astype(jnp.bfloat16)
    wo[...] = (0.5 * product(outs, order, (0, 1))).astype(jnp.bfloat16)
    row, col = iota((24, 40), 0), iota((24, 40), 1)
    for i in range(3):
        target = jnp.where((row & 7) < 4, (row & 3) * 9 + 3 * i + (row >> 3), -1)
        part = product(one_hot(col, target), outs, (1, 0))
        w3[:, i * channels : (i + 1) * channels] = part.astype(jnp.bfloat16)
    eye = one_hot(iota((channels, channels), 0), iota((channels, channels), 1))
    wm[...] = (0.5 * product(w_mid[...], eye, (0, 0))).astype(jnp.bfloat16)


def local(records, dest, w_in, b_in, w_mid, b_mid, w_out):
    count = lax.axis_size("rec")
    me = lax.axis_index("rec")
    parts, blocks, traces, samples = records.shape
    ves = dest.shape[1]
    tiles = blocks * traces
    channels = w_in.shape[0]
    group = group_of(count)
    steps = count // group
    width = group * 2 * samples
    size = math.gcd(count, 8)
    within = [(r + k, r + k + 1) for r in range(0, count, size) for k in range(1, size - 1, 2)]
    within += [(r, r + size - 1) for r in range(0, count, size)]
    within += [(b, a) for a, b in within]
    across = [(r - 1 - k, r + k) for r in range(size, count, size) for k in range(2)]
    taken = {s for pair in across for s in pair}
    across += [(s, s + 1) for s in range(0, count, 2) if s not in taken]
    across += [(b, a) for a, b in across]
    near = [(s, s + 1) for s in range(0, count - 1, 2)]
    near += [(b, a) for a, b in near]

    flat = records.transpose(1, 2, 0, 3).reshape(tiles, parts, samples)
    from_across = lax.ppermute(flat, "rec", across)
    from_within = lax.ppermute(flat, "rec", within)
    from_near = lax.ppermute(flat, "rec", near)

    f32, bf16 = jnp.float32, jnp.bfloat16
    shape = (steps, channels, width)
    blocked = 24 * math.prod(shape) > RESIDENT
    saved = [
        jax.ShapeDtypeStruct(shape, kind) if blocked else pltpu.VMEM(shape, kind)
        for kind in (bf16, bf16, f32, f32)
    ]
    held = [VMEM] * 4
    if blocked:
        held = [pl.BlockSpec((1, channels, width), lambda n: (n, 0, 0))] * 4
    grid = (steps,) if blocked else ()
    params = pltpu.CompilerParams(vmem_limit_bytes=16 << 20)
    args = (
        dest.T, w_in.T, b_in.reshape(1, channels), w_mid, b_mid.reshape(1, channels), w_out.T
    )
    idx, w1, w2, w3, wo, wm = pl.pallas_call(
        functools.partial(prep_kernel, blocks),
        out_shape=[jax.ShapeDtypeStruct((8, max(128, count)), jnp.int32)]
        + [
            jax.ShapeDtypeStruct(size, bf16)
            for size in (
                (channels, 48), (channels, channels + 16), (24, 3 * channels), (channels, 48),
                (channels, channels),
            )
        ],
        in_specs=[pl.BlockSpec(memory_space=pltpu.HBM)] * 6,
        out_specs=[VMEM] * 6,
        scratch_shapes=[pltpu.VMEM((40, channels), f32)]
        + [pltpu.VMEM(arg.shape, arg.dtype) for arg in args]
        + [pltpu.SemaphoreType.DMA((6,))],
        compiler_params=params,
        name="prepare",
    )(*[pltpu.with_memory_space_constraint(arg, pltpu.HBM) for arg in args])
    def table(pieces, kind):
        return pltpu.VMEM((pieces * tiles + 2, 16, samples), kind)

    def call(kernel, ins, outs, scratch, args, name, owned):
        return pl.pallas_call(
            functools.partial(kernel, group, blocked),
            grid=grid,
            out_shape=outs[0] + saved * outs[1],
            in_specs=[VMEM] * (1 + ins[0]) + held[:1] * ins[1],
            out_specs=[VMEM] * len(outs[0]) + held * outs[1],
            scratch_shapes=scratch + [pltpu.SMEM(idx.shape, idx.dtype), pltpu.SemaphoreType.DMA],
            compiler_params=params,
            cost_estimate=pl.CostEstimate(
                flops=2 * owned * count * samples * channels * (3 * channels),
                bytes_accessed=owned * count * samples * channels * 12,
                transcendentals=0,
            ),
            name=name,
        )(*args)

    total = (112 + channels, channels)
    rows = (channels // 2 + 9 * parts + 1 + 7) // 8 * 8
    own, *inner = call(
        forward_inner, (3, 0), ([table(1, bf16)], 1), [],
        (idx, flat, w1, w2), "forward_inner", 2,
    )
    res, g, halo, *outer = call(
        forward_outer, (8, 1),
        (
            [
                jax.ShapeDtypeStruct(records.shape, f32),
                jax.ShapeDtypeStruct((tiles, parts, samples), bf16),
                table(2, bf16),
            ],
            1,
        ),
        [pltpu.VMEM((count * 4, 8, samples), f32)],
        (idx, from_near, flat, from_within, from_across, own, w1, w2, w3, inner[1]), "forward_outer", 4,
    )
    g_within = lax.ppermute(g, "rec", within)
    g_across = lax.ppermute(g, "rec", across)
    g_near = lax.ppermute(g, "rec", near)
    gown, part = call(
        backward_inner, (4, 4), ([table(1, bf16), pltpu.VMEM(total, f32)], 0), [],
        (idx, g, wo, wm, own, *inner), "backward_inner", 2,
    )
    (sums,) = call(
        backward_outer, (9, 4), ([jax.ShapeDtypeStruct((rows, 2 * channels), f32)], 0),
        [table(2, bf16), pltpu.VMEM(total, f32)],
        (idx, g_near, g_within, g_across, wo, wm, own, halo, gown, part, *outer), "backward_outer", 2,
    )

    if count & (count - 1):
        terms = [lax.psum(sums, "rec")]
    else:
        terms = [sums]
        at = 1
        while at < count:
            wide = 4 if at > 1 and 4 * at <= count else 2
            value = terms[0]
            if len(terms) == 2:
                value = terms[0] + terms[1]
            if len(terms) == 4:
                value = (terms[0] + terms[1]) + (terms[2] + terms[3])
            terms = [value] + [
                lax.ppermute(value, "rec", [(s, s ^ (k * at)) for s in range(count)])
                for k in range(1, wide)
            ]
            at *= wide

    scale = 1.0 / math.sqrt(parts * blocks * count * traces * samples)
    g_in, g_bin, g_mid, g_bmid, g_out = pl.pallas_call(
        functools.partial(finish_kernel, scale),
        out_shape=[
            jax.ShapeDtypeStruct(shape, f32)
            for shape in (
                (parts * 9, channels), (1, channels), (channels, channels), (1, channels),
                (parts * 9, channels),
            )
        ],
        in_specs=[VMEM] * len(terms),
        out_specs=[VMEM] * 5,
        scratch_shapes=[pltpu.VMEM(sums.shape, f32)],
        compiler_params=params,
        name="finish",
    )(*terms)
    return (
        res,
        g_in.T,
        g_bin.reshape(channels),
        g_mid,
        g_bmid.reshape(channels),
        g_out.T,
    )


def solution(mesh):
    return jax.shard_map(
        local,
        mesh=mesh,
        in_specs=(
            P(None, ("groups", "rec"), None, None),
            P("groups", None),
            P(),
            P(),
            P(),
            P(),
            P(),
        ),
        out_specs=(
            P(None, ("groups", "rec"), None, None),
            P("groups", None),
            P("groups"),
            P("groups", None),
            P("groups"),
            P("groups", None),
        ),
        check_vma=False,
    )
```
